32 devices in a mesh: dp: 4 (over z), expert: 8 (over y, x, core).
Axes of the slice: x: 2, y: 2, z: 4, core: 2. Of those that a mesh axis runs over, the one named last changes fastest.
Arguments:
- tokens: bfloat16 [4096, 1024], P(('dp', 'expert')), may hold values from -6 to 6
- segments: int32 [32, 128], P(('dp', 'expert')), may hold values from 0 to 7, never falling along the last dimension, each value on 1 to 32 neighbouring positions
- routes: int32 [4096, 8], P(('dp', 'expert')), may hold values from 0 to 31, all different within a row; in each aligned block of 128 rows (0 to 127, 128 to 255, ...) at most 40 rows name the same one
- query_weight: bfloat16 [1024, 1024], P(('dp', 'expert')), may hold values from -0.1875 to 0.1875
- keyval_weight: bfloat16 [1024, 1024], P(('dp', 'expert')), may hold values from -0.1875 to 0.1875
- output_weight: bfloat16 [1024, 1024], P(('dp', 'expert')), may hold values from -0.5 to 0.5
- router_weight: bfloat16 [1024, 32], P(('dp', 'expert')), may hold values from -0.09375 to 0.09375
- attn_gain: bfloat16 [1024], P(('dp', 'expert')), may hold values from 0.5 to 1.5
- moe_gain: bfloat16 [1024], P(('dp', 'expert')), may hold values from 0.5 to 1.5
- expert_up: bfloat16 [32, 1024, 1024], P('expert'), may hold values from -0.1875 to 0.1875
- expert_down: bfloat16 [32, 1024, 512], P('expert'), may hold values from -0.75 to 0.75
- out_grad: bfloat16 [4096, 1024], P(('dp', 'expert')), may hold values from -6 to 6
Outputs:
- layer_out: bfloat16 [4096, 1024], P(('dp', 'expert'))
- tokens_grad: float32 [4096, 1024], P(('dp', 'expert'))
- query_weight_grad: float32 [1024, 1024], P(('dp', 'expert'))
- keyval_weight_grad: float32 [1024, 1024], P(('dp', 'expert'))
- output_weight_grad: float32 [1024, 1024], P(('dp', 'expert'))
- router_weight_grad: float32 [1024, 32], P(('dp', 'expert'))
- attn_gain_grad: float32 [1024], P(('dp', 'expert'))
- moe_gain_grad: float32 [1024], P(('dp', 'expert'))
- expert_up_grad: float32 [32, 1024, 1024], P('expert', 'dp')
- expert_down_grad: float32 [32, 1024, 512], P('expert', 'dp')
The draws below stay inside these ranges and needn't reach their ends.
Inputs may be any that keep to these rules, and one draw needn't show every extreme that they name: `segments`: along each row segment numbers never fall; a segment spans 1 to 32 positions, and in every draw some segment spans exactly that many. `routes`: each token names 8 different experts. Among the 128 tokens of one device no expert is named more than 40 times, and in every draw some expert is named exactly 40 times by the tokens of some device.
All inputs are finite; a program needn't handle non-finite values.
Results may differ from the reference program's by a relative error of at most 0.018.
Values may be sent and summed in bfloat16 or wider, within the bound.
No kernel may reach another device: no remote copies, remote signals or barrier semaphores. Data moves between devices by JAX's collectives and lax.ppermute only.
A program may use at most 128 MiB of HBM per device.

```python
import math
import jax
import jax.numpy as jnp
import numpy as np
from jax import lax

D = 1024
HEADS = 16
KV_HEADS = 8
HEAD_DIM = 64
FF = 512
EXPERTS = 32
TOP = 8
TOK_DEV = 128
CAP = 40
TOKENS = 4096
DEVICES = 32


def strengthened(values, stream_key, source, target, shards_of, factor):
    owner, partner = [(jnp.arange(values.shape[axis_at]) // (values.shape[axis_at] // shards_of)).reshape([-1 if axis == axis_at else 1 for axis in range(values.ndim)]) for axis_at in (source, target)]
    chosen = jax.random.permutation(stream_key, shards_of)[partner]
    strong = (owner == chosen) | (owner == (partner + shards_of // 2) % shards_of)
    return jnp.where(strong, factor * values, values)


def level_of(stream_key, dims, shards, low, top_value):
    factor_of, own = 1.0, jax.random.fold_in(stream_key, 6)
    for dim, blocks in shards:
        heights = jnp.exp(jax.random.uniform(jax.random.fold_in(own, dim), (blocks,), jnp.float32, low / len(shards), top_value / len(shards)))
        factor_of = factor_of * jnp.repeat(heights, dims[dim] // blocks).reshape([-1 if axis == dim else 1 for axis in range(len(dims))])
    return factor_of


def profile(count, total, limit, skew):
    loads = [(1 << 20) // math.isqrt(rank ** skew) + 1 for rank in range(2, count + 1)]
    spare, given = total - limit - (count - 1), [1] * (count - 1)
    while spare > 0:
        candidates = [i for i in range(count - 1) if given[i] < limit]
        whole, remaining = sum([loads[i] for i in candidates]), spare
        for i in candidates:
            extra = min(limit - given[i], max(1, remaining * loads[i] // whole), spare)
            given[i] = given[i] + extra
            spare = spare - extra
    return np.array([limit] + given)


def ragged_sizes(stream_key, amount, total, most, slope):
    if amount == 2:
        one = jax.random.randint(stream_key, (), max(1, total - most), min(most, total - 1) + 1)
        return jnp.stack([one, total - one])
    sizes = jnp.asarray(profile(amount, total, most, slope), jnp.int32)
    couples = (amount - 1) // 2
    donor, receiver = sizes[1:1 + 2 * couples:2], sizes[2:2 + 2 * couples:2]
    slack = jnp.minimum(donor - 1, most - receiver)
    passed = jax.random.randint(jax.random.fold_in(stream_key, 1), (couples,), 0, 1 << 20) % (slack + 1)
    sizes = sizes.at[1:1 + 2 * couples:2].set(donor - passed).at[2:2 + 2 * couples:2].set(receiver + passed)
    return sizes[jax.random.permutation(jax.random.fold_in(stream_key, 2), amount)]


def routed_block(stream_key, own, number, rows, count, top, limit, skew):
    order = jax.random.permutation(stream_key, count)
    crowded, usual = portions_of(count, rows * top, limit, skew, True), portions_of(count, rows * top, limit, skew, False)
    places = jnp.arange(count)

    def named(tallies, offset_by):
        used = int((tallies > 0).sum())
        fixed = max(1, used // 4)
        passed = fixed + (places - fixed + offset_by * (used - fixed)) % max(1, count - fixed)
        return jnp.zeros((count,), jnp.int32).at[order[jnp.where(places < fixed, places, passed)]].set(jnp.asarray(tallies, jnp.int32))

    tallies = jnp.where(number % 4 == 0, named(crowded, number // 4), named(usual, number - number // 4 - 1))
    mixed = jax.random.permutation(jax.random.fold_in(own, 3), count)
    source_of, receiver = mixed[0:count // 2 * 2:2], mixed[1:count // 2 * 2:2]
    room = jnp.minimum(tallies[source_of] - 1, limit - tallies[receiver]) // 2
    room = jnp.where((source_of == order[0]) | (receiver == order[0]) | (tallies[receiver] == 0), 0, jnp.maximum(room, 0))
    passed = jax.random.randint(jax.random.fold_in(own, 4), (count // 2,), 0, 1 << 20) % (room + 1)
    tallies = tallies.at[source_of].add(-passed).at[receiver].add(passed)
    members = jnp.searchsorted(jnp.cumsum(tallies), jnp.arange(rows * top), side="right").astype(jnp.int32)
    listing = members.reshape(top, rows).T
    listing = listing[jax.random.permutation(jax.random.fold_in(own, 1), rows)]
    offset_by = jax.random.randint(jax.random.fold_in(own, 2), (rows, 1), 0, top)
    return jnp.take_along_axis(listing, (jnp.arange(top)[None, :] + offset_by) % top, axis=1)


def portions_of(amount, total, most, skew, full):
    portions = [(1 << 20) // math.isqrt(grade ** skew) + 1 for grade in range(1, amount + 1)]
    largest = most if full else min(most, max(-(-total // amount), total * portions[0] // sum(portions)))
    least = 1 if total - largest >= amount - 1 else 0
    given, spare = [largest] + [least] * (amount - 1), total - largest - least * (amount - 1)
    while spare > 0:
        candidates = [i for i in range(1, amount) if given[i] < largest] or [i for i in range(1, amount) if given[i] < most]
        mass, budget = sum([portions[i] for i in candidates]), spare
        for i in candidates:
            addition = min(most - given[i], max(1, budget * portions[i] // mass), spare)
            given[i] = given[i] + addition
            spare = spare - addition
    return np.array(given)


def scatter_about(key, dims, deviation, most, split=(), kind=jnp.bfloat16):
    gain = level_of(key, dims, split, -0.22, 0.18) if split else 1.0
    array = jax.random.normal(key, dims, jnp.float32) * deviation * gain
    return jnp.minimum(jnp.maximum(array, -most), most).astype(kind)


def heavy_noise(own_key, extent, spread, bound, pieces, heavy, kind=jnp.bfloat16):
    array = spread * jax.random.normal(own_key, extent, jnp.float32)
    if pieces:
        array = array * level_of(own_key, extent, pieces, -0.22, 0.18)
    return jnp.clip(strengthened(array, jax.random.fold_in(own_key, 3), *heavy), -bound, bound).astype(kind)


def setup_inputs(seed: int = 0) -> dict:
    key_of = jax.random.split(jax.random.key(seed), 13)
    tokens = heavy_noise(key_of[0], (TOKENS, D), 1.0, 6.0, ((0, 32),), (0, 1, 32, 2.75))
    segments = jax.vmap(lambda own: jnp.searchsorted(jnp.cumsum(ragged_sizes(own, 8, TOK_DEV, TOK_DEV // 4, 2)), jnp.arange(TOK_DEV), side="right"))(jax.random.split(key_of[1], DEVICES)).reshape((DEVICES, TOK_DEV)).astype(jnp.int32)
    routes_keys = jax.random.split(jax.random.fold_in(key_of[2], 1), TOKENS // TOK_DEV)
    routes_turns = jax.random.permutation(jax.random.fold_in(key_of[2], 3), TOKENS // TOK_DEV)
    routes = jax.vmap(lambda own, number: routed_block(jax.random.fold_in(key_of[2], 2), own, number, TOK_DEV, EXPERTS, TOP, CAP, 1))(routes_keys, routes_turns).reshape((TOKENS, TOP))
    query_weight = scatter_about(key_of[3], (D, HEADS * HEAD_DIM), D ** -0.5, 0.1875, ((0, 32),))
    keyval_weight = scatter_about(key_of[4], (D, 2 * KV_HEADS * HEAD_DIM), D ** -0.5, 0.1875, ((0, 32),))
    output_weight = scatter_about(key_of[5], (HEADS * HEAD_DIM, D), (HEADS * HEAD_DIM // 8) ** -0.5, 0.5, ((0, 32),))
    router_weight = scatter_about(key_of[6], (D, EXPERTS), (4 * D) ** -0.5, 0.09375, ((0, 32),))
    attn_gain = jnp.clip(1.0 + 0.1 * jax.random.normal(key_of[7], (D,), jnp.float32), 0.5, 1.5).astype(jnp.bfloat16)
    moe_gain = jnp.clip(1.0 + 0.1 * jax.random.normal(key_of[8], (D,), jnp.float32), 0.5, 1.5).astype(jnp.bfloat16)
    expert_up = scatter_about(key_of[9], (EXPERTS, D, 2 * FF), D ** -0.5, 0.1875, ((0, 8),))
    expert_down = scatter_about(key_of[10], (EXPERTS, D, FF), (FF // 8) ** -0.5, 0.75, ((0, 8),))
    out_grad = scatter_about(key_of[11], (TOKENS, D), 1.0, 6.0, ((0, 32),))
    return dict(tokens=tokens, segments=segments, routes=routes, query_weight=query_weight, keyval_weight=keyval_weight, output_weight=output_weight, router_weight=router_weight, attn_gain=attn_gain, moe_gain=moe_gain, expert_up=expert_up, expert_down=expert_down, out_grad=out_grad)


EPS = 1e-05
ROPE_BASE = 10000.0
MASKED = -1e+30
HIGH = lax.Precision.HIGHEST

@jax.custom_vjp
def low(v):
    return lax.optimization_barrier(v.astype(jnp.bfloat16)).astype(jnp.float32)

@jax.custom_vjp
def low_back(v):
    return v

def low_keep(v):
    return (low(v), None)

def low_pass(kept, grad):
    return (grad,)

def back_keep(v):
    return (v, None)

def back_low(kept, grad):
    return (low(grad),)
low.defvjp(low_keep, low_pass)
low_back.defvjp(back_keep, back_low)

def rotate(values, cosine, sine_table):
    half_dim = values.shape[-1] // 2
    turned = jnp.concatenate([-values[..., half_dim:], values[..., :half_dim]], axis=-1)
    return values * cosine + turned * sine_table

def rope_tables(segment_rows):
    length = segment_rows.shape[1]
    earlier = lax.optimization_barrier(jnp.sum((segment_rows[:, None, :] < segment_rows[:, :, None]).astype(jnp.int32), axis=-1))
    position = jnp.arange(length, dtype=jnp.int32)[None, :] - earlier
    half_dim = HEAD_DIM // 2
    frequency = ROPE_BASE ** (-(jnp.arange(half_dim, dtype=jnp.float32) * 2.0) / HEAD_DIM)
    angles = position.astype(jnp.float32)[..., None] * frequency
    cosine = jnp.concatenate([jnp.cos(angles), jnp.cos(angles)], axis=-1)
    sine_table = jnp.concatenate([jnp.sin(angles), jnp.sin(angles)], axis=-1)
    return (cosine[:, :, None, :], sine_table[:, :, None, :])

def layer_block(block_rows, segment_rows, route_rows, weights):
    query_weight, keyval_weight, output_weight, router_weight, attn_gain, moe_gain, expert_up, expert_down = weights
    rows_total = block_rows.shape[0]
    model_width = block_rows.shape[1]
    group_count = segment_rows.shape[0]
    length = segment_rows.shape[1]
    query_heads = query_weight.shape[1] // HEAD_DIM
    kv_heads = keyval_weight.shape[1] // (2 * HEAD_DIM)
    repeat = query_heads // kv_heads
    score_scale = HEAD_DIM ** (-0.5)
    inverse_one = lax.rsqrt(lax.optimization_barrier(jnp.mean(block_rows * block_rows, axis=-1, keepdims=True)) + EPS)
    attn_in = low(block_rows * inverse_one * attn_gain)
    query_proj = low_back(jnp.dot(attn_in, query_weight, precision=HIGH))
    keyval_proj = low_back(jnp.dot(attn_in, keyval_weight, precision=HIGH))
    query_proj = query_proj.reshape(group_count, length, query_heads, HEAD_DIM)
    key_rows = keyval_proj[:, :kv_heads * HEAD_DIM].reshape(group_count, length, kv_heads, HEAD_DIM)
    value_rows = keyval_proj[:, kv_heads * HEAD_DIM:].reshape(group_count, length, kv_heads, HEAD_DIM)
    cosine, sine_table = rope_tables(segment_rows)
    query_rot = low(rotate(query_proj, cosine, sine_table)).reshape(group_count, length, kv_heads, repeat, HEAD_DIM)
    keys_rot = low(rotate(key_rows, cosine, sine_table))
    values_low = low(value_rows)
    scores = low_back(jnp.einsum('gikrd,gjkd->gkrij', query_rot, keys_rot, precision=HIGH))
    places = jnp.arange(length)
    visible = (segment_rows[:, :, None] == segment_rows[:, None, :]) & (places[None, None, :] <= places[None, :, None])
    attn_logits = jnp.where(visible[:, None, None, :, :], scores * score_scale, MASKED)
    attn_exps = jnp.exp(attn_logits - lax.optimization_barrier(jnp.max(attn_logits, axis=-1, keepdims=True)))
    attn_probs = attn_exps / lax.optimization_barrier(jnp.sum(attn_exps, axis=-1, keepdims=True))
    mixed_heads = jnp.einsum('gkrij,gjkd->gikrd', low(attn_probs), values_low, precision=HIGH)
    mixed_heads = low(low_back(mixed_heads.reshape(rows_total, query_heads * HEAD_DIM)))
    hidden = block_rows + low_back(jnp.dot(mixed_heads, output_weight, precision=HIGH))
    inverse_two = lax.rsqrt(lax.optimization_barrier(jnp.mean(hidden * hidden, axis=-1, keepdims=True)) + EPS)
    moe_in = low(hidden * inverse_two * moe_gain)
    router_logits = jnp.dot(moe_in, router_weight, precision=HIGH)
    chosen = jnp.take_along_axis(router_logits, route_rows, axis=1)
    gate_exps = jnp.exp(chosen - lax.optimization_barrier(jnp.max(chosen, axis=-1, keepdims=True)))
    gate_probs = gate_exps / lax.optimization_barrier(jnp.sum(gate_exps, axis=-1, keepdims=True))
    entries = route_rows.reshape(-1)
    onehot = (entries[:, None] == jnp.arange(EXPERTS, dtype=jnp.int32)[None, :]).astype(jnp.int32)
    position = lax.optimization_barrier(jnp.sum((jnp.cumsum(onehot, axis=0) - 1) * onehot, axis=1)).astype(jnp.int32)
    capacity = group_count * CAP
    slot_index = (entries * capacity + position).astype(jnp.int32)
    routed = low_back(jnp.repeat(moe_in, TOP, axis=0))
    buffer = jnp.zeros((EXPERTS * capacity, model_width), dtype=block_rows.dtype).at[slot_index].set(routed)
    buffer = buffer.reshape(EXPERTS, capacity, model_width)
    pair_proj = low_back(jnp.einsum('ecd,edf->ecf', buffer, expert_up, precision=HIGH))
    activated = low(jax.nn.silu(pair_proj[..., :FF]) * pair_proj[..., FF:])
    expert_rows = low(low_back(jnp.einsum('ecf,edf->ecd', activated, expert_down, precision=HIGH)))
    gathered = expert_rows.reshape(EXPERTS * capacity, model_width)[slot_index].reshape(rows_total, TOP, model_width)
    return hidden + lax.optimization_barrier(jnp.sum(gate_probs[:, :, None] * gathered, axis=1))

def forward(tokens, query_weight, keyval_weight, output_weight, router_weight, attn_gain, moe_gain, expert_up, expert_down, segments, routes):
    weights = (query_weight, keyval_weight, output_weight, router_weight, attn_gain, moe_gain, expert_up, expert_down)
    rows_all = segments.shape[0]
    length = segments.shape[1]
    group_count = max(1, min(rows_all, 4096 // length))
    while rows_all % group_count:
        group_count -= 1
    blocks = rows_all // group_count
    block_tokens = tokens.reshape(blocks, group_count * length, tokens.shape[1])
    block_segments = segments.reshape(blocks, group_count, length)
    block_routes = routes.reshape(blocks, group_count * length, TOP)

    def block_step(carried, blocks_in):
        return (carried, layer_block(blocks_in[0], blocks_in[1], blocks_in[2], weights))
    _, results = lax.scan(jax.checkpoint(block_step), jnp.zeros((), jnp.float32), (block_tokens, block_segments, block_routes))
    return results.reshape(tokens.shape)

def reference(tokens, segments, routes, query_weight, keyval_weight, output_weight, router_weight, attn_gain, moe_gain, expert_up, expert_down, out_grad):

    def layer(tokens_in, query_in, keyval_in, output_in, router_in, attn_in, moe_in, up_in, down_in):
        return forward(tokens_in, query_in, keyval_in, output_in, router_in, attn_in, moe_in, up_in, down_in, segments, routes)
    layer_out, pullback = jax.vjp(layer, tokens.astype(jnp.float32), query_weight.astype(jnp.float32), keyval_weight.astype(jnp.float32), output_weight.astype(jnp.float32), router_weight.astype(jnp.float32), attn_gain.astype(jnp.float32), moe_gain.astype(jnp.float32), expert_up.astype(jnp.float32), expert_down.astype(jnp.float32))
    grads = pullback(out_grad.astype(jnp.float32))
    return (layer_out.astype(jnp.bfloat16), grads[0], grads[1], grads[2], grads[3], grads[4], grads[5], grads[6], grads[7], grads[8])
```

```python
import functools

import jax
import jax.numpy as jnp
from jax import lax
from jax.sharding import PartitionSpec as P
from jax.experimental import pallas as pl
from jax.experimental.pallas import tpu as pltpu

HEAD_DIM = 64
FF = 512
EXPERTS = 32
TOP = 8
CAP = 40


EPS = 1e-05
ROPE_BASE = 10000.0
MASKED = -1e30
HIGH = lax.Precision.HIGHEST


def norm_forward(values, gain_vec):
    inverse = lax.rsqrt(jnp.mean(values * values, axis=-1, keepdims=True) + EPS)
    normed = values * inverse
    return (normed, inverse, (normed * gain_vec).astype(jnp.bfloat16))


def norm_backward(grad_out, normed, inverse, gain_vec):
    gain_grad = jnp.sum(grad_out * normed, axis=0)
    scaled = grad_out * gain_vec
    grad_in = inverse * (scaled - normed * jnp.mean(scaled * normed, axis=-1, keepdims=True))
    return (grad_in, gain_grad)


def rope_tables(segment_row):
    length = segment_row.shape[0]
    earlier = jnp.sum((segment_row[None, :] < segment_row[:, None]).astype(jnp.int32), axis=1)
    position = jnp.arange(length, dtype=jnp.int32) - earlier
    half_dim = HEAD_DIM // 2
    frequency = ROPE_BASE ** (-(jnp.arange(half_dim, dtype=jnp.float32) * 2.0) / HEAD_DIM)
    angles = position.astype(jnp.float32)[:, None] * frequency[None, :]
    cosine = jnp.concatenate([jnp.cos(angles), jnp.cos(angles)], axis=-1)[:, None, :]
    sine_table = jnp.concatenate([jnp.sin(angles), jnp.sin(angles)], axis=-1)[:, None, :]
    return (cosine, sine_table)


def rotate(values, cosine, sine_table):
    half_dim = values.shape[-1] // 2
    turned = jnp.concatenate([-values[..., half_dim:], values[..., :half_dim]], axis=-1)
    return values * cosine + turned * sine_table


def unrotate(grad_rows, cosine, sine_table):
    half_dim = grad_rows.shape[-1] // 2
    weighted = grad_rows * sine_table
    turned = jnp.concatenate([weighted[..., half_dim:], -weighted[..., :half_dim]], axis=-1)
    return grad_rows * cosine + turned


def on_device_wide(
    tokens,
    segments,
    routes,
    query_weight,
    keyval_weight,
    output_weight,
    router_weight,
    attn_gain,
    moe_gain,
    expert_up,
    expert_down,
    out_grad,
):
    owners = lax.axis_size("expert")
    local_experts = expert_up.shape[0]
    length = tokens.shape[0]
    model_width = tokens.shape[1]
    kv_heads = keyval_weight.shape[1] // (2 * HEAD_DIM)
    query_heads = query_weight.shape[1] // HEAD_DIM
    repeat = query_heads // kv_heads
    score_scale = HEAD_DIM ** (-0.5)
    query_full, keyval_full, output_full, router_full, attn_gains, moe_gains = (
        lax.all_gather(query_weight, ("dp", "expert"), axis=0, tiled=True),
        lax.all_gather(keyval_weight, ("dp", "expert"), axis=0, tiled=True),
        lax.all_gather(output_weight, ("dp", "expert"), axis=0, tiled=True),
        lax.all_gather(router_weight, ("dp", "expert"), axis=0, tiled=True),
        lax.all_gather(attn_gain, ("dp", "expert"), axis=0, tiled=True),
        lax.all_gather(moe_gain, ("dp", "expert"), axis=0, tiled=True),
    )
    resident = tokens.astype(jnp.float32)
    normed_one, inverse_one, attn_in = norm_forward(resident, attn_gains.astype(jnp.float32))
    query_proj = jnp.dot(attn_in, query_full, preferred_element_type=jnp.float32).reshape(
        length, query_heads, HEAD_DIM
    )
    keyval_proj = jnp.dot(attn_in, keyval_full, preferred_element_type=jnp.float32)
    key_rows = keyval_proj[:, : kv_heads * HEAD_DIM].reshape(length, kv_heads, HEAD_DIM)
    value_rows = keyval_proj[:, kv_heads * HEAD_DIM :].reshape(length, kv_heads, HEAD_DIM)
    cosine, sine_table = rope_tables(segments[0])
    query_rot = (
        rotate(query_proj, cosine, sine_table)
        .astype(jnp.bfloat16)
        .reshape(length, kv_heads, repeat, HEAD_DIM)
    )
    keys_rot = rotate(key_rows, cosine, sine_table).astype(jnp.bfloat16)
    values_low = value_rows.astype(jnp.bfloat16)
    places = jnp.arange(length)
    visible = (segments[0][:, None] == segments[0][None, :]) & (places[None, :] <= places[:, None])
    scores = jnp.einsum("ikrd,jkd->krij", query_rot, keys_rot, preferred_element_type=jnp.float32)
    attn_logits = jnp.where(visible, scores * score_scale, MASKED)
    attn_exps = jnp.exp(attn_logits - jnp.max(attn_logits, axis=-1, keepdims=True))
    attn_probs = attn_exps / jnp.sum(attn_exps, axis=-1, keepdims=True)
    probs_low = attn_probs.astype(jnp.bfloat16)
    mixed_heads = jnp.einsum(
        "krij,jkd->ikrd", probs_low, values_low, preferred_element_type=jnp.float32
    )
    mixed_low = mixed_heads.reshape(length, query_heads * HEAD_DIM).astype(jnp.bfloat16)
    hidden = resident + jnp.dot(mixed_low, output_full, preferred_element_type=jnp.float32)
    normed_two, inverse_two, moe_in = norm_forward(hidden, moe_gains.astype(jnp.float32))
    router_logits = jnp.dot(moe_in, router_full, preferred_element_type=jnp.float32)
    choose = (routes[:, :, None] == jnp.arange(EXPERTS, dtype=jnp.int32)[None, None, :]).astype(
        jnp.float32
    )
    chosen = jnp.sum(choose * router_logits[:, None, :], axis=-1)
    gate_exps = jnp.exp(chosen - jnp.max(chosen, axis=-1, keepdims=True))
    gate_probs = gate_exps / jnp.sum(gate_exps, axis=-1, keepdims=True)
    entries = routes.reshape(-1)
    entry_count = entries.shape[0]
    onehot = (entries[:, None] == jnp.arange(EXPERTS, dtype=jnp.int32)[None, :]).astype(jnp.int32)
    position = jnp.sum((jnp.cumsum(onehot, axis=0) - 1) * onehot, axis=1)
    slot_index = entries * CAP + position
    owner_entry = (
        jnp.full((EXPERTS * CAP,), entry_count, jnp.int32)
        .at[slot_index]
        .set(jnp.arange(entry_count, dtype=jnp.int32))
    )
    padded_in = jnp.concatenate([moe_in, jnp.zeros((1, model_width), jnp.bfloat16)], axis=0)
    send_rows = jnp.take(padded_in, owner_entry // TOP, axis=0).reshape(EXPERTS, CAP, model_width)
    received = lax.all_to_all(send_rows, "expert", split_axis=0, concat_axis=0, tiled=True)
    slots_now = received.shape[1]
    grouped = received.reshape(owners, local_experts, slots_now, model_width)
    pair_proj = jnp.einsum("secd,edf->secf", grouped, expert_up, preferred_element_type=jnp.float32)
    activated = (jax.nn.silu(pair_proj[..., :FF]) * pair_proj[..., FF:]).astype(jnp.bfloat16)
    produced = jnp.einsum(
        "secf,edf->secd", activated, expert_down, preferred_element_type=jnp.float32
    ).astype(jnp.bfloat16)
    returned = lax.all_to_all(
        produced.reshape(EXPERTS, slots_now, model_width),
        "expert",
        split_axis=0,
        concat_axis=0,
        tiled=True,
    )
    returned, kept_rows, kept_pair = (
        returned,
        received,
        pair_proj.reshape(EXPERTS, slots_now, 2 * FF),
    )
    gathered = (
        jnp.take(returned.reshape(EXPERTS * CAP, model_width), slot_index, axis=0)
        .astype(jnp.float32)
        .reshape(length, TOP, model_width)
    )
    layer_out = (hidden + jnp.sum(gate_probs[:, :, None] * gathered, axis=1)).astype(jnp.bfloat16)
    grad_top = out_grad.astype(jnp.float32)
    gate_grad = jnp.sum(gathered * grad_top[:, None, :], axis=-1)
    chosen_grad = gate_probs * (gate_grad - jnp.sum(gate_probs * gate_grad, axis=-1, keepdims=True))
    logits_grad = jnp.sum(chosen_grad[:, :, None] * choose, axis=1)
    row_grads = (
        (gate_probs[:, :, None] * grad_top[:, None, :])
        .astype(jnp.bfloat16)
        .reshape(entry_count, model_width)
    )
    padded_grads = jnp.concatenate([row_grads, jnp.zeros((1, model_width), jnp.bfloat16)], axis=0)
    send_grads = jnp.take(padded_grads, owner_entry, axis=0).reshape(EXPERTS, CAP, model_width)
    grads_in = lax.all_to_all(send_grads, "expert", split_axis=0, concat_axis=0, tiled=True)
    grouped_rows = kept_rows.reshape(owners, local_experts, CAP, model_width)
    grouped_grads = grads_in.reshape(owners, local_experts, CAP, model_width)
    pair_kept = kept_pair.reshape(owners, local_experts, CAP, 2 * FF)
    gate_half = pair_kept[..., :FF]
    up_half = pair_kept[..., FF:]
    sigmoid_gate = jax.nn.sigmoid(gate_half)
    silu_gate = jax.nn.silu(gate_half)
    activated = (silu_gate * up_half).astype(jnp.bfloat16)
    act_grad = jnp.einsum(
        "secd,edf->secf", grouped_grads, expert_down, preferred_element_type=jnp.float32
    )
    pair_grad = jnp.concatenate(
        [
            act_grad * up_half * sigmoid_gate * (1.0 + gate_half * (1.0 - sigmoid_gate)),
            act_grad * silu_gate,
        ],
        axis=-1,
    ).astype(jnp.bfloat16)
    rows_back = jnp.einsum(
        "secf,edf->secd", pair_grad, expert_up, preferred_element_type=jnp.float32
    ).astype(jnp.bfloat16)
    up_grad = jnp.einsum(
        "secd,secf->edf", grouped_rows, pair_grad, preferred_element_type=jnp.float32
    )
    down_grad = jnp.einsum(
        "secd,secf->edf", grouped_grads, activated, preferred_element_type=jnp.float32
    )
    returned_grads = lax.all_to_all(
        rows_back.reshape(EXPERTS, CAP, model_width),
        "expert",
        split_axis=0,
        concat_axis=0,
        tiled=True,
    )
    expert_up_grad, expert_down_grad = (
        lax.psum_scatter(
            up_grad.astype(jnp.bfloat16), "dp", scatter_dimension=1, tiled=True
        ).astype(jnp.float32),
        lax.psum_scatter(
            down_grad.astype(jnp.bfloat16), "dp", scatter_dimension=1, tiled=True
        ).astype(jnp.float32),
    )
    token_grads = (
        jnp.take(returned_grads.reshape(EXPERTS * CAP, model_width), slot_index, axis=0)
        .astype(jnp.float32)
        .reshape(length, TOP, model_width)
    )
    router_wide = router_full.astype(jnp.float32)
    moe_grad = jnp.sum(token_grads, axis=1) + jnp.dot(logits_grad, router_wide.T, precision=HIGH)
    hidden_norm_grad, moe_gain_grad = norm_backward(
        moe_grad, normed_two, inverse_two, moe_gains.astype(jnp.float32)
    )
    hidden_grad = grad_top + hidden_norm_grad
    attn_out_grad = hidden_grad.astype(jnp.bfloat16)
    mixed_grad = (
        jnp.einsum("td,cd->tc", attn_out_grad, output_full, preferred_element_type=jnp.float32)
        .astype(jnp.bfloat16)
        .reshape(length, kv_heads, repeat, HEAD_DIM)
    )
    probs_grad = jnp.einsum(
        "ikrd,jkd->krij", mixed_grad, values_low, preferred_element_type=jnp.float32
    )
    values_grad = jnp.einsum(
        "krij,ikrd->jkd", probs_low, mixed_grad, preferred_element_type=jnp.float32
    )
    scores_grad = (
        attn_probs
        * (probs_grad - jnp.sum(attn_probs * probs_grad, axis=-1, keepdims=True))
        * score_scale
    ).astype(jnp.bfloat16)
    query_rot_grad = jnp.einsum(
        "krij,jkd->ikrd", scores_grad, keys_rot, preferred_element_type=jnp.float32
    ).reshape(length, query_heads, HEAD_DIM)
    keys_rot_grad = jnp.einsum(
        "krij,ikrd->jkd", scores_grad, query_rot, preferred_element_type=jnp.float32
    )
    query_low = (
        unrotate(query_rot_grad, cosine, sine_table)
        .reshape(length, query_heads * HEAD_DIM)
        .astype(jnp.bfloat16)
    )
    keyval_low = jnp.concatenate(
        [
            unrotate(keys_rot_grad, cosine, sine_table).reshape(length, kv_heads * HEAD_DIM),
            values_grad.reshape(length, kv_heads * HEAD_DIM),
        ],
        axis=1,
    ).astype(jnp.bfloat16)
    attn_in_grad = jnp.einsum(
        "tc,dc->td", query_low, query_full, preferred_element_type=jnp.float32
    ) + jnp.einsum("tc,dc->td", keyval_low, keyval_full, preferred_element_type=jnp.float32)
    token_norm_grad, attn_gain_grad = norm_backward(
        attn_in_grad, normed_one, inverse_one, attn_gains.astype(jnp.float32)
    )
    tokens_grad = hidden_grad + token_norm_grad
    slab_count = lax.axis_size("dp")
    slab_index = lax.axis_index("dp")
    width_rows = model_width // slab_count
    head_rows = query_heads * HEAD_DIM // slab_count
    all_attn, all_query, all_keyval, all_mixed, all_outgrad = (
        lax.all_gather(attn_in, "dp", axis=0, tiled=True),
        lax.all_gather(query_low, "dp", axis=0, tiled=True),
        lax.all_gather(keyval_low, "dp", axis=0, tiled=True),
        lax.all_gather(mixed_low, "dp", axis=0, tiled=True),
        lax.all_gather(attn_out_grad, "dp", axis=0, tiled=True),
    )
    all_moe, all_logits, attn_gain_rows, moe_gain_rows = (
        lax.all_gather(
            moe_in.astype(jnp.float32).astype(jnp.bfloat16), "dp", axis=0, tiled=True
        ).astype(jnp.float32),
        lax.all_gather(logits_grad.astype(jnp.bfloat16), "dp", axis=0, tiled=True).astype(
            logits_grad.dtype
        ),
        lax.all_gather(
            attn_gain_grad[None, :].astype(jnp.bfloat16), "dp", axis=0, tiled=True
        ).astype(jnp.float32),
        lax.all_gather(
            moe_gain_grad[None, :].astype(jnp.bfloat16), "dp", axis=0, tiled=True
        ).astype(jnp.float32),
    )
    attn_cols = lax.dynamic_slice_in_dim(all_attn, slab_index * width_rows, width_rows, 1)
    mixed_cols = lax.dynamic_slice_in_dim(all_mixed, slab_index * head_rows, head_rows, 1)
    moe_cols = lax.dynamic_slice_in_dim(all_moe, slab_index * width_rows, width_rows, 1)
    query_part = jnp.einsum("td,tc->dc", attn_cols, all_query, preferred_element_type=jnp.float32)
    keyval_part = jnp.einsum("td,tc->dc", attn_cols, all_keyval, preferred_element_type=jnp.float32)
    output_part = jnp.einsum(
        "tc,td->cd", mixed_cols, all_outgrad, preferred_element_type=jnp.float32
    )
    router_part = jnp.dot(moe_cols.T, all_logits, precision=HIGH)
    attn_gain_part = lax.dynamic_slice_in_dim(
        jnp.sum(attn_gain_rows, axis=0), slab_index * width_rows, width_rows, 0
    )
    moe_gain_part = lax.dynamic_slice_in_dim(
        jnp.sum(moe_gain_rows, axis=0), slab_index * width_rows, width_rows, 0
    )
    query_share, keyval_share, output_share, router_share, attn_share, moe_share = (
        lax.psum_scatter(
            query_part.astype(jnp.bfloat16), "expert", scatter_dimension=0, tiled=True
        ).astype(jnp.float32),
        lax.psum_scatter(
            keyval_part.astype(jnp.bfloat16), "expert", scatter_dimension=0, tiled=True
        ).astype(jnp.float32),
        lax.psum_scatter(
            output_part.astype(jnp.bfloat16), "expert", scatter_dimension=0, tiled=True
        ).astype(jnp.float32),
        lax.psum_scatter(
            router_part.astype(jnp.bfloat16), "expert", scatter_dimension=0, tiled=True
        ).astype(jnp.float32),
        lax.psum_scatter(
            attn_gain_part.astype(jnp.bfloat16), "expert", scatter_dimension=0, tiled=True
        ).astype(jnp.float32),
        lax.psum_scatter(
            moe_gain_part.astype(jnp.bfloat16), "expert", scatter_dimension=0, tiled=True
        ).astype(jnp.float32),
    )
    return (
        layer_out,
        tokens_grad,
        query_share,
        keyval_share,
        output_share,
        router_share,
        attn_share,
        moe_share,
        expert_up_grad,
        expert_down_grad,
    )


LANES = 128
TAIL = 16
PIECE_LIMIT = 4096
VMEM_BYTES = 60 * 1024 * 1024
F32 = jnp.float32
LOW = jnp.bfloat16


def contract(left, right, left_dim, right_dim):
    return lax.dot_general(
        left, right, (((left_dim,), (right_dim,)), ((), ())), preferred_element_type=F32
    )


def lane_index(shape):
    return lax.broadcasted_iota(jnp.int32, shape, len(shape) - 1)


def row_index(shape):
    return lax.broadcasted_iota(jnp.int32, shape, len(shape) - 2)


def half_turn(chunk):
    first = lane_index(chunk.shape) % HEAD_DIM < HEAD_DIM // 2
    ahead = pltpu.roll(chunk, LANES - HEAD_DIM // 2, 1)
    behind = pltpu.roll(chunk, HEAD_DIM // 2, 1)
    return jnp.where(first, ahead, behind)


def both_heads(chunk, pick):
    swapped = pltpu.roll(chunk, HEAD_DIM, 1)
    first = lane_index(chunk.shape) < HEAD_DIM
    if pick == 0:
        return jnp.where(first, chunk, swapped)
    return jnp.where(first, swapped, chunk)


def split_heads(chunk):
    first = lane_index(chunk.shape) < HEAD_DIM
    zero = jnp.zeros_like(chunk)
    return jnp.concatenate([jnp.where(first, chunk, zero), jnp.where(first, zero, chunk)], axis=0)


def join_heads(stacked):
    length = stacked.shape[0] // 2
    top, bottom = stacked[:length], stacked[length:]
    return jnp.where(lane_index(top.shape) < HEAD_DIM, top, bottom)


def three_parts(values):
    high = values.astype(LOW).astype(F32)
    rest = values - high
    middle = rest.astype(LOW).astype(F32)
    return (high, middle, rest - middle)


def gain_select():
    shape = (8, LANES)
    return (lane_index(shape) == EXPERTS + row_index(shape)) & (row_index(shape) < 2)


def load_weights(rows_ref, piece_refs, weights, sems):
    copies = []
    for p, piece in enumerate(piece_refs):
        for w in range(piece.shape[0]):
            size = piece.shape[1]
            start = pl.multiple_of(rows_ref[p, w] * size, size)
            copies.append(
                pltpu.make_async_copy(piece.at[w], weights.at[pl.ds(start, size)], sems.at[p, w])
            )
    for copy in copies:
        copy.start()
    return copies


def softmax_rows(q_pair, k_both, visible):
    scores = contract(q_pair, k_both, 1, 1) * (HEAD_DIM ** (-0.5))
    logits = jnp.where(visible, scores, MASKED)
    exps = jnp.exp(logits - jnp.max(logits, axis=-1, keepdims=True))
    return exps / jnp.sum(exps, axis=-1, keepdims=True)


def visible_pairs(seg_col, seg_row):
    length = seg_col.shape[0]
    shape = (length, length)
    seen = (seg_col == seg_row) & (lane_index(shape) <= row_index(shape))
    return jnp.concatenate([seen, seen], axis=0)


def attn_forward_kernel(count, *refs):
    rows_ref, tokens_ref, seg_col, seg_row, routes_ref, routes_t, cos_ref, sin_ref = refs[:8]
    pieces = refs[8 : 8 + count]
    payload, hidden_ref, query_ref, keyval_ref, mixed_ref, gates_ref, weights, sems = refs[8 + count :]
    copies = load_weights(rows_ref, pieces, weights, sems)
    tokens = tokens_ref[...].astype(F32)
    inverse = lax.rsqrt(jnp.mean(tokens * tokens, axis=-1, keepdims=True) + EPS)
    normed = tokens * inverse
    length, width = tokens.shape
    for copy in copies:
        copy.wait()
    tail = weights[:, 3 * width :]
    gains = contract(gain_select().astype(F32).astype(LOW), tail, 1, 1)
    attn_in = (normed * gains[0:1]).astype(LOW)
    cosine, sine = cos_ref[...], sin_ref[...]
    keyval = contract(attn_in, weights[:, width : 2 * width], 1, 0)
    query = contract(attn_in, weights[:, :width], 1, 0)
    visible = visible_pairs(seg_col[...], seg_row[...])
    half = width // 2
    for m in range(half // LANES):
        keys = keyval[:, m * LANES : (m + 1) * LANES]
        keys = (keys * cosine + half_turn(keys) * sine).astype(LOW)
        values = keyval[:, half + m * LANES : half + (m + 1) * LANES].astype(LOW)
        keyval_ref[:, m * LANES : (m + 1) * LANES] = keys
        keyval_ref[:, half + m * LANES : half + (m + 1) * LANES] = values
        for pick in range(2):
            k_both = both_heads(keys.astype(F32), pick).astype(LOW)
            v_both = both_heads(values.astype(F32), pick).astype(LOW)
            chunk = slice((2 * m + pick) * LANES, (2 * m + pick + 1) * LANES)
            queries = query[:, chunk]
            queries = (queries * cosine + half_turn(queries) * sine).astype(LOW)
            query_ref[:, chunk] = queries
            q_pair = split_heads(queries.astype(F32)).astype(LOW)
            probs = softmax_rows(q_pair, k_both, visible).astype(LOW)
            mixed_ref[:, chunk] = join_heads(contract(probs, v_both, 1, 0)).astype(LOW)
    hidden = tokens + contract(mixed_ref[...], weights[:, 2 * width : 3 * width], 1, 0)
    hidden_ref[...] = hidden
    inverse_two = lax.rsqrt(jnp.mean(hidden * hidden, axis=-1, keepdims=True) + EPS)
    moe_in = (hidden * inverse_two * gains[1:2]).astype(LOW)
    payload[:length] = moe_in
    logits = contract(moe_in, tail, 1, 0)
    routes = routes_ref[...]
    lanes = lane_index((length, LANES))
    chosen = lanes == routes[:, 0:1]
    for k in range(1, TOP):
        chosen = chosen | (lanes == routes[:, k : k + 1])
    logits = jnp.where(chosen, logits, MASKED)
    exps = jnp.where(chosen, jnp.exp(logits - jnp.max(logits, axis=-1, keepdims=True)), 0.0)
    gates = exps / jnp.sum(exps, axis=-1, keepdims=True)
    gates_ref[...] = gates
    gates_t = gates.T
    experts = row_index((LANES, length))
    turned = routes_t[...]
    for k in range(TOP):
        row = turned[k : k + 1]
        gate = jnp.sum(jnp.where(experts == row, gates_t, 0.0), axis=0, keepdims=True)
        high, middle, rest = three_parts(gate)
        place = row_index((TAIL, length))
        block = jnp.where(place == 0, high, jnp.where(place == 1, middle, jnp.where(place == 2, rest, 0.0)))
        block = jnp.where(place == 3, row.astype(F32), block)
        payload[length:, k * length : (k + 1) * length] = block.astype(LOW)


def gather_pair(first_expert, local, block, rows_a, rows_b, grads_a, grads_b, before, out):
    rows_out, grads_out, select_out, gate_out, pair = out
    length = rows_a.shape[0] - TAIL
    ids = row_index((8, length)) + first_expert
    ids = jnp.where(row_index((8, length)) < local, ids, -1).astype(F32)
    masks, gates = [], []
    for piece in (rows_a, rows_b):
        tail = piece[length:].astype(F32)
        mask = jnp.zeros((8, length), F32)
        gate = jnp.zeros((8, length), F32)
        for k in range(TOP):
            part = tail[:, k * length : (k + 1) * length]
            hit = part[3:4] == ids
            mask = jnp.where(hit, 1.0, mask)
            gate = jnp.where(hit, part[0:1] + part[1:2] + part[2:3], gate)
        masks.append(mask)
        gates.append(gate)
    mask = jnp.concatenate(masks, axis=1)
    gate = jnp.concatenate(gates, axis=1)
    place = contract(mask.astype(LOW), before, 1, 0)
    place = jnp.where(mask > 0, place, -1.0)
    slots = row_index((block, 2 * length)).astype(F32)
    parts = []
    for j in range(local):
        hit = slots == place[j : j + 1]
        parts.append(jnp.where(hit, 1.0, 0.0))
        held = jnp.sum(jnp.where(hit, gate[j : j + 1], 0.0), axis=1, keepdims=True)
        gate_out[j, pair * block : (pair + 1) * block] = jnp.broadcast_to(held, (block, LANES))
    select = jnp.concatenate(parts, axis=0).astype(LOW)
    if select_out is not None:
        select_out[pair] = select
    rows = jnp.concatenate([rows_a[:length], rows_b[:length]], axis=0)
    grads = jnp.concatenate([grads_a, grads_b], axis=0)
    rows = contract(select, rows, 1, 0).astype(LOW)
    grads = contract(select, grads, 1, 0).astype(LOW)
    for j in range(local):
        rows_out[j, pair * block : (pair + 1) * block] = rows[j * block : (j + 1) * block]
        grads_out[j, pair * block : (pair + 1) * block] = grads[j * block : (j + 1) * block]


def earlier_matrix(length):
    shape = (2 * length, 2 * length)
    return jnp.where(row_index(shape) < lane_index(shape), 1.0, 0.0).astype(LOW)


def expert_step(j, rows, grads, gate_ref, up, down):
    hidden_units = down.shape[1]
    pair = contract(rows[j], up, 1, 0)
    raw = contract(grads[j], down, 1, 0)
    gate_half, up_half = pair[:, :hidden_units], pair[:, hidden_units:]
    gate = gate_ref[j][:, 0:1]
    sigmoid = 1.0 / (1.0 + jnp.exp(-gate_half))
    silu = gate_half * sigmoid
    activated = silu * up_half
    scaled = (gate * activated).astype(LOW)
    act_grad = gate * raw
    pair_grad = jnp.concatenate(
        [act_grad * up_half * sigmoid * (1.0 + gate_half * (1.0 - sigmoid)), act_grad * silu],
        axis=1,
    ).astype(LOW)
    gate_grad = jnp.sum(activated * raw, axis=1, keepdims=True)
    return (scaled, pair_grad, gate_grad)


def expert_home_kernel(owners, local, block, *refs):
    place_ref = refs[0]
    rows_in = refs[1 : 1 + owners]
    grads_in = refs[1 + owners : 1 + 2 * owners]
    up_hbm, down_hbm = refs[1 + 2 * owners : 3 + 2 * owners]
    out_even, out_odd, back_even, back_odd, up_grad, down_grad = refs[3 + 2 * owners : 9 + 2 * owners]
    up, down, rows, grads, select, gate_ref, produced, returned, sems = refs[9 + 2 * owners :]
    copies = []
    for j in range(local):
        copies.append(
            (
                pltpu.make_async_copy(up_hbm.at[j], up.at[j], sems.at[0, j]),
                pltpu.make_async_copy(down_hbm.at[j], down.at[j], sems.at[1, j]),
            )
        )
        for copy in copies[j]:
            copy.start()
    length = rows_in[0].shape[0] - TAIL
    width = rows_in[0].shape[1]
    first_expert = place_ref[0] * local
    slab = up_grad.shape[1]
    columns = pl.ds(pl.multiple_of(place_ref[1] * slab, slab), slab)
    before = earlier_matrix(length)
    for s in range(owners // 2):
        gather_pair(
            first_expert,
            local,
            block,
            rows_in[2 * s][...],
            rows_in[2 * s + 1][...],
            grads_in[2 * s][0],
            grads_in[2 * s + 1][0],
            before,
            (rows, grads, select, gate_ref, s),
        )
    for j in range(local):
        for copy in copies[j]:
            copy.wait()
        scaled, pair_grad, gate_grad = expert_step(j, rows, grads, gate_ref, up[j], down[j])
        produced[j] = contract(scaled, down[j], 1, 1).astype(LOW)
        returned[j, :, :width] = contract(pair_grad, up[j], 1, 1).astype(LOW)
        lanes = lane_index((scaled.shape[0], LANES)) - first_expert - j
        high, middle, rest = three_parts(gate_grad)
        tail = jnp.where(lanes == 0, high, 0.0)
        tail = jnp.where(lanes == EXPERTS, middle, tail)
        tail = jnp.where(lanes == 2 * EXPERTS, rest, tail)
        returned[j, :, width:] = tail.astype(LOW)
        up_grad[j] = contract(rows[j, :, columns], pair_grad, 0, 0)
        down_grad[j] = contract(grads[j, :, columns], scaled, 0, 0)
    for s in range(owners // 2):
        span = slice(s * block, (s + 1) * block)
        made = jnp.concatenate([produced[j, span] for j in range(local)], axis=0)
        back = jnp.concatenate([returned[j, span] for j in range(local)], axis=0)
        made = contract(select[s], made, 0, 0).astype(LOW)
        back = contract(select[s], back, 0, 0).astype(LOW)
        out_even[s] = made[:length]
        out_odd[s] = made[length:]
        back_even[s] = back[:length]
        back_odd[s] = back[length:]


def expert_away_kernel(owners, local, block, *refs):
    place_ref = refs[0]
    rows_in = refs[1 : 1 + owners]
    grads_in = refs[1 + owners : 1 + 2 * owners]
    up, down, up_first, down_first = refs[1 + 2 * owners : 5 + 2 * owners]
    up_grad, down_grad, rows, grads, gate_ref = refs[5 + 2 * owners :]
    length = rows_in[0].shape[1] - TAIL
    first_expert = place_ref[0] * local
    slab = up_grad.shape[1]
    columns = pl.ds(pl.multiple_of(place_ref[1] * slab, slab), slab)

    @pl.when(pl.program_id(0) == 0)
    def _():
        up_grad[...] = up_first[...]
        down_grad[...] = down_first[...]

    before = earlier_matrix(length)
    for s in range(owners // 2):
        gather_pair(
            first_expert,
            local,
            block,
            rows_in[2 * s][0],
            rows_in[2 * s + 1][0],
            grads_in[2 * s][0],
            grads_in[2 * s + 1][0],
            before,
            (rows, grads, None, gate_ref, s),
        )
    for j in range(local):
        scaled, pair_grad, _ = expert_step(j, rows, grads, gate_ref, up[j], down[j])
        up_grad[j] += contract(rows[j, :, columns], pair_grad, 0, 0)
        down_grad[j] += contract(grads[j, :, columns], scaled, 0, 0)


def attn_backward_kernel(count, shares, *refs):
    rows_ref, tokens_ref, seg_col, seg_row, cos_ref, sin_ref, payload, hidden_ref = refs[:8]
    query_ref, keyval_ref, mixed_ref, gates_ref, out_grad_ref = refs[8:13]
    back = refs[13 : 13 + shares]
    pieces = refs[13 + shares : 13 + shares + count]
    tokens_grad, grads_even, grads_odd = refs[13 + shares + count : 16 + shares + count]
    weights, sums, query_low, keyval_low, sems, out_sems = refs[16 + shares + count :]
    copies = load_weights(rows_ref, pieces, weights, sems)
    length, width = tokens_ref.shape
    half = width // 2
    total = back[0][...].astype(F32)
    for share in back[1:]:
        total = total + share[...].astype(F32)
    parts = total[:, width:]
    lanes = lane_index(parts.shape)
    gate_grad = parts + pltpu.roll(parts, LANES - EXPERTS, 1) + pltpu.roll(parts, LANES - 2 * EXPERTS, 1)
    gate_grad = jnp.where(lanes < EXPERTS, gate_grad, 0.0)
    gates = gates_ref[...]
    logits_grad = gates * (gate_grad - jnp.sum(gates * gate_grad, axis=-1, keepdims=True))
    hidden = hidden_ref[...]
    inverse_two = lax.rsqrt(jnp.mean(hidden * hidden, axis=-1, keepdims=True) + EPS)
    normed_two = hidden * inverse_two
    tokens = tokens_ref[...].astype(F32)
    inverse_one = lax.rsqrt(jnp.mean(tokens * tokens, axis=-1, keepdims=True) + EPS)
    normed_one = tokens * inverse_one
    for copy in copies:
        copy.wait()
    tail = weights[:, 3 * width :]
    gains = contract(gain_select().astype(F32).astype(LOW), tail, 1, 1)
    high = logits_grad.astype(LOW)
    rest = (logits_grad - high.astype(F32)).astype(LOW)
    moe_grad = total[:, :width] + contract(high, tail, 1, 1) + contract(rest, tail, 1, 1)
    moe_gain_grad = jnp.sum(moe_grad * normed_two, axis=0, keepdims=True)
    scaled = moe_grad * gains[1:2]
    hidden_grad = out_grad_ref[...].astype(F32) + inverse_two * (
        scaled - normed_two * jnp.mean(scaled * normed_two, axis=-1, keepdims=True)
    )
    attn_out_grad = hidden_grad.astype(LOW)
    sums[:, 2 * width : 3 * width] = contract(mixed_ref[...], attn_out_grad, 0, 0).astype(LOW)
    mixed_grad = contract(attn_out_grad, weights[:, 2 * width : 3 * width], 1, 1)
    cosine, sine = cos_ref[...], sin_ref[...]
    visible = visible_pairs(seg_col[...], seg_row[...])
    for m in range(half // LANES):
        keys = keyval_ref[:, m * LANES : (m + 1) * LANES].astype(F32)
        values = keyval_ref[:, half + m * LANES : half + (m + 1) * LANES].astype(F32)
        key_sides, value_sides = [], []
        for pick in range(2):
            k_both = both_heads(keys, pick).astype(LOW)
            v_both = both_heads(values, pick).astype(LOW)
            chunk = slice((2 * m + pick) * LANES, (2 * m + pick + 1) * LANES)
            q_pair = split_heads(query_ref[:, chunk].astype(F32)).astype(LOW)
            m_pair = split_heads(mixed_grad[:, chunk]).astype(LOW)
            probs = softmax_rows(q_pair, k_both, visible)
            probs_grad = contract(m_pair, v_both, 1, 1)
            value_sides.append(contract(probs.astype(LOW), m_pair, 0, 0))
            scores_grad = (
                probs
                * (probs_grad - jnp.sum(probs * probs_grad, axis=-1, keepdims=True))
                * (HEAD_DIM ** (-0.5))
            ).astype(LOW)
            query_grad = join_heads(contract(scores_grad, k_both, 1, 0))
            query_low[:, chunk] = (query_grad * cosine - half_turn(query_grad) * sine).astype(LOW)
            key_sides.append(contract(scores_grad, q_pair, 0, 0))
        first = lane_index((length, LANES)) < HEAD_DIM
        key_sides = [side + pltpu.roll(side, HEAD_DIM, 1) for side in key_sides]
        value_sides = [side + pltpu.roll(side, HEAD_DIM, 1) for side in value_sides]
        keys_grad = jnp.where(first, key_sides[0], key_sides[1])
        values_grad = jnp.where(first, value_sides[0], value_sides[1])
        keyval_low[:, m * LANES : (m + 1) * LANES] = (
            keys_grad * cosine - half_turn(keys_grad) * sine
        ).astype(LOW)
        keyval_low[:, half + m * LANES : half + (m + 1) * LANES] = values_grad.astype(LOW)
    attn_in_grad = contract(query_low[...], weights[:, :width], 1, 1) + contract(
        keyval_low[...], weights[:, width : 2 * width], 1, 1
    )
    attn_in = (normed_one * gains[0:1]).astype(LOW)
    sums[:, :width] = contract(attn_in, query_low[...], 0, 0).astype(LOW)
    sums[:, width : 2 * width] = contract(attn_in, keyval_low[...], 0, 0).astype(LOW)
    attn_gain_grad = jnp.sum(attn_in_grad * normed_one, axis=0, keepdims=True)
    place = row_index((8, width))
    gain_grads = jnp.where(place == 0, attn_gain_grad, jnp.where(place == 1, moe_gain_grad, 0.0))
    tail_grad = contract(payload[:length], high, 0, 0) + contract(
        gain_grads.astype(LOW), gain_select().astype(F32).astype(LOW), 0, 0
    )
    sums[:, 3 * width :] = tail_grad.astype(LOW)
    copies = []
    for p in range(count):
        target = grads_even if p % 2 == 0 else grads_odd
        for w in range(target.shape[1]):
            size = target.shape[2]
            start = pl.multiple_of(rows_ref[p, w] * size, size)
            copies.append(
                pltpu.make_async_copy(
                    sums.at[pl.ds(start, size)], target.at[p // 2, w], out_sems.at[p, w]
                )
            )
    for copy in copies:
        copy.start()
    scaled = attn_in_grad * gains[0:1]
    tokens_grad[...] = hidden_grad + inverse_one * (
        scaled - normed_one * jnp.mean(scaled * normed_one, axis=-1, keepdims=True)
    )
    for copy in copies:
        copy.wait()


def swap(values, axis, size, distance):
    return lax.ppermute(values, axis, [(i, i ^ distance) for i in range(size)])


def over_planes(values, planes):
    return [values] + [swap(values, "dp", planes, w) for w in range(1, planes)]


def over_plane(values, owners):
    near = [values] + [swap(values, "expert", owners, 2 * s) for s in range(1, owners // 2)]
    pieces = []
    for piece in near:
        pieces += [piece, swap(piece, "expert", owners, 1)]
    return pieces


def params():
    return pltpu.CompilerParams(vmem_limit_bytes=VMEM_BYTES)


def whole_spec():
    return pl.BlockSpec(memory_space=pltpu.VMEM)


def hbm_spec():
    return pl.BlockSpec(memory_space=pl.ANY)


def smem_spec():
    return pl.BlockSpec(memory_space=pltpu.SMEM)


def on_device(
    planes,
    owners,
    tokens,
    segments,
    routes,
    query_weight,
    keyval_weight,
    output_weight,
    router_weight,
    attn_gain,
    moe_gain,
    expert_up,
    expert_down,
    out_grad,
):
    length, width = tokens.shape
    if planes * owners * length > PIECE_LIMIT:
        return on_device_wide(
            tokens,
            segments,
            routes,
            query_weight,
            keyval_weight,
            output_weight,
            router_weight,
            attn_gain,
            moe_gain,
            expert_up,
            expert_down,
            out_grad,
        )
    local = expert_up.shape[0]
    hidden_units = expert_down.shape[2]
    block = 2 * CAP
    slots = owners // 2 * block
    plane = lax.axis_index("dp")
    owner = lax.axis_index("expert")
    share = query_weight.shape[0]
    rows = (plane ^ jnp.arange(planes))[None, :] * owners + (owner ^ jnp.arange(owners))[:, None]
    rows = rows.astype(jnp.int32)
    place = jnp.stack([owner, plane]).astype(jnp.int32)
    extra = jnp.concatenate(
        [
            router_weight,
            attn_gain[:, None],
            moe_gain[:, None],
            jnp.zeros((share, LANES - EXPERTS - 2), LOW),
        ],
        axis=1,
    )
    packed = jnp.concatenate([query_weight, keyval_weight, output_weight, extra], axis=1)
    columns = packed.shape[1]
    pieces = over_plane(jnp.stack(over_planes(packed, planes)), owners)
    grad_pieces = over_plane(jnp.stack(over_planes(out_grad, planes)), owners)

    segment_row = segments[0]
    earlier = jnp.sum((segment_row[None, :] < segment_row[:, None]).astype(jnp.int32), axis=1)
    position = (jnp.arange(length, dtype=jnp.int32) - earlier).astype(F32)
    half_dim = HEAD_DIM // 2
    frequency = ROPE_BASE ** (-(jnp.arange(half_dim, dtype=F32) * 2.0) / HEAD_DIM)
    angles = position[:, None] * frequency[None, :]
    cosine = jnp.tile(jnp.cos(angles), (1, LANES // half_dim))
    sine = jnp.sin(angles)
    sine = jnp.concatenate([-sine, sine, -sine, sine], axis=1)
    seg_col, seg_row = segment_row[:, None], segment_row[None, :]

    payload, hidden, query_rot, keyval_low, mixed_low, gates = pl.pallas_call(
        functools.partial(attn_forward_kernel, owners),
        out_shape=(
            jax.ShapeDtypeStruct((length + TAIL, width), LOW),
            jax.ShapeDtypeStruct((length, width), F32),
            jax.ShapeDtypeStruct((length, width), LOW),
            jax.ShapeDtypeStruct((length, width), LOW),
            jax.ShapeDtypeStruct((length, width), LOW),
            jax.ShapeDtypeStruct((length, LANES), F32),
        ),
        in_specs=[smem_spec()] + [whole_spec()] * 7 + [hbm_spec()] * owners,
        out_specs=[whole_spec()] * 6,
        scratch_shapes=[
            pltpu.VMEM((width, columns), LOW),
            pltpu.SemaphoreType.DMA((owners, planes)),
        ],
        compiler_params=params(),
        name="attn_forward",
    )(rows, tokens, seg_col, seg_row, routes, routes.T, cosine, sine, *pieces)

    row_pieces = over_plane(payload, owners)
    away_rows = over_plane(
        jnp.stack([swap(payload, "dp", planes, w) for w in range(1, planes)]), owners
    )

    def all_of(shape):
        return pl.BlockSpec(shape, lambda i: (0,) * len(shape))

    slab = width // planes
    slabs = (
        jax.ShapeDtypeStruct((local, slab, 2 * hidden_units), F32),
        jax.ShapeDtypeStruct((local, slab, hidden_units), F32),
    )
    out_even, out_odd, back_even, back_odd, up_grad, down_grad = pl.pallas_call(
        functools.partial(expert_home_kernel, owners, local, block),
        grid=(1,),
        out_shape=(
            jax.ShapeDtypeStruct((owners // 2, length, width), LOW),
            jax.ShapeDtypeStruct((owners // 2, length, width), LOW),
            jax.ShapeDtypeStruct((owners // 2, length, width + LANES), LOW),
            jax.ShapeDtypeStruct((owners // 2, length, width + LANES), LOW),
        )
        + slabs,
        in_specs=[smem_spec()]
        + [all_of((length + TAIL, width))] * owners
        + [pl.BlockSpec((1, length, width), lambda i: (0, 0, 0))] * owners
        + [hbm_spec()] * 2,
        out_specs=[all_of((owners // 2, length, width))] * 2
        + [all_of((owners // 2, length, width + LANES))] * 2
        + [all_of(part.shape) for part in slabs],
        scratch_shapes=[
            pltpu.VMEM(expert_up.shape, LOW),
            pltpu.VMEM(expert_down.shape, LOW),
            pltpu.VMEM((local, slots, width), LOW),
            pltpu.VMEM((local, slots, width), LOW),
            pltpu.VMEM((owners // 2, local * block, 2 * length), LOW),
            pltpu.VMEM((local, slots, LANES), F32),
            pltpu.VMEM((local, slots, width), LOW),
            pltpu.VMEM((local, slots, width + LANES), LOW),
            pltpu.SemaphoreType.DMA((2, local)),
        ],
        compiler_params=params(),
        name="expert_home",
    )(place, *row_pieces, *grad_pieces, expert_up, expert_down)

    def to_owners(even, odd):
        other = swap(odd, "expert", owners, 1)
        joined = [
            (even[s].astype(F32) + other[s].astype(F32)).astype(LOW) for s in range(owners // 2)
        ]
        return [joined[0]] + [
            swap(joined[s], "expert", owners, 2 * s) for s in range(1, owners // 2)
        ]

    back = to_owners(back_even, back_odd)
    tokens_grad, grads_even, grads_odd = pl.pallas_call(
        functools.partial(attn_backward_kernel, owners, owners // 2),
        out_shape=(
            jax.ShapeDtypeStruct((length, width), F32),
            jax.ShapeDtypeStruct((owners // 2, planes, share, columns), LOW),
            jax.ShapeDtypeStruct((owners // 2, planes, share, columns), LOW),
        ),
        in_specs=[smem_spec()] + [whole_spec()] * (12 + owners // 2) + [hbm_spec()] * owners,
        out_specs=[whole_spec()] + [hbm_spec()] * 2,
        scratch_shapes=[
            pltpu.VMEM((width, columns), LOW),
            pltpu.VMEM((width, columns), LOW),
            pltpu.VMEM((length, width), LOW),
            pltpu.VMEM((length, width), LOW),
            pltpu.SemaphoreType.DMA((owners, planes)),
            pltpu.SemaphoreType.DMA((owners, planes)),
        ],
        compiler_params=params(),
        name="attn_backward",
    )(
        rows,
        tokens,
        seg_col,
        seg_row,
        cosine,
        sine,
        payload,
        hidden,
        query_rot,
        keyval_low,
        mixed_low,
        gates,
        out_grad,
        *back,
        *pieces,
    )

    mine = to_owners(grads_even, grads_odd)
    mine = sum(part.astype(F32) for part in mine)
    mine_low = mine.astype(LOW)
    summed = mine_low[0].astype(F32)
    for w in range(1, planes):
        summed = summed + swap(mine_low[w], "dp", planes, w).astype(F32)

    made = to_owners(out_even, out_odd)
    layer_out = (hidden + sum(part.astype(F32) for part in made)).astype(LOW)

    up_grad, down_grad = pl.pallas_call(
        functools.partial(expert_away_kernel, owners, local, block),
        grid=(planes - 1,),
        out_shape=slabs,
        in_specs=[smem_spec()]
        + [pl.BlockSpec((1, length + TAIL, width), lambda w: (w, 0, 0))] * owners
        + [pl.BlockSpec((1, length, width), lambda w: (w + 1, 0, 0))] * owners
        + [whole_spec()] * 4,
        out_specs=[whole_spec()] * 2,
        scratch_shapes=[
            pltpu.VMEM((local, slots, width), LOW),
            pltpu.VMEM((local, slots, width), LOW),
            pltpu.VMEM((local, slots, LANES), F32),
        ],
        compiler_params=params(),
        name="expert_away",
    )(place, *away_rows, *grad_pieces, expert_up, expert_down, up_grad, down_grad)

    return (
        layer_out,
        tokens_grad,
        summed[:, :width],
        summed[:, width : 2 * width],
        summed[:, 2 * width : 3 * width],
        summed[:, 3 * width : 3 * width + EXPERTS],
        summed[:, 3 * width + EXPERTS],
        summed[:, 3 * width + EXPERTS + 1],
        up_grad,
        down_grad,
    )


def solution(mesh):
    return jax.shard_map(
        functools.partial(on_device, mesh.shape["dp"], mesh.shape["expert"]),
        mesh=mesh,
        in_specs=(
            P(("dp", "expert"), None),
            P(("dp", "expert"), None),
            P(("dp", "expert"), None),
            P(("dp", "expert"), None),
            P(("dp", "expert"), None),
            P(("dp", "expert"), None),
            P(("dp", "expert"), None),
            P(("dp", "expert")),
            P(("dp", "expert")),
            P("expert", None, None),
            P("expert", None, None),
            P(("dp", "expert"), None),
        ),
        out_specs=(
            P(("dp", "expert"), None),
            P(("dp", "expert"), None),
            P(("dp", "expert"), None),
            P(("dp", "expert"), None),
            P(("dp", "expert"), None),
            P(("dp", "expert"), None),
            P(("dp", "expert")),
            P(("dp", "expert")),
            P("expert", "dp", None),
            P("expert", "dp", None),
        ),
        check_vma=False,
    )
```

```python
import functools

import jax
import jax.numpy as jnp
from jax import lax
from jax.sharding import PartitionSpec as P
from jax.experimental import pallas as pl
from jax.experimental.pallas import tpu as pltpu

HEAD_DIM = 64
FF = 512
EXPERTS = 32
TOP = 8
CAP = 40


EPS = 1e-05
ROPE_BASE = 10000.0
MASKED = -1e30
HIGH = lax.Precision.HIGHEST


def norm_forward(values, gain_vec):
    inverse = lax.rsqrt(jnp.mean(values * values, axis=-1, keepdims=True) + EPS)
    normed = values * inverse
    return (normed, inverse, (normed * gain_vec).astype(jnp.bfloat16))


def norm_backward(grad_out, normed, inverse, gain_vec):
    gain_grad = jnp.sum(grad_out * normed, axis=0)
    scaled = grad_out * gain_vec
    grad_in = inverse * (scaled - normed * jnp.mean(scaled * normed, axis=-1, keepdims=True))
    return (grad_in, gain_grad)


def rope_tables(segment_row):
    length = segment_row.shape[0]
    earlier = jnp.sum((segment_row[None, :] < segment_row[:, None]).astype(jnp.int32), axis=1)
    position = jnp.arange(length, dtype=jnp.int32) - earlier
    half_dim = HEAD_DIM // 2
    frequency = ROPE_BASE ** (-(jnp.arange(half_dim, dtype=jnp.float32) * 2.0) / HEAD_DIM)
    angles = position.astype(jnp.float32)[:, None] * frequency[None, :]
    cosine = jnp.concatenate([jnp.cos(angles), jnp.cos(angles)], axis=-1)[:, None, :]
    sine_table = jnp.concatenate([jnp.sin(angles), jnp.sin(angles)], axis=-1)[:, None, :]
    return (cosine, sine_table)


def rotate(values, cosine, sine_table):
    half_dim = values.shape[-1] // 2
    turned = jnp.concatenate([-values[..., half_dim:], values[..., :half_dim]], axis=-1)
    return values * cosine + turned * sine_table


def unrotate(grad_rows, cosine, sine_table):
    half_dim = grad_rows.shape[-1] // 2
    weighted = grad_rows * sine_table
    turned = jnp.concatenate([weighted[..., half_dim:], -weighted[..., :half_dim]], axis=-1)
    return grad_rows * cosine + turned


def on_device_wide(
    tokens,
    segments,
    routes,
    query_weight,
    keyval_weight,
    output_weight,
    router_weight,
    attn_gain,
    moe_gain,
    expert_up,
    expert_down,
    out_grad,
):
    owners = lax.axis_size("expert")
    local_experts = expert_up.shape[0]
    length = tokens.shape[0]
    model_width = tokens.shape[1]
    kv_heads = keyval_weight.shape[1] // (2 * HEAD_DIM)
    query_heads = query_weight.shape[1] // HEAD_DIM
    repeat = query_heads // kv_heads
    score_scale = HEAD_DIM ** (-0.5)
    query_full, keyval_full, output_full, router_full, attn_gains, moe_gains = (
        lax.all_gather(query_weight, ("dp", "expert"), axis=0, tiled=True),
        lax.all_gather(keyval_weight, ("dp", "expert"), axis=0, tiled=True),
        lax.all_gather(output_weight, ("dp", "expert"), axis=0, tiled=True),
        lax.all_gather(router_weight, ("dp", "expert"), axis=0, tiled=True),
        lax.all_gather(attn_gain, ("dp", "expert"), axis=0, tiled=True),
        lax.all_gather(moe_gain, ("dp", "expert"), axis=0, tiled=True),
    )
    resident = tokens.astype(jnp.float32)
    normed_one, inverse_one, attn_in = norm_forward(resident, attn_gains.astype(jnp.float32))
    query_proj = jnp.dot(attn_in, query_full, preferred_element_type=jnp.float32).reshape(
        length, query_heads, HEAD_DIM
    )
    keyval_proj = jnp.dot(attn_in, keyval_full, preferred_element_type=jnp.float32)
    key_rows = keyval_proj[:, : kv_heads * HEAD_DIM].reshape(length, kv_heads, HEAD_DIM)
    value_rows = keyval_proj[:, kv_heads * HEAD_DIM :].reshape(length, kv_heads, HEAD_DIM)
    cosine, sine_table = rope_tables(segments[0])
    query_rot = (
        rotate(query_proj, cosine, sine_table)
        .astype(jnp.bfloat16)
        .reshape(length, kv_heads, repeat, HEAD_DIM)
    )
    keys_rot = rotate(key_rows, cosine, sine_table).astype(jnp.bfloat16)
    values_low = value_rows.astype(jnp.bfloat16)
    places = jnp.arange(length)
    visible = (segments[0][:, None] == segments[0][None, :]) & (places[None, :] <= places[:, None])
    scores = jnp.einsum("ikrd,jkd->krij", query_rot, keys_rot, preferred_element_type=jnp.float32)
    attn_logits = jnp.where(visible, scores * score_scale, MASKED)
    attn_exps = jnp.exp(attn_logits - jnp.max(attn_logits, axis=-1, keepdims=True))
    attn_probs = attn_exps / jnp.sum(attn_exps, axis=-1, keepdims=True)
    probs_low = attn_probs.astype(jnp.bfloat16)
    mixed_heads = jnp.einsum(
        "krij,jkd->ikrd", probs_low, values_low, preferred_element_type=jnp.float32
    )
    mixed_low = mixed_heads.reshape(length, query_heads * HEAD_DIM).astype(jnp.bfloat16)
    hidden = resident + jnp.dot(mixed_low, output_full, preferred_element_type=jnp.float32)
    normed_two, inverse_two, moe_in = norm_forward(hidden, moe_gains.astype(jnp.float32))
    router_logits = jnp.dot(moe_in, router_full, preferred_element_type=jnp.float32)
    choose = (routes[:, :, None] == jnp.arange(EXPERTS, dtype=jnp.int32)[None, None, :]).astype(
        jnp.float32
    )
    chosen = jnp.sum(choose * router_logits[:, None, :], axis=-1)
    gate_exps = jnp.exp(chosen - jnp.max(chosen, axis=-1, keepdims=True))
    gate_probs = gate_exps / jnp.sum(gate_exps, axis=-1, keepdims=True)
    entries = routes.reshape(-1)
    entry_count = entries.shape[0]
    onehot = (entries[:, None] == jnp.arange(EXPERTS, dtype=jnp.int32)[None, :]).astype(jnp.int32)
    position = jnp.sum((jnp.cumsum(onehot, axis=0) - 1) * onehot, axis=1)
    slot_index = entries * CAP + position
    owner_entry = (
        jnp.full((EXPERTS * CAP,), entry_count, jnp.int32)
        .at[slot_index]
        .set(jnp.arange(entry_count, dtype=jnp.int32))
    )
    padded_in = jnp.concatenate([moe_in, jnp.zeros((1, model_width), jnp.bfloat16)], axis=0)
    send_rows = jnp.take(padded_in, owner_entry // TOP, axis=0).reshape(EXPERTS, CAP, model_width)
    received = lax.all_to_all(send_rows, "expert", split_axis=0, concat_axis=0, tiled=True)
    slots_now = received.shape[1]
    grouped = received.reshape(owners, local_experts, slots_now, model_width)
    pair_proj = jnp.einsum("secd,edf->secf", grouped, expert_up, preferred_element_type=jnp.float32)
    activated = (jax.nn.silu(pair_proj[..., :FF]) * pair_proj[..., FF:]).astype(jnp.bfloat16)
    produced = jnp.einsum(
        "secf,edf->secd", activated, expert_down, preferred_element_type=jnp.float32
    ).astype(jnp.bfloat16)
    returned = lax.all_to_all(
        produced.reshape(EXPERTS, slots_now, model_width),
        "expert",
        split_axis=0,
        concat_axis=0,
        tiled=True,
    )
    returned, kept_rows, kept_pair = (
        returned,
        received,
        pair_proj.reshape(EXPERTS, slots_now, 2 * FF),
    )
    gathered = (
        jnp.take(returned.reshape(EXPERTS * CAP, model_width), slot_index, axis=0)
        .astype(jnp.float32)
        .reshape(length, TOP, model_width)
    )
    layer_out = (hidden + jnp.sum(gate_probs[:, :, None] * gathered, axis=1)).astype(jnp.bfloat16)
    grad_top = out_grad.astype(jnp.float32)
    gate_grad = jnp.sum(gathered * grad_top[:, None, :], axis=-1)
    chosen_grad = gate_probs * (gate_grad - jnp.sum(gate_probs * gate_grad, axis=-1, keepdims=True))
    logits_grad = jnp.sum(chosen_grad[:, :, None] * choose, axis=1)
    row_grads = (
        (gate_probs[:, :, None] * grad_top[:, None, :])
        .astype(jnp.bfloat16)
        .reshape(entry_count, model_width)
    )
    padded_grads = jnp.concatenate([row_grads, jnp.zeros((1, model_width), jnp.bfloat16)], axis=0)
    send_grads = jnp.take(padded_grads, owner_entry, axis=0).reshape(EXPERTS, CAP, model_width)
    grads_in = lax.all_to_all(send_grads, "expert", split_axis=0, concat_axis=0, tiled=True)
    grouped_rows = kept_rows.reshape(owners, local_experts, CAP, model_width)
    grouped_grads = grads_in.reshape(owners, local_experts, CAP, model_width)
    pair_kept = kept_pair.reshape(owners, local_experts, CAP, 2 * FF)
    gate_half = pair_kept[..., :FF]
    up_half = pair_kept[..., FF:]
    sigmoid_gate = jax.nn.sigmoid(gate_half)
    silu_gate = jax.nn.silu(gate_half)
    activated = (silu_gate * up_half).astype(jnp.bfloat16)
    act_grad = jnp.einsum(
        "secd,edf->secf", grouped_grads, expert_down, preferred_element_type=jnp.float32
    )
    pair_grad = jnp.concatenate(
        [
            act_grad * up_half * sigmoid_gate * (1.0 + gate_half * (1.0 - sigmoid_gate)),
            act_grad * silu_gate,
        ],
        axis=-1,
    ).astype(jnp.bfloat16)
    rows_back = jnp.einsum(
        "secf,edf->secd", pair_grad, expert_up, preferred_element_type=jnp.float32
    ).astype(jnp.bfloat16)
    up_grad = jnp.einsum(
        "secd,secf->edf", grouped_rows, pair_grad, preferred_element_type=jnp.float32
    )
    down_grad = jnp.einsum(
        "secd,secf->edf", grouped_grads, activated, preferred_element_type=jnp.float32
    )
    returned_grads = lax.all_to_all(
        rows_back.reshape(EXPERTS, CAP, model_width),
        "expert",
        split_axis=0,
        concat_axis=0,
        tiled=True,
    )
    expert_up_grad, expert_down_grad = (
        lax.psum_scatter(
            up_grad.astype(jnp.bfloat16), "dp", scatter_dimension=1, tiled=True
        ).astype(jnp.float32),
        lax.psum_scatter(
            down_grad.astype(jnp.bfloat16), "dp", scatter_dimension=1, tiled=True
        ).astype(jnp.float32),
    )
    token_grads = (
        jnp.take(returned_grads.reshape(EXPERTS * CAP, model_width), slot_index, axis=0)
        .astype(jnp.float32)
        .reshape(length, TOP, model_width)
    )
    router_wide = router_full.astype(jnp.float32)
    moe_grad = jnp.sum(token_grads, axis=1) + jnp.dot(logits_grad, router_wide.T, precision=HIGH)
    hidden_norm_grad, moe_gain_grad = norm_backward(
        moe_grad, normed_two, inverse_two, moe_gains.astype(jnp.float32)
    )
    hidden_grad = grad_top + hidden_norm_grad
    attn_out_grad = hidden_grad.astype(jnp.bfloat16)
    mixed_grad = (
        jnp.einsum("td,cd->tc", attn_out_grad, output_full, preferred_element_type=jnp.float32)
        .astype(jnp.bfloat16)
        .reshape(length, kv_heads, repeat, HEAD_DIM)
    )
    probs_grad = jnp.einsum(
        "ikrd,jkd->krij", mixed_grad, values_low, preferred_element_type=jnp.float32
    )
    values_grad = jnp.einsum(
        "krij,ikrd->jkd", probs_low, mixed_grad, preferred_element_type=jnp.float32
    )
    scores_grad = (
        attn_probs
        * (probs_grad - jnp.sum(attn_probs * probs_grad, axis=-1, keepdims=True))
        * score_scale
    ).astype(jnp.bfloat16)
    query_rot_grad = jnp.einsum(
        "krij,jkd->ikrd", scores_grad, keys_rot, preferred_element_type=jnp.float32
    ).reshape(length, query_heads, HEAD_DIM)
    keys_rot_grad = jnp.einsum(
        "krij,ikrd->jkd", scores_grad, query_rot, preferred_element_type=jnp.float32
    )
    query_low = (
        unrotate(query_rot_grad, cosine, sine_table)
        .reshape(length, query_heads * HEAD_DIM)
        .astype(jnp.bfloat16)
    )
    keyval_low = jnp.concatenate(
        [
            unrotate(keys_rot_grad, cosine, sine_table).reshape(length, kv_heads * HEAD_DIM),
            values_grad.reshape(length, kv_heads * HEAD_DIM),
        ],
        axis=1,
    ).astype(jnp.bfloat16)
    attn_in_grad = jnp.einsum(
        "tc,dc->td", query_low, query_full, preferred_element_type=jnp.float32
    ) + jnp.einsum("tc,dc->td", keyval_low, keyval_full, preferred_element_type=jnp.float32)
    token_norm_grad, attn_gain_grad = norm_backward(
        attn_in_grad, normed_one, inverse_one, attn_gains.astype(jnp.float32)
    )
    tokens_grad = hidden_grad + token_norm_grad
    slab_count = lax.axis_size("dp")
    slab_index = lax.axis_index("dp")
    width_rows = model_width // slab_count
    head_rows = query_heads * HEAD_DIM // slab_count
    all_attn, all_query, all_keyval, all_mixed, all_outgrad = (
        lax.all_gather(attn_in, "dp", axis=0, tiled=True),
        lax.all_gather(query_low, "dp", axis=0, tiled=True),
        lax.all_gather(keyval_low, "dp", axis=0, tiled=True),
        lax.all_gather(mixed_low, "dp", axis=0, tiled=True),
        lax.all_gather(attn_out_grad, "dp", axis=0, tiled=True),
    )
    all_moe, all_logits, attn_gain_rows, moe_gain_rows = (
        lax.all_gather(
            moe_in.astype(jnp.float32).astype(jnp.bfloat16), "dp", axis=0, tiled=True
        ).astype(jnp.float32),
        lax.all_gather(logits_grad.astype(jnp.bfloat16), "dp", axis=0, tiled=True).astype(
            logits_grad.dtype
        ),
        lax.all_gather(
            attn_gain_grad[None, :].astype(jnp.bfloat16), "dp", axis=0, tiled=True
        ).astype(jnp.float32),
        lax.all_gather(
            moe_gain_grad[None, :].astype(jnp.bfloat16), "dp", axis=0, tiled=True
        ).astype(jnp.float32),
    )
    attn_cols = lax.dynamic_slice_in_dim(all_attn, slab_index * width_rows, width_rows, 1)
    mixed_cols = lax.dynamic_slice_in_dim(all_mixed, slab_index * head_rows, head_rows, 1)
    moe_cols = lax.dynamic_slice_in_dim(all_moe, slab_index * width_rows, width_rows, 1)
    query_part = jnp.einsum("td,tc->dc", attn_cols, all_query, preferred_element_type=jnp.float32)
    keyval_part = jnp.einsum("td,tc->dc", attn_cols, all_keyval, preferred_element_type=jnp.float32)
    output_part = jnp.einsum(
        "tc,td->cd", mixed_cols, all_outgrad, preferred_element_type=jnp.float32
    )
    router_part = jnp.dot(moe_cols.T, all_logits, precision=HIGH)
    attn_gain_part = lax.dynamic_slice_in_dim(
        jnp.sum(attn_gain_rows, axis=0), slab_index * width_rows, width_rows, 0
    )
    moe_gain_part = lax.dynamic_slice_in_dim(
        jnp.sum(moe_gain_rows, axis=0), slab_index * width_rows, width_rows, 0
    )
    query_share, keyval_share, output_share, router_share, attn_share, moe_share = (
        lax.psum_scatter(
            query_part.astype(jnp.bfloat16), "expert", scatter_dimension=0, tiled=True
        ).astype(jnp.float32),
        lax.psum_scatter(
            keyval_part.astype(jnp.bfloat16), "expert", scatter_dimension=0, tiled=True
        ).astype(jnp.float32),
        lax.psum_scatter(
            output_part.astype(jnp.bfloat16), "expert", scatter_dimension=0, tiled=True
        ).astype(jnp.float32),
        lax.psum_scatter(
            router_part.astype(jnp.bfloat16), "expert", scatter_dimension=0, tiled=True
        ).astype(jnp.float32),
        lax.psum_scatter(
            attn_gain_part.astype(jnp.bfloat16), "expert", scatter_dimension=0, tiled=True
        ).astype(jnp.float32),
        lax.psum_scatter(
            moe_gain_part.astype(jnp.bfloat16), "expert", scatter_dimension=0, tiled=True
        ).astype(jnp.float32),
    )
    return (
        layer_out,
        tokens_grad,
        query_share,
        keyval_share,
        output_share,
        router_share,
        attn_share,
        moe_share,
        expert_up_grad,
        expert_down_grad,
    )


LANES = 128
TAIL = 16
PIECE_LIMIT = 4096
VMEM_BYTES = 60 * 1024 * 1024
F32 = jnp.float32
LOW = jnp.bfloat16


def contract(left, right, left_dim, right_dim):
    return lax.dot_general(
        left, right, (((left_dim,), (right_dim,)), ((), ())), preferred_element_type=F32
    )


def lane_index(shape):
    return lax.broadcasted_iota(jnp.int32, shape, len(shape) - 1)


def row_index(shape):
    return lax.broadcasted_iota(jnp.int32, shape, len(shape) - 2)


def half_turn(chunk):
    first = lane_index(chunk.shape) % HEAD_DIM < HEAD_DIM // 2
    ahead = pltpu.roll(chunk, LANES - HEAD_DIM // 2, 1)
    behind = pltpu.roll(chunk, HEAD_DIM // 2, 1)
    return jnp.where(first, ahead, behind)


def both_heads(chunk, pick):
    swapped = pltpu.roll(chunk, HEAD_DIM, 1)
    first = lane_index(chunk.shape) < HEAD_DIM
    if pick == 0:
        return jnp.where(first, chunk, swapped)
    return jnp.where(first, swapped, chunk)


def split_heads(chunk):
    first = lane_index(chunk.shape) < HEAD_DIM
    zero = jnp.zeros_like(chunk)
    return jnp.concatenate([jnp.where(first, chunk, zero), jnp.where(first, zero, chunk)], axis=0)


def join_heads(stacked):
    length = stacked.shape[0] // 2
    top, bottom = stacked[:length], stacked[length:]
    return jnp.where(lane_index(top.shape) < HEAD_DIM, top, bottom)


def three_parts(values):
    high = values.astype(LOW).astype(F32)
    rest = values - high
    middle = rest.astype(LOW).astype(F32)
    return (high, middle, rest - middle)


def gain_select():
    shape = (8, LANES)
    return (lane_index(shape) == EXPERTS + row_index(shape)) & (row_index(shape) < 2)


def load_weights(rows_ref, spots, piece_refs, weights, sems):
    copies = []
    for (p, first), piece in zip(spots, piece_refs):
        for w in range(piece.shape[0]):
            size = piece.shape[1]
            start = pl.multiple_of(rows_ref[p, first + w] * size, size)
            copies.append(
                pltpu.make_async_copy(
                    piece.at[w], weights.at[pl.ds(start, size)], sems.at[p, first + w]
                )
            )
    for copy in copies:
        copy.start()
    return copies


def store_sums(rows_ref, sums, grads_even, grads_odd, sems):
    copies = []
    for p in range(2 * grads_even.shape[0]):
        target = grads_even if p % 2 == 0 else grads_odd
        for w in range(target.shape[1]):
            size = target.shape[2]
            start = pl.multiple_of(rows_ref[p, w] * size, size)
            copies.append(
                pltpu.make_async_copy(
                    sums.at[pl.ds(start, size)], target.at[p // 2, w], sems.at[p, w]
                )
            )
    for copy in copies:
        copy.start()
    return copies


def softmax_rows(q_pair, k_both, visible):
    scores = contract(q_pair, k_both, 1, 1) * (HEAD_DIM ** (-0.5))
    logits = jnp.where(visible, scores, MASKED)
    exps = jnp.exp(logits - jnp.max(logits, axis=-1, keepdims=True))
    return exps / jnp.sum(exps, axis=-1, keepdims=True)


def visible_pairs(seg_col, seg_row):
    length = seg_col.shape[0]
    shape = (length, length)
    seen = (seg_col == seg_row) & (lane_index(shape) <= row_index(shape))
    return jnp.concatenate([seen, seen], axis=0)


def attn_forward_kernel(spots, *refs):
    count = len(spots)
    rows_ref, tokens_ref, seg_col, seg_row, cos_ref, sin_ref = refs[:6]
    pieces = refs[6 : 6 + count]
    query_ref, keyval_ref, mixed_ref, tail_ref, weights, sems = refs[6 + count :]
    copies = load_weights(rows_ref, spots, pieces, weights, sems)
    tokens = tokens_ref[...].astype(F32)
    inverse = lax.rsqrt(jnp.mean(tokens * tokens, axis=-1, keepdims=True) + EPS)
    normed = tokens * inverse
    width = tokens.shape[1]
    for copy in copies:
        copy.wait()
    tail = weights[:, 2 * width :]
    tail_ref[...] = tail
    gains = contract(gain_select().astype(F32).astype(LOW), tail, 1, 1)
    attn_in = (normed * gains[0:1]).astype(LOW)
    cosine, sine = cos_ref[...], sin_ref[...]
    keyval = contract(attn_in, weights[:, width : 2 * width], 1, 0)
    query = contract(attn_in, weights[:, :width], 1, 0)
    visible = visible_pairs(seg_col[...], seg_row[...])
    half = width // 2
    for m in range(half // LANES):
        keys = keyval[:, m * LANES : (m + 1) * LANES]
        keys = (keys * cosine + half_turn(keys) * sine).astype(LOW)
        values = keyval[:, half + m * LANES : half + (m + 1) * LANES].astype(LOW)
        keyval_ref[:, m * LANES : (m + 1) * LANES] = keys
        keyval_ref[:, half + m * LANES : half + (m + 1) * LANES] = values
        for pick in range(2):
            k_both = both_heads(keys.astype(F32), pick).astype(LOW)
            v_both = both_heads(values.astype(F32), pick).astype(LOW)
            chunk = slice((2 * m + pick) * LANES, (2 * m + pick + 1) * LANES)
            queries = query[:, chunk]
            queries = (queries * cosine + half_turn(queries) * sine).astype(LOW)
            query_ref[:, chunk] = queries
            q_pair = split_heads(queries.astype(F32)).astype(LOW)
            probs = softmax_rows(q_pair, k_both, visible).astype(LOW)
            mixed_ref[:, chunk] = join_heads(contract(probs, v_both, 1, 0)).astype(LOW)


def router_kernel(spots, *refs):
    count = len(spots)
    rows_ref, tokens_ref, mixed_ref, tail_ref, routes_ref, routes_t = refs[:6]
    pieces = refs[6 : 6 + count]
    payload, hidden_ref, gates_ref, weights, sems = refs[6 + count :]
    copies = load_weights(rows_ref, spots, pieces, weights, sems)
    tokens = tokens_ref[...].astype(F32)
    length = tokens.shape[0]
    tail = tail_ref[...]
    gains = contract(gain_select().astype(F32).astype(LOW), tail, 1, 1)
    for copy in copies:
        copy.wait()
    hidden = tokens + contract(mixed_ref[...], weights[...], 1, 0)
    hidden_ref[...] = hidden
    inverse_two = lax.rsqrt(jnp.mean(hidden * hidden, axis=-1, keepdims=True) + EPS)
    moe_in = (hidden * inverse_two * gains[1:2]).astype(LOW)
    payload[:length] = moe_in
    logits = contract(moe_in, tail, 1, 0)
    routes = routes_ref[...]
    lanes = lane_index((length, LANES))
    chosen = lanes == routes[:, 0:1]
    for k in range(1, TOP):
        chosen = chosen | (lanes == routes[:, k : k + 1])
    logits = jnp.where(chosen, logits, MASKED)
    exps = jnp.where(chosen, jnp.exp(logits - jnp.max(logits, axis=-1, keepdims=True)), 0.0)
    gates = exps / jnp.sum(exps, axis=-1, keepdims=True)
    gates_ref[...] = gates
    gates_t = gates.T
    experts = row_index((LANES, length))
    turned = routes_t[...]
    for k in range(TOP):
        row = turned[k : k + 1]
        gate = jnp.sum(jnp.where(experts == row, gates_t, 0.0), axis=0, keepdims=True)
        high, middle, rest = three_parts(gate)
        place = row_index((TAIL, length))
        block = jnp.where(place == 0, high, jnp.where(place == 1, middle, jnp.where(place == 2, rest, 0.0)))
        block = jnp.where(place == 3, row.astype(F32), block)
        payload[length:, k * length : (k + 1) * length] = block.astype(LOW)


def gather_pair(first_expert, local, block, rows_a, rows_b, grads_a, grads_b, before, out):
    rows_out, grads_out, select_out, gate_out, pair = out
    length = rows_a.shape[0] - TAIL
    ids = row_index((8, length)) + first_expert
    ids = jnp.where(row_index((8, length)) < local, ids, -1).astype(F32)
    masks, gates = [], []
    for piece in (rows_a, rows_b):
        tail = piece[length:].astype(F32)
        mask = jnp.zeros((8, length), F32)
        gate = jnp.zeros((8, length), F32)
        for k in range(TOP):
            part = tail[:, k * length : (k + 1) * length]
            hit = part[3:4] == ids
            mask = jnp.where(hit, 1.0, mask)
            gate = jnp.where(hit, part[0:1] + part[1:2] + part[2:3], gate)
        masks.append(mask)
        gates.append(gate)
    mask = jnp.concatenate(masks, axis=1)
    gate = jnp.concatenate(gates, axis=1)
    place = contract(mask.astype(LOW), before, 1, 0)
    place = jnp.where(mask > 0, place, -1.0)
    slots = row_index((block, 2 * length)).astype(F32)
    parts = []
    for j in range(local):
        hit = slots == place[j : j + 1]
        parts.append(jnp.where(hit, 1.0, 0.0))
        held = jnp.sum(jnp.where(hit, gate[j : j + 1], 0.0), axis=1, keepdims=True)
        gate_out[j, pair * block : (pair + 1) * block] = jnp.broadcast_to(held, (block, LANES))
    select = jnp.concatenate(parts, axis=0).astype(LOW)
    if select_out is not None:
        select_out[pair] = select
    rows = jnp.concatenate([rows_a[:length], rows_b[:length]], axis=0)
    grads = jnp.concatenate([grads_a, grads_b], axis=0)
    rows = contract(select, rows, 1, 0).astype(LOW)
    grads = contract(select, grads, 1, 0).astype(LOW)
    for j in range(local):
        rows_out[j, pair * block : (pair + 1) * block] = rows[j * block : (j + 1) * block]
        grads_out[j, pair * block : (pair + 1) * block] = grads[j * block : (j + 1) * block]


def earlier_matrix(length):
    shape = (2 * length, 2 * length)
    return jnp.where(row_index(shape) < lane_index(shape), 1.0, 0.0).astype(LOW)


def expert_step(j, rows, grads, gate_ref, up, down):
    hidden_units = down.shape[1]
    pair = contract(rows[j], up, 1, 0)
    raw = contract(grads[j], down, 1, 0)
    gate_half, up_half = pair[:, :hidden_units], pair[:, hidden_units:]
    gate = gate_ref[j][:, 0:1]
    sigmoid = 1.0 / (1.0 + jnp.exp(-gate_half))
    silu = gate_half * sigmoid
    activated = silu * up_half
    scaled = (gate * activated).astype(LOW)
    act_grad = gate * raw
    pair_grad = jnp.concatenate(
        [act_grad * up_half * sigmoid * (1.0 + gate_half * (1.0 - sigmoid)), act_grad * silu],
        axis=1,
    ).astype(LOW)
    gate_grad = jnp.sum(activated * raw, axis=1, keepdims=True)
    return (scaled, pair_grad, gate_grad)


def fetch_experts(local, up_hbm, down_hbm, up, down, sems):
    copies = []
    for j in range(local):
        copies.append(
            (
                pltpu.make_async_copy(up_hbm.at[j], up.at[j], sems.at[0, j]),
                pltpu.make_async_copy(down_hbm.at[j], down.at[j], sems.at[1, j]),
            )
        )
        for copy in copies[j]:
            copy.start()
    return copies


def expert_home_kernel(owners, local, block, *refs):
    place_ref = refs[0]
    rows_in = refs[1 : 1 + owners]
    grads_in = refs[1 + owners : 1 + 2 * owners]
    up_hbm, down_hbm = refs[1 + 2 * owners : 3 + 2 * owners]
    out_even, out_odd, back_even, back_odd, up_grad, down_grad = refs[3 + 2 * owners : 9 + 2 * owners]
    up, down, rows, grads, select, gate_ref, produced, returned, sems = refs[9 + 2 * owners :]
    copies = fetch_experts(local, up_hbm, down_hbm, up, down, sems)
    length = rows_in[0].shape[0] - TAIL
    width = rows_in[0].shape[1]
    first_expert = place_ref[0] * local
    slab = up_grad.shape[1]
    columns = pl.ds(pl.multiple_of(place_ref[1] * slab, slab), slab)
    before = earlier_matrix(length)
    for s in range(owners // 2):
        gather_pair(
            first_expert,
            local,
            block,
            rows_in[2 * s][...],
            rows_in[2 * s + 1][...],
            grads_in[2 * s][...],
            grads_in[2 * s + 1][...],
            before,
            (rows, grads, select, gate_ref, s),
        )
    for j in range(local):
        for copy in copies[j]:
            copy.wait()
        scaled, pair_grad, gate_grad = expert_step(j, rows, grads, gate_ref, up[j], down[j])
        produced[j] = contract(scaled, down[j], 1, 1).astype(LOW)
        returned[j, :, :width] = contract(pair_grad, up[j], 1, 1).astype(LOW)
        lanes = lane_index((scaled.shape[0], LANES)) - first_expert - j
        high, middle, rest = three_parts(gate_grad)
        tail = jnp.where(lanes == 0, high, 0.0)
        tail = jnp.where(lanes == EXPERTS, middle, tail)
        tail = jnp.where(lanes == 2 * EXPERTS, rest, tail)
        returned[j, :, width:] = tail.astype(LOW)
        up_grad[j] = contract(rows[j, :, columns], pair_grad, 0, 0)
        down_grad[j] = contract(grads[j, :, columns], scaled, 0, 0)
    for s in range(owners // 2):
        span = slice(s * block, (s + 1) * block)
        made = jnp.concatenate([produced[j, span] for j in range(local)], axis=0)
        back = jnp.concatenate([returned[j, span] for j in range(local)], axis=0)
        made = contract(select[s], made, 0, 0).astype(LOW)
        back = contract(select[s], back, 0, 0).astype(LOW)
        out_even[s] = made[:length]
        out_odd[s] = made[length:]
        back_even[s] = back[:length]
        back_odd[s] = back[length:]


def expert_away_kernel(owners, local, block, *refs):
    place_ref = refs[0]
    rows_in = refs[1 : 1 + owners]
    grads_in = refs[1 + owners : 1 + 2 * owners]
    up_hbm, down_hbm, up_first, down_first = refs[1 + 2 * owners : 5 + 2 * owners]
    up_grad, down_grad = refs[5 + 2 * owners : 7 + 2 * owners]
    up, down, rows, grads, gate_ref, sems = refs[7 + 2 * owners :]
    copies = fetch_experts(local, up_hbm, down_hbm, up, down, sems)
    length = rows_in[0].shape[1] - TAIL
    first_expert = place_ref[0] * local
    slab = up_grad.shape[1]
    columns = pl.ds(pl.multiple_of(place_ref[1] * slab, slab), slab)
    before = earlier_matrix(length)
    for s in range(owners // 2):
        gather_pair(
            first_expert,
            local,
            block,
            rows_in[2 * s][0],
            rows_in[2 * s + 1][0],
            grads_in[2 * s][0],
            grads_in[2 * s + 1][0],
            before,
            (rows, grads, None, gate_ref, s),
        )
    for j in range(local):
        for copy in copies[j]:
            copy.wait()
        scaled, pair_grad, _ = expert_step(j, rows, grads, gate_ref, up[j], down[j])
        up_grad[j] = up_first[j] + contract(rows[j, :, columns], pair_grad, 0, 0)
        down_grad[j] = down_first[j] + contract(grads[j, :, columns], scaled, 0, 0)


def hidden_backward_kernel(spots, shares, *refs):
    count = len(spots)
    rows_ref, payload, hidden_ref, mixed_ref, gates_ref, out_grad_ref, tail_ref = refs[:7]
    back = refs[7 : 7 + shares]
    pieces = refs[7 + shares : 7 + shares + count]
    hidden_grad_ref, mixed_grad, tail_grad, grads_even, grads_odd = refs[7 + shares + count : 12 + shares + count]
    weights, sums, sems, out_sems = refs[12 + shares + count :]
    copies = load_weights(rows_ref, spots, pieces, weights, sems)
    length, width = hidden_ref.shape
    total = back[0][...].astype(F32)
    for share in back[1:]:
        total = total + share[...].astype(F32)
    parts = total[:, width:]
    lanes = lane_index(parts.shape)
    gate_grad = parts + pltpu.roll(parts, LANES - EXPERTS, 1) + pltpu.roll(parts, LANES - 2 * EXPERTS, 1)
    gate_grad = jnp.where(lanes < EXPERTS, gate_grad, 0.0)
    gates = gates_ref[...]
    logits_grad = gates * (gate_grad - jnp.sum(gates * gate_grad, axis=-1, keepdims=True))
    hidden = hidden_ref[...]
    inverse_two = lax.rsqrt(jnp.mean(hidden * hidden, axis=-1, keepdims=True) + EPS)
    normed_two = hidden * inverse_two
    tail = tail_ref[...]
    gains = contract(gain_select().astype(F32).astype(LOW), tail, 1, 1)
    high = logits_grad.astype(LOW)
    rest = (logits_grad - high.astype(F32)).astype(LOW)
    moe_grad = total[:, :width] + contract(high, tail, 1, 1) + contract(rest, tail, 1, 1)
    moe_gain_grad = jnp.sum(moe_grad * normed_two, axis=0, keepdims=True)
    scaled = moe_grad * gains[1:2]
    hidden_grad = out_grad_ref[...].astype(F32) + inverse_two * (
        scaled - normed_two * jnp.mean(scaled * normed_two, axis=-1, keepdims=True)
    )
    hidden_grad_ref[...] = hidden_grad
    attn_out_grad = hidden_grad.astype(LOW)
    sums[...] = contract(mixed_ref[...], attn_out_grad, 0, 0).astype(LOW)
    out_copies = store_sums(rows_ref, sums, grads_even, grads_odd, out_sems)
    for copy in copies:
        copy.wait()
    mixed_grad[...] = contract(attn_out_grad, weights[...], 1, 1).astype(LOW)
    gain_grads = jnp.where(row_index((8, width)) == 1, moe_gain_grad, 0.0)
    tail_grad[...] = contract(payload[:length], high, 0, 0) + contract(
        gain_grads.astype(LOW), gain_select().astype(F32).astype(LOW), 0, 0
    )
    for copy in out_copies:
        copy.wait()


def attn_backward_kernel(spots, *refs):
    count = len(spots)
    rows_ref, tokens_ref, seg_col, seg_row, cos_ref, sin_ref = refs[:6]
    query_ref, keyval_ref, mixed_grad, hidden_grad, tail_ref, tail_grad = refs[6:12]
    pieces = refs[12 : 12 + count]
    tokens_grad, grads_even, grads_odd = refs[12 + count : 15 + count]
    weights, sums, query_low, keyval_low, sems, out_sems = refs[15 + count :]
    copies = load_weights(rows_ref, spots, pieces, weights, sems)
    length, width = tokens_ref.shape
    half = width // 2
    tokens = tokens_ref[...].astype(F32)
    inverse_one = lax.rsqrt(jnp.mean(tokens * tokens, axis=-1, keepdims=True) + EPS)
    normed_one = tokens * inverse_one
    gains = contract(gain_select().astype(F32).astype(LOW), tail_ref[...], 1, 1)
    cosine, sine = cos_ref[...], sin_ref[...]
    visible = visible_pairs(seg_col[...], seg_row[...])
    for m in range(half // LANES):
        keys = keyval_ref[:, m * LANES : (m + 1) * LANES].astype(F32)
        values = keyval_ref[:, half + m * LANES : half + (m + 1) * LANES].astype(F32)
        key_sides, value_sides = [], []
        for pick in range(2):
            k_both = both_heads(keys, pick).astype(LOW)
            v_both = both_heads(values, pick).astype(LOW)
            chunk = slice((2 * m + pick) * LANES, (2 * m + pick + 1) * LANES)
            q_pair = split_heads(query_ref[:, chunk].astype(F32)).astype(LOW)
            m_pair = split_heads(mixed_grad[:, chunk].astype(F32)).astype(LOW)
            probs = softmax_rows(q_pair, k_both, visible)
            probs_grad = contract(m_pair, v_both, 1, 1)
            value_sides.append(contract(probs.astype(LOW), m_pair, 0, 0))
            scores_grad = (
                probs
                * (probs_grad - jnp.sum(probs * probs_grad, axis=-1, keepdims=True))
                * (HEAD_DIM ** (-0.5))
            ).astype(LOW)
            query_grad = join_heads(contract(scores_grad, k_both, 1, 0))
            query_low[:, chunk] = (query_grad * cosine - half_turn(query_grad) * sine).astype(LOW)
            key_sides.append(contract(scores_grad, q_pair, 0, 0))
        first = lane_index((length, LANES)) < HEAD_DIM
        key_sides = [side + pltpu.roll(side, HEAD_DIM, 1) for side in key_sides]
        value_sides = [side + pltpu.roll(side, HEAD_DIM, 1) for side in value_sides]
        keys_grad = jnp.where(first, key_sides[0], key_sides[1])
        values_grad = jnp.where(first, value_sides[0], value_sides[1])
        keyval_low[:, m * LANES : (m + 1) * LANES] = (
            keys_grad * cosine - half_turn(keys_grad) * sine
        ).astype(LOW)
        keyval_low[:, half + m * LANES : half + (m + 1) * LANES] = values_grad.astype(LOW)
    for copy in copies:
        copy.wait()
    attn_in_grad = contract(query_low[...], weights[:, :width], 1, 1) + contract(
        keyval_low[...], weights[:, width : 2 * width], 1, 1
    )
    attn_in = (normed_one * gains[0:1]).astype(LOW)
    sums[:, :width] = contract(attn_in, query_low[...], 0, 0).astype(LOW)
    sums[:, width : 2 * width] = contract(attn_in, keyval_low[...], 0, 0).astype(LOW)
    attn_gain_grad = jnp.sum(attn_in_grad * normed_one, axis=0, keepdims=True)
    gain_grads = jnp.where(row_index((8, width)) == 0, attn_gain_grad, 0.0)
    sums[:, 2 * width :] = (
        tail_grad[...]
        + contract(gain_grads.astype(LOW), gain_select().astype(F32).astype(LOW), 0, 0)
    ).astype(LOW)
    out_copies = store_sums(rows_ref, sums, grads_even, grads_odd, out_sems)
    scaled = attn_in_grad * gains[0:1]
    tokens_grad[...] = hidden_grad[...] + inverse_one * (
        scaled - normed_one * jnp.mean(scaled * normed_one, axis=-1, keepdims=True)
    )
    for copy in out_copies:
        copy.wait()


def swap(values, axis, size, distance):
    return lax.ppermute(values, axis, [(i, i ^ distance) for i in range(size)])


def across(values, distance, planes):
    return swap(values, "dp", planes, distance)


def aside(values, s, owners):
    return swap(values, "expert", owners, 2 * s)


def partner(values, owners):
    return swap(values, "expert", owners, 1)


def after(values, *earlier):
    return lax.optimization_barrier((values,) + earlier)[0]


def over_chips(values, owners):
    return [values] + [aside(values, s, owners) for s in range(1, owners // 2)]


def over_cores(near, owners):
    pieces = []
    for piece in near:
        pieces += [piece, partner(piece, owners)]
    return pieces


def chips_split(values, owners, *earlier):
    chips = owners // 2
    if chips != 4:
        return [[values]] + [[aside(values, s, owners)] for s in range(1, chips)]
    half = values.shape[0] // 2
    first, second = aside(values, 1, owners), aside(values, 2, owners)
    far = [
        aside(after(first[:half], *earlier), 2, owners),
        aside(after(second[half:], *earlier), 1, owners),
    ]
    return [[values], [first], [second], far]


def core_pieces(near, owners):
    pieces, spots, chips = [], [], []
    for s, parts in enumerate(near):
        first = 0
        for part in parts:
            pieces += [part, partner(part, owners)]
            spots += [(2 * s, first), (2 * s + 1, first)]
            chips.append(part)
            first += part.shape[0]
    return (pieces, spots, chips)


def core_pieces_whole(near, owners):
    pieces = []
    for parts in near:
        piece = parts[0] if len(parts) == 1 else jnp.concatenate(parts, axis=0)
        pieces += [piece, partner(piece, owners)]
    return pieces


def added(left, right):
    return (left.astype(F32) + right.astype(F32)).astype(LOW)


def to_owners(even, odd, owners):
    other = partner(odd, owners)
    joined = [added(even[s], other[s]) for s in range(owners // 2)]
    return [joined[0]] + [aside(joined[s], s, owners) for s in range(1, owners // 2)]


def to_owners_split(even, odd, owners):
    chips = owners // 2
    if chips != 4:
        parts = to_owners(even, odd, owners)
        return [sum(part.astype(F32) for part in parts)]
    other = partner(odd, owners)
    half = even.shape[1] // 2
    low = [added(even[s, :half], other[s, :half]) for s in range(chips)]
    top = [added(even[s, half:], other[s, half:]) for s in range(chips)]
    low_turn = aside(low[3], 1, owners)
    top_turn = aside(top[3], 2, owners)
    low_sum = [low[0], aside(low[1], 1, owners), aside(added(low[2], low_turn), 2, owners)]
    top_sum = [top[0], aside(top[2], 2, owners), aside(added(top[1], top_turn), 1, owners)]
    return [sum(part.astype(F32) for part in parts) for parts in (low_sum, top_sum)]


def over_planes_sum(halves, planes):
    parts = [half[i] for half in halves for i in range(half.shape[0])]
    low = [part.astype(LOW) for part in parts]
    total = low[0].astype(F32)
    for w in range(1, planes):
        total = total + across(low[w], w, planes).astype(F32)
    return total


def cost(us):
    return pl.CostEstimate(flops=int(us * 1153e6), bytes_accessed=0, transcendentals=0)


def params():
    return pltpu.CompilerParams(vmem_limit_bytes=VMEM_BYTES)


def whole_spec():
    return pl.BlockSpec(memory_space=pltpu.VMEM)


def hbm_spec():
    return pl.BlockSpec(memory_space=pl.ANY)


def smem_spec():
    return pl.BlockSpec(memory_space=pltpu.SMEM)


def on_device(
    planes,
    owners,
    tokens,
    segments,
    routes,
    query_weight,
    keyval_weight,
    output_weight,
    router_weight,
    attn_gain,
    moe_gain,
    expert_up,
    expert_down,
    out_grad,
):
    length, width = tokens.shape
    if planes * owners * length > PIECE_LIMIT:
        return on_device_wide(
            tokens,
            segments,
            routes,
            query_weight,
            keyval_weight,
            output_weight,
            router_weight,
            attn_gain,
            moe_gain,
            expert_up,
            expert_down,
            out_grad,
        )
    local = expert_up.shape[0]
    hidden_units = expert_down.shape[2]
    block = 2 * CAP
    slots = owners // 2 * block
    plane = lax.axis_index("dp")
    owner = lax.axis_index("expert")
    share = query_weight.shape[0]
    rows = (plane ^ jnp.arange(planes))[None, :] * owners + (owner ^ jnp.arange(owners))[:, None]
    rows = rows.astype(jnp.int32)
    place = jnp.stack([owner, plane]).astype(jnp.int32)
    extra = jnp.concatenate(
        [
            router_weight,
            attn_gain[:, None],
            moe_gain[:, None],
            jnp.zeros((share, LANES - EXPERTS - 2), LOW),
        ],
        axis=1,
    )
    packed = jnp.concatenate([query_weight, keyval_weight, extra], axis=1)
    columns = packed.shape[1]

    early = [across(packed, w, planes) for w in range(1, planes)]
    grad_chips = over_chips(out_grad, owners)
    near = chips_split(after(jnp.stack([packed] + early), *grad_chips), owners)
    pieces, spots, chips = core_pieces(near, owners)
    output_start = after(output_weight, *early)
    late = [across(output_start, w, planes) for w in range(1, planes)]
    output_stack = after(jnp.stack([output_weight] + late), *chips)
    grad_start = after(out_grad, *late)
    grad_planes = [across(grad_start, w, planes) for w in range(1, planes)]

    segment_row = segments[0]
    earlier = jnp.sum((segment_row[None, :] < segment_row[:, None]).astype(jnp.int32), axis=1)
    position = (jnp.arange(length, dtype=jnp.int32) - earlier).astype(F32)
    half_dim = HEAD_DIM // 2
    frequency = ROPE_BASE ** (-(jnp.arange(half_dim, dtype=F32) * 2.0) / HEAD_DIM)
    angles = position[:, None] * frequency[None, :]
    cosine = jnp.tile(jnp.cos(angles), (1, LANES // half_dim))
    sine = jnp.sin(angles)
    sine = jnp.concatenate([-sine, sine, -sine, sine], axis=1)
    seg_col, seg_row = segment_row[:, None], segment_row[None, :]

    token_low = jax.ShapeDtypeStruct((length, width), LOW)
    token_wide = jax.ShapeDtypeStruct((length, width), F32)
    query_rot, keyval_low, mixed_low, tail = pl.pallas_call(
        functools.partial(attn_forward_kernel, spots),
        out_shape=(token_low, token_low, token_low, jax.ShapeDtypeStruct((width, LANES), LOW)),
        in_specs=[smem_spec()] + [whole_spec()] * 5 + [hbm_spec()] * len(pieces),
        out_specs=[whole_spec()] * 4,
        scratch_shapes=[
            pltpu.VMEM((width, columns), LOW),
            pltpu.SemaphoreType.DMA((owners, planes)),
        ],
        compiler_params=params(),
        cost_estimate=cost(6),
        name="attn_forward",
    )(rows, after(tokens, *grad_planes), seg_col, seg_row, cosine, sine, *pieces)

    output_near = chips_split(output_stack, owners, mixed_low)
    output_pieces, output_spots, output_chips = core_pieces(output_near, owners)
    grad_home = over_cores(grad_chips, owners)

    payload, hidden, gates = pl.pallas_call(
        functools.partial(router_kernel, output_spots),
        out_shape=(
            jax.ShapeDtypeStruct((length + TAIL, width), LOW),
            token_wide,
            jax.ShapeDtypeStruct((length, LANES), F32),
        ),
        in_specs=[smem_spec()] + [whole_spec()] * 5 + [hbm_spec()] * len(output_pieces),
        out_specs=[whole_spec()] * 3,
        scratch_shapes=[
            pltpu.VMEM((width, width), LOW),
            pltpu.SemaphoreType.DMA((owners, planes)),
        ],
        compiler_params=params(),
        cost_estimate=cost(4),
        name="router",
    )(rows, tokens, mixed_low, tail, routes, routes.T, *output_pieces)

    row_chips = over_chips(payload, owners)
    row_home = over_cores(row_chips, owners)
    row_planes = [across(payload, w, planes) for w in range(1, planes)]
    away_near = chips_split(after(jnp.concatenate(grad_planes, axis=0), *row_chips), owners)
    grad_away = core_pieces_whole(away_near, owners)

    def all_of(shape):
        return pl.BlockSpec(shape, lambda i: (0,) * len(shape))

    slab = width // planes
    slabs = (
        jax.ShapeDtypeStruct((local, slab, 2 * hidden_units), F32),
        jax.ShapeDtypeStruct((local, slab, hidden_units), F32),
    )
    home_rows = after(row_home[0], *row_planes)
    out_even, out_odd, back_even, back_odd, up_grad, down_grad = pl.pallas_call(
        functools.partial(expert_home_kernel, owners, local, block),
        grid=(1,),
        out_shape=(
            jax.ShapeDtypeStruct((owners // 2, length, width), LOW),
            jax.ShapeDtypeStruct((owners // 2, length, width), LOW),
            jax.ShapeDtypeStruct((owners // 2, length, width + LANES), LOW),
            jax.ShapeDtypeStruct((owners // 2, length, width + LANES), LOW),
        )
        + slabs,
        in_specs=[smem_spec()]
        + [all_of((length + TAIL, width))] * owners
        + [all_of((length, width))] * owners
        + [hbm_spec()] * 2,
        out_specs=[all_of((owners // 2, length, width))] * 2
        + [all_of((owners // 2, length, width + LANES))] * 2
        + [all_of(part.shape) for part in slabs],
        scratch_shapes=[
            pltpu.VMEM(expert_up.shape, LOW),
            pltpu.VMEM(expert_down.shape, LOW),
            pltpu.VMEM((local, slots, width), LOW),
            pltpu.VMEM((local, slots, width), LOW),
            pltpu.VMEM((owners // 2, local * block, 2 * length), LOW),
            pltpu.VMEM((local, slots, LANES), F32),
            pltpu.VMEM((local, slots, width), LOW),
            pltpu.VMEM((local, slots, width + LANES), LOW),
            pltpu.SemaphoreType.DMA((2, local)),
        ],
        compiler_params=params(),
        cost_estimate=cost(22),
        name="expert_home",
    )(place, home_rows, *row_home[1:], *grad_home, expert_up, expert_down)

    back = to_owners(back_even, after(back_odd, away_near[1][0], away_near[2][0]), owners)
    row_near = chips_split(after(jnp.concatenate(row_planes, axis=0), *back), owners)
    row_away = core_pieces_whole(row_near, owners)

    def share_pieces(wide):
        return jax.ShapeDtypeStruct((owners // 2, planes, share, wide), LOW)

    hidden_grad, mixed_grad, tail_grad, output_even, output_odd = pl.pallas_call(
        functools.partial(hidden_backward_kernel, output_spots, owners // 2),
        out_shape=(
            token_wide,
            token_low,
            jax.ShapeDtypeStruct((width, LANES), F32),
            share_pieces(width),
            share_pieces(width),
        ),
        in_specs=[smem_spec()]
        + [whole_spec()] * (6 + owners // 2)
        + [hbm_spec()] * len(output_pieces),
        out_specs=[whole_spec()] * 3 + [hbm_spec()] * 2,
        scratch_shapes=[
            pltpu.VMEM((width, width), LOW),
            pltpu.VMEM((width, width), LOW),
            pltpu.SemaphoreType.DMA((owners, planes)),
            pltpu.SemaphoreType.DMA((owners, planes)),
        ],
        compiler_params=params(),
        cost_estimate=cost(6),
        name="hidden_backward",
    )(
        rows,
        payload,
        hidden,
        mixed_low,
        gates,
        out_grad,
        tail,
        *back,
        *output_pieces,
    )

    tokens_grad, grads_even, grads_odd = pl.pallas_call(
        functools.partial(attn_backward_kernel, spots),
        out_shape=(token_wide, share_pieces(columns), share_pieces(columns)),
        in_specs=[smem_spec()] + [whole_spec()] * 11 + [hbm_spec()] * len(pieces),
        out_specs=[whole_spec()] + [hbm_spec()] * 2,
        scratch_shapes=[
            pltpu.VMEM((width, columns), LOW),
            pltpu.VMEM((width, columns), LOW),
            pltpu.VMEM((length, width), LOW),
            pltpu.VMEM((length, width), LOW),
            pltpu.SemaphoreType.DMA((owners, planes)),
            pltpu.SemaphoreType.DMA((owners, planes)),
        ],
        compiler_params=params(),
        cost_estimate=cost(13),
        name="attn_backward",
    )(
        rows,
        tokens,
        seg_col,
        seg_row,
        cosine,
        sine,
        query_rot,
        keyval_low,
        mixed_grad,
        after(hidden_grad, *away_near[3]),
        tail,
        tail_grad,
        *pieces,
    )

    output_share = over_planes_sum(to_owners_split(output_even, output_odd, owners), planes)
    summed = over_planes_sum(to_owners_split(grads_even, grads_odd, owners), planes)
    made = jnp.concatenate(
        to_owners_split(after(out_even, tokens_grad), after(out_odd, tokens_grad), owners), axis=0
    )
    layer_out = (hidden + made).astype(LOW)

    for w in range(planes - 1):
        up_grad, down_grad = pl.pallas_call(
            functools.partial(expert_away_kernel, owners, local, block),
            grid=(1,),
            out_shape=slabs,
            in_specs=[smem_spec()]
            + [pl.BlockSpec((1, length + TAIL, width), lambda i, w=w: (w, 0, 0))] * owners
            + [pl.BlockSpec((1, length, width), lambda i, w=w: (w, 0, 0))] * owners
            + [hbm_spec()] * 2
            + [all_of(part.shape) for part in slabs],
            out_specs=[all_of(part.shape) for part in slabs],
            scratch_shapes=[
                pltpu.VMEM(expert_up.shape, LOW),
                pltpu.VMEM(expert_down.shape, LOW),
                pltpu.VMEM((local, slots, width), LOW),
                pltpu.VMEM((local, slots, width), LOW),
                pltpu.VMEM((local, slots, LANES), F32),
                pltpu.SemaphoreType.DMA((2, local)),
            ],
            input_output_aliases={2 * owners + 3: 0, 2 * owners + 4: 1},
            compiler_params=params(),
            cost_estimate=cost(15),
            name="expert_away",
        )(
            place,
            *[piece.reshape(planes - 1, length + TAIL, width) for piece in row_away],
            *[piece.reshape(planes - 1, length, width) for piece in grad_away],
            expert_up,
            expert_down,
            up_grad,
            down_grad,
        )

    return (
        layer_out,
        tokens_grad,
        summed[:, :width],
        summed[:, width : 2 * width],
        output_share,
        summed[:, 2 * width : 2 * width + EXPERTS],
        summed[:, 2 * width + EXPERTS],
        summed[:, 2 * width + EXPERTS + 1],
        up_grad,
        down_grad,
    )


def solution(mesh):
    return jax.shard_map(
        functools.partial(on_device, mesh.shape["dp"], mesh.shape["expert"]),
        mesh=mesh,
        in_specs=(
            P(("dp", "expert"), None),
            P(("dp", "expert"), None),
            P(("dp", "expert"), None),
            P(("dp", "expert"), None),
            P(("dp", "expert"), None),
            P(("dp", "expert"), None),
            P(("dp", "expert"), None),
            P(("dp", "expert")),
            P(("dp", "expert")),
            P("expert", None, None),
            P("expert", None, None),
            P(("dp", "expert"), None),
        ),
        out_specs=(
            P(("dp", "expert"), None),
            P(("dp", "expert"), None),
            P(("dp", "expert"), None),
            P(("dp", "expert"), None),
            P(("dp", "expert"), None),
            P(("dp", "expert"), None),
            P(("dp", "expert")),
            P(("dp", "expert")),
            P("expert", "dp", None),
            P("expert", "dp", None),
        ),
        check_vma=False,
    )
```

```python
import functools

import jax
import jax.numpy as jnp
from jax import lax
from jax.sharding import PartitionSpec as P
from jax.experimental import pallas as pl
from jax.experimental.pallas import tpu as pltpu

HEAD_DIM = 64
FF = 512
EXPERTS = 32
TOP = 8
CAP = 40


EPS = 1e-05
ROPE_BASE = 10000.0
MASKED = -1e30
HIGH = lax.Precision.HIGHEST


def norm_forward(values, gain_vec):
    inverse = lax.rsqrt(jnp.mean(values * values, axis=-1, keepdims=True) + EPS)
    normed = values * inverse
    return (normed, inverse, (normed * gain_vec).astype(jnp.bfloat16))


def norm_backward(grad_out, normed, inverse, gain_vec):
    gain_grad = jnp.sum(grad_out * normed, axis=0)
    scaled = grad_out * gain_vec
    grad_in = inverse * (scaled - normed * jnp.mean(scaled * normed, axis=-1, keepdims=True))
    return (grad_in, gain_grad)


def rope_tables(segment_row):
    length = segment_row.shape[0]
    earlier = jnp.sum((segment_row[None, :] < segment_row[:, None]).astype(jnp.int32), axis=1)
    position = jnp.arange(length, dtype=jnp.int32) - earlier
    half_dim = HEAD_DIM // 2
    frequency = ROPE_BASE ** (-(jnp.arange(half_dim, dtype=jnp.float32) * 2.0) / HEAD_DIM)
    angles = position.astype(jnp.float32)[:, None] * frequency[None, :]
    cosine = jnp.concatenate([jnp.cos(angles), jnp.cos(angles)], axis=-1)[:, None, :]
    sine_table = jnp.concatenate([jnp.sin(angles), jnp.sin(angles)], axis=-1)[:, None, :]
    return (cosine, sine_table)


def rotate(values, cosine, sine_table):
    half_dim = values.shape[-1] // 2
    turned = jnp.concatenate([-values[..., half_dim:], values[..., :half_dim]], axis=-1)
    return values * cosine + turned * sine_table


def unrotate(grad_rows, cosine, sine_table):
    half_dim = grad_rows.shape[-1] // 2
    weighted = grad_rows * sine_table
    turned = jnp.concatenate([weighted[..., half_dim:], -weighted[..., :half_dim]], axis=-1)
    return grad_rows * cosine + turned


def on_device_wide(
    tokens,
    segments,
    routes,
    query_weight,
    keyval_weight,
    output_weight,
    router_weight,
    attn_gain,
    moe_gain,
    expert_up,
    expert_down,
    out_grad,
):
    owners = lax.axis_size("expert")
    local_experts = expert_up.shape[0]
    length = tokens.shape[0]
    model_width = tokens.shape[1]
    kv_heads = keyval_weight.shape[1] // (2 * HEAD_DIM)
    query_heads = query_weight.shape[1] // HEAD_DIM
    repeat = query_heads // kv_heads
    score_scale = HEAD_DIM ** (-0.5)
    query_full, keyval_full, output_full, router_full, attn_gains, moe_gains = (
        lax.all_gather(query_weight, ("dp", "expert"), axis=0, tiled=True),
        lax.all_gather(keyval_weight, ("dp", "expert"), axis=0, tiled=True),
        lax.all_gather(output_weight, ("dp", "expert"), axis=0, tiled=True),
        lax.all_gather(router_weight, ("dp", "expert"), axis=0, tiled=True),
        lax.all_gather(attn_gain, ("dp", "expert"), axis=0, tiled=True),
        lax.all_gather(moe_gain, ("dp", "expert"), axis=0, tiled=True),
    )
    resident = tokens.astype(jnp.float32)
    normed_one, inverse_one, attn_in = norm_forward(resident, attn_gains.astype(jnp.float32))
    query_proj = jnp.dot(attn_in, query_full, preferred_element_type=jnp.float32).reshape(
        length, query_heads, HEAD_DIM
    )
    keyval_proj = jnp.dot(attn_in, keyval_full, preferred_element_type=jnp.float32)
    key_rows = keyval_proj[:, : kv_heads * HEAD_DIM].reshape(length, kv_heads, HEAD_DIM)
    value_rows = keyval_proj[:, kv_heads * HEAD_DIM :].reshape(length, kv_heads, HEAD_DIM)
    cosine, sine_table = rope_tables(segments[0])
    query_rot = (
        rotate(query_proj, cosine, sine_table)
        .astype(jnp.bfloat16)
        .reshape(length, kv_heads, repeat, HEAD_DIM)
    )
    keys_rot = rotate(key_rows, cosine, sine_table).astype(jnp.bfloat16)
    values_low = value_rows.astype(jnp.bfloat16)
    places = jnp.arange(length)
    visible = (segments[0][:, None] == segments[0][None, :]) & (places[None, :] <= places[:, None])
    scores = jnp.einsum("ikrd,jkd->krij", query_rot, keys_rot, preferred_element_type=jnp.float32)
    attn_logits = jnp.where(visible, scores * score_scale, MASKED)
    attn_exps = jnp.exp(attn_logits - jnp.max(attn_logits, axis=-1, keepdims=True))
    attn_probs = attn_exps / jnp.sum(attn_exps, axis=-1, keepdims=True)
    probs_low = attn_probs.astype(jnp.bfloat16)
    mixed_heads = jnp.einsum(
        "krij,jkd->ikrd", probs_low, values_low, preferred_element_type=jnp.float32
    )
    mixed_low = mixed_heads.reshape(length, query_heads * HEAD_DIM).astype(jnp.bfloat16)
    hidden = resident + jnp.dot(mixed_low, output_full, preferred_element_type=jnp.float32)
    normed_two, inverse_two, moe_in = norm_forward(hidden, moe_gains.astype(jnp.float32))
    router_logits = jnp.dot(moe_in, router_full, preferred_element_type=jnp.float32)
    choose = (routes[:, :, None] == jnp.arange(EXPERTS, dtype=jnp.int32)[None, None, :]).astype(
        jnp.float32
    )
    chosen = jnp.sum(choose * router_logits[:, None, :], axis=-1)
    gate_exps = jnp.exp(chosen - jnp.max(chosen, axis=-1, keepdims=True))
    gate_probs = gate_exps / jnp.sum(gate_exps, axis=-1, keepdims=True)
    entries = routes.reshape(-1)
    entry_count = entries.shape[0]
    onehot = (entries[:, None] == jnp.arange(EXPERTS, dtype=jnp.int32)[None, :]).astype(jnp.int32)
    position = jnp.sum((jnp.cumsum(onehot, axis=0) - 1) * onehot, axis=1)
    slot_index = entries * CAP + position
    owner_entry = (
        jnp.full((EXPERTS * CAP,), entry_count, jnp.int32)
        .at[slot_index]
        .set(jnp.arange(entry_count, dtype=jnp.int32))
    )
    padded_in = jnp.concatenate([moe_in, jnp.zeros((1, model_width), jnp.bfloat16)], axis=0)
    send_rows = jnp.take(padded_in, owner_entry // TOP, axis=0).reshape(EXPERTS, CAP, model_width)
    received = lax.all_to_all(send_rows, "expert", split_axis=0, concat_axis=0, tiled=True)
    slots_now = received.shape[1]
    grouped = received.reshape(owners, local_experts, slots_now, model_width)
    pair_proj = jnp.einsum("secd,edf->secf", grouped, expert_up, preferred_element_type=jnp.float32)
    activated = (jax.nn.silu(pair_proj[..., :FF]) * pair_proj[..., FF:]).astype(jnp.bfloat16)
    produced = jnp.einsum(
        "secf,edf->secd", activated, expert_down, preferred_element_type=jnp.float32
    ).astype(jnp.bfloat16)
    returned = lax.all_to_all(
        produced.reshape(EXPERTS, slots_now, model_width),
        "expert",
        split_axis=0,
        concat_axis=0,
        tiled=True,
    )
    returned, kept_rows, kept_pair = (
        returned,
        received,
        pair_proj.reshape(EXPERTS, slots_now, 2 * FF),
    )
    gathered = (
        jnp.take(returned.reshape(EXPERTS * CAP, model_width), slot_index, axis=0)
        .astype(jnp.float32)
        .reshape(length, TOP, model_width)
    )
    layer_out = (hidden + jnp.sum(gate_probs[:, :, None] * gathered, axis=1)).astype(jnp.bfloat16)
    grad_top = out_grad.astype(jnp.float32)
    gate_grad = jnp.sum(gathered * grad_top[:, None, :], axis=-1)
    chosen_grad = gate_probs * (gate_grad - jnp.sum(gate_probs * gate_grad, axis=-1, keepdims=True))
    logits_grad = jnp.sum(chosen_grad[:, :, None] * choose, axis=1)
    row_grads = (
        (gate_probs[:, :, None] * grad_top[:, None, :])
        .astype(jnp.bfloat16)
        .reshape(entry_count, model_width)
    )
    padded_grads = jnp.concatenate([row_grads, jnp.zeros((1, model_width), jnp.bfloat16)], axis=0)
    send_grads = jnp.take(padded_grads, owner_entry, axis=0).reshape(EXPERTS, CAP, model_width)
    grads_in = lax.all_to_all(send_grads, "expert", split_axis=0, concat_axis=0, tiled=True)
    grouped_rows = kept_rows.reshape(owners, local_experts, CAP, model_width)
    grouped_grads = grads_in.reshape(owners, local_experts, CAP, model_width)
    pair_kept = kept_pair.reshape(owners, local_experts, CAP, 2 * FF)
    gate_half = pair_kept[..., :FF]
    up_half = pair_kept[..., FF:]
    sigmoid_gate = jax.nn.sigmoid(gate_half)
    silu_gate = jax.nn.silu(gate_half)
    activated = (silu_gate * up_half).astype(jnp.bfloat16)
    act_grad = jnp.einsum(
        "secd,edf->secf", grouped_grads, expert_down, preferred_element_type=jnp.float32
    )
    pair_grad = jnp.concatenate(
        [
            act_grad * up_half * sigmoid_gate * (1.0 + gate_half * (1.0 - sigmoid_gate)),
            act_grad * silu_gate,
        ],
        axis=-1,
    ).astype(jnp.bfloat16)
    rows_back = jnp.einsum(
        "secf,edf->secd", pair_grad, expert_up, preferred_element_type=jnp.float32
    ).astype(jnp.bfloat16)
    up_grad = jnp.einsum(
        "secd,secf->edf", grouped_rows, pair_grad, preferred_element_type=jnp.float32
    )
    down_grad = jnp.einsum(
        "secd,secf->edf", grouped_grads, activated, preferred_element_type=jnp.float32
    )
    returned_grads = lax.all_to_all(
        rows_back.reshape(EXPERTS, CAP, model_width),
        "expert",
        split_axis=0,
        concat_axis=0,
        tiled=True,
    )
    expert_up_grad, expert_down_grad = (
        lax.psum_scatter(
            up_grad.astype(jnp.bfloat16), "dp", scatter_dimension=1, tiled=True
        ).astype(jnp.float32),
        lax.psum_scatter(
            down_grad.astype(jnp.bfloat16), "dp", scatter_dimension=1, tiled=True
        ).astype(jnp.float32),
    )
    token_grads = (
        jnp.take(returned_grads.reshape(EXPERTS * CAP, model_width), slot_index, axis=0)
        .astype(jnp.float32)
        .reshape(length, TOP, model_width)
    )
    router_wide = router_full.astype(jnp.float32)
    moe_grad = jnp.sum(token_grads, axis=1) + jnp.dot(logits_grad, router_wide.T, precision=HIGH)
    hidden_norm_grad, moe_gain_grad = norm_backward(
        moe_grad, normed_two, inverse_two, moe_gains.astype(jnp.float32)
    )
    hidden_grad = grad_top + hidden_norm_grad
    attn_out_grad = hidden_grad.astype(jnp.bfloat16)
    mixed_grad = (
        jnp.einsum("td,cd->tc", attn_out_grad, output_full, preferred_element_type=jnp.float32)
        .astype(jnp.bfloat16)
        .reshape(length, kv_heads, repeat, HEAD_DIM)
    )
    probs_grad = jnp.einsum(
        "ikrd,jkd->krij", mixed_grad, values_low, preferred_element_type=jnp.float32
    )
    values_grad = jnp.einsum(
        "krij,ikrd->jkd", probs_low, mixed_grad, preferred_element_type=jnp.float32
    )
    scores_grad = (
        attn_probs
        * (probs_grad - jnp.sum(attn_probs * probs_grad, axis=-1, keepdims=True))
        * score_scale
    ).astype(jnp.bfloat16)
    query_rot_grad = jnp.einsum(
        "krij,jkd->ikrd", scores_grad, keys_rot, preferred_element_type=jnp.float32
    ).reshape(length, query_heads, HEAD_DIM)
    keys_rot_grad = jnp.einsum(
        "krij,ikrd->jkd", scores_grad, query_rot, preferred_element_type=jnp.float32
    )
    query_low = (
        unrotate(query_rot_grad, cosine, sine_table)
        .reshape(length, query_heads * HEAD_DIM)
        .astype(jnp.bfloat16)
    )
    keyval_low = jnp.concatenate(
        [
            unrotate(keys_rot_grad, cosine, sine_table).reshape(length, kv_heads * HEAD_DIM),
            values_grad.reshape(length, kv_heads * HEAD_DIM),
        ],
        axis=1,
    ).astype(jnp.bfloat16)
    attn_in_grad = jnp.einsum(
        "tc,dc->td", query_low, query_full, preferred_element_type=jnp.float32
    ) + jnp.einsum("tc,dc->td", keyval_low, keyval_full, preferred_element_type=jnp.float32)
    token_norm_grad, attn_gain_grad = norm_backward(
        attn_in_grad, normed_one, inverse_one, attn_gains.astype(jnp.float32)
    )
    tokens_grad = hidden_grad + token_norm_grad
    slab_count = lax.axis_size("dp")
    slab_index = lax.axis_index("dp")
    width_rows = model_width // slab_count
    head_rows = query_heads * HEAD_DIM // slab_count
    all_attn, all_query, all_keyval, all_mixed, all_outgrad = (
        lax.all_gather(attn_in, "dp", axis=0, tiled=True),
        lax.all_gather(query_low, "dp", axis=0, tiled=True),
        lax.all_gather(keyval_low, "dp", axis=0, tiled=True),
        lax.all_gather(mixed_low, "dp", axis=0, tiled=True),
        lax.all_gather(attn_out_grad, "dp", axis=0, tiled=True),
    )
    all_moe, all_logits, attn_gain_rows, moe_gain_rows = (
        lax.all_gather(
            moe_in.astype(jnp.float32).astype(jnp.bfloat16), "dp", axis=0, tiled=True
        ).astype(jnp.float32),
        lax.all_gather(logits_grad.astype(jnp.bfloat16), "dp", axis=0, tiled=True).astype(
            logits_grad.dtype
        ),
        lax.all_gather(
            attn_gain_grad[None, :].astype(jnp.bfloat16), "dp", axis=0, tiled=True
        ).astype(jnp.float32),
        lax.all_gather(
            moe_gain_grad[None, :].astype(jnp.bfloat16), "dp", axis=0, tiled=True
        ).astype(jnp.float32),
    )
    attn_cols = lax.dynamic_slice_in_dim(all_attn, slab_index * width_rows, width_rows, 1)
    mixed_cols = lax.dynamic_slice_in_dim(all_mixed, slab_index * head_rows, head_rows, 1)
    moe_cols = lax.dynamic_slice_in_dim(all_moe, slab_index * width_rows, width_rows, 1)
    query_part = jnp.einsum("td,tc->dc", attn_cols, all_query, preferred_element_type=jnp.float32)
    keyval_part = jnp.einsum("td,tc->dc", attn_cols, all_keyval, preferred_element_type=jnp.float32)
    output_part = jnp.einsum(
        "tc,td->cd", mixed_cols, all_outgrad, preferred_element_type=jnp.float32
    )
    router_part = jnp.dot(moe_cols.T, all_logits, precision=HIGH)
    attn_gain_part = lax.dynamic_slice_in_dim(
        jnp.sum(attn_gain_rows, axis=0), slab_index * width_rows, width_rows, 0
    )
    moe_gain_part = lax.dynamic_slice_in_dim(
        jnp.sum(moe_gain_rows, axis=0), slab_index * width_rows, width_rows, 0
    )
    query_share, keyval_share, output_share, router_share, attn_share, moe_share = (
        lax.psum_scatter(
            query_part.astype(jnp.bfloat16), "expert", scatter_dimension=0, tiled=True
        ).astype(jnp.float32),
        lax.psum_scatter(
            keyval_part.astype(jnp.bfloat16), "expert", scatter_dimension=0, tiled=True
        ).astype(jnp.float32),
        lax.psum_scatter(
            output_part.astype(jnp.bfloat16), "expert", scatter_dimension=0, tiled=True
        ).astype(jnp.float32),
        lax.psum_scatter(
            router_part.astype(jnp.bfloat16), "expert", scatter_dimension=0, tiled=True
        ).astype(jnp.float32),
        lax.psum_scatter(
            attn_gain_part.astype(jnp.bfloat16), "expert", scatter_dimension=0, tiled=True
        ).astype(jnp.float32),
        lax.psum_scatter(
            moe_gain_part.astype(jnp.bfloat16), "expert", scatter_dimension=0, tiled=True
        ).astype(jnp.float32),
    )
    return (
        layer_out,
        tokens_grad,
        query_share,
        keyval_share,
        output_share,
        router_share,
        attn_share,
        moe_share,
        expert_up_grad,
        expert_down_grad,
    )


LANES = 128
TAIL = 16
PIECE_LIMIT = 4096
VMEM_BYTES = 60 * 1024 * 1024
F32 = jnp.float32
LOW = jnp.bfloat16


def contract(left, right, left_dim, right_dim):
    return lax.dot_general(
        left, right, (((left_dim,), (right_dim,)), ((), ())), preferred_element_type=F32
    )


def lane_index(shape):
    return lax.broadcasted_iota(jnp.int32, shape, len(shape) - 1)


def row_index(shape):
    return lax.broadcasted_iota(jnp.int32, shape, len(shape) - 2)


def half_turn(chunk):
    first = lane_index(chunk.shape) % HEAD_DIM < HEAD_DIM // 2
    ahead = pltpu.roll(chunk, LANES - HEAD_DIM // 2, 1)
    behind = pltpu.roll(chunk, HEAD_DIM // 2, 1)
    return jnp.where(first, ahead, behind)


def both_heads(chunk, pick):
    swapped = pltpu.roll(chunk, HEAD_DIM, 1)
    first = lane_index(chunk.shape) < HEAD_DIM
    if pick == 0:
        return jnp.where(first, chunk, swapped)
    return jnp.where(first, swapped, chunk)


def split_heads(chunk):
    first = lane_index(chunk.shape) < HEAD_DIM
    zero = jnp.zeros_like(chunk)
    return jnp.concatenate([jnp.where(first, chunk, zero), jnp.where(first, zero, chunk)], axis=0)


def join_heads(stacked):
    length = stacked.shape[0] // 2
    top, bottom = stacked[:length], stacked[length:]
    return jnp.where(lane_index(top.shape) < HEAD_DIM, top, bottom)


def three_parts(values):
    high = values.astype(LOW).astype(F32)
    rest = values - high
    middle = rest.astype(LOW).astype(F32)
    return (high, middle, rest - middle)


def gain_select():
    shape = (8, LANES)
    return (lane_index(shape) == EXPERTS + row_index(shape)) & (row_index(shape) < 2)


def load_weights(rows_ref, spots, piece_refs, weights, sems):
    copies = []
    for (p, first), piece in zip(spots, piece_refs):
        for w in range(piece.shape[0]):
            size = piece.shape[1]
            start = pl.multiple_of(rows_ref[p, first + w] * size, size)
            copies.append(
                pltpu.make_async_copy(
                    piece.at[w], weights.at[pl.ds(start, size)], sems.at[p, first + w]
                )
            )
    for copy in copies:
        copy.start()
    return copies


def store_sums(rows_ref, sums, grads_even, grads_odd, sems):
    copies = []
    for p in range(2 * grads_even.shape[0]):
        target = grads_even if p % 2 == 0 else grads_odd
        for w in range(target.shape[1]):
            size = target.shape[2]
            start = pl.multiple_of(rows_ref[p, w] * size, size)
            copies.append(
                pltpu.make_async_copy(
                    sums.at[pl.ds(start, size)], target.at[p // 2, w], sems.at[p, w]
                )
            )
    for copy in copies:
        copy.start()
    return copies


def softmax_rows(q_pair, k_both, visible):
    scores = contract(q_pair, k_both, 1, 1) * (HEAD_DIM ** (-0.5))
    logits = jnp.where(visible, scores, MASKED)
    exps = jnp.exp(logits - jnp.max(logits, axis=-1, keepdims=True))
    return exps / jnp.sum(exps, axis=-1, keepdims=True)


def visible_pairs(seg_col, seg_row):
    length = seg_col.shape[0]
    shape = (length, length)
    seen = (seg_col == seg_row) & (lane_index(shape) <= row_index(shape))
    return jnp.concatenate([seen, seen], axis=0)


def attn_forward_kernel(spots, *refs):
    count = len(spots)
    rows_ref, tokens_ref, seg_col, seg_row, cos_ref, sin_ref = refs[:6]
    pieces = refs[6 : 6 + count]
    query_ref, keyval_ref, mixed_ref, tail_ref, weights, sems = refs[6 + count :]
    copies = load_weights(rows_ref, spots, pieces, weights, sems)
    tokens = tokens_ref[...].astype(F32)
    inverse = lax.rsqrt(jnp.mean(tokens * tokens, axis=-1, keepdims=True) + EPS)
    normed = tokens * inverse
    width = tokens.shape[1]
    for copy in copies:
        copy.wait()
    tail = weights[:, 2 * width :]
    tail_ref[...] = tail
    gains = contract(gain_select().astype(F32).astype(LOW), tail, 1, 1)
    attn_in = (normed * gains[0:1]).astype(LOW)
    cosine, sine = cos_ref[...], sin_ref[...]
    keyval = contract(attn_in, weights[:, width : 2 * width], 1, 0)
    query = contract(attn_in, weights[:, :width], 1, 0)
    visible = visible_pairs(seg_col[...], seg_row[...])
    half = width // 2
    for m in range(half // LANES):
        keys = keyval[:, m * LANES : (m + 1) * LANES]
        keys = (keys * cosine + half_turn(keys) * sine).astype(LOW)
        values = keyval[:, half + m * LANES : half + (m + 1) * LANES].astype(LOW)
        keyval_ref[:, m * LANES : (m + 1) * LANES] = keys
        keyval_ref[:, half + m * LANES : half + (m + 1) * LANES] = values
        for pick in range(2):
            k_both = both_heads(keys.astype(F32), pick).astype(LOW)
            v_both = both_heads(values.astype(F32), pick).astype(LOW)
            chunk = slice((2 * m + pick) * LANES, (2 * m + pick + 1) * LANES)
            queries = query[:, chunk]
            queries = (queries * cosine + half_turn(queries) * sine).astype(LOW)
            query_ref[:, chunk] = queries
            q_pair = split_heads(queries.astype(F32)).astype(LOW)
            probs = softmax_rows(q_pair, k_both, visible).astype(LOW)
            mixed_ref[:, chunk] = join_heads(contract(probs, v_both, 1, 0)).astype(LOW)


def router_kernel(spots, *refs):
    count = len(spots)
    rows_ref, tokens_ref, mixed_ref, tail_ref, routes_ref, routes_t = refs[:6]
    pieces = refs[6 : 6 + count]
    payload, hidden_ref, gates_ref, weights, sems = refs[6 + count :]
    copies = load_weights(rows_ref, spots, pieces, weights, sems)
    tokens = tokens_ref[...].astype(F32)
    length = tokens.shape[0]
    tail = tail_ref[...]
    gains = contract(gain_select().astype(F32).astype(LOW), tail, 1, 1)
    for copy in copies:
        copy.wait()
    hidden = tokens + contract(mixed_ref[...], weights[...], 1, 0)
    hidden_ref[...] = hidden
    inverse_two = lax.rsqrt(jnp.mean(hidden * hidden, axis=-1, keepdims=True) + EPS)
    moe_in = (hidden * inverse_two * gains[1:2]).astype(LOW)
    payload[:length] = moe_in
    logits = contract(moe_in, tail, 1, 0)
    routes = routes_ref[...]
    lanes = lane_index((length, LANES))
    chosen = lanes == routes[:, 0:1]
    for k in range(1, TOP):
        chosen = chosen | (lanes == routes[:, k : k + 1])
    logits = jnp.where(chosen, logits, MASKED)
    exps = jnp.where(chosen, jnp.exp(logits - jnp.max(logits, axis=-1, keepdims=True)), 0.0)
    gates = exps / jnp.sum(exps, axis=-1, keepdims=True)
    gates_ref[...] = gates
    gates_t = gates.T
    experts = row_index((LANES, length))
    turned = routes_t[...]
    for k in range(TOP):
        row = turned[k : k + 1]
        gate = jnp.sum(jnp.where(experts == row, gates_t, 0.0), axis=0, keepdims=True)
        high, middle, rest = three_parts(gate)
        place = row_index((TAIL, length))
        block = jnp.where(place == 0, high, jnp.where(place == 1, middle, jnp.where(place == 2, rest, 0.0)))
        block = jnp.where(place == 3, row.astype(F32), block)
        payload[length:, k * length : (k + 1) * length] = block.astype(LOW)


def gather_pair(first_expert, local, block, rows_a, rows_b, grads_a, grads_b, before, out):
    rows_out, grads_out, select_out, gate_out, pair = out
    length = rows_a.shape[0] - TAIL
    ids = row_index((8, length)) + first_expert
    ids = jnp.where(row_index((8, length)) < local, ids, -1).astype(F32)
    masks, gates = [], []
    for piece in (rows_a, rows_b):
        tail = piece[length:].astype(F32)
        mask = jnp.zeros((8, length), F32)
        gate = jnp.zeros((8, length), F32)
        for k in range(TOP):
            part = tail[:, k * length : (k + 1) * length]
            hit = part[3:4] == ids
            mask = jnp.where(hit, 1.0, mask)
            gate = jnp.where(hit, part[0:1] + part[1:2] + part[2:3], gate)
        masks.append(mask)
        gates.append(gate)
    mask = jnp.concatenate(masks, axis=1)
    gate = jnp.concatenate(gates, axis=1)
    place = contract(mask.astype(LOW), before, 1, 0)
    place = jnp.where(mask > 0, place, -1.0)
    slots = row_index((block, 2 * length)).astype(F32)
    parts = []
    for j in range(local):
        hit = slots == place[j : j + 1]
        parts.append(jnp.where(hit, 1.0, 0.0))
        held = jnp.sum(jnp.where(hit, gate[j : j + 1], 0.0), axis=1, keepdims=True)
        gate_out[j, pair * block : (pair + 1) * block] = jnp.broadcast_to(held, (block, LANES))
    select = jnp.concatenate(parts, axis=0).astype(LOW)
    if select_out is not None:
        select_out[pair] = select
    rows = jnp.concatenate([rows_a[:length], rows_b[:length]], axis=0)
    grads = jnp.concatenate([grads_a, grads_b], axis=0)
    rows = contract(select, rows, 1, 0).astype(LOW)
    grads = contract(select, grads, 1, 0).astype(LOW)
    for j in range(local):
        rows_out[j, pair * block : (pair + 1) * block] = rows[j * block : (j + 1) * block]
        grads_out[j, pair * block : (pair + 1) * block] = grads[j * block : (j + 1) * block]


def earlier_matrix(length):
    shape = (2 * length, 2 * length)
    return jnp.where(row_index(shape) < lane_index(shape), 1.0, 0.0).astype(LOW)


def expert_step(j, rows, grads, gate_ref, up, down):
    hidden_units = down.shape[1]
    pair = contract(rows[j], up, 1, 0)
    raw = contract(grads[j], down, 1, 0)
    gate_half, up_half = pair[:, :hidden_units], pair[:, hidden_units:]
    gate = gate_ref[j][:, 0:1]
    sigmoid = 1.0 / (1.0 + jnp.exp(-gate_half))
    silu = gate_half * sigmoid
    activated = silu * up_half
    scaled = (gate * activated).astype(LOW)
    act_grad = gate * raw
    pair_grad = jnp.concatenate(
        [act_grad * up_half * sigmoid * (1.0 + gate_half * (1.0 - sigmoid)), act_grad * silu],
        axis=1,
    ).astype(LOW)
    gate_grad = jnp.sum(activated * raw, axis=1, keepdims=True)
    return (scaled, pair_grad, gate_grad)


def fetch_experts(local, up_hbm, down_hbm, up, down, sems):
    copies = []
    for j in range(local):
        copies.append(
            (
                pltpu.make_async_copy(up_hbm.at[j], up.at[j], sems.at[0, j]),
                pltpu.make_async_copy(down_hbm.at[j], down.at[j], sems.at[1, j]),
            )
        )
        for copy in copies[j]:
            copy.start()
    return copies


def expert_home_kernel(owners, local, block, *refs):
    place_ref = refs[0]
    rows_in = refs[1 : 1 + owners]
    grads_in = refs[1 + owners : 1 + 2 * owners]
    up_hbm, down_hbm = refs[1 + 2 * owners : 3 + 2 * owners]
    out_even, out_odd, back_even, back_odd, up_grad, down_grad = refs[3 + 2 * owners : 9 + 2 * owners]
    up, down, rows, grads, select, gate_ref, produced, returned, sems = refs[9 + 2 * owners :]
    copies = fetch_experts(local, up_hbm, down_hbm, up, down, sems)
    length = rows_in[0].shape[0] - TAIL
    width = rows_in[0].shape[1]
    first_expert = place_ref[0] * local
    slab = up_grad.shape[1]
    columns = pl.ds(pl.multiple_of(place_ref[1] * slab, slab), slab)
    before = earlier_matrix(length)
    for s in range(owners // 2):
        gather_pair(
            first_expert,
            local,
            block,
            rows_in[2 * s][...],
            rows_in[2 * s + 1][...],
            grads_in[2 * s][...],
            grads_in[2 * s + 1][...],
            before,
            (rows, grads, select, gate_ref, s),
        )
    for j in range(local):
        for copy in copies[j]:
            copy.wait()
        scaled, pair_grad, gate_grad = expert_step(j, rows, grads, gate_ref, up[j], down[j])
        produced[j] = contract(scaled, down[j], 1, 1).astype(LOW)
        returned[j, :, :width] = contract(pair_grad, up[j], 1, 1).astype(LOW)
        lanes = lane_index((scaled.shape[0], LANES)) - first_expert - j
        high, middle, rest = three_parts(gate_grad)
        tail = jnp.where(lanes == 0, high, 0.0)
        tail = jnp.where(lanes == EXPERTS, middle, tail)
        tail = jnp.where(lanes == 2 * EXPERTS, rest, tail)
        returned[j, :, width:] = tail.astype(LOW)
        up_grad[j] = contract(rows[j, :, columns], pair_grad, 0, 0)
        down_grad[j] = contract(grads[j, :, columns], scaled, 0, 0)
    for s in range(owners // 2):
        span = slice(s * block, (s + 1) * block)
        made = jnp.concatenate([produced[j, span] for j in range(local)], axis=0)
        back = jnp.concatenate([returned[j, span] for j in range(local)], axis=0)
        made = contract(select[s], made, 0, 0).astype(LOW)
        back = contract(select[s], back, 0, 0).astype(LOW)
        out_even[s] = made[:length]
        out_odd[s] = made[length:]
        back_even[s] = back[:length]
        back_odd[s] = back[length:]


def expert_away_kernel(local, block, far, *refs):
    place_ref = refs[0]
    near_rows, near_rows_other, far_rows, far_rows_other = refs[1:5]
    near_grads, near_grads_other, far_grads, far_grads_other = refs[5:9]
    up_hbm, down_hbm, up_first, down_first = refs[9:13]
    up_grad, down_grad = refs[13:15]
    up, down, rows, grads, gate_ref, sems = refs[15:]
    copies = fetch_experts(local, up_hbm, down_hbm, up, down, sems)
    length = near_grads.shape[1]
    tall = length + TAIL
    first_expert = place_ref[0] * local
    slab = up_grad.shape[1]
    columns = pl.ds(pl.multiple_of(place_ref[1] * slab, slab), slab)
    before = earlier_matrix(length)
    pairs = [(near_rows[0], near_rows_other[0], near_grads[0], near_grads_other[0])]
    for i in range(far):
        high = slice(i * tall, (i + 1) * tall)
        flat = slice(i * length, (i + 1) * length)
        pairs.append((far_rows[high], far_rows_other[high], far_grads[flat], far_grads_other[flat]))
    for i, pair in enumerate(pairs):
        gather_pair(first_expert, local, block, *pair, before, (rows, grads, None, gate_ref, i))
    for j in range(local):
        for copy in copies[j]:
            copy.wait()
        scaled, pair_grad, _ = expert_step(j, rows, grads, gate_ref, up[j], down[j])
        up_grad[j] = up_first[j] + contract(rows[j, :, columns], pair_grad, 0, 0)
        down_grad[j] = down_first[j] + contract(grads[j, :, columns], scaled, 0, 0)


def hidden_backward_kernel(spots, shares, *refs):
    count = len(spots)
    rows_ref, payload, hidden_ref, mixed_ref, gates_ref, out_grad_ref, tail_ref = refs[:7]
    back = refs[7 : 7 + shares]
    pieces = refs[7 + shares : 7 + shares + count]
    hidden_grad_ref, mixed_grad, tail_grad, grads_even, grads_odd = refs[7 + shares + count : 12 + shares + count]
    weights, sums, sems, out_sems = refs[12 + shares + count :]
    copies = load_weights(rows_ref, spots, pieces, weights, sems)
    length, width = hidden_ref.shape
    total = back[0][...].astype(F32)
    for share in back[1:]:
        total = total + share[...].astype(F32)
    parts = total[:, width:]
    lanes = lane_index(parts.shape)
    gate_grad = parts + pltpu.roll(parts, LANES - EXPERTS, 1) + pltpu.roll(parts, LANES - 2 * EXPERTS, 1)
    gate_grad = jnp.where(lanes < EXPERTS, gate_grad, 0.0)
    gates = gates_ref[...]
    logits_grad = gates * (gate_grad - jnp.sum(gates * gate_grad, axis=-1, keepdims=True))
    hidden = hidden_ref[...]
    inverse_two = lax.rsqrt(jnp.mean(hidden * hidden, axis=-1, keepdims=True) + EPS)
    normed_two = hidden * inverse_two
    tail = tail_ref[...]
    gains = contract(gain_select().astype(F32).astype(LOW), tail, 1, 1)
    high = logits_grad.astype(LOW)
    rest = (logits_grad - high.astype(F32)).astype(LOW)
    moe_grad = total[:, :width] + contract(high, tail, 1, 1) + contract(rest, tail, 1, 1)
    moe_gain_grad = jnp.sum(moe_grad * normed_two, axis=0, keepdims=True)
    scaled = moe_grad * gains[1:2]
    hidden_grad = out_grad_ref[...].astype(F32) + inverse_two * (
        scaled - normed_two * jnp.mean(scaled * normed_two, axis=-1, keepdims=True)
    )
    hidden_grad_ref[...] = hidden_grad
    attn_out_grad = hidden_grad.astype(LOW)
    sums[...] = contract(mixed_ref[...], attn_out_grad, 0, 0).astype(LOW)
    out_copies = store_sums(rows_ref, sums, grads_even, grads_odd, out_sems)
    for copy in copies:
        copy.wait()
    mixed_grad[...] = contract(attn_out_grad, weights[...], 1, 1).astype(LOW)
    gain_grads = jnp.where(row_index((8, width)) == 1, moe_gain_grad, 0.0)
    tail_grad[...] = contract(payload[:length], high, 0, 0) + contract(
        gain_grads.astype(LOW), gain_select().astype(F32).astype(LOW), 0, 0
    )
    for copy in out_copies:
        copy.wait()


def attn_backward_kernel(spots, *refs):
    count = len(spots)
    rows_ref, tokens_ref, seg_col, seg_row, cos_ref, sin_ref = refs[:6]
    query_ref, keyval_ref, mixed_grad, hidden_grad, tail_ref, tail_grad = refs[6:12]
    pieces = refs[12 : 12 + count]
    tokens_grad, grads_even, grads_odd = refs[12 + count : 15 + count]
    weights, sums, query_low, keyval_low, sems, out_sems = refs[15 + count :]
    copies = load_weights(rows_ref, spots, pieces, weights, sems)
    length, width = tokens_ref.shape
    half = width // 2
    tokens = tokens_ref[...].astype(F32)
    inverse_one = lax.rsqrt(jnp.mean(tokens * tokens, axis=-1, keepdims=True) + EPS)
    normed_one = tokens * inverse_one
    gains = contract(gain_select().astype(F32).astype(LOW), tail_ref[...], 1, 1)
    cosine, sine = cos_ref[...], sin_ref[...]
    visible = visible_pairs(seg_col[...], seg_row[...])
    for m in range(half // LANES):
        keys = keyval_ref[:, m * LANES : (m + 1) * LANES].astype(F32)
        values = keyval_ref[:, half + m * LANES : half + (m + 1) * LANES].astype(F32)
        key_sides, value_sides = [], []
        for pick in range(2):
            k_both = both_heads(keys, pick).astype(LOW)
            v_both = both_heads(values, pick).astype(LOW)
            chunk = slice((2 * m + pick) * LANES, (2 * m + pick + 1) * LANES)
            q_pair = split_heads(query_ref[:, chunk].astype(F32)).astype(LOW)
            m_pair = split_heads(mixed_grad[:, chunk].astype(F32)).astype(LOW)
            probs = softmax_rows(q_pair, k_both, visible)
            probs_grad = contract(m_pair, v_both, 1, 1)
            value_sides.append(contract(probs.astype(LOW), m_pair, 0, 0))
            scores_grad = (
                probs
                * (probs_grad - jnp.sum(probs * probs_grad, axis=-1, keepdims=True))
                * (HEAD_DIM ** (-0.5))
            ).astype(LOW)
            query_grad = join_heads(contract(scores_grad, k_both, 1, 0))
            query_low[:, chunk] = (query_grad * cosine - half_turn(query_grad) * sine).astype(LOW)
            key_sides.append(contract(scores_grad, q_pair, 0, 0))
        first = lane_index((length, LANES)) < HEAD_DIM
        key_sides = [side + pltpu.roll(side, HEAD_DIM, 1) for side in key_sides]
        value_sides = [side + pltpu.roll(side, HEAD_DIM, 1) for side in value_sides]
        keys_grad = jnp.where(first, key_sides[0], key_sides[1])
        values_grad = jnp.where(first, value_sides[0], value_sides[1])
        keyval_low[:, m * LANES : (m + 1) * LANES] = (
            keys_grad * cosine - half_turn(keys_grad) * sine
        ).astype(LOW)
        keyval_low[:, half + m * LANES : half + (m + 1) * LANES] = values_grad.astype(LOW)
    for copy in copies:
        copy.wait()
    attn_in_grad = contract(query_low[...], weights[:, :width], 1, 1) + contract(
        keyval_low[...], weights[:, width : 2 * width], 1, 1
    )
    attn_in = (normed_one * gains[0:1]).astype(LOW)
    sums[:, :width] = contract(attn_in, query_low[...], 0, 0).astype(LOW)
    sums[:, width : 2 * width] = contract(attn_in, keyval_low[...], 0, 0).astype(LOW)
    attn_gain_grad = jnp.sum(attn_in_grad * normed_one, axis=0, keepdims=True)
    gain_grads = jnp.where(row_index((8, width)) == 0, attn_gain_grad, 0.0)
    sums[:, 2 * width :] = (
        tail_grad[...]
        + contract(gain_grads.astype(LOW), gain_select().astype(F32).astype(LOW), 0, 0)
    ).astype(LOW)
    out_copies = store_sums(rows_ref, sums, grads_even, grads_odd, out_sems)
    scaled = attn_in_grad * gains[0:1]
    tokens_grad[...] = hidden_grad[...] + inverse_one * (
        scaled - normed_one * jnp.mean(scaled * normed_one, axis=-1, keepdims=True)
    )
    for copy in out_copies:
        copy.wait()


def swap(values, axis, size, distance):
    return lax.ppermute(values, axis, [(i, i ^ distance) for i in range(size)])


def across(values, distance, planes):
    return swap(values, "dp", planes, distance)


def aside(values, s, owners):
    return swap(values, "expert", owners, 2 * s)


def partner(values, owners):
    return swap(values, "expert", owners, 1)


def after(values, *earlier):
    return lax.optimization_barrier((values,) + earlier)[0]


def over_chips(values, owners):
    return [values] + [aside(values, s, owners) for s in range(1, owners // 2)]


def over_cores(near, owners, *earlier):
    pieces = []
    for piece in near:
        pieces += [piece, partner(after(piece, *earlier) if earlier else piece, owners)]
    return pieces


def chips_split(values, owners, *earlier):
    half = values.shape[0] // 2
    first, second = aside(values, 1, owners), aside(values, 2, owners)
    far = [first[:half], second[half:]]
    if earlier:
        far = [after(part, *earlier) for part in far]
    far = [aside(far[0], 2, owners), aside(far[1], 1, owners)]
    return [[values], [first], [second], far]


def core_pieces(near, owners):
    pieces, spots = [], []
    for s, parts in enumerate(near):
        first = 0
        for part in parts:
            pieces += [part, partner(part, owners)]
            spots += [(2 * s, first), (2 * s + 1, first)]
            first += part.shape[0]
    return (pieces, spots)


def core_pieces_whole(near, owners):
    pieces = []
    for parts in near:
        piece = parts[0] if len(parts) == 1 else jnp.concatenate(parts, axis=0)
        pieces.append((piece, partner(piece, owners)))
    return pieces


def added(left, right):
    return (left.astype(F32) + right.astype(F32)).astype(LOW)


def to_owners(even, odd, owners):
    other = partner(odd, owners)
    joined = [added(even[s], other[s]) for s in range(owners // 2)]
    sent = [joined[0]] + [aside(joined[s], s, owners) for s in range(1, owners // 2)]
    return (joined, sent)


def to_neighbours(joined, owners):
    half = joined[3].shape[0] // 2
    low_turn = aside(joined[3][:half], 1, owners)
    top_turn = aside(joined[3][half:], 2, owners)
    first = jnp.concatenate([joined[1][:half], added(joined[1][half:], top_turn)], axis=0)
    second = jnp.concatenate([added(joined[2][:half], low_turn), joined[2][half:]], axis=0)
    return (first, second)


def from_neighbours(joined, first, second, owners):
    parts = [joined[0], aside(first, 1, owners), aside(second, 2, owners)]
    return sum(part.astype(F32) for part in parts).astype(LOW)


def over_planes_sum(parts, planes):
    total = parts[0].astype(F32)
    for w in range(1, planes):
        total = total + across(parts[w], w, planes).astype(F32)
    return total


def cost(us):
    return pl.CostEstimate(flops=int(us * 1153e6), bytes_accessed=0, transcendentals=0)


def params():
    return pltpu.CompilerParams(vmem_limit_bytes=VMEM_BYTES)


def whole_spec():
    return pl.BlockSpec(memory_space=pltpu.VMEM)


def hbm_spec():
    return pl.BlockSpec(memory_space=pl.ANY)


def smem_spec():
    return pl.BlockSpec(memory_space=pltpu.SMEM)


def on_device(
    planes,
    owners,
    tokens,
    segments,
    routes,
    query_weight,
    keyval_weight,
    output_weight,
    router_weight,
    attn_gain,
    moe_gain,
    expert_up,
    expert_down,
    out_grad,
):
    length, width = tokens.shape
    if planes != 4 or owners != 8 or planes * owners * length > PIECE_LIMIT:
        return on_device_wide(
            tokens,
            segments,
            routes,
            query_weight,
            keyval_weight,
            output_weight,
            router_weight,
            attn_gain,
            moe_gain,
            expert_up,
            expert_down,
            out_grad,
        )
    local = expert_up.shape[0]
    hidden_units = expert_down.shape[2]
    block = 2 * CAP
    slots = owners // 2 * block
    plane = lax.axis_index("dp")
    owner = lax.axis_index("expert")
    share = query_weight.shape[0]
    rows = (plane ^ jnp.arange(planes))[None, :] * owners + (owner ^ jnp.arange(owners))[:, None]
    rows = rows.astype(jnp.int32)
    place = jnp.stack([owner, plane]).astype(jnp.int32)
    extra = jnp.concatenate(
        [
            router_weight,
            attn_gain[:, None],
            moe_gain[:, None],
            jnp.zeros((share, LANES - EXPERTS - 2), LOW),
        ],
        axis=1,
    )
    packed = jnp.concatenate([query_weight, keyval_weight, extra], axis=1)
    columns = packed.shape[1]

    early = [across(packed, w, planes) for w in range(1, planes)]
    grad_chips = over_chips(out_grad, owners)
    near = chips_split(after(jnp.stack([packed] + early), *grad_chips), owners)
    pieces, spots = core_pieces(near, owners)
    output_start = after(output_weight, *early)
    late = [across(output_start, w, planes) for w in range(1, planes)]
    output_stack = after(jnp.stack([output_weight] + late), *pieces[:6], *near[3])
    grad_start = after(out_grad, *late)
    grad_planes = [across(grad_start, w, planes) for w in range(2, planes)]
    grad_near = across(after(jnp.stack(grad_chips), *late), 1, planes)

    segment_row = segments[0]
    earlier = jnp.sum((segment_row[None, :] < segment_row[:, None]).astype(jnp.int32), axis=1)
    position = (jnp.arange(length, dtype=jnp.int32) - earlier).astype(F32)
    half_dim = HEAD_DIM // 2
    frequency = ROPE_BASE ** (-(jnp.arange(half_dim, dtype=F32) * 2.0) / HEAD_DIM)
    angles = position[:, None] * frequency[None, :]
    cosine = jnp.tile(jnp.cos(angles), (1, LANES // half_dim))
    sine = jnp.sin(angles)
    sine = jnp.concatenate([-sine, sine, -sine, sine], axis=1)
    seg_col, seg_row = segment_row[:, None], segment_row[None, :]

    token_low = jax.ShapeDtypeStruct((length, width), LOW)
    token_wide = jax.ShapeDtypeStruct((length, width), F32)
    query_rot, keyval_low, mixed_low, tail = pl.pallas_call(
        functools.partial(attn_forward_kernel, spots),
        out_shape=(token_low, token_low, token_low, jax.ShapeDtypeStruct((width, LANES), LOW)),
        in_specs=[smem_spec()] + [whole_spec()] * 5 + [hbm_spec()] * len(pieces),
        out_specs=[whole_spec()] * 4,
        scratch_shapes=[
            pltpu.VMEM((width, columns), LOW),
            pltpu.SemaphoreType.DMA((owners, planes)),
        ],
        compiler_params=params(),
        cost_estimate=cost(6),
        name="attn_forward",
    )(rows, tokens, seg_col, seg_row, cosine, sine, *pieces)

    output_near = chips_split(output_stack, owners, mixed_low)
    grad_home = over_cores(grad_chips, owners, mixed_low)
    output_pieces, output_spots = core_pieces(output_near, owners)

    payload, hidden, gates = pl.pallas_call(
        functools.partial(router_kernel, output_spots),
        out_shape=(
            jax.ShapeDtypeStruct((length + TAIL, width), LOW),
            token_wide,
            jax.ShapeDtypeStruct((length, LANES), F32),
        ),
        in_specs=[smem_spec()] + [whole_spec()] * 5 + [hbm_spec()] * len(output_pieces),
        out_specs=[whole_spec()] * 3,
        scratch_shapes=[
            pltpu.VMEM((width, width), LOW),
            pltpu.SemaphoreType.DMA((owners, planes)),
        ],
        compiler_params=params(),
        cost_estimate=cost(4),
        name="router",
    )(
        rows,
        tokens,
        after(mixed_low, grad_near, *grad_planes, *grad_home[1::2]),
        tail,
        routes,
        routes.T,
        *output_pieces,
    )

    row_chips = over_chips(payload, owners)
    row_home = over_cores(row_chips, owners)
    row_start = after(payload, row_home[1])
    row_planes = [across(row_start, w, planes) for w in range(2, planes)]
    row_near = across(jnp.stack(row_chips), 1, planes)
    grad_far = chips_split(after(jnp.concatenate(grad_planes, axis=0), *row_chips), owners)

    def all_of(shape):
        return pl.BlockSpec(shape, lambda i: (0,) * len(shape))

    slab = width // planes
    slabs = (
        jax.ShapeDtypeStruct((local, slab, 2 * hidden_units), F32),
        jax.ShapeDtypeStruct((local, slab, hidden_units), F32),
    )
    out_even, out_odd, back_even, back_odd, up_grad, down_grad = pl.pallas_call(
        functools.partial(expert_home_kernel, owners, local, block),
        grid=(1,),
        out_shape=(
            jax.ShapeDtypeStruct((owners // 2, length, width), LOW),
            jax.ShapeDtypeStruct((owners // 2, length, width), LOW),
            jax.ShapeDtypeStruct((owners // 2, length, width + LANES), LOW),
            jax.ShapeDtypeStruct((owners // 2, length, width + LANES), LOW),
        )
        + slabs,
        in_specs=[smem_spec()]
        + [all_of((length + TAIL, width))] * owners
        + [all_of((length, width))] * owners
        + [hbm_spec()] * 2,
        out_specs=[all_of((owners // 2, length, width))] * 2
        + [all_of((owners // 2, length, width + LANES))] * 2
        + [all_of(part.shape) for part in slabs],
        scratch_shapes=[
            pltpu.VMEM(expert_up.shape, LOW),
            pltpu.VMEM(expert_down.shape, LOW),
            pltpu.VMEM((local, slots, width), LOW),
            pltpu.VMEM((local, slots, width), LOW),
            pltpu.VMEM((owners // 2, local * block, 2 * length), LOW),
            pltpu.VMEM((local, slots, LANES), F32),
            pltpu.VMEM((local, slots, width), LOW),
            pltpu.VMEM((local, slots, width + LANES), LOW),
            pltpu.SemaphoreType.DMA((2, local)),
        ],
        compiler_params=params(),
        cost_estimate=cost(22),
        name="expert_home",
    )(place, *row_home, *grad_home, expert_up, expert_down)

    joined, back = to_owners(
        back_even, after(back_odd, grad_far[1][0], grad_far[2][0], *row_planes), owners
    )
    row_far = chips_split(after(jnp.concatenate(row_planes, axis=0), *back), owners)
    grad_pairs = core_pieces_whole(grad_far, owners)
    row_pairs = core_pieces_whole(row_far, owners)
    grad_near_pair = (grad_near, partner(grad_near, owners))
    row_near_pair = (row_near, partner(row_near, owners))

    def expert_away(s, place, up_grad, down_grad):
        away_slots = (planes - 1) * block
        tall = length + TAIL
        return pl.pallas_call(
            functools.partial(expert_away_kernel, local, block, planes - 2),
            grid=(1,),
            out_shape=slabs,
            in_specs=[smem_spec()]
            + [pl.BlockSpec((1, tall, width), lambda i: (s, 0, 0))] * 2
            + [all_of(((planes - 2) * tall, width))] * 2
            + [pl.BlockSpec((1, length, width), lambda i: (s, 0, 0))] * 2
            + [all_of(((planes - 2) * length, width))] * 2
            + [hbm_spec()] * 2
            + [all_of(part.shape) for part in slabs],
            out_specs=[all_of(part.shape) for part in slabs],
            scratch_shapes=[
                pltpu.VMEM(expert_up.shape, LOW),
                pltpu.VMEM(expert_down.shape, LOW),
                pltpu.VMEM((local, away_slots, width), LOW),
                pltpu.VMEM((local, away_slots, width), LOW),
                pltpu.VMEM((local, away_slots, LANES), F32),
                pltpu.SemaphoreType.DMA((2, local)),
            ],
            input_output_aliases={11: 0, 12: 1},
            compiler_params=params(),
            cost_estimate=cost(13),
            name="expert_away",
        )(
            place,
            *row_near_pair,
            *row_pairs[s],
            *grad_near_pair,
            *grad_pairs[s],
            expert_up,
            expert_down,
            up_grad,
            down_grad,
        )

    up_grad, down_grad = expert_away(0, after(place, *joined), up_grad, down_grad)

    def share_pieces(wide):
        return jax.ShapeDtypeStruct((owners // 2, planes, share, wide), LOW)

    hidden_grad, mixed_grad, tail_grad, output_even, output_odd = pl.pallas_call(
        functools.partial(hidden_backward_kernel, output_spots, owners // 2),
        out_shape=(
            token_wide,
            token_low,
            jax.ShapeDtypeStruct((width, LANES), F32),
            share_pieces(width),
            share_pieces(width),
        ),
        in_specs=[smem_spec()]
        + [whole_spec()] * (6 + owners // 2)
        + [hbm_spec()] * len(output_pieces),
        out_specs=[whole_spec()] * 3 + [hbm_spec()] * 2,
        scratch_shapes=[
            pltpu.VMEM((width, width), LOW),
            pltpu.VMEM((width, width), LOW),
            pltpu.SemaphoreType.DMA((owners, planes)),
            pltpu.SemaphoreType.DMA((owners, planes)),
        ],
        compiler_params=params(),
        cost_estimate=cost(6),
        name="hidden_backward",
    )(
        rows,
        payload,
        after(hidden, *grad_far[3]),
        mixed_low,
        gates,
        out_grad,
        tail,
        *back,
        *output_pieces,
    )
    output_other = partner(after(output_odd, row_far[1][0], row_far[2][0]), owners)
    made = to_owners(out_even, after(out_odd, *back), owners)[1]
    layer_out = (hidden + sum(part.astype(F32) for part in made)).astype(LOW)

    tokens_grad, grads_even, grads_odd = pl.pallas_call(
        functools.partial(attn_backward_kernel, spots),
        out_shape=(token_wide, share_pieces(columns), share_pieces(columns)),
        in_specs=[smem_spec()] + [whole_spec()] * 11 + [hbm_spec()] * len(pieces),
        out_specs=[whole_spec()] + [hbm_spec()] * 2,
        scratch_shapes=[
            pltpu.VMEM((width, columns), LOW),
            pltpu.VMEM((width, columns), LOW),
            pltpu.VMEM((length, width), LOW),
            pltpu.VMEM((length, width), LOW),
            pltpu.SemaphoreType.DMA((owners, planes)),
            pltpu.SemaphoreType.DMA((owners, planes)),
        ],
        compiler_params=params(),
        cost_estimate=cost(13),
        name="attn_backward",
    )(
        rows,
        tokens,
        seg_col,
        seg_row,
        cosine,
        sine,
        query_rot,
        keyval_low,
        mixed_grad,
        after(hidden_grad, output_other),
        tail,
        tail_grad,
        *pieces,
    )

    grads_other = partner(after(grads_odd, *row_far[3]), owners)
    shares = [
        jnp.concatenate(
            [added(output_even[s], output_other[s]), added(grads_even[s], grads_other[s])], axis=-1
        )
        for s in range(owners // 2)
    ]
    shares[3] = after(shares[3], up_grad)
    first, second = to_neighbours(shares, owners)
    up_grad, down_grad = expert_away(1, after(place, layer_out, *shares), up_grad, down_grad)
    plane_sums = from_neighbours(shares, first, second, owners)
    up_grad, down_grad = expert_away(2, after(place, first, second), up_grad, down_grad)
    summed = over_planes_sum(plane_sums, planes)
    up_grad, down_grad = expert_away(3, after(place, plane_sums), up_grad, down_grad)

    return (
        layer_out,
        tokens_grad,
        summed[:, width : 2 * width],
        summed[:, 2 * width : 3 * width],
        summed[:, :width],
        summed[:, 3 * width : 3 * width + EXPERTS],
        summed[:, 3 * width + EXPERTS],
        summed[:, 3 * width + EXPERTS + 1],
        up_grad,
        down_grad,
    )


def solution(mesh):
    return jax.shard_map(
        functools.partial(on_device, mesh.shape["dp"], mesh.shape["expert"]),
        mesh=mesh,
        in_specs=(
            P(("dp", "expert"), None),
            P(("dp", "expert"), None),
            P(("dp", "expert"), None),
            P(("dp", "expert"), None),
            P(("dp", "expert"), None),
            P(("dp", "expert"), None),
            P(("dp", "expert"), None),
            P(("dp", "expert")),
            P(("dp", "expert")),
            P("expert", None, None),
            P("expert", None, None),
            P(("dp", "expert"), None),
        ),
        out_specs=(
            P(("dp", "expert"), None),
            P(("dp", "expert"), None),
            P(("dp", "expert"), None),
            P(("dp", "expert"), None),
            P(("dp", "expert"), None),
            P(("dp", "expert"), None),
            P(("dp", "expert")),
            P(("dp", "expert")),
            P("expert", "dp", None),
            P("expert", "dp", None),
        ),
        check_vma=False,
    )
```

```python
import functools

import jax
import jax.numpy as jnp
from jax import lax
from jax.sharding import PartitionSpec as P
from jax.experimental import pallas as pl
from jax.experimental.pallas import tpu as pltpu

HEAD_DIM = 64
FF = 512
EXPERTS = 32
TOP = 8
CAP = 40


EPS = 1e-05
ROPE_BASE = 10000.0
MASKED = -1e30
HIGH = lax.Precision.HIGHEST


def norm_forward(values, gain_vec):
    inverse = lax.rsqrt(jnp.mean(values * values, axis=-1, keepdims=True) + EPS)
    normed = values * inverse
    return (normed, inverse, (normed * gain_vec).astype(jnp.bfloat16))


def norm_backward(grad_out, normed, inverse, gain_vec):
    gain_grad = jnp.sum(grad_out * normed, axis=0)
    scaled = grad_out * gain_vec
    grad_in = inverse * (scaled - normed * jnp.mean(scaled * normed, axis=-1, keepdims=True))
    return (grad_in, gain_grad)


def rope_tables(segment_row):
    length = segment_row.shape[0]
    earlier = jnp.sum((segment_row[None, :] < segment_row[:, None]).astype(jnp.int32), axis=1)
    position = jnp.arange(length, dtype=jnp.int32) - earlier
    half_dim = HEAD_DIM // 2
    frequency = ROPE_BASE ** (-(jnp.arange(half_dim, dtype=jnp.float32) * 2.0) / HEAD_DIM)
    angles = position.astype(jnp.float32)[:, None] * frequency[None, :]
    cosine = jnp.concatenate([jnp.cos(angles), jnp.cos(angles)], axis=-1)[:, None, :]
    sine_table = jnp.concatenate([jnp.sin(angles), jnp.sin(angles)], axis=-1)[:, None, :]
    return (cosine, sine_table)


def rotate(values, cosine, sine_table):
    half_dim = values.shape[-1] // 2
    turned = jnp.concatenate([-values[..., half_dim:], values[..., :half_dim]], axis=-1)
    return values * cosine + turned * sine_table


def unrotate(grad_rows, cosine, sine_table):
    half_dim = grad_rows.shape[-1] // 2
    weighted = grad_rows * sine_table
    turned = jnp.concatenate([weighted[..., half_dim:], -weighted[..., :half_dim]], axis=-1)
    return grad_rows * cosine + turned


def on_device_wide(
    tokens,
    segments,
    routes,
    query_weight,
    keyval_weight,
    output_weight,
    router_weight,
    attn_gain,
    moe_gain,
    expert_up,
    expert_down,
    out_grad,
):
    owners = lax.axis_size("expert")
    local_experts = expert_up.shape[0]
    length = tokens.shape[0]
    model_width = tokens.shape[1]
    kv_heads = keyval_weight.shape[1] // (2 * HEAD_DIM)
    query_heads = query_weight.shape[1] // HEAD_DIM
    repeat = query_heads // kv_heads
    score_scale = HEAD_DIM ** (-0.5)
    query_full, keyval_full, output_full, router_full, attn_gains, moe_gains = (
        lax.all_gather(query_weight, ("dp", "expert"), axis=0, tiled=True),
        lax.all_gather(keyval_weight, ("dp", "expert"), axis=0, tiled=True),
        lax.all_gather(output_weight, ("dp", "expert"), axis=0, tiled=True),
        lax.all_gather(router_weight, ("dp", "expert"), axis=0, tiled=True),
        lax.all_gather(attn_gain, ("dp", "expert"), axis=0, tiled=True),
        lax.all_gather(moe_gain, ("dp", "expert"), axis=0, tiled=True),
    )
    resident = tokens.astype(jnp.float32)
    normed_one, inverse_one, attn_in = norm_forward(resident, attn_gains.astype(jnp.float32))
    query_proj = jnp.dot(attn_in, query_full, preferred_element_type=jnp.float32).reshape(
        length, query_heads, HEAD_DIM
    )
    keyval_proj = jnp.dot(attn_in, keyval_full, preferred_element_type=jnp.float32)
    key_rows = keyval_proj[:, : kv_heads * HEAD_DIM].reshape(length, kv_heads, HEAD_DIM)
    value_rows = keyval_proj[:, kv_heads * HEAD_DIM :].reshape(length, kv_heads, HEAD_DIM)
    cosine, sine_table = rope_tables(segments[0])
    query_rot = (
        rotate(query_proj, cosine, sine_table)
        .astype(jnp.bfloat16)
        .reshape(length, kv_heads, repeat, HEAD_DIM)
    )
    keys_rot = rotate(key_rows, cosine, sine_table).astype(jnp.bfloat16)
    values_low = value_rows.astype(jnp.bfloat16)
    places = jnp.arange(length)
    visible = (segments[0][:, None] == segments[0][None, :]) & (places[None, :] <= places[:, None])
    scores = jnp.einsum("ikrd,jkd->krij", query_rot, keys_rot, preferred_element_type=jnp.float32)
    attn_logits = jnp.where(visible, scores * score_scale, MASKED)
    attn_exps = jnp.exp(attn_logits - jnp.max(attn_logits, axis=-1, keepdims=True))
    attn_probs = attn_exps / jnp.sum(attn_exps, axis=-1, keepdims=True)
    probs_low = attn_probs.astype(jnp.bfloat16)
    mixed_heads = jnp.einsum(
        "krij,jkd->ikrd", probs_low, values_low, preferred_element_type=jnp.float32
    )
    mixed_low = mixed_heads.reshape(length, query_heads * HEAD_DIM).astype(jnp.bfloat16)
    hidden = resident + jnp.dot(mixed_low, output_full, preferred_element_type=jnp.float32)
    normed_two, inverse_two, moe_in = norm_forward(hidden, moe_gains.astype(jnp.float32))
    router_logits = jnp.dot(moe_in, router_full, preferred_element_type=jnp.float32)
    choose = (routes[:, :, None] == jnp.arange(EXPERTS, dtype=jnp.int32)[None, None, :]).astype(
        jnp.float32
    )
    chosen = jnp.sum(choose * router_logits[:, None, :], axis=-1)
    gate_exps = jnp.exp(chosen - jnp.max(chosen, axis=-1, keepdims=True))
    gate_probs = gate_exps / jnp.sum(gate_exps, axis=-1, keepdims=True)
    entries = routes.reshape(-1)
    entry_count = entries.shape[0]
    onehot = (entries[:, None] == jnp.arange(EXPERTS, dtype=jnp.int32)[None, :]).astype(jnp.int32)
    position = jnp.sum((jnp.cumsum(onehot, axis=0) - 1) * onehot, axis=1)
    slot_index = entries * CAP + position
    owner_entry = (
        jnp.full((EXPERTS * CAP,), entry_count, jnp.int32)
        .at[slot_index]
        .set(jnp.arange(entry_count, dtype=jnp.int32))
    )
    padded_in = jnp.concatenate([moe_in, jnp.zeros((1, model_width), jnp.bfloat16)], axis=0)
    send_rows = jnp.take(padded_in, owner_entry // TOP, axis=0).reshape(EXPERTS, CAP, model_width)
    received = lax.all_to_all(send_rows, "expert", split_axis=0, concat_axis=0, tiled=True)
    slots_now = received.shape[1]
    grouped = received.reshape(owners, local_experts, slots_now, model_width)
    pair_proj = jnp.einsum("secd,edf->secf", grouped, expert_up, preferred_element_type=jnp.float32)
    activated = (jax.nn.silu(pair_proj[..., :FF]) * pair_proj[..., FF:]).astype(jnp.bfloat16)
    produced = jnp.einsum(
        "secf,edf->secd", activated, expert_down, preferred_element_type=jnp.float32
    ).astype(jnp.bfloat16)
    returned = lax.all_to_all(
        produced.reshape(EXPERTS, slots_now, model_width),
        "expert",
        split_axis=0,
        concat_axis=0,
        tiled=True,
    )
    returned, kept_rows, kept_pair = (
        returned,
        received,
        pair_proj.reshape(EXPERTS, slots_now, 2 * FF),
    )
    gathered = (
        jnp.take(returned.reshape(EXPERTS * CAP, model_width), slot_index, axis=0)
        .astype(jnp.float32)
        .reshape(length, TOP, model_width)
    )
    layer_out = (hidden + jnp.sum(gate_probs[:, :, None] * gathered, axis=1)).astype(jnp.bfloat16)
    grad_top = out_grad.astype(jnp.float32)
    gate_grad = jnp.sum(gathered * grad_top[:, None, :], axis=-1)
    chosen_grad = gate_probs * (gate_grad - jnp.sum(gate_probs * gate_grad, axis=-1, keepdims=True))
    logits_grad = jnp.sum(chosen_grad[:, :, None] * choose, axis=1)
    row_grads = (
        (gate_probs[:, :, None] * grad_top[:, None, :])
        .astype(jnp.bfloat16)
        .reshape(entry_count, model_width)
    )
    padded_grads = jnp.concatenate([row_grads, jnp.zeros((1, model_width), jnp.bfloat16)], axis=0)
    send_grads = jnp.take(padded_grads, owner_entry, axis=0).reshape(EXPERTS, CAP, model_width)
    grads_in = lax.all_to_all(send_grads, "expert", split_axis=0, concat_axis=0, tiled=True)
    grouped_rows = kept_rows.reshape(owners, local_experts, CAP, model_width)
    grouped_grads = grads_in.reshape(owners, local_experts, CAP, model_width)
    pair_kept = kept_pair.reshape(owners, local_experts, CAP, 2 * FF)
    gate_half = pair_kept[..., :FF]
    up_half = pair_kept[..., FF:]
    sigmoid_gate = jax.nn.sigmoid(gate_half)
    silu_gate = jax.nn.silu(gate_half)
    activated = (silu_gate * up_half).astype(jnp.bfloat16)
    act_grad = jnp.einsum(
        "secd,edf->secf", grouped_grads, expert_down, preferred_element_type=jnp.float32
    )
    pair_grad = jnp.concatenate(
        [
            act_grad * up_half * sigmoid_gate * (1.0 + gate_half * (1.0 - sigmoid_gate)),
            act_grad * silu_gate,
        ],
        axis=-1,
    ).astype(jnp.bfloat16)
    rows_back = jnp.einsum(
        "secf,edf->secd", pair_grad, expert_up, preferred_element_type=jnp.float32
    ).astype(jnp.bfloat16)
    up_grad = jnp.einsum(
        "secd,secf->edf", grouped_rows, pair_grad, preferred_element_type=jnp.float32
    )
    down_grad = jnp.einsum(
        "secd,secf->edf", grouped_grads, activated, preferred_element_type=jnp.float32
    )
    returned_grads = lax.all_to_all(
        rows_back.reshape(EXPERTS, CAP, model_width),
        "expert",
        split_axis=0,
        concat_axis=0,
        tiled=True,
    )
    expert_up_grad, expert_down_grad = (
        lax.psum_scatter(
            up_grad.astype(jnp.bfloat16), "dp", scatter_dimension=1, tiled=True
        ).astype(jnp.float32),
        lax.psum_scatter(
            down_grad.astype(jnp.bfloat16), "dp", scatter_dimension=1, tiled=True
        ).astype(jnp.float32),
    )
    token_grads = (
        jnp.take(returned_grads.reshape(EXPERTS * CAP, model_width), slot_index, axis=0)
        .astype(jnp.float32)
        .reshape(length, TOP, model_width)
    )
    router_wide = router_full.astype(jnp.float32)
    moe_grad = jnp.sum(token_grads, axis=1) + jnp.dot(logits_grad, router_wide.T, precision=HIGH)
    hidden_norm_grad, moe_gain_grad = norm_backward(
        moe_grad, normed_two, inverse_two, moe_gains.astype(jnp.float32)
    )
    hidden_grad = grad_top + hidden_norm_grad
    attn_out_grad = hidden_grad.astype(jnp.bfloat16)
    mixed_grad = (
        jnp.einsum("td,cd->tc", attn_out_grad, output_full, preferred_element_type=jnp.float32)
        .astype(jnp.bfloat16)
        .reshape(length, kv_heads, repeat, HEAD_DIM)
    )
    probs_grad = jnp.einsum(
        "ikrd,jkd->krij", mixed_grad, values_low, preferred_element_type=jnp.float32
    )
    values_grad = jnp.einsum(
        "krij,ikrd->jkd", probs_low, mixed_grad, preferred_element_type=jnp.float32
    )
    scores_grad = (
        attn_probs
        * (probs_grad - jnp.sum(attn_probs * probs_grad, axis=-1, keepdims=True))
        * score_scale
    ).astype(jnp.bfloat16)
    query_rot_grad = jnp.einsum(
        "krij,jkd->ikrd", scores_grad, keys_rot, preferred_element_type=jnp.float32
    ).reshape(length, query_heads, HEAD_DIM)
    keys_rot_grad = jnp.einsum(
        "krij,ikrd->jkd", scores_grad, query_rot, preferred_element_type=jnp.float32
    )
    query_low = (
        unrotate(query_rot_grad, cosine, sine_table)
        .reshape(length, query_heads * HEAD_DIM)
        .astype(jnp.bfloat16)
    )
    keyval_low = jnp.concatenate(
        [
            unrotate(keys_rot_grad, cosine, sine_table).reshape(length, kv_heads * HEAD_DIM),
            values_grad.reshape(length, kv_heads * HEAD_DIM),
        ],
        axis=1,
    ).astype(jnp.bfloat16)
    attn_in_grad = jnp.einsum(
        "tc,dc->td", query_low, query_full, preferred_element_type=jnp.float32
    ) + jnp.einsum("tc,dc->td", keyval_low, keyval_full, preferred_element_type=jnp.float32)
    token_norm_grad, attn_gain_grad = norm_backward(
        attn_in_grad, normed_one, inverse_one, attn_gains.astype(jnp.float32)
    )
    tokens_grad = hidden_grad + token_norm_grad
    slab_count = lax.axis_size("dp")
    slab_index = lax.axis_index("dp")
    width_rows = model_width // slab_count
    head_rows = query_heads * HEAD_DIM // slab_count
    all_attn, all_query, all_keyval, all_mixed, all_outgrad = (
        lax.all_gather(attn_in, "dp", axis=0, tiled=True),
        lax.all_gather(query_low, "dp", axis=0, tiled=True),
        lax.all_gather(keyval_low, "dp", axis=0, tiled=True),
        lax.all_gather(mixed_low, "dp", axis=0, tiled=True),
        lax.all_gather(attn_out_grad, "dp", axis=0, tiled=True),
    )
    all_moe, all_logits, attn_gain_rows, moe_gain_rows = (
        lax.all_gather(
            moe_in.astype(jnp.float32).astype(jnp.bfloat16), "dp", axis=0, tiled=True
        ).astype(jnp.float32),
        lax.all_gather(logits_grad.astype(jnp.bfloat16), "dp", axis=0, tiled=True).astype(
            logits_grad.dtype
        ),
        lax.all_gather(
            attn_gain_grad[None, :].astype(jnp.bfloat16), "dp", axis=0, tiled=True
        ).astype(jnp.float32),
        lax.all_gather(
            moe_gain_grad[None, :].astype(jnp.bfloat16), "dp", axis=0, tiled=True
        ).astype(jnp.float32),
    )
    attn_cols = lax.dynamic_slice_in_dim(all_attn, slab_index * width_rows, width_rows, 1)
    mixed_cols = lax.dynamic_slice_in_dim(all_mixed, slab_index * head_rows, head_rows, 1)
    moe_cols = lax.dynamic_slice_in_dim(all_moe, slab_index * width_rows, width_rows, 1)
    query_part = jnp.einsum("td,tc->dc", attn_cols, all_query, preferred_element_type=jnp.float32)
    keyval_part = jnp.einsum("td,tc->dc", attn_cols, all_keyval, preferred_element_type=jnp.float32)
    output_part = jnp.einsum(
        "tc,td->cd", mixed_cols, all_outgrad, preferred_element_type=jnp.float32
    )
    router_part = jnp.dot(moe_cols.T, all_logits, precision=HIGH)
    attn_gain_part = lax.dynamic_slice_in_dim(
        jnp.sum(attn_gain_rows, axis=0), slab_index * width_rows, width_rows, 0
    )
    moe_gain_part = lax.dynamic_slice_in_dim(
        jnp.sum(moe_gain_rows, axis=0), slab_index * width_rows, width_rows, 0
    )
    query_share, keyval_share, output_share, router_share, attn_share, moe_share = (
        lax.psum_scatter(
            query_part.astype(jnp.bfloat16), "expert", scatter_dimension=0, tiled=True
        ).astype(jnp.float32),
        lax.psum_scatter(
            keyval_part.astype(jnp.bfloat16), "expert", scatter_dimension=0, tiled=True
        ).astype(jnp.float32),
        lax.psum_scatter(
            output_part.astype(jnp.bfloat16), "expert", scatter_dimension=0, tiled=True
        ).astype(jnp.float32),
        lax.psum_scatter(
            router_part.astype(jnp.bfloat16), "expert", scatter_dimension=0, tiled=True
        ).astype(jnp.float32),
        lax.psum_scatter(
            attn_gain_part.astype(jnp.bfloat16), "expert", scatter_dimension=0, tiled=True
        ).astype(jnp.float32),
        lax.psum_scatter(
            moe_gain_part.astype(jnp.bfloat16), "expert", scatter_dimension=0, tiled=True
        ).astype(jnp.float32),
    )
    return (
        layer_out,
        tokens_grad,
        query_share,
        keyval_share,
        output_share,
        router_share,
        attn_share,
        moe_share,
        expert_up_grad,
        expert_down_grad,
    )


LANES = 128
TAIL = 16
PIECE_LIMIT = 4096
AWAY_EXPERTS = 2
VMEM_BYTES = 60 * 1024 * 1024
F32 = jnp.float32
LOW = jnp.bfloat16


def contract(left, right, left_dim, right_dim):
    return lax.dot_general(
        left, right, (((left_dim,), (right_dim,)), ((), ())), preferred_element_type=F32
    )


def lane_index(shape):
    return lax.broadcasted_iota(jnp.int32, shape, len(shape) - 1)


def row_index(shape):
    return lax.broadcasted_iota(jnp.int32, shape, len(shape) - 2)


def half_turn(chunk):
    first = lane_index(chunk.shape) % HEAD_DIM < HEAD_DIM // 2
    ahead = pltpu.roll(chunk, LANES - HEAD_DIM // 2, 1)
    behind = pltpu.roll(chunk, HEAD_DIM // 2, 1)
    return jnp.where(first, ahead, behind)


def both_heads(chunk, pick):
    swapped = pltpu.roll(chunk, HEAD_DIM, 1)
    first = lane_index(chunk.shape) < HEAD_DIM
    if pick == 0:
        return jnp.where(first, chunk, swapped)
    return jnp.where(first, swapped, chunk)


def split_heads(chunk):
    first = lane_index(chunk.shape) < HEAD_DIM
    zero = jnp.zeros_like(chunk)
    return jnp.concatenate([jnp.where(first, chunk, zero), jnp.where(first, zero, chunk)], axis=0)


def join_heads(stacked):
    length = stacked.shape[0] // 2
    top, bottom = stacked[:length], stacked[length:]
    return jnp.where(lane_index(top.shape) < HEAD_DIM, top, bottom)


def three_parts(values):
    high = values.astype(LOW).astype(F32)
    rest = values - high
    middle = rest.astype(LOW).astype(F32)
    return (high, middle, rest - middle)


def gain_select():
    shape = (8, LANES)
    return (lane_index(shape) == EXPERTS + row_index(shape)) & (row_index(shape) < 2)


def load_weights(rows_ref, spots, piece_refs, weights, sems):
    copies = []
    for (p, first), piece in zip(spots, piece_refs):
        for w in range(piece.shape[0]):
            size = piece.shape[1]
            start = pl.multiple_of(rows_ref[p, first + w] * size, size)
            copies.append(
                pltpu.make_async_copy(
                    piece.at[w], weights.at[pl.ds(start, size)], sems.at[p, first + w]
                )
            )
    for copy in copies:
        copy.start()
    return copies


def store_sums(rows_ref, sums, grads_even, grads_odd, sems):
    copies = []
    for p in range(2 * grads_even.shape[0]):
        target = grads_even if p % 2 == 0 else grads_odd
        for w in range(target.shape[1]):
            size = target.shape[2]
            start = pl.multiple_of(rows_ref[p, w] * size, size)
            copies.append(
                pltpu.make_async_copy(
                    sums.at[pl.ds(start, size)], target.at[p // 2, w], sems.at[p, w]
                )
            )
    for copy in copies:
        copy.start()
    return copies


def softmax_rows(q_pair, k_both, visible):
    scores = contract(q_pair, k_both, 1, 1) * (HEAD_DIM ** (-0.5))
    logits = jnp.where(visible, scores, MASKED)
    exps = jnp.exp(logits - jnp.max(logits, axis=-1, keepdims=True))
    return exps / jnp.sum(exps, axis=-1, keepdims=True)


def visible_pairs(seg_col, seg_row):
    length = seg_col.shape[0]
    shape = (length, length)
    seen = (seg_col == seg_row) & (lane_index(shape) <= row_index(shape))
    return jnp.concatenate([seen, seen], axis=0)


def attn_forward_kernel(spots, *refs):
    count = len(spots)
    rows_ref, tokens_ref, seg_col, seg_row, cos_ref, sin_ref = refs[:6]
    pieces = refs[6 : 6 + count]
    query_ref, keyval_ref, mixed_ref, tail_ref, weights, sems = refs[6 + count :]
    copies = load_weights(rows_ref, spots, pieces, weights, sems)
    tokens = tokens_ref[...].astype(F32)
    inverse = lax.rsqrt(jnp.mean(tokens * tokens, axis=-1, keepdims=True) + EPS)
    normed = tokens * inverse
    width = tokens.shape[1]
    for copy in copies:
        copy.wait()
    tail = weights[:, 2 * width :]
    tail_ref[...] = tail
    gains = contract(gain_select().astype(F32).astype(LOW), tail, 1, 1)
    attn_in = (normed * gains[0:1]).astype(LOW)
    cosine, sine = cos_ref[...], sin_ref[...]
    keyval = contract(attn_in, weights[:, width : 2 * width], 1, 0)
    query = contract(attn_in, weights[:, :width], 1, 0)
    visible = visible_pairs(seg_col[...], seg_row[...])
    half = width // 2
    for m in range(half // LANES):
        keys = keyval[:, m * LANES : (m + 1) * LANES]
        keys = (keys * cosine + half_turn(keys) * sine).astype(LOW)
        values = keyval[:, half + m * LANES : half + (m + 1) * LANES].astype(LOW)
        keyval_ref[:, m * LANES : (m + 1) * LANES] = keys
        keyval_ref[:, half + m * LANES : half + (m + 1) * LANES] = values
        for pick in range(2):
            k_both = both_heads(keys.astype(F32), pick).astype(LOW)
            v_both = both_heads(values.astype(F32), pick).astype(LOW)
            chunk = slice((2 * m + pick) * LANES, (2 * m + pick + 1) * LANES)
            queries = query[:, chunk]
            queries = (queries * cosine + half_turn(queries) * sine).astype(LOW)
            query_ref[:, chunk] = queries
            q_pair = split_heads(queries.astype(F32)).astype(LOW)
            probs = softmax_rows(q_pair, k_both, visible).astype(LOW)
            mixed_ref[:, chunk] = join_heads(contract(probs, v_both, 1, 0)).astype(LOW)


def router_kernel(spots, *refs):
    count = len(spots)
    rows_ref, tokens_ref, mixed_ref, tail_ref, routes_ref, routes_t = refs[:6]
    pieces = refs[6 : 6 + count]
    payload, hidden_ref, gates_ref, weights, sems = refs[6 + count :]
    copies = load_weights(rows_ref, spots, pieces, weights, sems)
    tokens = tokens_ref[...].astype(F32)
    length = tokens.shape[0]
    tail = tail_ref[...]
    gains = contract(gain_select().astype(F32).astype(LOW), tail, 1, 1)
    for copy in copies:
        copy.wait()
    hidden = tokens + contract(mixed_ref[...], weights[...], 1, 0)
    hidden_ref[...] = hidden
    inverse_two = lax.rsqrt(jnp.mean(hidden * hidden, axis=-1, keepdims=True) + EPS)
    moe_in = (hidden * inverse_two * gains[1:2]).astype(LOW)
    payload[:length] = moe_in
    logits = contract(moe_in, tail, 1, 0)
    routes = routes_ref[...]
    lanes = lane_index((length, LANES))
    chosen = lanes == routes[:, 0:1]
    for k in range(1, TOP):
        chosen = chosen | (lanes == routes[:, k : k + 1])
    logits = jnp.where(chosen, logits, MASKED)
    exps = jnp.where(chosen, jnp.exp(logits - jnp.max(logits, axis=-1, keepdims=True)), 0.0)
    gates = exps / jnp.sum(exps, axis=-1, keepdims=True)
    gates_ref[...] = gates
    gates_t = gates.T
    experts = row_index((LANES, length))
    turned = routes_t[...]
    for k in range(TOP):
        row = turned[k : k + 1]
        gate = jnp.sum(jnp.where(experts == row, gates_t, 0.0), axis=0, keepdims=True)
        high, middle, rest = three_parts(gate)
        place = row_index((TAIL, length))
        block = jnp.where(place == 0, high, jnp.where(place == 1, middle, jnp.where(place == 2, rest, 0.0)))
        block = jnp.where(place == 3, row.astype(F32), block)
        payload[length:, k * length : (k + 1) * length] = block.astype(LOW)


def gather_pair(first_expert, local, block, rows_a, rows_b, grads_a, grads_b, before, out):
    rows_out, grads_out, select_out, gate_out, pair = out
    length = rows_a.shape[0] - TAIL
    ids = row_index((8, length)) + first_expert
    ids = jnp.where(row_index((8, length)) < local, ids, -1).astype(F32)
    masks, gates = [], []
    for piece in (rows_a, rows_b):
        tail = piece[length:].astype(F32)
        mask = jnp.zeros((8, length), F32)
        gate = jnp.zeros((8, length), F32)
        for k in range(TOP):
            part = tail[:, k * length : (k + 1) * length]
            hit = part[3:4] == ids
            mask = jnp.where(hit, 1.0, mask)
            gate = jnp.where(hit, part[0:1] + part[1:2] + part[2:3], gate)
        masks.append(mask)
        gates.append(gate)
    mask = jnp.concatenate(masks, axis=1)
    gate = jnp.concatenate(gates, axis=1)
    place = contract(mask.astype(LOW), before, 1, 0)
    place = jnp.where(mask > 0, place, -1.0)
    slots = row_index((block, 2 * length)).astype(F32)
    parts = []
    for j in range(local):
        hit = slots == place[j : j + 1]
        parts.append(jnp.where(hit, 1.0, 0.0))
        held = jnp.sum(jnp.where(hit, gate[j : j + 1], 0.0), axis=1, keepdims=True)
        gate_out[j, pair * block : (pair + 1) * block] = jnp.broadcast_to(held, (block, LANES))
    select = jnp.concatenate(parts, axis=0).astype(LOW)
    if select_out is not None:
        select_out[pair] = select
    rows = jnp.concatenate([rows_a[:length], rows_b[:length]], axis=0)
    grads = jnp.concatenate([grads_a, grads_b], axis=0)
    rows = contract(select, rows, 1, 0).astype(LOW)
    grads = contract(select, grads, 1, 0).astype(LOW)
    for j in range(local):
        rows_out[j, pair * block : (pair + 1) * block] = rows[j * block : (j + 1) * block]
        grads_out[j, pair * block : (pair + 1) * block] = grads[j * block : (j + 1) * block]


def earlier_matrix(length):
    shape = (2 * length, 2 * length)
    return jnp.where(row_index(shape) < lane_index(shape), 1.0, 0.0).astype(LOW)


def expert_step(j, rows, grads, gate_ref, up, down):
    hidden_units = down.shape[1]
    pair = contract(rows[j], up, 1, 0)
    raw = contract(grads[j], down, 1, 0)
    gate_half, up_half = pair[:, :hidden_units], pair[:, hidden_units:]
    gate = gate_ref[j][:, 0:1]
    sigmoid = 1.0 / (1.0 + jnp.exp(-gate_half))
    silu = gate_half * sigmoid
    activated = silu * up_half
    scaled = (gate * activated).astype(LOW)
    act_grad = gate * raw
    pair_grad = jnp.concatenate(
        [act_grad * up_half * sigmoid * (1.0 + gate_half * (1.0 - sigmoid)), act_grad * silu],
        axis=1,
    ).astype(LOW)
    gate_grad = jnp.sum(activated * raw, axis=1, keepdims=True)
    return (scaled, pair_grad, gate_grad)


def fetch_experts(local, up_hbm, down_hbm, up, down, sems):
    copies = []
    for j in range(local):
        copies.append(
            (
                pltpu.make_async_copy(up_hbm.at[j], up.at[j], sems.at[0, j]),
                pltpu.make_async_copy(down_hbm.at[j], down.at[j], sems.at[1, j]),
            )
        )
        for copy in copies[j]:
            copy.start()
    return copies


def expert_home_kernel(owners, local, block, *refs):
    place_ref = refs[0]
    rows_in = refs[1 : 1 + owners]
    grads_in = refs[1 + owners : 1 + 2 * owners]
    up_hbm, down_hbm = refs[1 + 2 * owners : 3 + 2 * owners]
    out_even, out_odd, back_even, back_odd, up_grad, down_grad = refs[3 + 2 * owners : 9 + 2 * owners]
    up, down, rows, grads, select, gate_ref, produced, returned, sems = refs[9 + 2 * owners :]
    copies = fetch_experts(local, up_hbm, down_hbm, up, down, sems)
    length = rows_in[0].shape[0] - TAIL
    width = rows_in[0].shape[1]
    first_expert = place_ref[0] * local
    slab = up_grad.shape[1]
    columns = pl.ds(pl.multiple_of(place_ref[1] * slab, slab), slab)
    before = earlier_matrix(length)
    for s in range(owners // 2):
        gather_pair(
            first_expert,
            local,
            block,
            rows_in[2 * s][...],
            rows_in[2 * s + 1][...],
            grads_in[2 * s][...],
            grads_in[2 * s + 1][...],
            before,
            (rows, grads, select, gate_ref, s),
        )
    for j in range(local):
        for copy in copies[j]:
            copy.wait()
        scaled, pair_grad, gate_grad = expert_step(j, rows, grads, gate_ref, up[j], down[j])
        produced[j] = contract(scaled, down[j], 1, 1).astype(LOW)
        returned[j, :, :width] = contract(pair_grad, up[j], 1, 1).astype(LOW)
        lanes = lane_index((scaled.shape[0], LANES)) - first_expert - j
        high, middle, rest = three_parts(gate_grad)
        tail = jnp.where(lanes == 0, high, 0.0)
        tail = jnp.where(lanes == EXPERTS, middle, tail)
        tail = jnp.where(lanes == 2 * EXPERTS, rest, tail)
        returned[j, :, width:] = tail.astype(LOW)
        up_grad[j] = contract(rows[j, :, columns], pair_grad, 0, 0)
        down_grad[j] = contract(grads[j, :, columns], scaled, 0, 0)
    for s in range(owners // 2):
        span = slice(s * block, (s + 1) * block)
        made = jnp.concatenate([produced[j, span] for j in range(local)], axis=0)
        back = jnp.concatenate([returned[j, span] for j in range(local)], axis=0)
        made = contract(select[s], made, 0, 0).astype(LOW)
        back = contract(select[s], back, 0, 0).astype(LOW)
        out_even[s] = made[:length]
        out_odd[s] = made[length:]
        back_even[s] = back[:length]
        back_odd[s] = back[length:]


def expert_away_kernel(start, count, block, chips, far, *refs):
    place_ref = refs[0]
    rows_in = refs[1 : 3 + 2 * chips]
    grads_in = refs[3 + 2 * chips : 3 + 4 * chips]
    up_hbm, down_hbm, up_first, down_first = refs[3 + 4 * chips : 7 + 4 * chips]
    up_grad, down_grad = refs[7 + 4 * chips : 9 + 4 * chips]
    scratch = refs[9 + 4 * chips :]
    up, down, up_sum, down_sum, rows_buf, grads_buf, rows, grads, gate_ref, sems, pair_sems = scratch
    length = grads_buf.shape[1] // 2
    tall = length + TAIL
    pairs = []
    for i in range(far + 1):
        for s in range(chips):
            spot = len(pairs)
            copies = []
            for side in range(2):
                grad_from = grads_in[2 * s + side].at[pl.ds(i * length, length)]
                if i == 0:
                    row_from = rows_in[side].at[s]
                else:
                    row_from = rows_in[2 + 2 * s + side].at[pl.ds((i - 1) * tall, tall)]
                row_to = rows_buf.at[spot, pl.ds(side * tall, tall)]
                grad_to = grads_buf.at[spot, pl.ds(side * length, length)]
                copies.append(pltpu.make_async_copy(row_from, row_to, pair_sems.at[0, side, spot]))
                copies.append(pltpu.make_async_copy(grad_from, grad_to, pair_sems.at[1, side, spot]))
            pairs.append(copies)
    for copies in pairs:
        for copy in copies:
            copy.start()
    held = []
    for j in range(count):
        held.append(
            [
                pltpu.make_async_copy(up_hbm.at[start + j], up.at[j], sems.at[0, j]),
                pltpu.make_async_copy(down_hbm.at[start + j], down.at[j], sems.at[1, j]),
                pltpu.make_async_copy(up_first.at[start + j], up_sum.at[j], sems.at[2, j]),
                pltpu.make_async_copy(down_first.at[start + j], down_sum.at[j], sems.at[3, j]),
            ]
        )
    for copies in held:
        for copy in copies:
            copy.start()
    first_expert = place_ref[0] * (up_hbm.shape[0]) + start
    slab = up_sum.shape[1]
    columns = pl.ds(pl.multiple_of(place_ref[1] * slab, slab), slab)
    before = earlier_matrix(length)
    for i, copies in enumerate(pairs):
        for copy in copies:
            copy.wait()
        gather_pair(
            first_expert,
            count,
            block,
            rows_buf[i, :tall],
            rows_buf[i, tall:],
            grads_buf[i, :length],
            grads_buf[i, length:],
            before,
            (rows, grads, None, gate_ref, i),
        )
    sent = []
    for j in range(count):
        for copy in held[j]:
            copy.wait()
        scaled, pair_grad, _ = expert_step(j, rows, grads, gate_ref, up[j], down[j])
        up_sum[j] += contract(rows[j, :, columns], pair_grad, 0, 0)
        down_sum[j] += contract(grads[j, :, columns], scaled, 0, 0)
        sent.append(pltpu.make_async_copy(up_sum.at[j], up_grad.at[start + j], sems.at[4, j]))
        sent.append(pltpu.make_async_copy(down_sum.at[j], down_grad.at[start + j], sems.at[5, j]))
        sent[-2].start()
        sent[-1].start()
    for copy in sent:
        copy.wait()


def backward_kernel(spots, output_spots, shares, *refs):
    rows_ref, tokens_ref, seg_col, seg_row, cos_ref, sin_ref, payload, hidden_ref = refs[:8]
    query_ref, keyval_ref, mixed_ref, gates_ref, out_grad_ref, tail_ref = refs[8:14]
    refs = refs[14:]
    back, refs = refs[:shares], refs[shares:]
    pieces, refs = refs[: len(spots)], refs[len(spots) :]
    output_pieces, refs = refs[: len(output_spots)], refs[len(output_spots) :]
    tokens_grad, grads_even, grads_odd = refs[:3]
    weights, output, sums, query_low, keyval_low, sems, output_sems, out_sems = refs[3:]
    output_copies = load_weights(rows_ref, output_spots, output_pieces, output, output_sems)
    copies = load_weights(rows_ref, spots, pieces, weights, sems)
    length, width = tokens_ref.shape
    half = width // 2
    columns = weights.shape[1]
    total = back[0][...].astype(F32)
    for share in back[1:]:
        total = total + share[...].astype(F32)
    parts = total[:, width:]
    lanes = lane_index(parts.shape)
    gate_grad = parts + pltpu.roll(parts, LANES - EXPERTS, 1) + pltpu.roll(parts, LANES - 2 * EXPERTS, 1)
    gate_grad = jnp.where(lanes < EXPERTS, gate_grad, 0.0)
    gates = gates_ref[...]
    logits_grad = gates * (gate_grad - jnp.sum(gates * gate_grad, axis=-1, keepdims=True))
    hidden = hidden_ref[...]
    inverse_two = lax.rsqrt(jnp.mean(hidden * hidden, axis=-1, keepdims=True) + EPS)
    normed_two = hidden * inverse_two
    tail = tail_ref[...]
    gains = contract(gain_select().astype(F32).astype(LOW), tail, 1, 1)
    high = logits_grad.astype(LOW)
    rest = (logits_grad - high.astype(F32)).astype(LOW)
    moe_grad = total[:, :width] + contract(high, tail, 1, 1) + contract(rest, tail, 1, 1)
    moe_gain_grad = jnp.sum(moe_grad * normed_two, axis=0, keepdims=True)
    scaled = moe_grad * gains[1:2]
    hidden_grad = out_grad_ref[...].astype(F32) + inverse_two * (
        scaled - normed_two * jnp.mean(scaled * normed_two, axis=-1, keepdims=True)
    )
    attn_out_grad = hidden_grad.astype(LOW)
    for copy in output_copies:
        copy.wait()
    mixed_grad = contract(attn_out_grad, output[...], 1, 1)
    sums[:, columns:] = contract(mixed_ref[...], attn_out_grad, 0, 0).astype(LOW)
    tokens = tokens_ref[...].astype(F32)
    inverse_one = lax.rsqrt(jnp.mean(tokens * tokens, axis=-1, keepdims=True) + EPS)
    normed_one = tokens * inverse_one
    cosine, sine = cos_ref[...], sin_ref[...]
    visible = visible_pairs(seg_col[...], seg_row[...])
    for m in range(half // LANES):
        keys = keyval_ref[:, m * LANES : (m + 1) * LANES].astype(F32)
        values = keyval_ref[:, half + m * LANES : half + (m + 1) * LANES].astype(F32)
        key_sides, value_sides = [], []
        for pick in range(2):
            k_both = both_heads(keys, pick).astype(LOW)
            v_both = both_heads(values, pick).astype(LOW)
            chunk = slice((2 * m + pick) * LANES, (2 * m + pick + 1) * LANES)
            q_pair = split_heads(query_ref[:, chunk].astype(F32)).astype(LOW)
            m_pair = split_heads(mixed_grad[:, chunk]).astype(LOW)
            probs = softmax_rows(q_pair, k_both, visible)
            probs_grad = contract(m_pair, v_both, 1, 1)
            value_sides.append(contract(probs.astype(LOW), m_pair, 0, 0))
            scores_grad = (
                probs
                * (probs_grad - jnp.sum(probs * probs_grad, axis=-1, keepdims=True))
                * (HEAD_DIM ** (-0.5))
            ).astype(LOW)
            query_grad = join_heads(contract(scores_grad, k_both, 1, 0))
            query_low[:, chunk] = (query_grad * cosine - half_turn(query_grad) * sine).astype(LOW)
            key_sides.append(contract(scores_grad, q_pair, 0, 0))
        first = lane_index((length, LANES)) < HEAD_DIM
        key_sides = [side + pltpu.roll(side, HEAD_DIM, 1) for side in key_sides]
        value_sides = [side + pltpu.roll(side, HEAD_DIM, 1) for side in value_sides]
        keys_grad = jnp.where(first, key_sides[0], key_sides[1])
        values_grad = jnp.where(first, value_sides[0], value_sides[1])
        keyval_low[:, m * LANES : (m + 1) * LANES] = (
            keys_grad * cosine - half_turn(keys_grad) * sine
        ).astype(LOW)
        keyval_low[:, half + m * LANES : half + (m + 1) * LANES] = values_grad.astype(LOW)
    for copy in copies:
        copy.wait()
    attn_in_grad = contract(query_low[...], weights[:, :width], 1, 1) + contract(
        keyval_low[...], weights[:, width : 2 * width], 1, 1
    )
    attn_in = (normed_one * gains[0:1]).astype(LOW)
    sums[:, :width] = contract(attn_in, query_low[...], 0, 0).astype(LOW)
    sums[:, width : 2 * width] = contract(attn_in, keyval_low[...], 0, 0).astype(LOW)
    attn_gain_grad = jnp.sum(attn_in_grad * normed_one, axis=0, keepdims=True)
    place = row_index((8, width))
    gain_grads = jnp.where(place == 0, attn_gain_grad, jnp.where(place == 1, moe_gain_grad, 0.0))
    sums[:, 2 * width : columns] = (
        contract(payload[:length], high, 0, 0)
        + contract(gain_grads.astype(LOW), gain_select().astype(F32).astype(LOW), 0, 0)
    ).astype(LOW)
    out_copies = store_sums(rows_ref, sums, grads_even, grads_odd, out_sems)
    scaled = attn_in_grad * gains[0:1]
    tokens_grad[...] = hidden_grad + inverse_one * (
        scaled - normed_one * jnp.mean(scaled * normed_one, axis=-1, keepdims=True)
    )
    for copy in out_copies:
        copy.wait()


def swap(values, axis, size, distance):
    return lax.ppermute(values, axis, [(i, i ^ distance) for i in range(size)])


def across(values, distance, planes):
    return swap(values, "dp", planes, distance)


def aside(values, s, owners):
    return swap(values, "expert", owners, 2 * s)


def partner(values, owners):
    return swap(values, "expert", owners, 1)


def after(values, *earlier):
    return lax.optimization_barrier((values,) + earlier)[0]


def over_chips(values, owners):
    return [values] + [aside(values, s, owners) for s in range(1, owners // 2)]


def over_cores(near, owners, *earlier):
    pieces = []
    for piece in near:
        pieces += [piece, partner(after(piece, *earlier) if earlier else piece, owners)]
    return pieces


def chips_split(values, owners, *earlier):
    half = values.shape[0] // 2
    first, second = aside(values, 1, owners), aside(values, 2, owners)
    far = [first[:half], second[half:]]
    if earlier:
        far = [after(part, *earlier) for part in far]
    far = [aside(far[0], 2, owners), aside(far[1], 1, owners)]
    return [[values], [first], [second], far]


def core_pieces(near, owners):
    pieces, spots = [], []
    for s, parts in enumerate(near):
        first = 0
        for part in parts:
            pieces += [part, partner(part, owners)]
            spots += [(2 * s, first), (2 * s + 1, first)]
            first += part.shape[0]
    return (pieces, spots)


def core_pieces_whole(near, owners):
    pieces = []
    for parts in near:
        piece = parts[0] if len(parts) == 1 else jnp.concatenate(parts, axis=0)
        pieces.append((piece, partner(piece, owners)))
    return pieces


def added(left, right):
    return (left.astype(F32) + right.astype(F32)).astype(LOW)


def to_owners(even, odd, owners, *earlier):
    other = partner(odd, owners)
    joined = [added(even[s], other[s]) for s in range(owners // 2)]
    if earlier:
        joined = lax.optimization_barrier(tuple(joined) + earlier)[: owners // 2]
    sent = [joined[0]] + [aside(joined[s], s, owners) for s in range(1, owners // 2)]
    return (joined, sent)


def to_neighbours(joined, owners):
    half = joined[3].shape[0] // 2
    low_turn = aside(joined[3][:half], 1, owners)
    top_turn = aside(joined[3][half:], 2, owners)
    low_turn, top_turn = lax.optimization_barrier((low_turn, top_turn))
    first = jnp.concatenate([joined[1][:half], added(joined[1][half:], top_turn)], axis=0)
    second = jnp.concatenate([added(joined[2][:half], low_turn), joined[2][half:]], axis=0)
    return (first, second)


def from_neighbours(joined, first, second, owners):
    parts = [joined[0], aside(first, 1, owners), aside(second, 2, owners)]
    return sum(part.astype(F32) for part in parts).astype(LOW)


def over_planes_sum(parts, planes):
    total = parts[0].astype(F32)
    for w in range(1, planes):
        total = total + across(parts[w], w, planes).astype(F32)
    return total


def cost(us):
    return pl.CostEstimate(flops=int(us * 1153e6), bytes_accessed=0, transcendentals=0)


def params():
    return pltpu.CompilerParams(vmem_limit_bytes=VMEM_BYTES)


def whole_spec():
    return pl.BlockSpec(memory_space=pltpu.VMEM)


def hbm_spec():
    return pl.BlockSpec(memory_space=pl.ANY)


def smem_spec():
    return pl.BlockSpec(memory_space=pltpu.SMEM)


def on_device(
    planes,
    owners,
    tokens,
    segments,
    routes,
    query_weight,
    keyval_weight,
    output_weight,
    router_weight,
    attn_gain,
    moe_gain,
    expert_up,
    expert_down,
    out_grad,
):
    length, width = tokens.shape
    if planes != 4 or owners != 8 or planes * owners * length > PIECE_LIMIT:
        return on_device_wide(
            tokens,
            segments,
            routes,
            query_weight,
            keyval_weight,
            output_weight,
            router_weight,
            attn_gain,
            moe_gain,
            expert_up,
            expert_down,
            out_grad,
        )
    local = expert_up.shape[0]
    hidden_units = expert_down.shape[2]
    block = 2 * CAP
    slots = owners // 2 * block
    plane = lax.axis_index("dp")
    owner = lax.axis_index("expert")
    share = query_weight.shape[0]
    rows = (plane ^ jnp.arange(planes))[None, :] * owners + (owner ^ jnp.arange(owners))[:, None]
    rows = rows.astype(jnp.int32)
    place = jnp.stack([owner, plane]).astype(jnp.int32)
    extra = jnp.concatenate(
        [
            router_weight,
            attn_gain[:, None],
            moe_gain[:, None],
            jnp.zeros((share, LANES - EXPERTS - 2), LOW),
        ],
        axis=1,
    )
    packed = jnp.concatenate([query_weight, keyval_weight, extra, output_weight], axis=1)
    columns = packed.shape[1] - width

    early = [across(packed, w, planes) for w in range(1, planes)]
    grad_chips = over_chips(out_grad, owners)
    gathered = jnp.stack([packed] + early)
    grad_start = after(out_grad, *early)
    grad_planes = [across(grad_start, w, planes) for w in range(1, planes)]
    near = chips_split(
        after(gathered[:, :, :columns], *grad_chips), owners, *grad_planes[:2]
    )
    pieces, spots = core_pieces(near, owners)
    output_near = over_chips(after(gathered[:, :, columns:], *pieces[:6], *near[3]), owners)

    segment_row = segments[0]
    earlier = jnp.sum((segment_row[None, :] < segment_row[:, None]).astype(jnp.int32), axis=1)
    position = (jnp.arange(length, dtype=jnp.int32) - earlier).astype(F32)
    half_dim = HEAD_DIM // 2
    frequency = ROPE_BASE ** (-(jnp.arange(half_dim, dtype=F32) * 2.0) / HEAD_DIM)
    angles = position[:, None] * frequency[None, :]
    cosine = jnp.tile(jnp.cos(angles), (1, LANES // half_dim))
    sine = jnp.sin(angles)
    sine = jnp.concatenate([-sine, sine, -sine, sine], axis=1)
    seg_col, seg_row = segment_row[:, None], segment_row[None, :]

    token_low = jax.ShapeDtypeStruct((length, width), LOW)
    token_wide = jax.ShapeDtypeStruct((length, width), F32)
    query_rot, keyval_low, mixed_low, tail = pl.pallas_call(
        functools.partial(attn_forward_kernel, spots),
        out_shape=(token_low, token_low, token_low, jax.ShapeDtypeStruct((width, LANES), LOW)),
        in_specs=[smem_spec()] + [whole_spec()] * 5 + [hbm_spec()] * len(pieces),
        out_specs=[whole_spec()] * 4,
        scratch_shapes=[
            pltpu.VMEM((width, columns), LOW),
            pltpu.SemaphoreType.DMA((owners, planes)),
        ],
        compiler_params=params(),
        cost_estimate=cost(6),
        name="attn_forward",
    )(rows, after(tokens, grad_planes[2]), seg_col, seg_row, cosine, sine, *pieces)

    output_pieces = over_cores(output_near, owners, mixed_low)
    output_spots = [(p, 0) for p in range(owners)]

    payload, hidden, gates = pl.pallas_call(
        functools.partial(router_kernel, output_spots),
        out_shape=(
            jax.ShapeDtypeStruct((length + TAIL, width), LOW),
            token_wide,
            jax.ShapeDtypeStruct((length, LANES), F32),
        ),
        in_specs=[smem_spec()] + [whole_spec()] * 5 + [hbm_spec()] * len(output_pieces),
        out_specs=[whole_spec()] * 3,
        scratch_shapes=[
            pltpu.VMEM((width, width), LOW),
            pltpu.SemaphoreType.DMA((owners, planes)),
        ],
        compiler_params=params(),
        cost_estimate=cost(4),
        name="router",
    )(
        rows,
        tokens,
        mixed_low,
        tail,
        routes,
        routes.T,
        *output_pieces,
    )

    row_chips = over_chips(payload, owners)
    grad_home = over_cores(grad_chips, owners, payload)
    row_home = over_cores(row_chips, owners)
    row_start = after(payload, row_home[1])
    row_planes = [across(row_start, w, planes) for w in range(2, planes)]
    row_near = across(jnp.stack(row_chips), 1, planes)
    grad_stack = jnp.concatenate(grad_planes, axis=0)
    grad_direct = after(grad_stack, *row_chips)
    grad_near = [aside(grad_direct, s, owners) for s in (1, 2)]
    grad_own = partner(after(grad_stack, payload), owners)

    def all_of(shape):
        return pl.BlockSpec(shape, lambda i: (0,) * len(shape))

    slab = width // planes
    slabs = (
        jax.ShapeDtypeStruct((local, slab, 2 * hidden_units), F32),
        jax.ShapeDtypeStruct((local, slab, hidden_units), F32),
    )
    out_even, out_odd, back_even, back_odd, up_grad, down_grad = pl.pallas_call(
        functools.partial(expert_home_kernel, owners, local, block),
        grid=(1,),
        out_shape=(
            jax.ShapeDtypeStruct((owners // 2, length, width), LOW),
            jax.ShapeDtypeStruct((owners // 2, length, width), LOW),
            jax.ShapeDtypeStruct((owners // 2, length, width + LANES), LOW),
            jax.ShapeDtypeStruct((owners // 2, length, width + LANES), LOW),
        )
        + slabs,
        in_specs=[smem_spec()]
        + [all_of((length + TAIL, width))] * owners
        + [all_of((length, width))] * owners
        + [hbm_spec()] * 2,
        out_specs=[all_of((owners // 2, length, width))] * 2
        + [all_of((owners // 2, length, width + LANES))] * 2
        + [all_of(part.shape) for part in slabs],
        scratch_shapes=[
            pltpu.VMEM(expert_up.shape, LOW),
            pltpu.VMEM(expert_down.shape, LOW),
            pltpu.VMEM((local, slots, width), LOW),
            pltpu.VMEM((local, slots, width), LOW),
            pltpu.VMEM((owners // 2, local * block, 2 * length), LOW),
            pltpu.VMEM((local, slots, LANES), F32),
            pltpu.VMEM((local, slots, width), LOW),
            pltpu.VMEM((local, slots, width + LANES), LOW),
            pltpu.SemaphoreType.DMA((2, local)),
        ],
        compiler_params=params(),
        cost_estimate=cost(22),
        name="expert_home",
    )(after(place, grad_own), *row_home, *grad_home, expert_up, expert_down)

    joined, back = to_owners(back_even, after(back_odd, *grad_near, *row_planes), owners)
    row_far = chips_split(after(jnp.concatenate(row_planes, axis=0), *back), owners)
    half = grad_stack.shape[0] // 2
    grad_turn = [
        aside(grad_near[0][:half], 2, owners),
        aside(grad_near[1][half:], 1, owners),
    ]
    grad_away = [grad_stack, grad_own]
    grad_away += over_cores(grad_near, owners, *back)
    grad_away += over_cores([jnp.concatenate(grad_turn, axis=0)], owners, *back)
    row_away = over_cores([row_near] + [jnp.concatenate(parts, axis=0) for parts in row_far], owners)

    def expert_away(start, place, up_grad, down_grad):
        chips = owners // 2
        pairs = chips * (planes - 1)
        return pl.pallas_call(
            functools.partial(
                expert_away_kernel, start, AWAY_EXPERTS, block, chips, planes - 2
            ),
            out_shape=slabs,
            in_specs=[smem_spec()] + [hbm_spec()] * (6 + 4 * chips),
            out_specs=[hbm_spec()] * 2,
            scratch_shapes=[
                pltpu.VMEM((AWAY_EXPERTS,) + expert_up.shape[1:], LOW),
                pltpu.VMEM((AWAY_EXPERTS,) + expert_down.shape[1:], LOW),
                pltpu.VMEM((AWAY_EXPERTS,) + slabs[0].shape[1:], F32),
                pltpu.VMEM((AWAY_EXPERTS,) + slabs[1].shape[1:], F32),
                pltpu.VMEM((pairs, 2 * (length + TAIL), width), LOW),
                pltpu.VMEM((pairs, 2 * length, width), LOW),
                pltpu.VMEM((AWAY_EXPERTS, pairs * block, width), LOW),
                pltpu.VMEM((AWAY_EXPERTS, pairs * block, width), LOW),
                pltpu.VMEM((AWAY_EXPERTS, pairs * block, LANES), F32),
                pltpu.SemaphoreType.DMA((6, AWAY_EXPERTS)),
                pltpu.SemaphoreType.DMA((2, 2, pairs)),
            ],
            input_output_aliases={5 + 4 * chips: 0, 6 + 4 * chips: 1},
            compiler_params=params(),
            cost_estimate=cost(8 * AWAY_EXPERTS),
            name="expert_away",
        )(place, *row_away, *grad_away, expert_up, expert_down, up_grad, down_grad)

    def share_pieces(wide):
        return jax.ShapeDtypeStruct((owners // 2, planes, share, wide), LOW)

    wide = columns + width
    tokens_grad, grads_even, grads_odd = pl.pallas_call(
        functools.partial(backward_kernel, spots, output_spots, owners // 2),
        out_shape=(token_wide, share_pieces(wide), share_pieces(wide)),
        in_specs=[smem_spec()]
        + [whole_spec()] * (13 + owners // 2)
        + [hbm_spec()] * (len(pieces) + len(output_pieces)),
        out_specs=[whole_spec()] + [hbm_spec()] * 2,
        scratch_shapes=[
            pltpu.VMEM((width, columns), LOW),
            pltpu.VMEM((width, width), LOW),
            pltpu.VMEM((width, wide), LOW),
            pltpu.VMEM((length, width), LOW),
            pltpu.VMEM((length, width), LOW),
            pltpu.SemaphoreType.DMA((owners, planes)),
            pltpu.SemaphoreType.DMA((owners, planes)),
            pltpu.SemaphoreType.DMA((owners, planes)),
        ],
        compiler_params=params(),
        cost_estimate=cost(17),
        name="backward",
    )(
        rows,
        tokens,
        seg_col,
        seg_row,
        cosine,
        sine,
        payload,
        after(hidden, *grad_turn),
        query_rot,
        keyval_low,
        mixed_low,
        gates,
        out_grad,
        tail,
        *back,
        *pieces,
        *output_pieces,
    )

    grads_other = partner(
        after(grads_odd, row_near, row_far[1][0], row_far[2][0], *grad_away[3:6:2]), owners
    )
    shares = [added(grads_even[s], grads_other[s]) for s in range(owners // 2)]
    out_other = partner(after(out_odd, *back), owners)
    made = [added(out_even[s], out_other[s]) for s in range(owners // 2)]
    made[3] = aside(made[3], 3, owners)
    shares[3] = after(shares[3], made[3], *row_far[3])
    first, second = to_neighbours(shares, owners)
    plane_sums = from_neighbours(shares, first, second, owners)
    up_grad, down_grad = expert_away(0, after(place, first, second), up_grad, down_grad)
    for start in range(AWAY_EXPERTS, local, AWAY_EXPERTS):
        up_grad, down_grad = expert_away(start, after(place, plane_sums), up_grad, down_grad)
    summed = over_planes_sum(plane_sums, planes)
    made = [made[0]] + [aside(after(made[s], plane_sums), s, owners) for s in (1, 2)] + [made[3]]
    layer_out = (hidden + sum(part.astype(F32) for part in made)).astype(LOW)

    return (
        layer_out,
        tokens_grad,
        summed[:, :width],
        summed[:, width : 2 * width],
        summed[:, columns:],
        summed[:, 2 * width : 2 * width + EXPERTS],
        summed[:, 2 * width + EXPERTS],
        summed[:, 2 * width + EXPERTS + 1],
        up_grad,
        down_grad,
    )


def solution(mesh):
    return jax.shard_map(
        functools.partial(on_device, mesh.shape["dp"], mesh.shape["expert"]),
        mesh=mesh,
        in_specs=(
            P(("dp", "expert"), None),
            P(("dp", "expert"), None),
            P(("dp", "expert"), None),
            P(("dp", "expert"), None),
            P(("dp", "expert"), None),
            P(("dp", "expert"), None),
            P(("dp", "expert"), None),
            P(("dp", "expert")),
            P(("dp", "expert")),
            P("expert", None, None),
            P("expert", None, None),
            P(("dp", "expert"), None),
        ),
        out_specs=(
            P(("dp", "expert"), None),
            P(("dp", "expert"), None),
            P(("dp", "expert"), None),
            P(("dp", "expert"), None),
            P(("dp", "expert"), None),
            P(("dp", "expert"), None),
            P(("dp", "expert")),
            P(("dp", "expert")),
            P("expert", "dp", None),
            P("expert", "dp", None),
        ),
        check_vma=False,
    )
```

```python
import functools

import jax
import jax.numpy as jnp
from jax import lax
from jax.sharding import PartitionSpec as P
from jax.experimental import pallas as pl
from jax.experimental.pallas import tpu as pltpu

HEAD_DIM = 64
FF = 512
EXPERTS = 32
TOP = 8
CAP = 40


EPS = 1e-05
ROPE_BASE = 10000.0
MASKED = -1e30
HIGH = lax.Precision.HIGHEST


def norm_forward(values, gain_vec):
    inverse = lax.rsqrt(jnp.mean(values * values, axis=-1, keepdims=True) + EPS)
    normed = values * inverse
    return (normed, inverse, (normed * gain_vec).astype(jnp.bfloat16))


def norm_backward(grad_out, normed, inverse, gain_vec):
    gain_grad = jnp.sum(grad_out * normed, axis=0)
    scaled = grad_out * gain_vec
    grad_in = inverse * (scaled - normed * jnp.mean(scaled * normed, axis=-1, keepdims=True))
    return (grad_in, gain_grad)


def rope_tables(segment_row):
    length = segment_row.shape[0]
    earlier = jnp.sum((segment_row[None, :] < segment_row[:, None]).astype(jnp.int32), axis=1)
    position = jnp.arange(length, dtype=jnp.int32) - earlier
    half_dim = HEAD_DIM // 2
    frequency = ROPE_BASE ** (-(jnp.arange(half_dim, dtype=jnp.float32) * 2.0) / HEAD_DIM)
    angles = position.astype(jnp.float32)[:, None] * frequency[None, :]
    cosine = jnp.concatenate([jnp.cos(angles), jnp.cos(angles)], axis=-1)[:, None, :]
    sine_table = jnp.concatenate([jnp.sin(angles), jnp.sin(angles)], axis=-1)[:, None, :]
    return (cosine, sine_table)


def rotate(values, cosine, sine_table):
    half_dim = values.shape[-1] // 2
    turned = jnp.concatenate([-values[..., half_dim:], values[..., :half_dim]], axis=-1)
    return values * cosine + turned * sine_table


def unrotate(grad_rows, cosine, sine_table):
    half_dim = grad_rows.shape[-1] // 2
    weighted = grad_rows * sine_table
    turned = jnp.concatenate([weighted[..., half_dim:], -weighted[..., :half_dim]], axis=-1)
    return grad_rows * cosine + turned


def on_device_wide(
    tokens,
    segments,
    routes,
    query_weight,
    keyval_weight,
    output_weight,
    router_weight,
    attn_gain,
    moe_gain,
    expert_up,
    expert_down,
    out_grad,
):
    owners = lax.axis_size("expert")
    local_experts = expert_up.shape[0]
    length = tokens.shape[0]
    model_width = tokens.shape[1]
    kv_heads = keyval_weight.shape[1] // (2 * HEAD_DIM)
    query_heads = query_weight.shape[1] // HEAD_DIM
    repeat = query_heads // kv_heads
    score_scale = HEAD_DIM ** (-0.5)
    query_full, keyval_full, output_full, router_full, attn_gains, moe_gains = (
        lax.all_gather(query_weight, ("dp", "expert"), axis=0, tiled=True),
        lax.all_gather(keyval_weight, ("dp", "expert"), axis=0, tiled=True),
        lax.all_gather(output_weight, ("dp", "expert"), axis=0, tiled=True),
        lax.all_gather(router_weight, ("dp", "expert"), axis=0, tiled=True),
        lax.all_gather(attn_gain, ("dp", "expert"), axis=0, tiled=True),
        lax.all_gather(moe_gain, ("dp", "expert"), axis=0, tiled=True),
    )
    resident = tokens.astype(jnp.float32)
    normed_one, inverse_one, attn_in = norm_forward(resident, attn_gains.astype(jnp.float32))
    query_proj = jnp.dot(attn_in, query_full, preferred_element_type=jnp.float32).reshape(
        length, query_heads, HEAD_DIM
    )
    keyval_proj = jnp.dot(attn_in, keyval_full, preferred_element_type=jnp.float32)
    key_rows = keyval_proj[:, : kv_heads * HEAD_DIM].reshape(length, kv_heads, HEAD_DIM)
    value_rows = keyval_proj[:, kv_heads * HEAD_DIM :].reshape(length, kv_heads, HEAD_DIM)
    cosine, sine_table = rope_tables(segments[0])
    query_rot = (
        rotate(query_proj, cosine, sine_table)
        .astype(jnp.bfloat16)
        .reshape(length, kv_heads, repeat, HEAD_DIM)
    )
    keys_rot = rotate(key_rows, cosine, sine_table).astype(jnp.bfloat16)
    values_low = value_rows.astype(jnp.bfloat16)
    places = jnp.arange(length)
    visible = (segments[0][:, None] == segments[0][None, :]) & (places[None, :] <= places[:, None])
    scores = jnp.einsum("ikrd,jkd->krij", query_rot, keys_rot, preferred_element_type=jnp.float32)
    attn_logits = jnp.where(visible, scores * score_scale, MASKED)
    attn_exps = jnp.exp(attn_logits - jnp.max(attn_logits, axis=-1, keepdims=True))
    attn_probs = attn_exps / jnp.sum(attn_exps, axis=-1, keepdims=True)
    probs_low = attn_probs.astype(jnp.bfloat16)
    mixed_heads = jnp.einsum(
        "krij,jkd->ikrd", probs_low, values_low, preferred_element_type=jnp.float32
    )
    mixed_low = mixed_heads.reshape(length, query_heads * HEAD_DIM).astype(jnp.bfloat16)
    hidden = resident + jnp.dot(mixed_low, output_full, preferred_element_type=jnp.float32)
    normed_two, inverse_two, moe_in = norm_forward(hidden, moe_gains.astype(jnp.float32))
    router_logits = jnp.dot(moe_in, router_full, preferred_element_type=jnp.float32)
    choose = (routes[:, :, None] == jnp.arange(EXPERTS, dtype=jnp.int32)[None, None, :]).astype(
        jnp.float32
    )
    chosen = jnp.sum(choose * router_logits[:, None, :], axis=-1)
    gate_exps = jnp.exp(chosen - jnp.max(chosen, axis=-1, keepdims=True))
    gate_probs = gate_exps / jnp.sum(gate_exps, axis=-1, keepdims=True)
    entries = routes.reshape(-1)
    entry_count = entries.shape[0]
    onehot = (entries[:, None] == jnp.arange(EXPERTS, dtype=jnp.int32)[None, :]).astype(jnp.int32)
    position = jnp.sum((jnp.cumsum(onehot, axis=0) - 1) * onehot, axis=1)
    slot_index = entries * CAP + position
    owner_entry = (
        jnp.full((EXPERTS * CAP,), entry_count, jnp.int32)
        .at[slot_index]
        .set(jnp.arange(entry_count, dtype=jnp.int32))
    )
    padded_in = jnp.concatenate([moe_in, jnp.zeros((1, model_width), jnp.bfloat16)], axis=0)
    send_rows = jnp.take(padded_in, owner_entry // TOP, axis=0).reshape(EXPERTS, CAP, model_width)
    received = lax.all_to_all(send_rows, "expert", split_axis=0, concat_axis=0, tiled=True)
    slots_now = received.shape[1]
    grouped = received.reshape(owners, local_experts, slots_now, model_width)
    pair_proj = jnp.einsum("secd,edf->secf", grouped, expert_up, preferred_element_type=jnp.float32)
    activated = (jax.nn.silu(pair_proj[..., :FF]) * pair_proj[..., FF:]).astype(jnp.bfloat16)
    produced = jnp.einsum(
        "secf,edf->secd", activated, expert_down, preferred_element_type=jnp.float32
    ).astype(jnp.bfloat16)
    returned = lax.all_to_all(
        produced.reshape(EXPERTS, slots_now, model_width),
        "expert",
        split_axis=0,
        concat_axis=0,
        tiled=True,
    )
    returned, kept_rows, kept_pair = (
        returned,
        received,
        pair_proj.reshape(EXPERTS, slots_now, 2 * FF),
    )
    gathered = (
        jnp.take(returned.reshape(EXPERTS * CAP, model_width), slot_index, axis=0)
        .astype(jnp.float32)
        .reshape(length, TOP, model_width)
    )
    layer_out = (hidden + jnp.sum(gate_probs[:, :, None] * gathered, axis=1)).astype(jnp.bfloat16)
    grad_top = out_grad.astype(jnp.float32)
    gate_grad = jnp.sum(gathered * grad_top[:, None, :], axis=-1)
    chosen_grad = gate_probs * (gate_grad - jnp.sum(gate_probs * gate_grad, axis=-1, keepdims=True))
    logits_grad = jnp.sum(chosen_grad[:, :, None] * choose, axis=1)
    row_grads = (
        (gate_probs[:, :, None] * grad_top[:, None, :])
        .astype(jnp.bfloat16)
        .reshape(entry_count, model_width)
    )
    padded_grads = jnp.concatenate([row_grads, jnp.zeros((1, model_width), jnp.bfloat16)], axis=0)
    send_grads = jnp.take(padded_grads, owner_entry, axis=0).reshape(EXPERTS, CAP, model_width)
    grads_in = lax.all_to_all(send_grads, "expert", split_axis=0, concat_axis=0, tiled=True)
    grouped_rows = kept_rows.reshape(owners, local_experts, CAP, model_width)
    grouped_grads = grads_in.reshape(owners, local_experts, CAP, model_width)
    pair_kept = kept_pair.reshape(owners, local_experts, CAP, 2 * FF)
    gate_half = pair_kept[..., :FF]
    up_half = pair_kept[..., FF:]
    sigmoid_gate = jax.nn.sigmoid(gate_half)
    silu_gate = jax.nn.silu(gate_half)
    activated = (silu_gate * up_half).astype(jnp.bfloat16)
    act_grad = jnp.einsum(
        "secd,edf->secf", grouped_grads, expert_down, preferred_element_type=jnp.float32
    )
    pair_grad = jnp.concatenate(
        [
            act_grad * up_half * sigmoid_gate * (1.0 + gate_half * (1.0 - sigmoid_gate)),
            act_grad * silu_gate,
        ],
        axis=-1,
    ).astype(jnp.bfloat16)
    rows_back = jnp.einsum(
        "secf,edf->secd", pair_grad, expert_up, preferred_element_type=jnp.float32
    ).astype(jnp.bfloat16)
    up_grad = jnp.einsum(
        "secd,secf->edf", grouped_rows, pair_grad, preferred_element_type=jnp.float32
    )
    down_grad = jnp.einsum(
        "secd,secf->edf", grouped_grads, activated, preferred_element_type=jnp.float32
    )
    returned_grads = lax.all_to_all(
        rows_back.reshape(EXPERTS, CAP, model_width),
        "expert",
        split_axis=0,
        concat_axis=0,
        tiled=True,
    )
    expert_up_grad, expert_down_grad = (
        lax.psum_scatter(
            up_grad.astype(jnp.bfloat16), "dp", scatter_dimension=1, tiled=True
        ).astype(jnp.float32),
        lax.psum_scatter(
            down_grad.astype(jnp.bfloat16), "dp", scatter_dimension=1, tiled=True
        ).astype(jnp.float32),
    )
    token_grads = (
        jnp.take(returned_grads.reshape(EXPERTS * CAP, model_width), slot_index, axis=0)
        .astype(jnp.float32)
        .reshape(length, TOP, model_width)
    )
    router_wide = router_full.astype(jnp.float32)
    moe_grad = jnp.sum(token_grads, axis=1) + jnp.dot(logits_grad, router_wide.T, precision=HIGH)
    hidden_norm_grad, moe_gain_grad = norm_backward(
        moe_grad, normed_two, inverse_two, moe_gains.astype(jnp.float32)
    )
    hidden_grad = grad_top + hidden_norm_grad
    attn_out_grad = hidden_grad.astype(jnp.bfloat16)
    mixed_grad = (
        jnp.einsum("td,cd->tc", attn_out_grad, output_full, preferred_element_type=jnp.float32)
        .astype(jnp.bfloat16)
        .reshape(length, kv_heads, repeat, HEAD_DIM)
    )
    probs_grad = jnp.einsum(
        "ikrd,jkd->krij", mixed_grad, values_low, preferred_element_type=jnp.float32
    )
    values_grad = jnp.einsum(
        "krij,ikrd->jkd", probs_low, mixed_grad, preferred_element_type=jnp.float32
    )
    scores_grad = (
        attn_probs
        * (probs_grad - jnp.sum(attn_probs * probs_grad, axis=-1, keepdims=True))
        * score_scale
    ).astype(jnp.bfloat16)
    query_rot_grad = jnp.einsum(
        "krij,jkd->ikrd", scores_grad, keys_rot, preferred_element_type=jnp.float32
    ).reshape(length, query_heads, HEAD_DIM)
    keys_rot_grad = jnp.einsum(
        "krij,ikrd->jkd", scores_grad, query_rot, preferred_element_type=jnp.float32
    )
    query_low = (
        unrotate(query_rot_grad, cosine, sine_table)
        .reshape(length, query_heads * HEAD_DIM)
        .astype(jnp.bfloat16)
    )
    keyval_low = jnp.concatenate(
        [
            unrotate(keys_rot_grad, cosine, sine_table).reshape(length, kv_heads * HEAD_DIM),
            values_grad.reshape(length, kv_heads * HEAD_DIM),
        ],
        axis=1,
    ).astype(jnp.bfloat16)
    attn_in_grad = jnp.einsum(
        "tc,dc->td", query_low, query_full, preferred_element_type=jnp.float32
    ) + jnp.einsum("tc,dc->td", keyval_low, keyval_full, preferred_element_type=jnp.float32)
    token_norm_grad, attn_gain_grad = norm_backward(
        attn_in_grad, normed_one, inverse_one, attn_gains.astype(jnp.float32)
    )
    tokens_grad = hidden_grad + token_norm_grad
    slab_count = lax.axis_size("dp")
    slab_index = lax.axis_index("dp")
    width_rows = model_width // slab_count
    head_rows = query_heads * HEAD_DIM // slab_count
    all_attn, all_query, all_keyval, all_mixed, all_outgrad = (
        lax.all_gather(attn_in, "dp", axis=0, tiled=True),
        lax.all_gather(query_low, "dp", axis=0, tiled=True),
        lax.all_gather(keyval_low, "dp", axis=0, tiled=True),
        lax.all_gather(mixed_low, "dp", axis=0, tiled=True),
        lax.all_gather(attn_out_grad, "dp", axis=0, tiled=True),
    )
    all_moe, all_logits, attn_gain_rows, moe_gain_rows = (
        lax.all_gather(
            moe_in.astype(jnp.float32).astype(jnp.bfloat16), "dp", axis=0, tiled=True
        ).astype(jnp.float32),
        lax.all_gather(logits_grad.astype(jnp.bfloat16), "dp", axis=0, tiled=True).astype(
            logits_grad.dtype
        ),
        lax.all_gather(
            attn_gain_grad[None, :].astype(jnp.bfloat16), "dp", axis=0, tiled=True
        ).astype(jnp.float32),
        lax.all_gather(
            moe_gain_grad[None, :].astype(jnp.bfloat16), "dp", axis=0, tiled=True
        ).astype(jnp.float32),
    )
    attn_cols = lax.dynamic_slice_in_dim(all_attn, slab_index * width_rows, width_rows, 1)
    mixed_cols = lax.dynamic_slice_in_dim(all_mixed, slab_index * head_rows, head_rows, 1)
    moe_cols = lax.dynamic_slice_in_dim(all_moe, slab_index * width_rows, width_rows, 1)
    query_part = jnp.einsum("td,tc->dc", attn_cols, all_query, preferred_element_type=jnp.float32)
    keyval_part = jnp.einsum("td,tc->dc", attn_cols, all_keyval, preferred_element_type=jnp.float32)
    output_part = jnp.einsum(
        "tc,td->cd", mixed_cols, all_outgrad, preferred_element_type=jnp.float32
    )
    router_part = jnp.dot(moe_cols.T, all_logits, precision=HIGH)
    attn_gain_part = lax.dynamic_slice_in_dim(
        jnp.sum(attn_gain_rows, axis=0), slab_index * width_rows, width_rows, 0
    )
    moe_gain_part = lax.dynamic_slice_in_dim(
        jnp.sum(moe_gain_rows, axis=0), slab_index * width_rows, width_rows, 0
    )
    query_share, keyval_share, output_share, router_share, attn_share, moe_share = (
        lax.psum_scatter(
            query_part.astype(jnp.bfloat16), "expert", scatter_dimension=0, tiled=True
        ).astype(jnp.float32),
        lax.psum_scatter(
            keyval_part.astype(jnp.bfloat16), "expert", scatter_dimension=0, tiled=True
        ).astype(jnp.float32),
        lax.psum_scatter(
            output_part.astype(jnp.bfloat16), "expert", scatter_dimension=0, tiled=True
        ).astype(jnp.float32),
        lax.psum_scatter(
            router_part.astype(jnp.bfloat16), "expert", scatter_dimension=0, tiled=True
        ).astype(jnp.float32),
        lax.psum_scatter(
            attn_gain_part.astype(jnp.bfloat16), "expert", scatter_dimension=0, tiled=True
        ).astype(jnp.float32),
        lax.psum_scatter(
            moe_gain_part.astype(jnp.bfloat16), "expert", scatter_dimension=0, tiled=True
        ).astype(jnp.float32),
    )
    return (
        layer_out,
        tokens_grad,
        query_share,
        keyval_share,
        output_share,
        router_share,
        attn_share,
        moe_share,
        expert_up_grad,
        expert_down_grad,
    )


LANES = 128
TAIL = 16
PIECE_LIMIT = 4096
VMEM_BYTES = 60 * 1024 * 1024
F32 = jnp.float32
LOW = jnp.bfloat16


def contract(left, right, left_dim, right_dim):
    return lax.dot_general(
        left, right, (((left_dim,), (right_dim,)), ((), ())), preferred_element_type=F32
    )


def lane_index(shape):
    return lax.broadcasted_iota(jnp.int32, shape, len(shape) - 1)


def row_index(shape):
    return lax.broadcasted_iota(jnp.int32, shape, len(shape) - 2)


def half_turn(chunk):
    first = lane_index(chunk.shape) % HEAD_DIM < HEAD_DIM // 2
    ahead = pltpu.roll(chunk, LANES - HEAD_DIM // 2, 1)
    behind = pltpu.roll(chunk, HEAD_DIM // 2, 1)
    return jnp.where(first, ahead, behind)


def both_heads(chunk, pick):
    swapped = pltpu.roll(chunk, HEAD_DIM, 1)
    first = lane_index(chunk.shape) < HEAD_DIM
    if pick == 0:
        return jnp.where(first, chunk, swapped)
    return jnp.where(first, swapped, chunk)


def split_heads(chunk):
    first = lane_index(chunk.shape) < HEAD_DIM
    zero = jnp.zeros_like(chunk)
    return jnp.concatenate([jnp.where(first, chunk, zero), jnp.where(first, zero, chunk)], axis=0)


def join_heads(stacked):
    length = stacked.shape[0] // 2
    top, bottom = stacked[:length], stacked[length:]
    return jnp.where(lane_index(top.shape) < HEAD_DIM, top, bottom)


def three_parts(values):
    high = values.astype(LOW).astype(F32)
    rest = values - high
    middle = rest.astype(LOW).astype(F32)
    return (high, middle, rest - middle)


def gain_select():
    shape = (8, LANES)
    return (lane_index(shape) == EXPERTS + row_index(shape)) & (row_index(shape) < 2)


def load_weights(rows_ref, spots, piece_refs, weights, sems):
    copies = []
    for (p, first), piece in zip(spots, piece_refs):
        for w in range(piece.shape[0]):
            size = piece.shape[1]
            start = pl.multiple_of(rows_ref[p, first + w] * size, size)
            copies.append(
                pltpu.make_async_copy(
                    piece.at[w], weights.at[pl.ds(start, size)], sems.at[p, first + w]
                )
            )
    for copy in copies:
        copy.start()
    return copies


def store_sums(rows_ref, sums, grads_even, grads_odd, sems):
    copies = []
    for p in range(2 * grads_even.shape[0]):
        target = grads_even if p % 2 == 0 else grads_odd
        for w in range(target.shape[1]):
            size = target.shape[2]
            start = pl.multiple_of(rows_ref[p, w] * size, size)
            copies.append(
                pltpu.make_async_copy(
                    sums.at[pl.ds(start, size)], target.at[p // 2, w], sems.at[p, w]
                )
            )
    for copy in copies:
        copy.start()
    return copies


def softmax_rows(q_pair, k_both, visible):
    scores = contract(q_pair, k_both, 1, 1) * (HEAD_DIM ** (-0.5))
    logits = jnp.where(visible, scores, MASKED)
    exps = jnp.exp(logits - jnp.max(logits, axis=-1, keepdims=True))
    return exps / jnp.sum(exps, axis=-1, keepdims=True)


def segment_tables(seg_row, frequency):
    length = seg_row.shape[1]
    shape = (length, length)
    across_row = jnp.broadcast_to(seg_row.astype(F32), shape)
    down_col = across_row.T
    seen = (down_col == across_row) & (lane_index(shape) <= row_index(shape))
    visible = jnp.concatenate([seen, seen], axis=0)
    if frequency is None:
        return visible
    earlier = jnp.sum(jnp.where(across_row < down_col, 1.0, 0.0), axis=1, keepdims=True)
    angles = (row_index(shape).astype(F32) - earlier) * frequency
    sine = jnp.sin(angles)
    first = lane_index(shape) % HEAD_DIM < HEAD_DIM // 2
    return (visible, jnp.cos(angles), jnp.where(first, -sine, sine))


def attn_forward_kernel(spots, *refs):
    count = len(spots)
    rows_ref, tokens_ref, seg_row, frequency = refs[:4]
    pieces = refs[4 : 4 + count]
    query_ref, keyval_ref, mixed_ref, tail_ref, cos_ref, sin_ref, weights, sems = refs[4 + count :]
    copies = load_weights(rows_ref, spots, pieces, weights, sems)
    tokens = tokens_ref[...].astype(F32)
    inverse = lax.rsqrt(jnp.mean(tokens * tokens, axis=-1, keepdims=True) + EPS)
    normed = tokens * inverse
    width = tokens.shape[1]
    visible, cosine, sine = segment_tables(seg_row[...], frequency[...])
    cos_ref[...] = cosine
    sin_ref[...] = sine
    for copy in copies:
        copy.wait()
    tail = weights[:, 2 * width :]
    tail_ref[...] = tail
    gains = contract(gain_select().astype(F32).astype(LOW), tail, 1, 1)
    attn_in = (normed * gains[0:1]).astype(LOW)
    keyval = contract(attn_in, weights[:, width : 2 * width], 1, 0)
    query = contract(attn_in, weights[:, :width], 1, 0)
    half = width // 2
    for m in range(half // LANES):
        keys = keyval[:, m * LANES : (m + 1) * LANES]
        keys = (keys * cosine + half_turn(keys) * sine).astype(LOW)
        values = keyval[:, half + m * LANES : half + (m + 1) * LANES].astype(LOW)
        keyval_ref[:, m * LANES : (m + 1) * LANES] = keys
        keyval_ref[:, half + m * LANES : half + (m + 1) * LANES] = values
        for pick in range(2):
            k_both = both_heads(keys.astype(F32), pick).astype(LOW)
            v_both = both_heads(values.astype(F32), pick).astype(LOW)
            chunk = slice((2 * m + pick) * LANES, (2 * m + pick + 1) * LANES)
            queries = query[:, chunk]
            queries = (queries * cosine + half_turn(queries) * sine).astype(LOW)
            query_ref[:, chunk] = queries
            q_pair = split_heads(queries.astype(F32)).astype(LOW)
            probs = softmax_rows(q_pair, k_both, visible).astype(LOW)
            mixed_ref[:, chunk] = join_heads(contract(probs, v_both, 1, 0)).astype(LOW)


def router_kernel(spots, *refs):
    count = len(spots)
    rows_ref, tokens_ref, mixed_ref, tail_ref, routes_t = refs[:5]
    pieces = refs[5 : 5 + count]
    payload, hidden_ref, gates_ref, weights, sems = refs[5 + count :]
    copies = load_weights(rows_ref, spots, pieces, weights, sems)
    tokens = tokens_ref[...].astype(F32)
    length = tokens.shape[0]
    tail = tail_ref[...]
    gains = contract(gain_select().astype(F32).astype(LOW), tail, 1, 1)
    for copy in copies:
        copy.wait()
    hidden = tokens + contract(mixed_ref[...], weights[...], 1, 0)
    hidden_ref[...] = hidden
    inverse_two = lax.rsqrt(jnp.mean(hidden * hidden, axis=-1, keepdims=True) + EPS)
    moe_in = (hidden * inverse_two * gains[1:2]).astype(LOW)
    payload[:length] = moe_in
    logits = contract(moe_in, tail, 1, 0)
    turned = routes_t[...]
    experts = row_index((LANES, length))
    chosen = experts == turned[0:1]
    for k in range(1, TOP):
        chosen = chosen | (experts == turned[k : k + 1])
    chosen = jnp.where(chosen, 1.0, 0.0).T > 0.5
    logits = jnp.where(chosen, logits, MASKED)
    exps = jnp.where(chosen, jnp.exp(logits - jnp.max(logits, axis=-1, keepdims=True)), 0.0)
    gates = exps / jnp.sum(exps, axis=-1, keepdims=True)
    gates_ref[...] = gates
    gates_t = gates.T
    for k in range(TOP):
        row = turned[k : k + 1]
        gate = jnp.sum(jnp.where(experts == row, gates_t, 0.0), axis=0, keepdims=True)
        high, middle, rest = three_parts(gate)
        place = row_index((TAIL, length))
        block = jnp.where(place == 0, high, jnp.where(place == 1, middle, jnp.where(place == 2, rest, 0.0)))
        block = jnp.where(place == 3, row.astype(F32), block)
        payload[length:, k * length : (k + 1) * length] = block.astype(LOW)


def slot_places(first_expert, local, tails, before):
    length = tails[0].shape[1] // TOP
    ids = row_index((8, length))
    ids = jnp.where(ids < local, ids + first_expert, -1).astype(F32)
    masks, gates = [], []
    for tail in tails:
        mask = jnp.zeros((8, length), F32)
        gate = jnp.zeros((8, length), F32)
        for k in range(TOP):
            part = tail[:, k * length : (k + 1) * length].astype(F32)
            hit = part[3:4] == ids
            mask = jnp.where(hit, 1.0, mask)
            gate = jnp.where(hit, part[0:1] + part[1:2] + part[2:3], gate)
        masks.append(mask)
        gates.append(gate)
    pairs = range(0, len(tails), 2)
    mask = jnp.concatenate([jnp.concatenate(masks[i : i + 2], axis=1) for i in pairs], axis=0)
    gate = jnp.concatenate([jnp.concatenate(gates[i : i + 2], axis=1) for i in pairs], axis=0)
    place = contract(mask.astype(LOW), before, 1, 0)
    return (jnp.where(mask > 0, place, -1.0), gate)


def gather_pair(local, block, place, gate, row_pair, grad_pair, out):
    rows_out, grads_out, select_out, gate_out, pair = out
    slots = row_index((block, place.shape[1])).astype(F32)
    parts = []
    for j in range(local):
        hit = slots == place[8 * pair + j : 8 * pair + j + 1]
        parts.append(jnp.where(hit, 1.0, 0.0))
        held = jnp.where(hit, gate[8 * pair + j : 8 * pair + j + 1], 0.0)
        held = jnp.sum(held, axis=1, keepdims=True)
        gate_out[j, pair * block : (pair + 1) * block] = jnp.broadcast_to(held, (block, LANES))
    select = jnp.concatenate(parts, axis=0).astype(LOW)
    if select_out is not None:
        select_out[pair] = select
    rows = contract(select, jnp.concatenate(row_pair, axis=0), 1, 0).astype(LOW)
    grads = contract(select, jnp.concatenate(grad_pair, axis=0), 1, 0).astype(LOW)
    for j in range(local):
        rows_out[j, pair * block : (pair + 1) * block] = rows[j * block : (j + 1) * block]
        grads_out[j, pair * block : (pair + 1) * block] = grads[j * block : (j + 1) * block]


def earlier_matrix(length):
    shape = (2 * length, 2 * length)
    return jnp.where(row_index(shape) < lane_index(shape), 1.0, 0.0).astype(LOW)


def expert_step(j, rows, grads, gate_ref, up, down):
    hidden_units = down.shape[1]
    pair = contract(rows[j], up, 1, 0)
    raw = contract(grads[j], down, 1, 0)
    gate_half, up_half = pair[:, :hidden_units], pair[:, hidden_units:]
    gate = gate_ref[j][:, 0:1]
    sigmoid = 1.0 / (1.0 + jnp.exp(-gate_half))
    silu = gate_half * sigmoid
    activated = silu * up_half
    scaled = (gate * activated).astype(LOW)
    act_grad = gate * raw
    pair_grad = jnp.concatenate(
        [act_grad * up_half * sigmoid * (1.0 + gate_half * (1.0 - sigmoid)), act_grad * silu],
        axis=1,
    ).astype(LOW)
    gate_grad = jnp.sum(activated * raw, axis=1, keepdims=True)
    return (scaled, pair_grad, gate_grad)


def fetch_experts(local, up_hbm, down_hbm, up, down, sems):
    copies = []
    for j in range(local):
        copies.append(
            (
                pltpu.make_async_copy(up_hbm.at[j], up.at[j], sems.at[0, j]),
                pltpu.make_async_copy(down_hbm.at[j], down.at[j], sems.at[1, j]),
            )
        )
        for copy in copies[j]:
            copy.start()
    return copies


def expert_home_kernel(owners, local, block, *refs):
    place_ref = refs[0]
    rows_in = refs[1 : 1 + owners]
    grads_in = refs[1 + owners : 1 + 2 * owners]
    up_hbm, down_hbm = refs[1 + 2 * owners : 3 + 2 * owners]
    out_even, out_odd, back_even, back_odd, up_out, down_out = refs[3 + 2 * owners : 9 + 2 * owners]
    scratch = refs[9 + 2 * owners :]
    up, down, rows, grads, select, gate_ref, produced, returned, up_grad, down_grad, sems = scratch
    copies = fetch_experts(local, up_hbm, down_hbm, up, down, sems)
    length = rows_in[0].shape[0] - TAIL
    width = rows_in[0].shape[1]
    first_expert = place_ref[0] * local
    slab = up_grad.shape[1]
    columns = pl.ds(pl.multiple_of(place_ref[1] * slab, slab), slab)
    before = earlier_matrix(length)
    place, gate = slot_places(first_expert, local, [ref[length:] for ref in rows_in], before)
    for s in range(owners // 2):
        gather_pair(
            local,
            block,
            place,
            gate,
            [rows_in[2 * s][:length], rows_in[2 * s + 1][:length]],
            [grads_in[2 * s][...], grads_in[2 * s + 1][...]],
            (rows, grads, select, gate_ref, s),
        )
    for j in range(local):
        for copy in copies[j]:
            copy.wait()
    sent = []
    for j in range(local):
        scaled, pair_grad, gate_grad = expert_step(j, rows, grads, gate_ref, up[j], down[j])
        produced[j] = contract(scaled, down[j], 1, 1).astype(LOW)
        returned[j, :, :width] = contract(pair_grad, up[j], 1, 1).astype(LOW)
        lanes = lane_index((scaled.shape[0], LANES)) - first_expert - j
        high, middle, rest = three_parts(gate_grad)
        tail = jnp.where(lanes == 0, high, 0.0)
        tail = jnp.where(lanes == EXPERTS, middle, tail)
        tail = jnp.where(lanes == 2 * EXPERTS, rest, tail)
        returned[j, :, width:] = tail.astype(LOW)
        up_grad[j] = contract(rows[j, :, columns], pair_grad, 0, 0)
        down_grad[j] = contract(grads[j, :, columns], scaled, 0, 0)
        sent.append(pltpu.make_async_copy(up_grad.at[j], up_out.at[j], sems.at[2, j]))
        sent.append(pltpu.make_async_copy(down_grad.at[j], down_out.at[j], sems.at[3, j]))
        sent[-2].start()
        sent[-1].start()
    for s in range(owners // 2):
        span = slice(s * block, (s + 1) * block)
        made = jnp.concatenate([produced[j, span] for j in range(local)], axis=0)
        back = jnp.concatenate([returned[j, span] for j in range(local)], axis=0)
        made = contract(select[s], made, 0, 0).astype(LOW)
        back = contract(select[s], back, 0, 0).astype(LOW)
        out_even[s] = made[:length]
        out_odd[s] = made[length:]
        back_even[s] = back[:length]
        back_odd[s] = back[length:]
    for copy in sent:
        copy.wait()


def expert_away_kernel(start, count, block, chips, far, *refs):
    place_ref = refs[0]
    rows_in = refs[1 : 3 + 2 * chips]
    grads_in = refs[3 + 2 * chips : 3 + 4 * chips]
    up_hbm, down_hbm, up_first, down_first = refs[3 + 4 * chips : 7 + 4 * chips]
    up_grad, down_grad = refs[7 + 4 * chips : 9 + 4 * chips]
    scratch = refs[9 + 4 * chips :]
    up, down, up_sum, down_sum, rows_buf, grads_buf, rows, grads, gate_ref, sems, pair_sems = scratch
    length = grads_buf.shape[1] // 2
    tall = length + TAIL
    pairs = []
    for i in range(far + 1):
        for s in range(chips):
            spot = len(pairs)
            copies = []
            for side in range(2):
                skip = chips * length if s == 0 and side == 1 else 0
                grad_from = grads_in[2 * s + side].at[pl.ds(skip + i * length, length)]
                if i == 0:
                    row_from = rows_in[side].at[s]
                else:
                    row_from = rows_in[2 + 2 * s + side].at[pl.ds((i - 1) * tall, tall)]
                row_to = rows_buf.at[spot, pl.ds(side * tall, tall)]
                grad_to = grads_buf.at[spot, pl.ds(side * length, length)]
                copies.append(pltpu.make_async_copy(row_from, row_to, pair_sems.at[0, side, spot]))
                copies.append(pltpu.make_async_copy(grad_from, grad_to, pair_sems.at[1, side, spot]))
            pairs.append(copies)
    for copies in pairs:
        for copy in copies:
            copy.start()
    held = []
    for j in range(count):
        held.append(
            [
                pltpu.make_async_copy(up_hbm.at[start + j], up.at[j], sems.at[0, j]),
                pltpu.make_async_copy(down_hbm.at[start + j], down.at[j], sems.at[1, j]),
                pltpu.make_async_copy(up_first.at[start + j], up_sum.at[j], sems.at[2, j]),
                pltpu.make_async_copy(down_first.at[start + j], down_sum.at[j], sems.at[3, j]),
            ]
        )
    for copies in held:
        for copy in copies:
            copy.start()
    first_expert = place_ref[0] * (up_hbm.shape[0]) + start
    slab = up_sum.shape[1]
    columns = pl.ds(pl.multiple_of(place_ref[1] * slab, slab), slab)
    before = earlier_matrix(length)
    for copies in pairs:
        for copy in copies:
            copy.wait()
    tails = []
    for i in range(len(pairs)):
        tails += [rows_buf[i, length:tall], rows_buf[i, tall + length :]]
    place, gate = slot_places(first_expert, count, tails, before)
    for i in range(len(pairs)):
        gather_pair(
            count,
            block,
            place,
            gate,
            [rows_buf[i, :length], rows_buf[i, tall : tall + length]],
            [grads_buf[i]],
            (rows, grads, None, gate_ref, i),
        )
    for copies in held:
        for copy in copies:
            copy.wait()
    sent = []
    for j in range(count):
        scaled, pair_grad, _ = expert_step(j, rows, grads, gate_ref, up[j], down[j])
        up_sum[j] += contract(rows[j, :, columns], pair_grad, 0, 0)
        down_sum[j] += contract(grads[j, :, columns], scaled, 0, 0)
        sent.append(pltpu.make_async_copy(up_sum.at[j], up_grad.at[start + j], sems.at[4, j]))
        sent.append(pltpu.make_async_copy(down_sum.at[j], down_grad.at[start + j], sems.at[5, j]))
        sent[-2].start()
        sent[-1].start()
    for copy in sent:
        copy.wait()


def backward_kernel(spots, output_spots, shares, *refs):
    rows_ref, tokens_ref, seg_row, cos_ref, sin_ref, payload, hidden_ref = refs[:7]
    query_ref, keyval_ref, mixed_ref, gates_ref, out_grad_ref, tail_ref = refs[7:13]
    refs = refs[13:]
    back, refs = refs[:shares], refs[shares:]
    pieces, refs = refs[: len(spots)], refs[len(spots) :]
    output_pieces, refs = refs[: len(output_spots)], refs[len(output_spots) :]
    tokens_grad, grads_even, grads_odd = refs[:3]
    weights, output, sums, query_low, keyval_low, sems, output_sems, out_sems = refs[3:]
    output_copies = load_weights(rows_ref, output_spots, output_pieces, output, output_sems)
    copies = load_weights(rows_ref, spots, pieces, weights, sems)
    length, width = tokens_ref.shape
    half = width // 2
    columns = weights.shape[1]
    total = back[0][...].astype(F32)
    for share in back[1:]:
        total = total + share[...].astype(F32)
    parts = total[:, width:]
    lanes = lane_index(parts.shape)
    gate_grad = parts + pltpu.roll(parts, LANES - EXPERTS, 1) + pltpu.roll(parts, LANES - 2 * EXPERTS, 1)
    gate_grad = jnp.where(lanes < EXPERTS, gate_grad, 0.0)
    gates = gates_ref[...]
    logits_grad = gates * (gate_grad - jnp.sum(gates * gate_grad, axis=-1, keepdims=True))
    hidden = hidden_ref[...]
    inverse_two = lax.rsqrt(jnp.mean(hidden * hidden, axis=-1, keepdims=True) + EPS)
    normed_two = hidden * inverse_two
    tail = tail_ref[...]
    gains = contract(gain_select().astype(F32).astype(LOW), tail, 1, 1)
    high = logits_grad.astype(LOW)
    rest = (logits_grad - high.astype(F32)).astype(LOW)
    moe_grad = total[:, :width] + contract(high, tail, 1, 1) + contract(rest, tail, 1, 1)
    moe_gain_grad = jnp.sum(moe_grad * normed_two, axis=0, keepdims=True)
    scaled = moe_grad * gains[1:2]
    hidden_grad = out_grad_ref[...].astype(F32) + inverse_two * (
        scaled - normed_two * jnp.mean(scaled * normed_two, axis=-1, keepdims=True)
    )
    attn_out_grad = hidden_grad.astype(LOW)
    for copy in output_copies:
        copy.wait()
    mixed_grad = contract(attn_out_grad, output[...], 1, 1)
    sums[:, columns:] = contract(mixed_ref[...], attn_out_grad, 0, 0).astype(LOW)
    tokens = tokens_ref[...].astype(F32)
    inverse_one = lax.rsqrt(jnp.mean(tokens * tokens, axis=-1, keepdims=True) + EPS)
    normed_one = tokens * inverse_one
    cosine, sine = cos_ref[...], sin_ref[...]
    visible = segment_tables(seg_row[...], None)
    for m in range(half // LANES):
        keys = keyval_ref[:, m * LANES : (m + 1) * LANES].astype(F32)
        values = keyval_ref[:, half + m * LANES : half + (m + 1) * LANES].astype(F32)
        key_sides, value_sides = [], []
        for pick in range(2):
            k_both = both_heads(keys, pick).astype(LOW)
            v_both = both_heads(values, pick).astype(LOW)
            chunk = slice((2 * m + pick) * LANES, (2 * m + pick + 1) * LANES)
            q_pair = split_heads(query_ref[:, chunk].astype(F32)).astype(LOW)
            m_pair = split_heads(mixed_grad[:, chunk]).astype(LOW)
            probs = softmax_rows(q_pair, k_both, visible)
            probs_grad = contract(m_pair, v_both, 1, 1)
            value_sides.append(contract(probs.astype(LOW), m_pair, 0, 0))
            scores_grad = (
                probs
                * (probs_grad - jnp.sum(probs * probs_grad, axis=-1, keepdims=True))
                * (HEAD_DIM ** (-0.5))
            ).astype(LOW)
            query_grad = join_heads(contract(scores_grad, k_both, 1, 0))
            query_low[:, chunk] = (query_grad * cosine - half_turn(query_grad) * sine).astype(LOW)
            key_sides.append(contract(scores_grad, q_pair, 0, 0))
        first = lane_index((length, LANES)) < HEAD_DIM
        key_sides = [side + pltpu.roll(side, HEAD_DIM, 1) for side in key_sides]
        value_sides = [side + pltpu.roll(side, HEAD_DIM, 1) for side in value_sides]
        keys_grad = jnp.where(first, key_sides[0], key_sides[1])
        values_grad = jnp.where(first, value_sides[0], value_sides[1])
        keyval_low[:, m * LANES : (m + 1) * LANES] = (
            keys_grad * cosine - half_turn(keys_grad) * sine
        ).astype(LOW)
        keyval_low[:, half + m * LANES : half + (m + 1) * LANES] = values_grad.astype(LOW)
    for copy in copies:
        copy.wait()
    attn_in_grad = contract(query_low[...], weights[:, :width], 1, 1) + contract(
        keyval_low[...], weights[:, width : 2 * width], 1, 1
    )
    attn_in = (normed_one * gains[0:1]).astype(LOW)
    sums[:, :width] = contract(attn_in, query_low[...], 0, 0).astype(LOW)
    sums[:, width : 2 * width] = contract(attn_in, keyval_low[...], 0, 0).astype(LOW)
    attn_gain_grad = jnp.sum(attn_in_grad * normed_one, axis=0, keepdims=True)
    place = row_index((8, width))
    gain_grads = jnp.where(place == 0, attn_gain_grad, jnp.where(place == 1, moe_gain_grad, 0.0))
    sums[:, 2 * width : columns] = (
        contract(payload[:length], high, 0, 0)
        + contract(gain_grads.astype(LOW), gain_select().astype(F32).astype(LOW), 0, 0)
    ).astype(LOW)
    out_copies = store_sums(rows_ref, sums, grads_even, grads_odd, out_sems)
    scaled = attn_in_grad * gains[0:1]
    tokens_grad[...] = hidden_grad + inverse_one * (
        scaled - normed_one * jnp.mean(scaled * normed_one, axis=-1, keepdims=True)
    )
    for copy in out_copies:
        copy.wait()


def swap(values, axis, size, distance):
    return lax.ppermute(values, axis, [(i, i ^ distance) for i in range(size)])


def across(values, distance, planes):
    return swap(values, "dp", planes, distance)


def aside(values, s, owners):
    return swap(values, "expert", owners, 2 * s)


def partner(values, owners):
    return swap(values, "expert", owners, 1)


def after(values, *earlier):
    return lax.optimization_barrier((values,) + earlier)[0]


def over_chips(values, owners):
    return [values] + [aside(values, s, owners) for s in range(1, owners // 2)]


def over_cores(near, owners, *earlier):
    pieces = []
    for piece in near:
        pieces += [piece, partner(after(piece, *earlier) if earlier else piece, owners)]
    return pieces


def chips_split(values, owners, *earlier):
    half = values.shape[0] // 2
    first, second = aside(values, 1, owners), aside(values, 2, owners)
    far = [first[:half], second[half:]]
    if earlier:
        far = [after(part, *earlier) for part in far]
    far = [aside(far[0], 2, owners), aside(far[1], 1, owners)]
    return [[values], [first], [second], far]


def core_pieces(near, owners):
    pieces, spots = [], []
    for s, parts in enumerate(near):
        first = 0
        for part in parts:
            pieces += [part, partner(part, owners)]
            spots += [(2 * s, first), (2 * s + 1, first)]
            first += part.shape[0]
    return (pieces, spots)


def core_pieces_whole(near, owners):
    pieces = []
    for parts in near:
        piece = parts[0] if len(parts) == 1 else jnp.concatenate(parts, axis=0)
        pieces.append((piece, partner(piece, owners)))
    return pieces


def added(left, right):
    return (left.astype(F32) + right.astype(F32)).astype(LOW)


def to_owners(even, odd, owners, *earlier):
    other = partner(odd, owners)
    joined = [added(even[s], other[s]) for s in range(owners // 2)]
    if earlier:
        joined = lax.optimization_barrier(tuple(joined) + earlier)[: owners // 2]
    sent = [joined[0]] + [aside(joined[s], s, owners) for s in range(1, owners // 2)]
    return (joined, sent)


def to_neighbours(joined, owners):
    half = joined[3].shape[0] // 2
    low_turn = aside(joined[3][:half], 1, owners)
    top_turn = aside(joined[3][half:], 2, owners)
    low_turn, top_turn = lax.optimization_barrier((low_turn, top_turn))
    first = jnp.concatenate([joined[1][:half], added(joined[1][half:], top_turn)], axis=0)
    second = jnp.concatenate([added(joined[2][:half], low_turn), joined[2][half:]], axis=0)
    return (first, second)


def from_neighbours(joined, first, second, owners):
    parts = [joined[0], aside(first, 1, owners), aside(second, 2, owners)]
    return sum(part.astype(F32) for part in parts).astype(LOW)


def over_planes_sum(parts, planes):
    total = parts[0].astype(F32)
    for w in range(1, planes):
        total = total + across(parts[w], w, planes).astype(F32)
    return total


def cost(us):
    return pl.CostEstimate(flops=int(us * 1153e6), bytes_accessed=0, transcendentals=0)


def params():
    return pltpu.CompilerParams(vmem_limit_bytes=VMEM_BYTES)


def whole_spec():
    return pl.BlockSpec(memory_space=pltpu.VMEM)


def hbm_spec():
    return pl.BlockSpec(memory_space=pl.ANY)


def smem_spec():
    return pl.BlockSpec(memory_space=pltpu.SMEM)


def on_device(
    planes,
    owners,
    tokens,
    segments,
    routes,
    query_weight,
    keyval_weight,
    output_weight,
    router_weight,
    attn_gain,
    moe_gain,
    expert_up,
    expert_down,
    out_grad,
):
    length, width = tokens.shape
    if planes != 4 or owners != 8 or planes * owners * length > PIECE_LIMIT:
        return on_device_wide(
            tokens,
            segments,
            routes,
            query_weight,
            keyval_weight,
            output_weight,
            router_weight,
            attn_gain,
            moe_gain,
            expert_up,
            expert_down,
            out_grad,
        )
    local = expert_up.shape[0]
    hidden_units = expert_down.shape[2]
    block = 2 * CAP
    slots = owners // 2 * block
    plane = lax.axis_index("dp")
    owner = lax.axis_index("expert")
    share = query_weight.shape[0]
    rows = (plane ^ jnp.arange(planes))[None, :] * owners + (owner ^ jnp.arange(owners))[:, None]
    rows = rows.astype(jnp.int32)
    place = jnp.stack([owner, plane]).astype(jnp.int32)
    extra = jnp.concatenate(
        [
            router_weight,
            attn_gain[:, None],
            moe_gain[:, None],
            jnp.zeros((share, LANES - EXPERTS - 2), LOW),
        ],
        axis=1,
    )
    packed = jnp.concatenate([query_weight, keyval_weight, extra, output_weight], axis=1)
    columns = packed.shape[1] - width

    early = [across(packed, w, planes) for w in range(1, planes)]
    grad_chips = over_chips(out_grad, owners)
    gathered = jnp.stack([packed] + early)
    grad_start = after(out_grad, *early)
    grad_planes = [across(grad_start, w, planes) for w in range(1, planes)]
    near = chips_split(
        after(gathered[:, :, :columns], *grad_chips), owners, grad_planes[0]
    )
    pieces, spots = core_pieces(near, owners)
    output_near = over_chips(after(gathered[:, :, columns:], *pieces[:6], *near[3]), owners)

    half_dim = HEAD_DIM // 2
    frequency = ROPE_BASE ** (-(jnp.arange(half_dim, dtype=F32) * 2.0) / HEAD_DIM)
    frequency = jnp.tile(frequency, LANES // half_dim)[None, :]

    token_low = jax.ShapeDtypeStruct((length, width), LOW)
    token_wide = jax.ShapeDtypeStruct((length, width), F32)
    table = jax.ShapeDtypeStruct((length, LANES), F32)
    query_rot, keyval_low, mixed_low, tail, cosine, sine = pl.pallas_call(
        functools.partial(attn_forward_kernel, spots),
        out_shape=(token_low, token_low, token_low, jax.ShapeDtypeStruct((width, LANES), LOW))
        + (table, table),
        in_specs=[smem_spec()] + [whole_spec()] * 3 + [hbm_spec()] * len(pieces),
        out_specs=[whole_spec()] * 6,
        scratch_shapes=[
            pltpu.VMEM((width, columns), LOW),
            pltpu.SemaphoreType.DMA((owners, planes)),
        ],
        compiler_params=params(),
        cost_estimate=cost(6),
        name="attn_forward",
    )(rows, after(tokens, *grad_planes[1:]), segments, frequency, *pieces)

    output_pieces = over_cores(output_near, owners, mixed_low)
    output_spots = [(p, 0) for p in range(owners)]

    grad_stack = jnp.concatenate(grad_planes, axis=0)

    payload, hidden, gates = pl.pallas_call(
        functools.partial(router_kernel, output_spots),
        out_shape=(
            jax.ShapeDtypeStruct((length + TAIL, width), LOW),
            token_wide,
            jax.ShapeDtypeStruct((length, LANES), F32),
        ),
        in_specs=[smem_spec()] + [whole_spec()] * 4 + [hbm_spec()] * len(output_pieces),
        out_specs=[whole_spec()] * 3,
        scratch_shapes=[
            pltpu.VMEM((width, width), LOW),
            pltpu.SemaphoreType.DMA((owners, planes)),
        ],
        compiler_params=params(),
        cost_estimate=cost(4),
        name="router",
    )(
        rows,
        tokens,
        mixed_low,
        tail,
        routes.T,
        *output_pieces,
    )

    row_chips = over_chips(payload, owners)
    row_home = over_cores(row_chips, owners)
    grad_other = partner(
        after(jnp.concatenate(grad_chips + [grad_stack], axis=0), payload), owners
    )
    row_start = after(payload, row_home[1])
    row_planes = [across(row_start, w, planes) for w in range(2, planes)]
    row_near = across(jnp.stack(row_chips), 1, planes)
    grad_direct = after(grad_stack, *row_chips)
    grad_near = [aside(grad_direct, s, owners) for s in (1, 2)]

    def all_of(shape):
        return pl.BlockSpec(shape, lambda i: (0,) * len(shape))

    slab = width // planes
    slabs = (
        jax.ShapeDtypeStruct((local, slab, 2 * hidden_units), F32),
        jax.ShapeDtypeStruct((local, slab, hidden_units), F32),
    )
    home_blocks = [s * (p % 2) for s in range(owners // 2) for p in range(2)]
    grad_home = [part for s in range(owners // 2) for part in (grad_chips[s], grad_other)]
    out_even, out_odd, back_even, back_odd, up_grad, down_grad = pl.pallas_call(
        functools.partial(expert_home_kernel, owners, local, block),
        grid=(1,),
        out_shape=(
            jax.ShapeDtypeStruct((owners // 2, length, width), LOW),
            jax.ShapeDtypeStruct((owners // 2, length, width), LOW),
            jax.ShapeDtypeStruct((owners // 2, length, width + LANES), LOW),
            jax.ShapeDtypeStruct((owners // 2, length, width + LANES), LOW),
        )
        + slabs,
        in_specs=[smem_spec()]
        + [all_of((length + TAIL, width))] * owners
        + [pl.BlockSpec((length, width), lambda i, s=s: (s, 0)) for s in home_blocks]
        + [hbm_spec()] * 2,
        out_specs=[all_of((owners // 2, length, width))] * 2
        + [all_of((owners // 2, length, width + LANES))] * 2
        + [hbm_spec()] * 2,
        scratch_shapes=[
            pltpu.VMEM(expert_up.shape, LOW),
            pltpu.VMEM(expert_down.shape, LOW),
            pltpu.VMEM((local, slots, width), LOW),
            pltpu.VMEM((local, slots, width), LOW),
            pltpu.VMEM((owners // 2, local * block, 2 * length), LOW),
            pltpu.VMEM((local, slots, LANES), F32),
            pltpu.VMEM((local, slots, width), LOW),
            pltpu.VMEM((local, slots, width + LANES), LOW),
            pltpu.VMEM(slabs[0].shape, F32),
            pltpu.VMEM(slabs[1].shape, F32),
            pltpu.SemaphoreType.DMA((4, local)),
        ],
        compiler_params=params(),
        cost_estimate=cost(22),
        name="expert_home",
    )(place, *row_home, *grad_home, expert_up, expert_down)

    joined, back = to_owners(back_even, after(back_odd, *grad_near, *row_planes), owners)
    row_stack = jnp.concatenate(row_planes, axis=0)
    row_far = chips_split(after(row_stack, *back), owners)
    grad_away = [grad_stack, grad_other]
    grad_away += over_cores(grad_near, owners, *back)
    row_own = partner(after(row_stack, *joined), owners)
    row_away = over_cores([row_near], owners) + [row_stack, row_own]
    row_away += over_cores([jnp.concatenate(parts, axis=0) for parts in row_far[1:]], owners)

    def expert_away(start, count, place, up_grad, down_grad):
        chips = owners // 2
        pairs = chips * (planes - 1)
        return pl.pallas_call(
            functools.partial(
                expert_away_kernel, start, count, block, chips, planes - 2
            ),
            out_shape=slabs,
            in_specs=[smem_spec()] + [hbm_spec()] * (6 + 4 * chips),
            out_specs=[hbm_spec()] * 2,
            scratch_shapes=[
                pltpu.VMEM((count,) + expert_up.shape[1:], LOW),
                pltpu.VMEM((count,) + expert_down.shape[1:], LOW),
                pltpu.VMEM((count,) + slabs[0].shape[1:], F32),
                pltpu.VMEM((count,) + slabs[1].shape[1:], F32),
                pltpu.VMEM((pairs, 2 * (length + TAIL), width), LOW),
                pltpu.VMEM((pairs, 2 * length, width), LOW),
                pltpu.VMEM((count, pairs * block, width), LOW),
                pltpu.VMEM((count, pairs * block, width), LOW),
                pltpu.VMEM((count, pairs * block, LANES), F32),
                pltpu.SemaphoreType.DMA((6, count)),
                pltpu.SemaphoreType.DMA((2, 2, pairs)),
            ],
            input_output_aliases={5 + 4 * chips: 0, 6 + 4 * chips: 1},
            compiler_params=params(),
            cost_estimate=cost(7 * count),
            name="expert_away",
        )(place, *row_away, *grad_away, expert_up, expert_down, up_grad, down_grad)

    def share_pieces(wide):
        return jax.ShapeDtypeStruct((owners // 2, planes, share, wide), LOW)

    wide = columns + width
    tokens_grad, grads_even, grads_odd = pl.pallas_call(
        functools.partial(backward_kernel, spots, output_spots, owners // 2),
        out_shape=(token_wide, share_pieces(wide), share_pieces(wide)),
        in_specs=[smem_spec()]
        + [whole_spec()] * (12 + owners // 2)
        + [hbm_spec()] * (len(pieces) + len(output_pieces)),
        out_specs=[whole_spec()] + [hbm_spec()] * 2,
        scratch_shapes=[
            pltpu.VMEM((width, columns), LOW),
            pltpu.VMEM((width, width), LOW),
            pltpu.VMEM((width, wide), LOW),
            pltpu.VMEM((length, width), LOW),
            pltpu.VMEM((length, width), LOW),
            pltpu.SemaphoreType.DMA((owners, planes)),
            pltpu.SemaphoreType.DMA((owners, planes)),
            pltpu.SemaphoreType.DMA((owners, planes)),
        ],
        compiler_params=params(),
        cost_estimate=cost(17),
        name="backward",
    )(
        rows,
        tokens,
        segments,
        cosine,
        sine,
        payload,
        after(hidden, row_own),
        query_rot,
        keyval_low,
        mixed_low,
        gates,
        out_grad,
        tail,
        *back,
        *pieces,
        *output_pieces,
    )

    grads_other = partner(
        after(grads_odd, row_near, row_far[1][0], row_far[2][0], *grad_away[3::2]), owners
    )
    half = grad_stack.shape[0] // 2
    grad_turn = [
        aside(after(grad_near[0][:half], tokens_grad), 2, owners),
        aside(after(grad_near[1][half:], tokens_grad), 1, owners),
    ]
    grad_away += over_cores([jnp.concatenate(grad_turn, axis=0)], owners)
    shares = [added(grads_even[s], grads_other[s]) for s in range(owners // 2)]
    shares[3] = after(shares[3], *row_far[3], *grad_turn)
    first, second = to_neighbours(shares, owners)
    out_other = partner(after(out_odd, shares[0]), owners)
    made = [added(out_even[s], out_other[s]) for s in range(owners // 2)]
    held = (first, second) + tuple(row_away[1::2]) + tuple(grad_away[7:]) + tuple(made)
    first, second = lax.optimization_barrier(held)[:2]
    far_made = aside(after(made[3], first), 3, owners)
    up_grad, down_grad = expert_away(0, 2, after(place, first, second), up_grad, down_grad)
    plane_sums = after(from_neighbours(shares, first, second, owners), up_grad, far_made)
    up_grad, down_grad = expert_away(2, 2, after(place, plane_sums), up_grad, down_grad)
    made = lax.optimization_barrier(tuple(made) + (plane_sums,))[: owners // 2]
    near_made = [aside(made[s], s, owners) for s in (1, 2)]
    summed = over_planes_sum(plane_sums, planes)
    made = [made[0]] + near_made + [far_made]
    layer_out = (hidden + sum(part.astype(F32) for part in made)).astype(LOW)

    return (
        layer_out,
        tokens_grad,
        summed[:, :width],
        summed[:, width : 2 * width],
        summed[:, columns:],
        summed[:, 2 * width : 2 * width + EXPERTS],
        summed[:, 2 * width + EXPERTS],
        summed[:, 2 * width + EXPERTS + 1],
        up_grad,
        down_grad,
    )


def solution(mesh):
    return jax.shard_map(
        functools.partial(on_device, mesh.shape["dp"], mesh.shape["expert"]),
        mesh=mesh,
        in_specs=(
            P(("dp", "expert"), None),
            P(("dp", "expert"), None),
            P(("dp", "expert"), None),
            P(("dp", "expert"), None),
            P(("dp", "expert"), None),
            P(("dp", "expert"), None),
            P(("dp", "expert"), None),
            P(("dp", "expert")),
            P(("dp", "expert")),
            P("expert", None, None),
            P("expert", None, None),
            P(("dp", "expert"), None),
        ),
        out_specs=(
            P(("dp", "expert"), None),
            P(("dp", "expert"), None),
            P(("dp", "expert"), None),
            P(("dp", "expert"), None),
            P(("dp", "expert"), None),
            P(("dp", "expert"), None),
            P(("dp", "expert")),
            P(("dp", "expert")),
            P("expert", "dp", None),
            P("expert", "dp", None),
        ),
        check_vma=False,
    )
```

```python
import functools

import jax
import jax.numpy as jnp
from jax import lax
from jax.sharding import PartitionSpec as P
from jax.experimental import pallas as pl
from jax.experimental.pallas import tpu as pltpu

HEAD_DIM = 64
FF = 512
EXPERTS = 32
TOP = 8
CAP = 40


EPS = 1e-05
ROPE_BASE = 10000.0
MASKED = -1e30
HIGH = lax.Precision.HIGHEST


def norm_forward(values, gain_vec):
    inverse = lax.rsqrt(jnp.mean(values * values, axis=-1, keepdims=True) + EPS)
    normed = values * inverse
    return (normed, inverse, (normed * gain_vec).astype(jnp.bfloat16))


def norm_backward(grad_out, normed, inverse, gain_vec):
    gain_grad = jnp.sum(grad_out * normed, axis=0)
    scaled = grad_out * gain_vec
    grad_in = inverse * (scaled - normed * jnp.mean(scaled * normed, axis=-1, keepdims=True))
    return (grad_in, gain_grad)


def rope_tables(segment_row):
    length = segment_row.shape[0]
    earlier = jnp.sum((segment_row[None, :] < segment_row[:, None]).astype(jnp.int32), axis=1)
    position = jnp.arange(length, dtype=jnp.int32) - earlier
    half_dim = HEAD_DIM // 2
    frequency = ROPE_BASE ** (-(jnp.arange(half_dim, dtype=jnp.float32) * 2.0) / HEAD_DIM)
    angles = position.astype(jnp.float32)[:, None] * frequency[None, :]
    cosine = jnp.concatenate([jnp.cos(angles), jnp.cos(angles)], axis=-1)[:, None, :]
    sine_table = jnp.concatenate([jnp.sin(angles), jnp.sin(angles)], axis=-1)[:, None, :]
    return (cosine, sine_table)


def rotate(values, cosine, sine_table):
    half_dim = values.shape[-1] // 2
    turned = jnp.concatenate([-values[..., half_dim:], values[..., :half_dim]], axis=-1)
    return values * cosine + turned * sine_table


def unrotate(grad_rows, cosine, sine_table):
    half_dim = grad_rows.shape[-1] // 2
    weighted = grad_rows * sine_table
    turned = jnp.concatenate([weighted[..., half_dim:], -weighted[..., :half_dim]], axis=-1)
    return grad_rows * cosine + turned


def on_device_wide(
    tokens,
    segments,
    routes,
    query_weight,
    keyval_weight,
    output_weight,
    router_weight,
    attn_gain,
    moe_gain,
    expert_up,
    expert_down,
    out_grad,
):
    owners = lax.axis_size("expert")
    local_experts = expert_up.shape[0]
    length = tokens.shape[0]
    model_width = tokens.shape[1]
    kv_heads = keyval_weight.shape[1] // (2 * HEAD_DIM)
    query_heads = query_weight.shape[1] // HEAD_DIM
    repeat = query_heads // kv_heads
    score_scale = HEAD_DIM ** (-0.5)
    query_full, keyval_full, output_full, router_full, attn_gains, moe_gains = (
        lax.all_gather(query_weight, ("dp", "expert"), axis=0, tiled=True),
        lax.all_gather(keyval_weight, ("dp", "expert"), axis=0, tiled=True),
        lax.all_gather(output_weight, ("dp", "expert"), axis=0, tiled=True),
        lax.all_gather(router_weight, ("dp", "expert"), axis=0, tiled=True),
        lax.all_gather(attn_gain, ("dp", "expert"), axis=0, tiled=True),
        lax.all_gather(moe_gain, ("dp", "expert"), axis=0, tiled=True),
    )
    resident = tokens.astype(jnp.float32)
    normed_one, inverse_one, attn_in = norm_forward(resident, attn_gains.astype(jnp.float32))
    query_proj = jnp.dot(attn_in, query_full, preferred_element_type=jnp.float32).reshape(
        length, query_heads, HEAD_DIM
    )
    keyval_proj = jnp.dot(attn_in, keyval_full, preferred_element_type=jnp.float32)
    key_rows = keyval_proj[:, : kv_heads * HEAD_DIM].reshape(length, kv_heads, HEAD_DIM)
    value_rows = keyval_proj[:, kv_heads * HEAD_DIM :].reshape(length, kv_heads, HEAD_DIM)
    cosine, sine_table = rope_tables(segments[0])
    query_rot = (
        rotate(query_proj, cosine, sine_table)
        .astype(jnp.bfloat16)
        .reshape(length, kv_heads, repeat, HEAD_DIM)
    )
    keys_rot = rotate(key_rows, cosine, sine_table).astype(jnp.bfloat16)
    values_low = value_rows.astype(jnp.bfloat16)
    places = jnp.arange(length)
    visible = (segments[0][:, None] == segments[0][None, :]) & (places[None, :] <= places[:, None])
    scores = jnp.einsum("ikrd,jkd->krij", query_rot, keys_rot, preferred_element_type=jnp.float32)
    attn_logits = jnp.where(visible, scores * score_scale, MASKED)
    attn_exps = jnp.exp(attn_logits - jnp.max(attn_logits, axis=-1, keepdims=True))
    attn_probs = attn_exps / jnp.sum(attn_exps, axis=-1, keepdims=True)
    probs_low = attn_probs.astype(jnp.bfloat16)
    mixed_heads = jnp.einsum(
        "krij,jkd->ikrd", probs_low, values_low, preferred_element_type=jnp.float32
    )
    mixed_low = mixed_heads.reshape(length, query_heads * HEAD_DIM).astype(jnp.bfloat16)
    hidden = resident + jnp.dot(mixed_low, output_full, preferred_element_type=jnp.float32)
    normed_two, inverse_two, moe_in = norm_forward(hidden, moe_gains.astype(jnp.float32))
    router_logits = jnp.dot(moe_in, router_full, preferred_element_type=jnp.float32)
    choose = (routes[:, :, None] == jnp.arange(EXPERTS, dtype=jnp.int32)[None, None, :]).astype(
        jnp.float32
    )
    chosen = jnp.sum(choose * router_logits[:, None, :], axis=-1)
    gate_exps = jnp.exp(chosen - jnp.max(chosen, axis=-1, keepdims=True))
    gate_probs = gate_exps / jnp.sum(gate_exps, axis=-1, keepdims=True)
    entries = routes.reshape(-1)
    entry_count = entries.shape[0]
    onehot = (entries[:, None] == jnp.arange(EXPERTS, dtype=jnp.int32)[None, :]).astype(jnp.int32)
    position = jnp.sum((jnp.cumsum(onehot, axis=0) - 1) * onehot, axis=1)
    slot_index = entries * CAP + position
    owner_entry = (
        jnp.full((EXPERTS * CAP,), entry_count, jnp.int32)
        .at[slot_index]
        .set(jnp.arange(entry_count, dtype=jnp.int32))
    )
    padded_in = jnp.concatenate([moe_in, jnp.zeros((1, model_width), jnp.bfloat16)], axis=0)
    send_rows = jnp.take(padded_in, owner_entry // TOP, axis=0).reshape(EXPERTS, CAP, model_width)
    received = lax.all_to_all(send_rows, "expert", split_axis=0, concat_axis=0, tiled=True)
    slots_now = received.shape[1]
    grouped = received.reshape(owners, local_experts, slots_now, model_width)
    pair_proj = jnp.einsum("secd,edf->secf", grouped, expert_up, preferred_element_type=jnp.float32)
    activated = (jax.nn.silu(pair_proj[..., :FF]) * pair_proj[..., FF:]).astype(jnp.bfloat16)
    produced = jnp.einsum(
        "secf,edf->secd", activated, expert_down, preferred_element_type=jnp.float32
    ).astype(jnp.bfloat16)
    returned = lax.all_to_all(
        produced.reshape(EXPERTS, slots_now, model_width),
        "expert",
        split_axis=0,
        concat_axis=0,
        tiled=True,
    )
    returned, kept_rows, kept_pair = (
        returned,
        received,
        pair_proj.reshape(EXPERTS, slots_now, 2 * FF),
    )
    gathered = (
        jnp.take(returned.reshape(EXPERTS * CAP, model_width), slot_index, axis=0)
        .astype(jnp.float32)
        .reshape(length, TOP, model_width)
    )
    layer_out = (hidden + jnp.sum(gate_probs[:, :, None] * gathered, axis=1)).astype(jnp.bfloat16)
    grad_top = out_grad.astype(jnp.float32)
    gate_grad = jnp.sum(gathered * grad_top[:, None, :], axis=-1)
    chosen_grad = gate_probs * (gate_grad - jnp.sum(gate_probs * gate_grad, axis=-1, keepdims=True))
    logits_grad = jnp.sum(chosen_grad[:, :, None] * choose, axis=1)
    row_grads = (
        (gate_probs[:, :, None] * grad_top[:, None, :])
        .astype(jnp.bfloat16)
        .reshape(entry_count, model_width)
    )
    padded_grads = jnp.concatenate([row_grads, jnp.zeros((1, model_width), jnp.bfloat16)], axis=0)
    send_grads = jnp.take(padded_grads, owner_entry, axis=0).reshape(EXPERTS, CAP, model_width)
    grads_in = lax.all_to_all(send_grads, "expert", split_axis=0, concat_axis=0, tiled=True)
    grouped_rows = kept_rows.reshape(owners, local_experts, CAP, model_width)
    grouped_grads = grads_in.reshape(owners, local_experts, CAP, model_width)
    pair_kept = kept_pair.reshape(owners, local_experts, CAP, 2 * FF)
    gate_half = pair_kept[..., :FF]
    up_half = pair_kept[..., FF:]
    sigmoid_gate = jax.nn.sigmoid(gate_half)
    silu_gate = jax.nn.silu(gate_half)
    activated = (silu_gate * up_half).astype(jnp.bfloat16)
    act_grad = jnp.einsum(
        "secd,edf->secf", grouped_grads, expert_down, preferred_element_type=jnp.float32
    )
    pair_grad = jnp.concatenate(
        [
            act_grad * up_half * sigmoid_gate * (1.0 + gate_half * (1.0 - sigmoid_gate)),
            act_grad * silu_gate,
        ],
        axis=-1,
    ).astype(jnp.bfloat16)
    rows_back = jnp.einsum(
        "secf,edf->secd", pair_grad, expert_up, preferred_element_type=jnp.float32
    ).astype(jnp.bfloat16)
    up_grad = jnp.einsum(
        "secd,secf->edf", grouped_rows, pair_grad, preferred_element_type=jnp.float32
    )
    down_grad = jnp.einsum(
        "secd,secf->edf", grouped_grads, activated, preferred_element_type=jnp.float32
    )
    returned_grads = lax.all_to_all(
        rows_back.reshape(EXPERTS, CAP, model_width),
        "expert",
        split_axis=0,
        concat_axis=0,
        tiled=True,
    )
    expert_up_grad, expert_down_grad = (
        lax.psum_scatter(
            up_grad.astype(jnp.bfloat16), "dp", scatter_dimension=1, tiled=True
        ).astype(jnp.float32),
        lax.psum_scatter(
            down_grad.astype(jnp.bfloat16), "dp", scatter_dimension=1, tiled=True
        ).astype(jnp.float32),
    )
    token_grads = (
        jnp.take(returned_grads.reshape(EXPERTS * CAP, model_width), slot_index, axis=0)
        .astype(jnp.float32)
        .reshape(length, TOP, model_width)
    )
    router_wide = router_full.astype(jnp.float32)
    moe_grad = jnp.sum(token_grads, axis=1) + jnp.dot(logits_grad, router_wide.T, precision=HIGH)
    hidden_norm_grad, moe_gain_grad = norm_backward(
        moe_grad, normed_two, inverse_two, moe_gains.astype(jnp.float32)
    )
    hidden_grad = grad_top + hidden_norm_grad
    attn_out_grad = hidden_grad.astype(jnp.bfloat16)
    mixed_grad = (
        jnp.einsum("td,cd->tc", attn_out_grad, output_full, preferred_element_type=jnp.float32)
        .astype(jnp.bfloat16)
        .reshape(length, kv_heads, repeat, HEAD_DIM)
    )
    probs_grad = jnp.einsum(
        "ikrd,jkd->krij", mixed_grad, values_low, preferred_element_type=jnp.float32
    )
    values_grad = jnp.einsum(
        "krij,ikrd->jkd", probs_low, mixed_grad, preferred_element_type=jnp.float32
    )
    scores_grad = (
        attn_probs
        * (probs_grad - jnp.sum(attn_probs * probs_grad, axis=-1, keepdims=True))
        * score_scale
    ).astype(jnp.bfloat16)
    query_rot_grad = jnp.einsum(
        "krij,jkd->ikrd", scores_grad, keys_rot, preferred_element_type=jnp.float32
    ).reshape(length, query_heads, HEAD_DIM)
    keys_rot_grad = jnp.einsum(
        "krij,ikrd->jkd", scores_grad, query_rot, preferred_element_type=jnp.float32
    )
    query_low = (
        unrotate(query_rot_grad, cosine, sine_table)
        .reshape(length, query_heads * HEAD_DIM)
        .astype(jnp.bfloat16)
    )
    keyval_low = jnp.concatenate(
        [
            unrotate(keys_rot_grad, cosine, sine_table).reshape(length, kv_heads * HEAD_DIM),
            values_grad.reshape(length, kv_heads * HEAD_DIM),
        ],
        axis=1,
    ).astype(jnp.bfloat16)
    attn_in_grad = jnp.einsum(
        "tc,dc->td", query_low, query_full, preferred_element_type=jnp.float32
    ) + jnp.einsum("tc,dc->td", keyval_low, keyval_full, preferred_element_type=jnp.float32)
    token_norm_grad, attn_gain_grad = norm_backward(
        attn_in_grad, normed_one, inverse_one, attn_gains.astype(jnp.float32)
    )
    tokens_grad = hidden_grad + token_norm_grad
    slab_count = lax.axis_size("dp")
    slab_index = lax.axis_index("dp")
    width_rows = model_width // slab_count
    head_rows = query_heads * HEAD_DIM // slab_count
    all_attn, all_query, all_keyval, all_mixed, all_outgrad = (
        lax.all_gather(attn_in, "dp", axis=0, tiled=True),
        lax.all_gather(query_low, "dp", axis=0, tiled=True),
        lax.all_gather(keyval_low, "dp", axis=0, tiled=True),
        lax.all_gather(mixed_low, "dp", axis=0, tiled=True),
        lax.all_gather(attn_out_grad, "dp", axis=0, tiled=True),
    )
    all_moe, all_logits, attn_gain_rows, moe_gain_rows = (
        lax.all_gather(
            moe_in.astype(jnp.float32).astype(jnp.bfloat16), "dp", axis=0, tiled=True
        ).astype(jnp.float32),
        lax.all_gather(logits_grad.astype(jnp.bfloat16), "dp", axis=0, tiled=True).astype(
            logits_grad.dtype
        ),
        lax.all_gather(
            attn_gain_grad[None, :].astype(jnp.bfloat16), "dp", axis=0, tiled=True
        ).astype(jnp.float32),
        lax.all_gather(
            moe_gain_grad[None, :].astype(jnp.bfloat16), "dp", axis=0, tiled=True
        ).astype(jnp.float32),
    )
    attn_cols = lax.dynamic_slice_in_dim(all_attn, slab_index * width_rows, width_rows, 1)
    mixed_cols = lax.dynamic_slice_in_dim(all_mixed, slab_index * head_rows, head_rows, 1)
    moe_cols = lax.dynamic_slice_in_dim(all_moe, slab_index * width_rows, width_rows, 1)
    query_part = jnp.einsum("td,tc->dc", attn_cols, all_query, preferred_element_type=jnp.float32)
    keyval_part = jnp.einsum("td,tc->dc", attn_cols, all_keyval, preferred_element_type=jnp.float32)
    output_part = jnp.einsum(
        "tc,td->cd", mixed_cols, all_outgrad, preferred_element_type=jnp.float32
    )
    router_part = jnp.dot(moe_cols.T, all_logits, precision=HIGH)
    attn_gain_part = lax.dynamic_slice_in_dim(
        jnp.sum(attn_gain_rows, axis=0), slab_index * width_rows, width_rows, 0
    )
    moe_gain_part = lax.dynamic_slice_in_dim(
        jnp.sum(moe_gain_rows, axis=0), slab_index * width_rows, width_rows, 0
    )
    query_share, keyval_share, output_share, router_share, attn_share, moe_share = (
        lax.psum_scatter(
            query_part.astype(jnp.bfloat16), "expert", scatter_dimension=0, tiled=True
        ).astype(jnp.float32),
        lax.psum_scatter(
            keyval_part.astype(jnp.bfloat16), "expert", scatter_dimension=0, tiled=True
        ).astype(jnp.float32),
        lax.psum_scatter(
            output_part.astype(jnp.bfloat16), "expert", scatter_dimension=0, tiled=True
        ).astype(jnp.float32),
        lax.psum_scatter(
            router_part.astype(jnp.bfloat16), "expert", scatter_dimension=0, tiled=True
        ).astype(jnp.float32),
        lax.psum_scatter(
            attn_gain_part.astype(jnp.bfloat16), "expert", scatter_dimension=0, tiled=True
        ).astype(jnp.float32),
        lax.psum_scatter(
            moe_gain_part.astype(jnp.bfloat16), "expert", scatter_dimension=0, tiled=True
        ).astype(jnp.float32),
    )
    return (
        layer_out,
        tokens_grad,
        query_share,
        keyval_share,
        output_share,
        router_share,
        attn_share,
        moe_share,
        expert_up_grad,
        expert_down_grad,
    )


LANES = 128
TAIL = 16
PIECE_LIMIT = 4096
VMEM_BYTES = 60 * 1024 * 1024
F32 = jnp.float32
LOW = jnp.bfloat16


def contract(left, right, left_dim, right_dim):
    return lax.dot_general(
        left, right, (((left_dim,), (right_dim,)), ((), ())), preferred_element_type=F32
    )


def lane_index(shape):
    return lax.broadcasted_iota(jnp.int32, shape, len(shape) - 1)


def row_index(shape):
    return lax.broadcasted_iota(jnp.int32, shape, len(shape) - 2)


def half_turn(chunk):
    first = lane_index(chunk.shape) % HEAD_DIM < HEAD_DIM // 2
    ahead = pltpu.roll(chunk, LANES - HEAD_DIM // 2, 1)
    behind = pltpu.roll(chunk, HEAD_DIM // 2, 1)
    return jnp.where(first, ahead, behind)


def both_heads(chunk, pick):
    swapped = pltpu.roll(chunk, HEAD_DIM, 1)
    first = lane_index(chunk.shape) < HEAD_DIM
    if pick == 0:
        return jnp.where(first, chunk, swapped)
    return jnp.where(first, swapped, chunk)


def split_heads(chunk):
    first = lane_index(chunk.shape) < HEAD_DIM
    zero = jnp.zeros_like(chunk)
    return jnp.concatenate([jnp.where(first, chunk, zero), jnp.where(first, zero, chunk)], axis=0)


def join_heads(stacked):
    length = stacked.shape[0] // 2
    top, bottom = stacked[:length], stacked[length:]
    return jnp.where(lane_index(top.shape) < HEAD_DIM, top, bottom)


def three_parts(values):
    high = values.astype(LOW).astype(F32)
    rest = values - high
    middle = rest.astype(LOW).astype(F32)
    return (high, middle, rest - middle)


def gain_select():
    shape = (8, LANES)
    return (lane_index(shape) == EXPERTS + row_index(shape)) & (row_index(shape) < 2)


def load_weights(rows_ref, spots, piece_refs, weights, sems):
    copies = []
    for spot, piece in zip(spots, piece_refs):
        for i, (p, w) in enumerate(spot):
            size = piece.shape[1]
            start = pl.multiple_of(rows_ref[p, w] * size, size)
            copies.append(
                pltpu.make_async_copy(piece.at[i], weights.at[pl.ds(start, size)], sems.at[p, w])
            )
    for copy in copies:
        copy.start()
    return copies


def store_sums(rows_ref, sums, grads_even, grads_odd, sems):
    copies = []
    for p in range(2 * grads_even.shape[0]):
        target = grads_even if p % 2 == 0 else grads_odd
        for w in range(target.shape[1]):
            size = target.shape[2]
            start = pl.multiple_of(rows_ref[p, w] * size, size)
            copies.append(
                pltpu.make_async_copy(
                    sums.at[pl.ds(start, size)], target.at[p // 2, w], sems.at[p, w]
                )
            )
    for copy in copies:
        copy.start()
    return copies


def softmax_rows(q_pair, k_both, visible):
    scores = contract(q_pair, k_both, 1, 1) * (HEAD_DIM ** (-0.5))
    logits = jnp.where(visible, scores, MASKED)
    exps = jnp.exp(logits - jnp.max(logits, axis=-1, keepdims=True))
    return exps / jnp.sum(exps, axis=-1, keepdims=True)


def segment_tables(seg_row, frequency):
    length = seg_row.shape[1]
    shape = (length, length)
    across_row = jnp.broadcast_to(seg_row.astype(F32), shape)
    down_col = across_row.T
    seen = (down_col == across_row) & (lane_index(shape) <= row_index(shape))
    visible = jnp.concatenate([seen, seen], axis=0)
    if frequency is None:
        return visible
    earlier = jnp.sum(jnp.where(across_row < down_col, 1.0, 0.0), axis=1, keepdims=True)
    angles = (row_index(shape).astype(F32) - earlier) * frequency
    sine = jnp.sin(angles)
    first = lane_index(shape) % HEAD_DIM < HEAD_DIM // 2
    return (visible, jnp.cos(angles), jnp.where(first, -sine, sine))


def attn_forward_kernel(spots, *refs):
    count = len(spots)
    rows_ref, tokens_ref, seg_row, frequency = refs[:4]
    pieces = refs[4 : 4 + count]
    query_ref, keyval_ref, mixed_ref, tail_ref, cos_ref, sin_ref, weights, sems = refs[4 + count :]
    copies = load_weights(rows_ref, spots, pieces, weights, sems)
    tokens = tokens_ref[...].astype(F32)
    inverse = lax.rsqrt(jnp.mean(tokens * tokens, axis=-1, keepdims=True) + EPS)
    normed = tokens * inverse
    width = tokens.shape[1]
    visible, cosine, sine = segment_tables(seg_row[...], frequency[...])
    cos_ref[...] = cosine
    sin_ref[...] = sine
    for copy in copies:
        copy.wait()
    tail = weights[:, 2 * width :]
    tail_ref[...] = tail
    gains = contract(gain_select().astype(F32).astype(LOW), tail, 1, 1)
    attn_in = (normed * gains[0:1]).astype(LOW)
    keyval = contract(attn_in, weights[:, width : 2 * width], 1, 0)
    query = contract(attn_in, weights[:, :width], 1, 0)
    half = width // 2
    for m in range(half // LANES):
        keys = keyval[:, m * LANES : (m + 1) * LANES]
        keys = (keys * cosine + half_turn(keys) * sine).astype(LOW)
        values = keyval[:, half + m * LANES : half + (m + 1) * LANES].astype(LOW)
        keyval_ref[:, m * LANES : (m + 1) * LANES] = keys
        keyval_ref[:, half + m * LANES : half + (m + 1) * LANES] = values
        for pick in range(2):
            k_both = both_heads(keys.astype(F32), pick).astype(LOW)
            v_both = both_heads(values.astype(F32), pick).astype(LOW)
            chunk = slice((2 * m + pick) * LANES, (2 * m + pick + 1) * LANES)
            queries = query[:, chunk]
            queries = (queries * cosine + half_turn(queries) * sine).astype(LOW)
            query_ref[:, chunk] = queries
            q_pair = split_heads(queries.astype(F32)).astype(LOW)
            probs = softmax_rows(q_pair, k_both, visible).astype(LOW)
            mixed_ref[:, chunk] = join_heads(contract(probs, v_both, 1, 0)).astype(LOW)


def router_kernel(spots, *refs):
    count = len(spots)
    rows_ref, tokens_ref, mixed_ref, tail_ref, routes_t = refs[:5]
    pieces = refs[5 : 5 + count]
    payload, hidden_ref, gates_ref, weights, sems = refs[5 + count :]
    copies = load_weights(rows_ref, spots, pieces, weights, sems)
    tokens = tokens_ref[...].astype(F32)
    length = tokens.shape[0]
    tail = tail_ref[...]
    gains = contract(gain_select().astype(F32).astype(LOW), tail, 1, 1)
    for copy in copies:
        copy.wait()
    hidden = tokens + contract(mixed_ref[...], weights[...], 1, 0)
    hidden_ref[...] = hidden
    inverse_two = lax.rsqrt(jnp.mean(hidden * hidden, axis=-1, keepdims=True) + EPS)
    moe_in = (hidden * inverse_two * gains[1:2]).astype(LOW)
    payload[:length] = moe_in
    logits = contract(moe_in, tail, 1, 0)
    turned = routes_t[...]
    experts = row_index((LANES, length))
    chosen = experts == turned[0:1]
    for k in range(1, TOP):
        chosen = chosen | (experts == turned[k : k + 1])
    chosen = jnp.where(chosen, 1.0, 0.0).T > 0.5
    logits = jnp.where(chosen, logits, MASKED)
    exps = jnp.where(chosen, jnp.exp(logits - jnp.max(logits, axis=-1, keepdims=True)), 0.0)
    gates = exps / jnp.sum(exps, axis=-1, keepdims=True)
    gates_ref[...] = gates
    gates_t = gates.T
    for k in range(TOP):
        row = turned[k : k + 1]
        gate = jnp.sum(jnp.where(experts == row, gates_t, 0.0), axis=0, keepdims=True)
        high, middle, rest = three_parts(gate)
        place = row_index((TAIL, length))
        block = jnp.where(place == 0, high, jnp.where(place == 1, middle, jnp.where(place == 2, rest, 0.0)))
        block = jnp.where(place == 3, row.astype(F32), block)
        payload[length:, k * length : (k + 1) * length] = block.astype(LOW)


def slot_places(first_expert, local, tails, before):
    length = tails[0].shape[1] // TOP
    ids = row_index((8, length))
    ids = jnp.where(ids < local, ids + first_expert, -1).astype(F32)
    masks, gates = [], []
    for tail in tails:
        mask = jnp.zeros((8, length), F32)
        gate = jnp.zeros((8, length), F32)
        for k in range(TOP):
            part = tail[:, k * length : (k + 1) * length].astype(F32)
            hit = part[3:4] == ids
            mask = jnp.where(hit, 1.0, mask)
            gate = jnp.where(hit, part[0:1] + part[1:2] + part[2:3], gate)
        masks.append(mask)
        gates.append(gate)
    pairs = range(0, len(tails), 2)
    mask = jnp.concatenate([jnp.concatenate(masks[i : i + 2], axis=1) for i in pairs], axis=0)
    gate = jnp.concatenate([jnp.concatenate(gates[i : i + 2], axis=1) for i in pairs], axis=0)
    place = contract(mask.astype(LOW), before, 1, 0)
    return (jnp.where(mask > 0, place, -1.0), gate)


def gather_pair(local, block, pair, place, gate, row_pair, grad_pair, out):
    rows_out, grads_out, select_out, gate_out = out
    slots = row_index((block, place.shape[1])).astype(F32)
    parts = []
    for j in range(local):
        hit = slots == place[j : j + 1]
        parts.append(jnp.where(hit, 1.0, 0.0))
        held = jnp.where(hit, gate[j : j + 1], 0.0)
        held = jnp.sum(held, axis=1, keepdims=True)
        gate_out[j, pair * block : (pair + 1) * block] = jnp.broadcast_to(held, (block, LANES))
    select = jnp.concatenate(parts, axis=0).astype(LOW)
    if select_out is not None:
        select_out[pair] = select
    rows = contract(select, jnp.concatenate(row_pair, axis=0), 1, 0).astype(LOW)
    grads = contract(select, jnp.concatenate(grad_pair, axis=0), 1, 0).astype(LOW)
    for j in range(local):
        rows_out[j, pair * block : (pair + 1) * block] = rows[j * block : (j + 1) * block]
        grads_out[j, pair * block : (pair + 1) * block] = grads[j * block : (j + 1) * block]


def earlier_matrix(length):
    shape = (2 * length, 2 * length)
    return jnp.where(row_index(shape) < lane_index(shape), 1.0, 0.0).astype(LOW)


def expert_step(j, rows, grads, gate_ref, up, down):
    hidden_units = down.shape[1]
    pair = contract(rows[j], up, 1, 0)
    raw = contract(grads[j], down, 1, 0)
    gate_half, up_half = pair[:, :hidden_units], pair[:, hidden_units:]
    gate = gate_ref[j][:, 0:1]
    sigmoid = 1.0 / (1.0 + jnp.exp(-gate_half))
    silu = gate_half * sigmoid
    activated = silu * up_half
    scaled = (gate * activated).astype(LOW)
    act_grad = gate * raw
    pair_grad = jnp.concatenate(
        [act_grad * up_half * sigmoid * (1.0 + gate_half * (1.0 - sigmoid)), act_grad * silu],
        axis=1,
    ).astype(LOW)
    gate_grad = jnp.sum(activated * raw, axis=1, keepdims=True)
    return (scaled, pair_grad, gate_grad)


def fetch_experts(local, up_hbm, down_hbm, up, down, sems):
    copies = []
    for j in range(local):
        copies.append(
            (
                pltpu.make_async_copy(up_hbm.at[j], up.at[j], sems.at[0, j]),
                pltpu.make_async_copy(down_hbm.at[j], down.at[j], sems.at[1, j]),
            )
        )
        for copy in copies[j]:
            copy.start()
    return copies


def expert_home_kernel(owners, local, block, *refs):
    place_ref = refs[0]
    rows_in = refs[1 : 1 + owners]
    grads_in = refs[1 + owners : 1 + 2 * owners]
    up_hbm, down_hbm = refs[1 + 2 * owners : 3 + 2 * owners]
    out_even, out_odd, back_even, back_odd, up_out, down_out = refs[3 + 2 * owners : 9 + 2 * owners]
    scratch = refs[9 + 2 * owners :]
    up, down, rows, grads, select, gate_ref, produced, returned, up_grad, down_grad, sems = scratch
    copies = fetch_experts(local, up_hbm, down_hbm, up, down, sems)
    length = rows_in[0].shape[0] - TAIL
    width = rows_in[0].shape[1]
    first_expert = place_ref[0] * local
    slab = up_grad.shape[1]
    columns = pl.ds(pl.multiple_of(place_ref[1] * slab, slab), slab)
    before = earlier_matrix(length)
    place, gate = slot_places(first_expert, local, [ref[length:] for ref in rows_in], before)
    for s in range(owners // 2):
        gather_pair(
            local,
            block,
            s,
            place[8 * s : 8 * s + 8],
            gate[8 * s : 8 * s + 8],
            [rows_in[2 * s][:length], rows_in[2 * s + 1][:length]],
            [grads_in[2 * s][...], grads_in[2 * s + 1][...]],
            (rows, grads, select, gate_ref),
        )
    for j in range(local):
        for copy in copies[j]:
            copy.wait()
    sent = []
    for j in range(local):
        scaled, pair_grad, gate_grad = expert_step(j, rows, grads, gate_ref, up[j], down[j])
        produced[j] = contract(scaled, down[j], 1, 1).astype(LOW)
        returned[j, :, :width] = contract(pair_grad, up[j], 1, 1).astype(LOW)
        lanes = lane_index((scaled.shape[0], LANES)) - first_expert - j
        high, middle, rest = three_parts(gate_grad)
        tail = jnp.where(lanes == 0, high, 0.0)
        tail = jnp.where(lanes == EXPERTS, middle, tail)
        tail = jnp.where(lanes == 2 * EXPERTS, rest, tail)
        returned[j, :, width:] = tail.astype(LOW)
        up_grad[j] = contract(rows[j, :, columns], pair_grad, 0, 0)
        down_grad[j] = contract(grads[j, :, columns], scaled, 0, 0)
        sent.append(pltpu.make_async_copy(up_grad.at[j], up_out.at[j], sems.at[2, j]))
        sent.append(pltpu.make_async_copy(down_grad.at[j], down_out.at[j], sems.at[3, j]))
        sent[-2].start()
        sent[-1].start()
    for s in range(owners // 2):
        span = slice(s * block, (s + 1) * block)
        made = jnp.concatenate([produced[j, span] for j in range(local)], axis=0)
        back = jnp.concatenate([returned[j, span] for j in range(local)], axis=0)
        made = contract(select[s], made, 0, 0).astype(LOW)
        back = contract(select[s], back, 0, 0).astype(LOW)
        out_even[s] = made[:length]
        out_odd[s] = made[length:]
        back_even[s] = back[:length]
        back_odd[s] = back[length:]
    for copy in sent:
        copy.wait()


def expert_away_kernel(start, count, block, chips, far, *refs):
    place_ref = refs[0]
    rows_in = refs[1 : 3 + 2 * chips]
    grads_in = refs[3 + 2 * chips : 3 + 4 * chips]
    up_hbm, down_hbm, up_first, down_first = refs[3 + 4 * chips : 7 + 4 * chips]
    up_grad, down_grad = refs[7 + 4 * chips : 9 + 4 * chips]
    scratch = refs[9 + 4 * chips :]
    up, down, up_sum, down_sum, rows_buf, grads_buf, rows, grads, gate_ref, sems, pair_sems = scratch
    length = grads_buf.shape[1] // 2
    tall = length + TAIL
    pairs = []
    for i in range(far + 1):
        for s in range(chips):
            spot = len(pairs)
            copies = []
            for side in range(2):
                grad_from = grads_in[2 * s + side].at[pl.ds(i * length, length)]
                if i == 0:
                    row_from = rows_in[side].at[s]
                else:
                    row_from = rows_in[2 + 2 * s + side].at[pl.ds((i - 1) * tall, tall)]
                row_to = rows_buf.at[spot, pl.ds(side * tall, tall)]
                grad_to = grads_buf.at[spot, pl.ds(side * length, length)]
                copies.append(pltpu.make_async_copy(row_from, row_to, pair_sems.at[0, side, spot]))
                copies.append(pltpu.make_async_copy(grad_from, grad_to, pair_sems.at[1, side, spot]))
            pairs.append(copies)
    for copies in pairs:
        for copy in copies:
            copy.start()
    held = []
    for j in range(count):
        held.append(
            [
                pltpu.make_async_copy(up_hbm.at[start + j], up.at[j], sems.at[0, j]),
                pltpu.make_async_copy(down_hbm.at[start + j], down.at[j], sems.at[1, j]),
                pltpu.make_async_copy(up_first.at[start + j], up_sum.at[j], sems.at[2, j]),
                pltpu.make_async_copy(down_first.at[start + j], down_sum.at[j], sems.at[3, j]),
            ]
        )
    for copies in held:
        for copy in copies:
            copy.start()
    first_expert = place_ref[0] * (up_hbm.shape[0]) + start
    slab = up_sum.shape[1]
    columns = pl.ds(pl.multiple_of(place_ref[1] * slab, slab), slab)
    before = earlier_matrix(length)
    for i, copies in enumerate(pairs):
        for copy in copies:
            copy.wait()
        tails = [rows_buf[i, length:tall], rows_buf[i, tall + length :]]
        place, gate = slot_places(first_expert, count, tails, before)
        gather_pair(
            count,
            block,
            i,
            place,
            gate,
            [rows_buf[i, :length], rows_buf[i, tall : tall + length]],
            [grads_buf[i]],
            (rows, grads, None, gate_ref),
        )
    for copies in held:
        for copy in copies:
            copy.wait()
    sent = []
    for j in range(count):
        scaled, pair_grad, _ = expert_step(j, rows, grads, gate_ref, up[j], down[j])
        up_sum[j] += contract(rows[j, :, columns], pair_grad, 0, 0)
        down_sum[j] += contract(grads[j, :, columns], scaled, 0, 0)
        sent.append(pltpu.make_async_copy(up_sum.at[j], up_grad.at[start + j], sems.at[4, j]))
        sent.append(pltpu.make_async_copy(down_sum.at[j], down_grad.at[start + j], sems.at[5, j]))
        sent[-2].start()
        sent[-1].start()
    for copy in sent:
        copy.wait()


def backward_kernel(spots, output_spots, shares, *refs):
    rows_ref, tokens_ref, seg_row, cos_ref, sin_ref, payload, hidden_ref = refs[:7]
    query_ref, keyval_ref, mixed_ref, gates_ref, out_grad_ref, tail_ref = refs[7:13]
    refs = refs[13:]
    back, refs = refs[:shares], refs[shares:]
    pieces, refs = refs[: len(spots)], refs[len(spots) :]
    output_pieces, refs = refs[: len(output_spots)], refs[len(output_spots) :]
    tokens_grad, grads_even, grads_odd = refs[:3]
    weights, output, sums, query_low, keyval_low, sems, output_sems, out_sems = refs[3:]
    output_copies = load_weights(rows_ref, output_spots, output_pieces, output, output_sems)
    copies = load_weights(rows_ref, spots, pieces, weights, sems)
    length, width = tokens_ref.shape
    half = width // 2
    columns = weights.shape[1]
    total = back[0][...].astype(F32)
    for share in back[1:]:
        total = total + share[...].astype(F32)
    parts = total[:, width:]
    lanes = lane_index(parts.shape)
    gate_grad = parts + pltpu.roll(parts, LANES - EXPERTS, 1) + pltpu.roll(parts, LANES - 2 * EXPERTS, 1)
    gate_grad = jnp.where(lanes < EXPERTS, gate_grad, 0.0)
    gates = gates_ref[...]
    logits_grad = gates * (gate_grad - jnp.sum(gates * gate_grad, axis=-1, keepdims=True))
    hidden = hidden_ref[...]
    inverse_two = lax.rsqrt(jnp.mean(hidden * hidden, axis=-1, keepdims=True) + EPS)
    normed_two = hidden * inverse_two
    tail = tail_ref[...]
    gains = contract(gain_select().astype(F32).astype(LOW), tail, 1, 1)
    high = logits_grad.astype(LOW)
    rest = (logits_grad - high.astype(F32)).astype(LOW)
    moe_grad = total[:, :width] + contract(high, tail, 1, 1) + contract(rest, tail, 1, 1)
    moe_gain_grad = jnp.sum(moe_grad * normed_two, axis=0, keepdims=True)
    scaled = moe_grad * gains[1:2]
    hidden_grad = out_grad_ref[...].astype(F32) + inverse_two * (
        scaled - normed_two * jnp.mean(scaled * normed_two, axis=-1, keepdims=True)
    )
    attn_out_grad = hidden_grad.astype(LOW)
    for copy in output_copies:
        copy.wait()
    mixed_grad = contract(attn_out_grad, output[...], 1, 1)
    sums[:, columns:] = contract(mixed_ref[...], attn_out_grad, 0, 0).astype(LOW)
    tokens = tokens_ref[...].astype(F32)
    inverse_one = lax.rsqrt(jnp.mean(tokens * tokens, axis=-1, keepdims=True) + EPS)
    normed_one = tokens * inverse_one
    cosine, sine = cos_ref[...], sin_ref[...]
    visible = segment_tables(seg_row[...], None)
    groups = range(width // LANES)
    chunks = [slice(g * LANES, (g + 1) * LANES) for g in groups]
    keys = [keyval_ref[:, chunks[m]].astype(F32) for m in range(half // LANES)]
    values = [keyval_ref[:, half + m * LANES : half + (m + 1) * LANES].astype(F32) for m in range(half // LANES)]
    k_both = [both_heads(keys[g // 2], g % 2).astype(LOW) for g in groups]
    v_both = [both_heads(values[g // 2], g % 2).astype(LOW) for g in groups]
    q_pair = [split_heads(query_ref[:, chunk].astype(F32)).astype(LOW) for chunk in chunks]
    probs = [softmax_rows(q_pair[g], k_both[g], visible) for g in groups]
    m_pair = [split_heads(mixed_grad[:, chunk]).astype(LOW) for chunk in chunks]
    probs_grad = [contract(m_pair[g], v_both[g], 1, 1) for g in groups]
    value_sides = [contract(probs[g].astype(LOW), m_pair[g], 0, 0) for g in groups]
    scores_grad = [
        (
            probs[g]
            * (probs_grad[g] - jnp.sum(probs[g] * probs_grad[g], axis=-1, keepdims=True))
            * (HEAD_DIM ** (-0.5))
        ).astype(LOW)
        for g in groups
    ]
    query_grad = [join_heads(contract(scores_grad[g], k_both[g], 1, 0)) for g in groups]
    key_sides = [contract(scores_grad[g], q_pair[g], 0, 0) for g in groups]
    for g in groups:
        turned = query_grad[g] * cosine - half_turn(query_grad[g]) * sine
        query_low[:, chunks[g]] = turned.astype(LOW)
    key_sides = [side + pltpu.roll(side, HEAD_DIM, 1) for side in key_sides]
    value_sides = [side + pltpu.roll(side, HEAD_DIM, 1) for side in value_sides]
    first = lane_index((length, LANES)) < HEAD_DIM
    for m in range(half // LANES):
        keys_grad = jnp.where(first, key_sides[2 * m], key_sides[2 * m + 1])
        values_grad = jnp.where(first, value_sides[2 * m], value_sides[2 * m + 1])
        turned = keys_grad * cosine - half_turn(keys_grad) * sine
        keyval_low[:, chunks[m]] = turned.astype(LOW)
        keyval_low[:, half + m * LANES : half + (m + 1) * LANES] = values_grad.astype(LOW)
    for copy in copies:
        copy.wait()
    attn_in_grad = contract(query_low[...], weights[:, :width], 1, 1) + contract(
        keyval_low[...], weights[:, width : 2 * width], 1, 1
    )
    attn_in = (normed_one * gains[0:1]).astype(LOW)
    sums[:, :width] = contract(attn_in, query_low[...], 0, 0).astype(LOW)
    sums[:, width : 2 * width] = contract(attn_in, keyval_low[...], 0, 0).astype(LOW)
    attn_gain_grad = jnp.sum(attn_in_grad * normed_one, axis=0, keepdims=True)
    place = row_index((8, width))
    gain_grads = jnp.where(place == 0, attn_gain_grad, jnp.where(place == 1, moe_gain_grad, 0.0))
    sums[:, 2 * width : columns] = (
        contract(payload[:length], high, 0, 0)
        + contract(gain_grads.astype(LOW), gain_select().astype(F32).astype(LOW), 0, 0)
    ).astype(LOW)
    out_copies = store_sums(rows_ref, sums, grads_even, grads_odd, out_sems)
    scaled = attn_in_grad * gains[0:1]
    tokens_grad[...] = hidden_grad + inverse_one * (
        scaled - normed_one * jnp.mean(scaled * normed_one, axis=-1, keepdims=True)
    )
    for copy in out_copies:
        copy.wait()


def swap(values, axis, size, distance):
    return lax.ppermute(values, axis, [(i, i ^ distance) for i in range(size)])


def across(values, distance, planes):
    return swap(values, "dp", planes, distance)


def aside(values, s, owners):
    return swap(values, "expert", owners, 2 * s)


def partner(values, owners):
    return swap(values, "expert", owners, 1)


def after(values, *earlier):
    return lax.optimization_barrier((values,) + earlier)[0]


def over_chips(values, owners):
    return [values] + [aside(values, s, owners) for s in range(1, owners // 2)]


def over_cores(near, owners, *earlier):
    pieces = []
    for piece in near:
        pieces += [piece, partner(after(piece, *earlier) if earlier else piece, owners)]
    return pieces


def chips_split(values, owners, *earlier):
    half = values.shape[0] // 2
    first, second = aside(values, 1, owners), aside(values, 2, owners)
    far = [first[:half], second[half:]]
    if earlier:
        far = [after(part, *earlier) for part in far]
    far = [aside(far[0], 2, owners), aside(far[1], 1, owners)]
    return [[values], [first], [second], far]


def core_pieces(groups, owners, *earlier):
    pieces, spots = [], []
    for group in groups:
        parts = [part for part, _ in group]
        merged = parts[0] if len(parts) == 1 else jnp.concatenate(parts, axis=0)
        merged = after(merged, *earlier) if earlier else merged
        for part, spot in group:
            pieces.append(part)
            spots.append(spot)
        pieces.append(partner(merged, owners))
        spots.append([(p + 1, w) for _, spot in group for p, w in spot])
    return (pieces, spots)


def core_pieces_whole(near, owners):
    pieces = []
    for parts in near:
        piece = parts[0] if len(parts) == 1 else jnp.concatenate(parts, axis=0)
        pieces.append((piece, partner(piece, owners)))
    return pieces


def added(left, right):
    return (left.astype(F32) + right.astype(F32)).astype(LOW)


def to_owners(even, odd, owners, *earlier):
    other = partner(odd, owners)
    joined = [added(even[s], other[s]) for s in range(owners // 2)]
    if earlier:
        joined = lax.optimization_barrier(tuple(joined) + earlier)[: owners // 2]
    sent = [joined[0]] + [aside(joined[s], s, owners) for s in range(1, owners // 2)]
    return (joined, sent)


def to_neighbours(joined, owners):
    half = joined[3].shape[0] // 2
    low_turn = aside(joined[3][:half], 1, owners)
    top_turn = aside(joined[3][half:], 2, owners)
    low_turn, top_turn = lax.optimization_barrier((low_turn, top_turn))
    first = jnp.concatenate([joined[1][:half], added(joined[1][half:], top_turn)], axis=0)
    second = jnp.concatenate([added(joined[2][:half], low_turn), joined[2][half:]], axis=0)
    return (first, second)


def from_neighbours(joined, first, second, owners):
    parts = [joined[0], aside(first, 1, owners), aside(second, 2, owners)]
    return sum(part.astype(F32) for part in parts).astype(LOW)


def over_planes_sum(parts, planes):
    total = parts[0].astype(F32)
    for w in range(1, planes):
        total = total + across(parts[w], w, planes).astype(F32)
    return total


def cost(us):
    return pl.CostEstimate(flops=int(us * 1153e6), bytes_accessed=0, transcendentals=0)


def params():
    return pltpu.CompilerParams(vmem_limit_bytes=VMEM_BYTES)


def whole_spec():
    return pl.BlockSpec(memory_space=pltpu.VMEM)


def hbm_spec():
    return pl.BlockSpec(memory_space=pl.ANY)


def smem_spec():
    return pl.BlockSpec(memory_space=pltpu.SMEM)


def on_device(
    planes,
    owners,
    tokens,
    segments,
    routes,
    query_weight,
    keyval_weight,
    output_weight,
    router_weight,
    attn_gain,
    moe_gain,
    expert_up,
    expert_down,
    out_grad,
):
    length, width = tokens.shape
    if planes != 4 or owners != 8 or planes * owners * length > PIECE_LIMIT:
        return on_device_wide(
            tokens,
            segments,
            routes,
            query_weight,
            keyval_weight,
            output_weight,
            router_weight,
            attn_gain,
            moe_gain,
            expert_up,
            expert_down,
            out_grad,
        )
    local = expert_up.shape[0]
    hidden_units = expert_down.shape[2]
    block = 2 * CAP
    slots = owners // 2 * block
    plane = lax.axis_index("dp")
    owner = lax.axis_index("expert")
    share = query_weight.shape[0]
    rows = (plane ^ jnp.arange(planes))[None, :] * owners + (owner ^ jnp.arange(owners))[:, None]
    rows = rows.astype(jnp.int32)
    place = jnp.stack([owner, plane]).astype(jnp.int32)
    extra = jnp.concatenate(
        [
            router_weight,
            attn_gain[:, None],
            moe_gain[:, None],
            jnp.zeros((share, LANES - EXPERTS - 2), LOW),
        ],
        axis=1,
    )
    packed = jnp.concatenate([query_weight, keyval_weight, extra, output_weight], axis=1)
    columns = packed.shape[1] - width

    early = [across(packed, w, planes) for w in range(1, planes)]
    grad_chips = over_chips(out_grad, owners)
    grad_cores = partner(jnp.concatenate(grad_chips, axis=0), owners)
    gathered = jnp.stack([packed] + early)
    grad_start = after(out_grad, *early)
    grad_planes = [across(grad_start, w, planes) for w in range(1, planes)]
    near = chips_split(
        after(gathered[:, :, :columns], *grad_chips), owners, grad_planes[0]
    )
    every = list(range(planes))
    groups = [[(near[s][0], [(2 * s, w) for w in every])] for s in range(3)]
    groups += [
        [(near[3][0], [(6, w) for w in every[: planes // 2]])],
        [(near[3][1], [(6, w) for w in every[planes // 2 :]])],
    ]
    pieces, spots = core_pieces(groups, owners)
    output_near = over_chips(after(gathered[:, :, columns:], *pieces[:6], *near[3]), owners)

    half_dim = HEAD_DIM // 2
    frequency = ROPE_BASE ** (-(jnp.arange(half_dim, dtype=F32) * 2.0) / HEAD_DIM)
    frequency = jnp.tile(frequency, LANES // half_dim)[None, :]

    token_low = jax.ShapeDtypeStruct((length, width), LOW)
    token_wide = jax.ShapeDtypeStruct((length, width), F32)
    table = jax.ShapeDtypeStruct((length, LANES), F32)
    query_rot, keyval_low, mixed_low, tail, cosine, sine = pl.pallas_call(
        functools.partial(attn_forward_kernel, spots),
        out_shape=(token_low, token_low, token_low, jax.ShapeDtypeStruct((width, LANES), LOW))
        + (table, table),
        in_specs=[smem_spec()] + [whole_spec()] * 3 + [hbm_spec()] * len(pieces),
        out_specs=[whole_spec()] * 6,
        scratch_shapes=[
            pltpu.VMEM((width, columns), LOW),
            pltpu.SemaphoreType.DMA((owners, planes)),
        ],
        compiler_params=params(),
        cost_estimate=cost(6),
        name="attn_forward",
    )(rows, after(tokens, grad_planes[1]), segments, frequency, *pieces)

    output_pieces, output_spots = core_pieces(
        [[(output_near[s], [(2 * s, w) for w in every])] for s in range(owners // 2)],
        owners,
        mixed_low,
    )

    grad_stack = jnp.concatenate(grad_planes, axis=0)

    payload, hidden, gates = pl.pallas_call(
        functools.partial(router_kernel, output_spots),
        out_shape=(
            jax.ShapeDtypeStruct((length + TAIL, width), LOW),
            token_wide,
            jax.ShapeDtypeStruct((length, LANES), F32),
        ),
        in_specs=[smem_spec()] + [whole_spec()] * 4 + [hbm_spec()] * len(output_pieces),
        out_specs=[whole_spec()] * 3,
        scratch_shapes=[
            pltpu.VMEM((width, width), LOW),
            pltpu.SemaphoreType.DMA((owners, planes)),
        ],
        compiler_params=params(),
        cost_estimate=cost(4),
        name="router",
    )(
        rows,
        tokens,
        mixed_low,
        tail,
        routes.T,
        *output_pieces,
    )

    row_chips = over_chips(payload, owners)
    row_home = over_cores(row_chips, owners)
    grad_other = partner(after(grad_stack, payload), owners)
    row_start = after(payload, row_home[1])
    row_planes = [across(row_start, w, planes) for w in range(2, planes)]
    row_near = across(jnp.stack(row_chips), 1, planes)
    grad_direct = after(grad_stack, *row_chips)
    grad_near = [aside(grad_direct, s, owners) for s in (1, 2)]

    def all_of(shape):
        return pl.BlockSpec(shape, lambda i: (0,) * len(shape))

    slab = width // planes
    slabs = (
        jax.ShapeDtypeStruct((local, slab, 2 * hidden_units), F32),
        jax.ShapeDtypeStruct((local, slab, hidden_units), F32),
    )
    home_blocks = [s * (p % 2) for s in range(owners // 2) for p in range(2)]
    grad_home = [part for s in range(owners // 2) for part in (grad_chips[s], grad_cores)]
    out_even, out_odd, back_even, back_odd, up_grad, down_grad = pl.pallas_call(
        functools.partial(expert_home_kernel, owners, local, block),
        grid=(1,),
        out_shape=(
            jax.ShapeDtypeStruct((owners // 2, length, width), LOW),
            jax.ShapeDtypeStruct((owners // 2, length, width), LOW),
            jax.ShapeDtypeStruct((owners // 2, length, width + LANES), LOW),
            jax.ShapeDtypeStruct((owners // 2, length, width + LANES), LOW),
        )
        + slabs,
        in_specs=[smem_spec()]
        + [all_of((length + TAIL, width))] * owners
        + [pl.BlockSpec((length, width), lambda i, s=s: (s, 0)) for s in home_blocks]
        + [hbm_spec()] * 2,
        out_specs=[all_of((owners // 2, length, width))] * 2
        + [all_of((owners // 2, length, width + LANES))] * 2
        + [hbm_spec()] * 2,
        scratch_shapes=[
            pltpu.VMEM(expert_up.shape, LOW),
            pltpu.VMEM(expert_down.shape, LOW),
            pltpu.VMEM((local, slots, width), LOW),
            pltpu.VMEM((local, slots, width), LOW),
            pltpu.VMEM((owners // 2, local * block, 2 * length), LOW),
            pltpu.VMEM((local, slots, LANES), F32),
            pltpu.VMEM((local, slots, width), LOW),
            pltpu.VMEM((local, slots, width + LANES), LOW),
            pltpu.VMEM(slabs[0].shape, F32),
            pltpu.VMEM(slabs[1].shape, F32),
            pltpu.SemaphoreType.DMA((4, local)),
        ],
        compiler_params=params(),
        cost_estimate=cost(22),
        name="expert_home",
    )(place, *row_home, *grad_home, expert_up, expert_down)

    joined, back = to_owners(back_even, after(back_odd, *grad_near, *row_planes), owners)
    row_stack = jnp.concatenate(row_planes, axis=0)
    row_far = chips_split(after(row_stack, *back), owners)
    grad_away = [grad_stack, grad_other]
    grad_away += over_cores(grad_near, owners, *back)
    row_own = partner(after(row_stack, *joined), owners)

    def expert_away(start, count, place, up_grad, down_grad):
        chips = owners // 2
        pairs = chips * (planes - 1)
        return pl.pallas_call(
            functools.partial(
                expert_away_kernel, start, count, block, chips, planes - 2
            ),
            out_shape=slabs,
            in_specs=[smem_spec()] + [hbm_spec()] * (6 + 4 * chips),
            out_specs=[hbm_spec()] * 2,
            scratch_shapes=[
                pltpu.VMEM((count,) + expert_up.shape[1:], LOW),
                pltpu.VMEM((count,) + expert_down.shape[1:], LOW),
                pltpu.VMEM((count,) + slabs[0].shape[1:], F32),
                pltpu.VMEM((count,) + slabs[1].shape[1:], F32),
                pltpu.VMEM((pairs, 2 * (length + TAIL), width), LOW),
                pltpu.VMEM((pairs, 2 * length, width), LOW),
                pltpu.VMEM((count, pairs * block, width), LOW),
                pltpu.VMEM((count, pairs * block, width), LOW),
                pltpu.VMEM((count, pairs * block, LANES), F32),
                pltpu.SemaphoreType.DMA((6, count)),
                pltpu.SemaphoreType.DMA((2, 2, pairs)),
            ],
            input_output_aliases={5 + 4 * chips: 0, 6 + 4 * chips: 1},
            compiler_params=params(),
            cost_estimate=cost(7 * count),
            name="expert_away",
        )(place, *row_away, *grad_away, expert_up, expert_down, up_grad, down_grad)

    def share_pieces(wide):
        return jax.ShapeDtypeStruct((owners // 2, planes, share, wide), LOW)

    wide = columns + width
    tokens_grad, grads_even, grads_odd = pl.pallas_call(
        functools.partial(backward_kernel, spots, output_spots, owners // 2),
        out_shape=(token_wide, share_pieces(wide), share_pieces(wide)),
        in_specs=[smem_spec()]
        + [whole_spec()] * (12 + owners // 2)
        + [hbm_spec()] * (len(pieces) + len(output_pieces)),
        out_specs=[whole_spec()] + [hbm_spec()] * 2,
        scratch_shapes=[
            pltpu.VMEM((width, columns), LOW),
            pltpu.VMEM((width, width), LOW),
            pltpu.VMEM((width, wide), LOW),
            pltpu.VMEM((length, width), LOW),
            pltpu.VMEM((length, width), LOW),
            pltpu.SemaphoreType.DMA((owners, planes)),
            pltpu.SemaphoreType.DMA((owners, planes)),
            pltpu.SemaphoreType.DMA((owners, planes)),
        ],
        compiler_params=params(),
        cost_estimate=cost(17),
        name="backward",
    )(
        rows,
        tokens,
        segments,
        cosine,
        sine,
        payload,
        after(hidden, row_own, grad_other),
        query_rot,
        keyval_low,
        mixed_low,
        gates,
        out_grad,
        tail,
        *back,
        *pieces,
        *output_pieces,
    )

    grads_other = partner(
        after(grads_odd, row_near, row_far[1][0], row_far[2][0], *grad_away[3::2]), owners
    )
    half = grad_stack.shape[0] // 2
    grad_turn = [
        aside(after(grad_near[0][:half], tokens_grad), 2, owners),
        aside(after(grad_near[1][half:], tokens_grad), 1, owners),
    ]
    shares = [added(grads_even[s], grads_other[s]) for s in range(owners // 2)]
    grad_away += over_cores([jnp.concatenate(grad_turn, axis=0)], owners, shares[0])
    row_away = over_cores([row_near], owners, shares[0]) + [row_stack, row_own]
    row_away += over_cores(
        [jnp.concatenate(parts, axis=0) for parts in row_far[1:]], owners, shares[0]
    )
    first, second = to_neighbours(shares, owners)
    out_other = partner(after(out_odd, shares[0], *row_far[3], *grad_turn), owners)
    made = [added(out_even[s], out_other[s]) for s in range(owners // 2)]
    held = (first, second) + tuple(row_away[1::2]) + tuple(grad_away[7:]) + tuple(made)
    first, second = lax.optimization_barrier(held)[:2]
    far_made = aside(after(made[3], first), 3, owners)
    up_grad, down_grad = expert_away(0, 2, after(place, first, second), up_grad, down_grad)
    plane_sums = after(from_neighbours(shares, first, second, owners), up_grad, far_made)
    up_grad, down_grad = expert_away(2, 2, after(place, plane_sums), up_grad, down_grad)
    made = lax.optimization_barrier(tuple(made) + (plane_sums,))[: owners // 2]
    near_made = [aside(made[s], s, owners) for s in (1, 2)]
    summed = over_planes_sum(plane_sums, planes)
    made = [made[0]] + near_made + [far_made]
    layer_out = (hidden + sum(part.astype(F32) for part in made)).astype(LOW)

    return (
        layer_out,
        tokens_grad,
        summed[:, :width],
        summed[:, width : 2 * width],
        summed[:, columns:],
        summed[:, 2 * width : 2 * width + EXPERTS],
        summed[:, 2 * width + EXPERTS],
        summed[:, 2 * width + EXPERTS + 1],
        up_grad,
        down_grad,
    )


def solution(mesh):
    return jax.shard_map(
        functools.partial(on_device, mesh.shape["dp"], mesh.shape["expert"]),
        mesh=mesh,
        in_specs=(
            P(("dp", "expert"), None),
            P(("dp", "expert"), None),
            P(("dp", "expert"), None),
            P(("dp", "expert"), None),
            P(("dp", "expert"), None),
            P(("dp", "expert"), None),
            P(("dp", "expert"), None),
            P(("dp", "expert")),
            P(("dp", "expert")),
            P("expert", None, None),
            P("expert", None, None),
            P(("dp", "expert"), None),
        ),
        out_specs=(
            P(("dp", "expert"), None),
            P(("dp", "expert"), None),
            P(("dp", "expert"), None),
            P(("dp", "expert"), None),
            P(("dp", "expert"), None),
            P(("dp", "expert"), None),
            P(("dp", "expert")),
            P(("dp", "expert")),
            P("expert", "dp", None),
            P("expert", "dp", None),
        ),
        check_vma=False,
    )
```

```python
import functools

import jax
import jax.numpy as jnp
from jax import lax
from jax.sharding import PartitionSpec as P
from jax.experimental import pallas as pl
from jax.experimental.pallas import tpu as pltpu

HEAD_DIM = 64
FF = 512
EXPERTS = 32
TOP = 8
CAP = 40


EPS = 1e-05
ROPE_BASE = 10000.0
MASKED = -1e30
HIGH = lax.Precision.HIGHEST


def norm_forward(values, gain_vec):
    inverse = lax.rsqrt(jnp.mean(values * values, axis=-1, keepdims=True) + EPS)
    normed = values * inverse
    return (normed, inverse, (normed * gain_vec).astype(jnp.bfloat16))


def norm_backward(grad_out, normed, inverse, gain_vec):
    gain_grad = jnp.sum(grad_out * normed, axis=0)
    scaled = grad_out * gain_vec
    grad_in = inverse * (scaled - normed * jnp.mean(scaled * normed, axis=-1, keepdims=True))
    return (grad_in, gain_grad)


def rope_tables(segment_row):
    length = segment_row.shape[0]
    earlier = jnp.sum((segment_row[None, :] < segment_row[:, None]).astype(jnp.int32), axis=1)
    position = jnp.arange(length, dtype=jnp.int32) - earlier
    half_dim = HEAD_DIM // 2
    frequency = ROPE_BASE ** (-(jnp.arange(half_dim, dtype=jnp.float32) * 2.0) / HEAD_DIM)
    angles = position.astype(jnp.float32)[:, None] * frequency[None, :]
    cosine = jnp.concatenate([jnp.cos(angles), jnp.cos(angles)], axis=-1)[:, None, :]
    sine_table = jnp.concatenate([jnp.sin(angles), jnp.sin(angles)], axis=-1)[:, None, :]
    return (cosine, sine_table)


def rotate(values, cosine, sine_table):
    half_dim = values.shape[-1] // 2
    turned = jnp.concatenate([-values[..., half_dim:], values[..., :half_dim]], axis=-1)
    return values * cosine + turned * sine_table


def unrotate(grad_rows, cosine, sine_table):
    half_dim = grad_rows.shape[-1] // 2
    weighted = grad_rows * sine_table
    turned = jnp.concatenate([weighted[..., half_dim:], -weighted[..., :half_dim]], axis=-1)
    return grad_rows * cosine + turned


def on_device_wide(
    tokens,
    segments,
    routes,
    query_weight,
    keyval_weight,
    output_weight,
    router_weight,
    attn_gain,
    moe_gain,
    expert_up,
    expert_down,
    out_grad,
):
    owners = lax.axis_size("expert")
    local_experts = expert_up.shape[0]
    length = tokens.shape[0]
    model_width = tokens.shape[1]
    kv_heads = keyval_weight.shape[1] // (2 * HEAD_DIM)
    query_heads = query_weight.shape[1] // HEAD_DIM
    repeat = query_heads // kv_heads
    score_scale = HEAD_DIM ** (-0.5)
    query_full, keyval_full, output_full, router_full, attn_gains, moe_gains = (
        lax.all_gather(query_weight, ("dp", "expert"), axis=0, tiled=True),
        lax.all_gather(keyval_weight, ("dp", "expert"), axis=0, tiled=True),
        lax.all_gather(output_weight, ("dp", "expert"), axis=0, tiled=True),
        lax.all_gather(router_weight, ("dp", "expert"), axis=0, tiled=True),
        lax.all_gather(attn_gain, ("dp", "expert"), axis=0, tiled=True),
        lax.all_gather(moe_gain, ("dp", "expert"), axis=0, tiled=True),
    )
    resident = tokens.astype(jnp.float32)
    normed_one, inverse_one, attn_in = norm_forward(resident, attn_gains.astype(jnp.float32))
    query_proj = jnp.dot(attn_in, query_full, preferred_element_type=jnp.float32).reshape(
        length, query_heads, HEAD_DIM
    )
    keyval_proj = jnp.dot(attn_in, keyval_full, preferred_element_type=jnp.float32)
    key_rows = keyval_proj[:, : kv_heads * HEAD_DIM].reshape(length, kv_heads, HEAD_DIM)
    value_rows = keyval_proj[:, kv_heads * HEAD_DIM :].reshape(length, kv_heads, HEAD_DIM)
    cosine, sine_table = rope_tables(segments[0])
    query_rot = (
        rotate(query_proj, cosine, sine_table)
        .astype(jnp.bfloat16)
        .reshape(length, kv_heads, repeat, HEAD_DIM)
    )
    keys_rot = rotate(key_rows, cosine, sine_table).astype(jnp.bfloat16)
    values_low = value_rows.astype(jnp.bfloat16)
    places = jnp.arange(length)
    visible = (segments[0][:, None] == segments[0][None, :]) & (places[None, :] <= places[:, None])
    scores = jnp.einsum("ikrd,jkd->krij", query_rot, keys_rot, preferred_element_type=jnp.float32)
    attn_logits = jnp.where(visible, scores * score_scale, MASKED)
    attn_exps = jnp.exp(attn_logits - jnp.max(attn_logits, axis=-1, keepdims=True))
    attn_probs = attn_exps / jnp.sum(attn_exps, axis=-1, keepdims=True)
    probs_low = attn_probs.astype(jnp.bfloat16)
    mixed_heads = jnp.einsum(
        "krij,jkd->ikrd", probs_low, values_low, preferred_element_type=jnp.float32
    )
    mixed_low = mixed_heads.reshape(length, query_heads * HEAD_DIM).astype(jnp.bfloat16)
    hidden = resident + jnp.dot(mixed_low, output_full, preferred_element_type=jnp.float32)
    normed_two, inverse_two, moe_in = norm_forward(hidden, moe_gains.astype(jnp.float32))
    router_logits = jnp.dot(moe_in, router_full, preferred_element_type=jnp.float32)
    choose = (routes[:, :, None] == jnp.arange(EXPERTS, dtype=jnp.int32)[None, None, :]).astype(
        jnp.float32
    )
    chosen = jnp.sum(choose * router_logits[:, None, :], axis=-1)
    gate_exps = jnp.exp(chosen - jnp.max(chosen, axis=-1, keepdims=True))
    gate_probs = gate_exps / jnp.sum(gate_exps, axis=-1, keepdims=True)
    entries = routes.reshape(-1)
    entry_count = entries.shape[0]
    onehot = (entries[:, None] == jnp.arange(EXPERTS, dtype=jnp.int32)[None, :]).astype(jnp.int32)
    position = jnp.sum((jnp.cumsum(onehot, axis=0) - 1) * onehot, axis=1)
    slot_index = entries * CAP + position
    owner_entry = (
        jnp.full((EXPERTS * CAP,), entry_count, jnp.int32)
        .at[slot_index]
        .set(jnp.arange(entry_count, dtype=jnp.int32))
    )
    padded_in = jnp.concatenate([moe_in, jnp.zeros((1, model_width), jnp.bfloat16)], axis=0)
    send_rows = jnp.take(padded_in, owner_entry // TOP, axis=0).reshape(EXPERTS, CAP, model_width)
    received = lax.all_to_all(send_rows, "expert", split_axis=0, concat_axis=0, tiled=True)
    slots_now = received.shape[1]
    grouped = received.reshape(owners, local_experts, slots_now, model_width)
    pair_proj = jnp.einsum("secd,edf->secf", grouped, expert_up, preferred_element_type=jnp.float32)
    activated = (jax.nn.silu(pair_proj[..., :FF]) * pair_proj[..., FF:]).astype(jnp.bfloat16)
    produced = jnp.einsum(
        "secf,edf->secd", activated, expert_down, preferred_element_type=jnp.float32
    ).astype(jnp.bfloat16)
    returned = lax.all_to_all(
        produced.reshape(EXPERTS, slots_now, model_width),
        "expert",
        split_axis=0,
        concat_axis=0,
        tiled=True,
    )
    returned, kept_rows, kept_pair = (
        returned,
        received,
        pair_proj.reshape(EXPERTS, slots_now, 2 * FF),
    )
    gathered = (
        jnp.take(returned.reshape(EXPERTS * CAP, model_width), slot_index, axis=0)
        .astype(jnp.float32)
        .reshape(length, TOP, model_width)
    )
    layer_out = (hidden + jnp.sum(gate_probs[:, :, None] * gathered, axis=1)).astype(jnp.bfloat16)
    grad_top = out_grad.astype(jnp.float32)
    gate_grad = jnp.sum(gathered * grad_top[:, None, :], axis=-1)
    chosen_grad = gate_probs * (gate_grad - jnp.sum(gate_probs * gate_grad, axis=-1, keepdims=True))
    logits_grad = jnp.sum(chosen_grad[:, :, None] * choose, axis=1)
    row_grads = (
        (gate_probs[:, :, None] * grad_top[:, None, :])
        .astype(jnp.bfloat16)
        .reshape(entry_count, model_width)
    )
    padded_grads = jnp.concatenate([row_grads, jnp.zeros((1, model_width), jnp.bfloat16)], axis=0)
    send_grads = jnp.take(padded_grads, owner_entry, axis=0).reshape(EXPERTS, CAP, model_width)
    grads_in = lax.all_to_all(send_grads, "expert", split_axis=0, concat_axis=0, tiled=True)
    grouped_rows = kept_rows.reshape(owners, local_experts, CAP, model_width)
    grouped_grads = grads_in.reshape(owners, local_experts, CAP, model_width)
    pair_kept = kept_pair.reshape(owners, local_experts, CAP, 2 * FF)
    gate_half = pair_kept[..., :FF]
    up_half = pair_kept[..., FF:]
    sigmoid_gate = jax.nn.sigmoid(gate_half)
    silu_gate = jax.nn.silu(gate_half)
    activated = (silu_gate * up_half).astype(jnp.bfloat16)
    act_grad = jnp.einsum(
        "secd,edf->secf", grouped_grads, expert_down, preferred_element_type=jnp.float32
    )
    pair_grad = jnp.concatenate(
        [
            act_grad * up_half * sigmoid_gate * (1.0 + gate_half * (1.0 - sigmoid_gate)),
            act_grad * silu_gate,
        ],
        axis=-1,
    ).astype(jnp.bfloat16)
    rows_back = jnp.einsum(
        "secf,edf->secd", pair_grad, expert_up, preferred_element_type=jnp.float32
    ).astype(jnp.bfloat16)
    up_grad = jnp.einsum(
        "secd,secf->edf", grouped_rows, pair_grad, preferred_element_type=jnp.float32
    )
    down_grad = jnp.einsum(
        "secd,secf->edf", grouped_grads, activated, preferred_element_type=jnp.float32
    )
    returned_grads = lax.all_to_all(
        rows_back.reshape(EXPERTS, CAP, model_width),
        "expert",
        split_axis=0,
        concat_axis=0,
        tiled=True,
    )
    expert_up_grad, expert_down_grad = (
        lax.psum_scatter(
            up_grad.astype(jnp.bfloat16), "dp", scatter_dimension=1, tiled=True
        ).astype(jnp.float32),
        lax.psum_scatter(
            down_grad.astype(jnp.bfloat16), "dp", scatter_dimension=1, tiled=True
        ).astype(jnp.float32),
    )
    token_grads = (
        jnp.take(returned_grads.reshape(EXPERTS * CAP, model_width), slot_index, axis=0)
        .astype(jnp.float32)
        .reshape(length, TOP, model_width)
    )
    router_wide = router_full.astype(jnp.float32)
    moe_grad = jnp.sum(token_grads, axis=1) + jnp.dot(logits_grad, router_wide.T, precision=HIGH)
    hidden_norm_grad, moe_gain_grad = norm_backward(
        moe_grad, normed_two, inverse_two, moe_gains.astype(jnp.float32)
    )
    hidden_grad = grad_top + hidden_norm_grad
    attn_out_grad = hidden_grad.astype(jnp.bfloat16)
    mixed_grad = (
        jnp.einsum("td,cd->tc", attn_out_grad, output_full, preferred_element_type=jnp.float32)
        .astype(jnp.bfloat16)
        .reshape(length, kv_heads, repeat, HEAD_DIM)
    )
    probs_grad = jnp.einsum(
        "ikrd,jkd->krij", mixed_grad, values_low, preferred_element_type=jnp.float32
    )
    values_grad = jnp.einsum(
        "krij,ikrd->jkd", probs_low, mixed_grad, preferred_element_type=jnp.float32
    )
    scores_grad = (
        attn_probs
        * (probs_grad - jnp.sum(attn_probs * probs_grad, axis=-1, keepdims=True))
        * score_scale
    ).astype(jnp.bfloat16)
    query_rot_grad = jnp.einsum(
        "krij,jkd->ikrd", scores_grad, keys_rot, preferred_element_type=jnp.float32
    ).reshape(length, query_heads, HEAD_DIM)
    keys_rot_grad = jnp.einsum(
        "krij,ikrd->jkd", scores_grad, query_rot, preferred_element_type=jnp.float32
    )
    query_low = (
        unrotate(query_rot_grad, cosine, sine_table)
        .reshape(length, query_heads * HEAD_DIM)
        .astype(jnp.bfloat16)
    )
    keyval_low = jnp.concatenate(
        [
            unrotate(keys_rot_grad, cosine, sine_table).reshape(length, kv_heads * HEAD_DIM),
            values_grad.reshape(length, kv_heads * HEAD_DIM),
        ],
        axis=1,
    ).astype(jnp.bfloat16)
    attn_in_grad = jnp.einsum(
        "tc,dc->td", query_low, query_full, preferred_element_type=jnp.float32
    ) + jnp.einsum("tc,dc->td", keyval_low, keyval_full, preferred_element_type=jnp.float32)
    token_norm_grad, attn_gain_grad = norm_backward(
        attn_in_grad, normed_one, inverse_one, attn_gains.astype(jnp.float32)
    )
    tokens_grad = hidden_grad + token_norm_grad
    slab_count = lax.axis_size("dp")
    slab_index = lax.axis_index("dp")
    width_rows = model_width // slab_count
    head_rows = query_heads * HEAD_DIM // slab_count
    all_attn, all_query, all_keyval, all_mixed, all_outgrad = (
        lax.all_gather(attn_in, "dp", axis=0, tiled=True),
        lax.all_gather(query_low, "dp", axis=0, tiled=True),
        lax.all_gather(keyval_low, "dp", axis=0, tiled=True),
        lax.all_gather(mixed_low, "dp", axis=0, tiled=True),
        lax.all_gather(attn_out_grad, "dp", axis=0, tiled=True),
    )
    all_moe, all_logits, attn_gain_rows, moe_gain_rows = (
        lax.all_gather(
            moe_in.astype(jnp.float32).astype(jnp.bfloat16), "dp", axis=0, tiled=True
        ).astype(jnp.float32),
        lax.all_gather(logits_grad.astype(jnp.bfloat16), "dp", axis=0, tiled=True).astype(
            logits_grad.dtype
        ),
        lax.all_gather(
            attn_gain_grad[None, :].astype(jnp.bfloat16), "dp", axis=0, tiled=True
        ).astype(jnp.float32),
        lax.all_gather(
            moe_gain_grad[None, :].astype(jnp.bfloat16), "dp", axis=0, tiled=True
        ).astype(jnp.float32),
    )
    attn_cols = lax.dynamic_slice_in_dim(all_attn, slab_index * width_rows, width_rows, 1)
    mixed_cols = lax.dynamic_slice_in_dim(all_mixed, slab_index * head_rows, head_rows, 1)
    moe_cols = lax.dynamic_slice_in_dim(all_moe, slab_index * width_rows, width_rows, 1)
    query_part = jnp.einsum("td,tc->dc", attn_cols, all_query, preferred_element_type=jnp.float32)
    keyval_part = jnp.einsum("td,tc->dc", attn_cols, all_keyval, preferred_element_type=jnp.float32)
    output_part = jnp.einsum(
        "tc,td->cd", mixed_cols, all_outgrad, preferred_element_type=jnp.float32
    )
    router_part = jnp.dot(moe_cols.T, all_logits, precision=HIGH)
    attn_gain_part = lax.dynamic_slice_in_dim(
        jnp.sum(attn_gain_rows, axis=0), slab_index * width_rows, width_rows, 0
    )
    moe_gain_part = lax.dynamic_slice_in_dim(
        jnp.sum(moe_gain_rows, axis=0), slab_index * width_rows, width_rows, 0
    )
    query_share, keyval_share, output_share, router_share, attn_share, moe_share = (
        lax.psum_scatter(
            query_part.astype(jnp.bfloat16), "expert", scatter_dimension=0, tiled=True
        ).astype(jnp.float32),
        lax.psum_scatter(
            keyval_part.astype(jnp.bfloat16), "expert", scatter_dimension=0, tiled=True
        ).astype(jnp.float32),
        lax.psum_scatter(
            output_part.astype(jnp.bfloat16), "expert", scatter_dimension=0, tiled=True
        ).astype(jnp.float32),
        lax.psum_scatter(
            router_part.astype(jnp.bfloat16), "expert", scatter_dimension=0, tiled=True
        ).astype(jnp.float32),
        lax.psum_scatter(
            attn_gain_part.astype(jnp.bfloat16), "expert", scatter_dimension=0, tiled=True
        ).astype(jnp.float32),
        lax.psum_scatter(
            moe_gain_part.astype(jnp.bfloat16), "expert", scatter_dimension=0, tiled=True
        ).astype(jnp.float32),
    )
    return (
        layer_out,
        tokens_grad,
        query_share,
        keyval_share,
        output_share,
        router_share,
        attn_share,
        moe_share,
        expert_up_grad,
        expert_down_grad,
    )


LANES = 128
TAIL = 16
PIECE_LIMIT = 4096
VMEM_BYTES = 60 * 1024 * 1024
F32 = jnp.float32
LOW = jnp.bfloat16


def contract(left, right, left_dim, right_dim):
    return lax.dot_general(
        left, right, (((left_dim,), (right_dim,)), ((), ())), preferred_element_type=F32
    )


def lane_index(shape):
    return lax.broadcasted_iota(jnp.int32, shape, len(shape) - 1)


def row_index(shape):
    return lax.broadcasted_iota(jnp.int32, shape, len(shape) - 2)


def half_turn(chunk):
    first = lane_index(chunk.shape) % HEAD_DIM < HEAD_DIM // 2
    ahead = pltpu.roll(chunk, LANES - HEAD_DIM // 2, 1)
    behind = pltpu.roll(chunk, HEAD_DIM // 2, 1)
    return jnp.where(first, ahead, behind)


def both_heads(chunk, pick):
    swapped = pltpu.roll(chunk, HEAD_DIM, 1)
    first = lane_index(chunk.shape) < HEAD_DIM
    if pick == 0:
        return jnp.where(first, chunk, swapped)
    return jnp.where(first, swapped, chunk)


def split_heads(chunk):
    first = lane_index(chunk.shape) < HEAD_DIM
    zero = jnp.zeros_like(chunk)
    return jnp.concatenate([jnp.where(first, chunk, zero), jnp.where(first, zero, chunk)], axis=0)


def join_heads(stacked):
    length = stacked.shape[0] // 2
    top, bottom = stacked[:length], stacked[length:]
    return jnp.where(lane_index(top.shape) < HEAD_DIM, top, bottom)


def three_parts(values):
    high = values.astype(LOW).astype(F32)
    rest = values - high
    middle = rest.astype(LOW).astype(F32)
    return (high, middle, rest - middle)


def gain_select():
    shape = (8, LANES)
    return (lane_index(shape) == EXPERTS + row_index(shape)) & (row_index(shape) < 2)


def load_weights(rows_ref, spots, piece_refs, weights, sems):
    copies = []
    for spot, piece in zip(spots, piece_refs):
        for i, (p, w) in enumerate(spot):
            size = piece.shape[1]
            start = pl.multiple_of(rows_ref[p, w] * size, size)
            copies.append(
                pltpu.make_async_copy(piece.at[i], weights.at[pl.ds(start, size)], sems.at[p, w])
            )
    for copy in copies:
        copy.start()
    return copies


def store_sums(rows_ref, sums, grads_even, grads_odd, sems):
    copies = []
    for p in range(2 * grads_even.shape[0]):
        target = grads_even if p % 2 == 0 else grads_odd
        for w in range(target.shape[1]):
            size = target.shape[2]
            start = pl.multiple_of(rows_ref[p, w] * size, size)
            copies.append(
                pltpu.make_async_copy(
                    sums.at[pl.ds(start, size)], target.at[p // 2, w], sems.at[p, w]
                )
            )
    for copy in copies:
        copy.start()
    return copies


def softmax_rows(q_pair, k_both, visible):
    scores = contract(q_pair, k_both, 1, 1) * (HEAD_DIM ** (-0.5))
    logits = jnp.where(visible, scores, MASKED)
    exps = jnp.exp(logits - jnp.max(logits, axis=-1, keepdims=True))
    return exps / jnp.sum(exps, axis=-1, keepdims=True)


def segment_tables(seg_row, frequency):
    length = seg_row.shape[1]
    shape = (length, length)
    across_row = jnp.broadcast_to(seg_row.astype(F32), shape)
    down_col = across_row.T
    seen = (down_col == across_row) & (lane_index(shape) <= row_index(shape))
    visible = jnp.concatenate([seen, seen], axis=0)
    if frequency is None:
        return visible
    earlier = jnp.sum(jnp.where(across_row < down_col, 1.0, 0.0), axis=1, keepdims=True)
    angles = (row_index(shape).astype(F32) - earlier) * frequency
    sine = jnp.sin(angles)
    first = lane_index(shape) % HEAD_DIM < HEAD_DIM // 2
    return (visible, jnp.cos(angles), jnp.where(first, -sine, sine))


def attn_forward_kernel(spots, *refs):
    count = len(spots)
    rows_ref, tokens_ref, seg_row, frequency = refs[:4]
    pieces = refs[4 : 4 + count]
    query_ref, keyval_ref, mixed_ref, tail_ref, cos_ref, sin_ref, weights, sems = refs[4 + count :]
    copies = load_weights(rows_ref, spots, pieces, weights, sems)
    tokens = tokens_ref[...].astype(F32)
    inverse = lax.rsqrt(jnp.mean(tokens * tokens, axis=-1, keepdims=True) + EPS)
    normed = tokens * inverse
    width = tokens.shape[1]
    visible, cosine, sine = segment_tables(seg_row[...], frequency[...])
    cos_ref[...] = cosine
    sin_ref[...] = sine
    for copy in copies:
        copy.wait()
    tail = weights[:, 2 * width :]
    tail_ref[...] = tail
    gains = contract(gain_select().astype(F32).astype(LOW), tail, 1, 1)
    attn_in = (normed * gains[0:1]).astype(LOW)
    keyval = contract(attn_in, weights[:, width : 2 * width], 1, 0)
    query = contract(attn_in, weights[:, :width], 1, 0)
    half = width // 2
    for m in range(half // LANES):
        keys = keyval[:, m * LANES : (m + 1) * LANES]
        keys = (keys * cosine + half_turn(keys) * sine).astype(LOW)
        values = keyval[:, half + m * LANES : half + (m + 1) * LANES].astype(LOW)
        keyval_ref[:, m * LANES : (m + 1) * LANES] = keys
        keyval_ref[:, half + m * LANES : half + (m + 1) * LANES] = values
        for pick in range(2):
            k_both = both_heads(keys.astype(F32), pick).astype(LOW)
            v_both = both_heads(values.astype(F32), pick).astype(LOW)
            chunk = slice((2 * m + pick) * LANES, (2 * m + pick + 1) * LANES)
            queries = query[:, chunk]
            queries = (queries * cosine + half_turn(queries) * sine).astype(LOW)
            query_ref[:, chunk] = queries
            q_pair = split_heads(queries.astype(F32)).astype(LOW)
            probs = softmax_rows(q_pair, k_both, visible).astype(LOW)
            mixed_ref[:, chunk] = join_heads(contract(probs, v_both, 1, 0)).astype(LOW)


def router_kernel(spots, *refs):
    count = len(spots)
    rows_ref, tokens_ref, mixed_ref, tail_ref, routes_t = refs[:5]
    pieces = refs[5 : 5 + count]
    payload, hidden_ref, gates_ref, weights, sems = refs[5 + count :]
    copies = load_weights(rows_ref, spots, pieces, weights, sems)
    tokens = tokens_ref[...].astype(F32)
    length = tokens.shape[0]
    tail = tail_ref[...]
    gains = contract(gain_select().astype(F32).astype(LOW), tail, 1, 1)
    for copy in copies:
        copy.wait()
    hidden = tokens + contract(mixed_ref[...], weights[...], 1, 0)
    hidden_ref[...] = hidden
    inverse_two = lax.rsqrt(jnp.mean(hidden * hidden, axis=-1, keepdims=True) + EPS)
    moe_in = (hidden * inverse_two * gains[1:2]).astype(LOW)
    payload[:length] = moe_in
    logits = contract(moe_in, tail, 1, 0)
    turned = routes_t[...]
    experts = row_index((LANES, length))
    chosen = experts == turned[0:1]
    for k in range(1, TOP):
        chosen = chosen | (experts == turned[k : k + 1])
    chosen = jnp.where(chosen, 1.0, 0.0).T > 0.5
    logits = jnp.where(chosen, logits, MASKED)
    exps = jnp.where(chosen, jnp.exp(logits - jnp.max(logits, axis=-1, keepdims=True)), 0.0)
    gates = exps / jnp.sum(exps, axis=-1, keepdims=True)
    gates_ref[...] = gates
    gates_t = gates.T
    for k in range(TOP):
        row = turned[k : k + 1]
        gate = jnp.sum(jnp.where(experts == row, gates_t, 0.0), axis=0, keepdims=True)
        high, middle, rest = three_parts(gate)
        place = row_index((TAIL, length))
        block = jnp.where(place == 0, high, jnp.where(place == 1, middle, jnp.where(place == 2, rest, 0.0)))
        block = jnp.where(place == 3, row.astype(F32), block)
        payload[length:, k * length : (k + 1) * length] = block.astype(LOW)


def slot_places(first_expert, local, tails, before):
    length = tails[0].shape[1] // TOP
    ids = row_index((8, length))
    ids = jnp.where(ids < local, ids + first_expert, -1).astype(F32)
    masks, gates = [], []
    for tail in tails:
        mask = jnp.zeros((8, length), F32)
        gate = jnp.zeros((8, length), F32)
        for k in range(TOP):
            part = tail[:, k * length : (k + 1) * length].astype(F32)
            hit = part[3:4] == ids
            mask = jnp.where(hit, 1.0, mask)
            gate = jnp.where(hit, part[0:1] + part[1:2] + part[2:3], gate)
        masks.append(mask)
        gates.append(gate)
    pairs = range(0, len(tails), 2)
    mask = jnp.concatenate([jnp.concatenate(masks[i : i + 2], axis=1) for i in pairs], axis=0)
    gate = jnp.concatenate([jnp.concatenate(gates[i : i + 2], axis=1) for i in pairs], axis=0)
    place = contract(mask.astype(LOW), before, 1, 0)
    return (jnp.where(mask > 0, place, -1.0), gate)


def gather_pair(local, block, pair, place, gate, row_pair, grad_pair, out):
    rows_out, grads_out, select_out, gate_out = out
    slots = row_index((block, place.shape[1])).astype(F32)
    parts = []
    for j in range(local):
        hit = slots == place[j : j + 1]
        parts.append(jnp.where(hit, 1.0, 0.0))
        held = jnp.where(hit, gate[j : j + 1], 0.0)
        held = jnp.sum(held, axis=1, keepdims=True)
        gate_out[j, pair * block : (pair + 1) * block] = jnp.broadcast_to(held, (block, LANES))
    select = jnp.concatenate(parts, axis=0).astype(LOW)
    if select_out is not None:
        select_out[pair] = select
    rows = contract(select, jnp.concatenate(row_pair, axis=0), 1, 0).astype(LOW)
    grads = contract(select, jnp.concatenate(grad_pair, axis=0), 1, 0).astype(LOW)
    for j in range(local):
        rows_out[j, pair * block : (pair + 1) * block] = rows[j * block : (j + 1) * block]
        grads_out[j, pair * block : (pair + 1) * block] = grads[j * block : (j + 1) * block]


def earlier_matrix(length):
    shape = (2 * length, 2 * length)
    return jnp.where(row_index(shape) < lane_index(shape), 1.0, 0.0).astype(LOW)


def expert_step(j, rows, grads, gate_ref, up, down):
    hidden_units = down.shape[1]
    pair = contract(rows[j], up, 1, 0)
    raw = contract(grads[j], down, 1, 0)
    gate_half, up_half = pair[:, :hidden_units], pair[:, hidden_units:]
    gate = gate_ref[j][:, 0:1]
    sigmoid = 1.0 / (1.0 + jnp.exp(-gate_half))
    silu = gate_half * sigmoid
    activated = silu * up_half
    scaled = (gate * activated).astype(LOW)
    act_grad = gate * raw
    pair_grad = jnp.concatenate(
        [act_grad * up_half * sigmoid * (1.0 + gate_half * (1.0 - sigmoid)), act_grad * silu],
        axis=1,
    ).astype(LOW)
    gate_grad = jnp.sum(activated * raw, axis=1, keepdims=True)
    return (scaled, pair_grad, gate_grad)


def fetch_experts(local, up_hbm, down_hbm, up, down, sems):
    copies = []
    for j in range(local):
        copies.append(
            (
                pltpu.make_async_copy(up_hbm.at[j], up.at[j], sems.at[0, j]),
                pltpu.make_async_copy(down_hbm.at[j], down.at[j], sems.at[1, j]),
            )
        )
        for copy in copies[j]:
            copy.start()
    return copies


def expert_home_kernel(owners, local, block, *refs):
    place_ref = refs[0]
    rows_in = refs[1 : 1 + owners]
    grads_in = refs[1 + owners : 1 + 2 * owners]
    up_hbm, down_hbm = refs[1 + 2 * owners : 3 + 2 * owners]
    back_even, back_odd = refs[3 + 2 * owners : 5 + 2 * owners]
    kept = refs[5 + 2 * owners : 10 + 2 * owners]
    scratch = refs[10 + 2 * owners :]
    up, down, rows, grads, select, gate_ref, scaled, pair_grads, returned, sems = scratch
    copies = fetch_experts(local, up_hbm, down_hbm, up, down, sems)
    length = rows_in[0].shape[0] - TAIL
    width = rows_in[0].shape[1]
    first_expert = place_ref[0] * local
    slab = kept[3].shape[2]
    columns = pl.ds(pl.multiple_of(place_ref[1] * slab, slab), slab)
    before = earlier_matrix(length)
    place, gate = slot_places(first_expert, local, [ref[length:] for ref in rows_in], before)
    for s in range(owners // 2):
        gather_pair(
            local,
            block,
            s,
            place[8 * s : 8 * s + 8],
            gate[8 * s : 8 * s + 8],
            [rows_in[2 * s][:length], rows_in[2 * s + 1][:length]],
            [grads_in[2 * s][...], grads_in[2 * s + 1][...]],
            (rows, grads, select, gate_ref),
        )
    sent = [
        pltpu.make_async_copy(select, kept[0], sems.at[2, 0]),
        pltpu.make_async_copy(rows.at[:, :, columns], kept[3], sems.at[2, 1]),
        pltpu.make_async_copy(grads.at[:, :, columns], kept[4], sems.at[2, 2]),
    ]
    for copy in sent:
        copy.start()
    for j in range(local):
        for copy in copies[j]:
            copy.wait()
    for j in range(local):
        made, pair_grad, gate_grad = expert_step(j, rows, grads, gate_ref, up[j], down[j])
        scaled[j] = made
        pair_grads[j] = pair_grad
        sent.append(pltpu.make_async_copy(scaled.at[j], kept[1].at[j], sems.at[3, j]))
        sent.append(pltpu.make_async_copy(pair_grads.at[j], kept[2].at[j], sems.at[4, j]))
        sent[-2].start()
        sent[-1].start()
        returned[j, :, :width] = contract(pair_grad, up[j], 1, 1).astype(LOW)
        lanes = lane_index((made.shape[0], LANES)) - first_expert - j
        high, middle, rest = three_parts(gate_grad)
        tail = jnp.where(lanes == 0, high, 0.0)
        tail = jnp.where(lanes == EXPERTS, middle, tail)
        tail = jnp.where(lanes == 2 * EXPERTS, rest, tail)
        returned[j, :, width:] = tail.astype(LOW)
    for s in range(owners // 2):
        span = slice(s * block, (s + 1) * block)
        back = jnp.concatenate([returned[j, span] for j in range(local)], axis=0)
        back = contract(select[s], back, 0, 0).astype(LOW)
        back_even[s] = back[:length]
        back_odd[s] = back[length:]
    for copy in sent:
        copy.wait()


def expert_finish_kernel(local, block, *refs):
    select, scaled, pair_grads, rows, grads, down = refs[:6]
    out_even, out_odd, up_grad, down_grad, produced = refs[6:]
    length = out_even.shape[1]
    for j in range(local):
        produced[j] = contract(scaled[j], down[j], 1, 1).astype(LOW)
        up_grad[j] = contract(rows[j], pair_grads[j], 0, 0)
        down_grad[j] = contract(grads[j], scaled[j], 0, 0)
    for s in range(out_even.shape[0]):
        span = slice(s * block, (s + 1) * block)
        made = jnp.concatenate([produced[j, span] for j in range(local)], axis=0)
        made = contract(select[s], made, 0, 0).astype(LOW)
        out_even[s] = made[:length]
        out_odd[s] = made[length:]


def expert_away_kernel(start, count, block, chips, far, *refs):
    place_ref = refs[0]
    rows_in = refs[1 : 3 + 2 * chips]
    grads_in = refs[3 + 2 * chips : 3 + 4 * chips]
    up_hbm, down_hbm, up_first, down_first = refs[3 + 4 * chips : 7 + 4 * chips]
    up_grad, down_grad = refs[7 + 4 * chips : 9 + 4 * chips]
    scratch = refs[9 + 4 * chips :]
    up, down, up_sum, down_sum, rows_buf, grads_buf, rows, grads, gate_ref, sems, pair_sems = scratch
    length = grads_buf.shape[1] // 2
    tall = length + TAIL
    pairs = []
    for i in range(far + 1):
        for s in range(chips):
            spot = len(pairs)
            copies = []
            for side in range(2):
                grad_from = grads_in[2 * s + side].at[pl.ds(i * length, length)]
                if i == 0:
                    row_from = rows_in[side].at[s]
                else:
                    row_from = rows_in[2 + 2 * s + side].at[pl.ds((i - 1) * tall, tall)]
                row_to = rows_buf.at[spot, pl.ds(side * tall, tall)]
                grad_to = grads_buf.at[spot, pl.ds(side * length, length)]
                copies.append(pltpu.make_async_copy(row_from, row_to, pair_sems.at[0, side, spot]))
                copies.append(pltpu.make_async_copy(grad_from, grad_to, pair_sems.at[1, side, spot]))
            pairs.append(copies)
    for copies in pairs:
        for copy in copies:
            copy.start()
    held = []
    for j in range(count):
        held.append(
            [
                pltpu.make_async_copy(up_hbm.at[start + j], up.at[j], sems.at[0, j]),
                pltpu.make_async_copy(down_hbm.at[start + j], down.at[j], sems.at[1, j]),
                pltpu.make_async_copy(up_first.at[start + j], up_sum.at[j], sems.at[2, j]),
                pltpu.make_async_copy(down_first.at[start + j], down_sum.at[j], sems.at[3, j]),
            ]
        )
    for copies in held:
        for copy in copies:
            copy.start()
    first_expert = place_ref[0] * (up_hbm.shape[0]) + start
    slab = up_sum.shape[1]
    columns = pl.ds(pl.multiple_of(place_ref[1] * slab, slab), slab)
    before = earlier_matrix(length)
    for i, copies in enumerate(pairs):
        for copy in copies:
            copy.wait()
        tails = [rows_buf[i, length:tall], rows_buf[i, tall + length :]]
        place, gate = slot_places(first_expert, count, tails, before)
        gather_pair(
            count,
            block,
            i,
            place,
            gate,
            [rows_buf[i, :length], rows_buf[i, tall : tall + length]],
            [grads_buf[i]],
            (rows, grads, None, gate_ref),
        )
    for copies in held:
        for copy in copies:
            copy.wait()
    sent = []
    for j in range(count):
        scaled, pair_grad, _ = expert_step(j, rows, grads, gate_ref, up[j], down[j])
        up_sum[j] += contract(rows[j, :, columns], pair_grad, 0, 0)
        down_sum[j] += contract(grads[j, :, columns], scaled, 0, 0)
        sent.append(pltpu.make_async_copy(up_sum.at[j], up_grad.at[start + j], sems.at[4, j]))
        sent.append(pltpu.make_async_copy(down_sum.at[j], down_grad.at[start + j], sems.at[5, j]))
        sent[-2].start()
        sent[-1].start()
    for copy in sent:
        copy.wait()


def backward_kernel(spots, output_spots, shares, *refs):
    rows_ref, tokens_ref, seg_row, cos_ref, sin_ref, payload, hidden_ref = refs[:7]
    query_ref, keyval_ref, mixed_ref, gates_ref, out_grad_ref, tail_ref = refs[7:13]
    refs = refs[13:]
    back, refs = refs[:shares], refs[shares:]
    pieces, refs = refs[: len(spots)], refs[len(spots) :]
    output_pieces, refs = refs[: len(output_spots)], refs[len(output_spots) :]
    tokens_grad, grads_even, grads_odd = refs[:3]
    weights, output, sums, query_low, keyval_low, sems, output_sems, out_sems = refs[3:]
    output_copies = load_weights(rows_ref, output_spots, output_pieces, output, output_sems)
    copies = load_weights(rows_ref, spots, pieces, weights, sems)
    length, width = tokens_ref.shape
    half = width // 2
    columns = weights.shape[1]
    total = back[0][...].astype(F32)
    for share in back[1:]:
        total = total + share[...].astype(F32)
    parts = total[:, width:]
    lanes = lane_index(parts.shape)
    gate_grad = parts + pltpu.roll(parts, LANES - EXPERTS, 1) + pltpu.roll(parts, LANES - 2 * EXPERTS, 1)
    gate_grad = jnp.where(lanes < EXPERTS, gate_grad, 0.0)
    gates = gates_ref[...]
    logits_grad = gates * (gate_grad - jnp.sum(gates * gate_grad, axis=-1, keepdims=True))
    hidden = hidden_ref[...]
    inverse_two = lax.rsqrt(jnp.mean(hidden * hidden, axis=-1, keepdims=True) + EPS)
    normed_two = hidden * inverse_two
    tail = tail_ref[...]
    gains = contract(gain_select().astype(F32).astype(LOW), tail, 1, 1)
    high = logits_grad.astype(LOW)
    rest = (logits_grad - high.astype(F32)).astype(LOW)
    moe_grad = total[:, :width] + contract(high, tail, 1, 1) + contract(rest, tail, 1, 1)
    moe_gain_grad = jnp.sum(moe_grad * normed_two, axis=0, keepdims=True)
    scaled = moe_grad * gains[1:2]
    hidden_grad = out_grad_ref[...].astype(F32) + inverse_two * (
        scaled - normed_two * jnp.mean(scaled * normed_two, axis=-1, keepdims=True)
    )
    attn_out_grad = hidden_grad.astype(LOW)
    for copy in output_copies:
        copy.wait()
    mixed_grad = contract(attn_out_grad, output[...], 1, 1)
    sums[:, columns:] = contract(mixed_ref[...], attn_out_grad, 0, 0).astype(LOW)
    tokens = tokens_ref[...].astype(F32)
    inverse_one = lax.rsqrt(jnp.mean(tokens * tokens, axis=-1, keepdims=True) + EPS)
    normed_one = tokens * inverse_one
    cosine, sine = cos_ref[...], sin_ref[...]
    visible = segment_tables(seg_row[...], None)
    groups = range(width // LANES)
    chunks = [slice(g * LANES, (g + 1) * LANES) for g in groups]
    keys = [keyval_ref[:, chunks[m]].astype(F32) for m in range(half // LANES)]
    values = [keyval_ref[:, half + m * LANES : half + (m + 1) * LANES].astype(F32) for m in range(half // LANES)]
    k_both = [both_heads(keys[g // 2], g % 2).astype(LOW) for g in groups]
    v_both = [both_heads(values[g // 2], g % 2).astype(LOW) for g in groups]
    q_pair = [split_heads(query_ref[:, chunk].astype(F32)).astype(LOW) for chunk in chunks]
    probs = [softmax_rows(q_pair[g], k_both[g], visible) for g in groups]
    m_pair = [split_heads(mixed_grad[:, chunk]).astype(LOW) for chunk in chunks]
    probs_grad = [contract(m_pair[g], v_both[g], 1, 1) for g in groups]
    value_sides = [contract(probs[g].astype(LOW), m_pair[g], 0, 0) for g in groups]
    scores_grad = [
        (
            probs[g]
            * (probs_grad[g] - jnp.sum(probs[g] * probs_grad[g], axis=-1, keepdims=True))
            * (HEAD_DIM ** (-0.5))
        ).astype(LOW)
        for g in groups
    ]
    query_grad = [join_heads(contract(scores_grad[g], k_both[g], 1, 0)) for g in groups]
    key_sides = [contract(scores_grad[g], q_pair[g], 0, 0) for g in groups]
    for g in groups:
        turned = query_grad[g] * cosine - half_turn(query_grad[g]) * sine
        query_low[:, chunks[g]] = turned.astype(LOW)
    key_sides = [side + pltpu.roll(side, HEAD_DIM, 1) for side in key_sides]
    value_sides = [side + pltpu.roll(side, HEAD_DIM, 1) for side in value_sides]
    first = lane_index((length, LANES)) < HEAD_DIM
    for m in range(half // LANES):
        keys_grad = jnp.where(first, key_sides[2 * m], key_sides[2 * m + 1])
        values_grad = jnp.where(first, value_sides[2 * m], value_sides[2 * m + 1])
        turned = keys_grad * cosine - half_turn(keys_grad) * sine
        keyval_low[:, chunks[m]] = turned.astype(LOW)
        keyval_low[:, half + m * LANES : half + (m + 1) * LANES] = values_grad.astype(LOW)
    for copy in copies:
        copy.wait()
    attn_in_grad = contract(query_low[...], weights[:, :width], 1, 1) + contract(
        keyval_low[...], weights[:, width : 2 * width], 1, 1
    )
    attn_in = (normed_one * gains[0:1]).astype(LOW)
    sums[:, :width] = contract(attn_in, query_low[...], 0, 0).astype(LOW)
    sums[:, width : 2 * width] = contract(attn_in, keyval_low[...], 0, 0).astype(LOW)
    attn_gain_grad = jnp.sum(attn_in_grad * normed_one, axis=0, keepdims=True)
    place = row_index((8, width))
    gain_grads = jnp.where(place == 0, attn_gain_grad, jnp.where(place == 1, moe_gain_grad, 0.0))
    sums[:, 2 * width : columns] = (
        contract(payload[:length], high, 0, 0)
        + contract(gain_grads.astype(LOW), gain_select().astype(F32).astype(LOW), 0, 0)
    ).astype(LOW)
    out_copies = store_sums(rows_ref, sums, grads_even, grads_odd, out_sems)
    scaled = attn_in_grad * gains[0:1]
    tokens_grad[...] = hidden_grad + inverse_one * (
        scaled - normed_one * jnp.mean(scaled * normed_one, axis=-1, keepdims=True)
    )
    for copy in out_copies:
        copy.wait()


def swap(values, axis, size, distance):
    return lax.ppermute(values, axis, [(i, i ^ distance) for i in range(size)])


def across(values, distance, planes):
    return swap(values, "dp", planes, distance)


def aside(values, s, owners):
    return swap(values, "expert", owners, 2 * s)


def partner(values, owners):
    return swap(values, "expert", owners, 1)


def after(values, *earlier):
    return lax.optimization_barrier((values,) + earlier)[0]


def over_chips(values, owners):
    return [values] + [aside(values, s, owners) for s in range(1, owners // 2)]


def over_cores(near, owners, *earlier):
    pieces = []
    for piece in near:
        pieces += [piece, partner(after(piece, *earlier) if earlier else piece, owners)]
    return pieces


def chips_split(values, owners, *earlier):
    half = values.shape[0] // 2
    first, second = aside(values, 1, owners), aside(values, 2, owners)
    far = [first[:half], second[half:]]
    if earlier:
        far = [after(part, *earlier) for part in far]
    far = [aside(far[0], 2, owners), aside(far[1], 1, owners)]
    return [[values], [first], [second], far]


def core_pieces(groups, owners, *earlier):
    pieces, spots = [], []
    for group in groups:
        parts = [part for part, _ in group]
        merged = parts[0] if len(parts) == 1 else jnp.concatenate(parts, axis=0)
        merged = after(merged, *earlier) if earlier else merged
        for part, spot in group:
            pieces.append(part)
            spots.append(spot)
        pieces.append(partner(merged, owners))
        spots.append([(p + 1, w) for _, spot in group for p, w in spot])
    return (pieces, spots)


def core_pieces_whole(near, owners):
    pieces = []
    for parts in near:
        piece = parts[0] if len(parts) == 1 else jnp.concatenate(parts, axis=0)
        pieces.append((piece, partner(piece, owners)))
    return pieces


def added(left, right):
    return (left.astype(F32) + right.astype(F32)).astype(LOW)


def to_owners(even, odd, owners, *earlier):
    other = partner(odd, owners)
    joined = [added(even[s], other[s]) for s in range(owners // 2)]
    if earlier:
        joined = lax.optimization_barrier(tuple(joined) + earlier)[: owners // 2]
    sent = [joined[0]] + [aside(joined[s], s, owners) for s in range(1, owners // 2)]
    return (joined, sent)


def to_neighbours(joined, owners):
    half = joined[3].shape[0] // 2
    low_turn = aside(joined[3][:half], 1, owners)
    top_turn = aside(joined[3][half:], 2, owners)
    low_turn, top_turn = lax.optimization_barrier((low_turn, top_turn))
    first = jnp.concatenate([joined[1][:half], added(joined[1][half:], top_turn)], axis=0)
    second = jnp.concatenate([added(joined[2][:half], low_turn), joined[2][half:]], axis=0)
    return (first, second)


def from_neighbours(joined, first, second, owners):
    parts = [joined[0], aside(first, 1, owners), aside(second, 2, owners)]
    return sum(part.astype(F32) for part in parts).astype(LOW)


def over_planes_sum(parts, planes):
    total = parts[0].astype(F32)
    for w in range(1, planes):
        total = total + across(parts[w], w, planes).astype(F32)
    return total


def cost(us):
    return pl.CostEstimate(flops=int(us * 1153e6), bytes_accessed=0, transcendentals=0)


def params():
    return pltpu.CompilerParams(vmem_limit_bytes=VMEM_BYTES)


def whole_spec():
    return pl.BlockSpec(memory_space=pltpu.VMEM)


def hbm_spec():
    return pl.BlockSpec(memory_space=pl.ANY)


def smem_spec():
    return pl.BlockSpec(memory_space=pltpu.SMEM)


def on_device(
    planes,
    owners,
    tokens,
    segments,
    routes,
    query_weight,
    keyval_weight,
    output_weight,
    router_weight,
    attn_gain,
    moe_gain,
    expert_up,
    expert_down,
    out_grad,
):
    length, width = tokens.shape
    if planes != 4 or owners != 8 or planes * owners * length > PIECE_LIMIT:
        return on_device_wide(
            tokens,
            segments,
            routes,
            query_weight,
            keyval_weight,
            output_weight,
            router_weight,
            attn_gain,
            moe_gain,
            expert_up,
            expert_down,
            out_grad,
        )
    local = expert_up.shape[0]
    hidden_units = expert_down.shape[2]
    block = 2 * CAP
    slots = owners // 2 * block
    plane = lax.axis_index("dp")
    owner = lax.axis_index("expert")
    share = query_weight.shape[0]
    rows = (plane ^ jnp.arange(planes))[None, :] * owners + (owner ^ jnp.arange(owners))[:, None]
    rows = rows.astype(jnp.int32)
    place = jnp.stack([owner, plane]).astype(jnp.int32)
    extra = jnp.concatenate(
        [
            router_weight,
            attn_gain[:, None],
            moe_gain[:, None],
            jnp.zeros((share, LANES - EXPERTS - 2), LOW),
        ],
        axis=1,
    )
    packed = jnp.concatenate([query_weight, keyval_weight, extra, output_weight], axis=1)
    columns = packed.shape[1] - width

    early = [across(packed, w, planes) for w in range(1, planes)]
    grad_chips = over_chips(out_grad, owners)
    grad_cores = partner(jnp.concatenate(grad_chips, axis=0), owners)
    gathered = jnp.stack([packed] + early)
    grad_start = after(out_grad, *early)
    grad_planes = [across(grad_start, w, planes) for w in range(1, planes - 1)]
    grad_planes.append(across(after(out_grad, grad_planes[-1]), planes - 1, planes))
    near = chips_split(
        after(gathered[:, :, :columns], *grad_chips), owners, grad_planes[0]
    )
    every = list(range(planes))
    groups = [[(near[s][0], [(2 * s, w) for w in every])] for s in range(3)]
    groups += [
        [(near[3][0], [(6, w) for w in every[: planes // 2]])],
        [(near[3][1], [(6, w) for w in every[planes // 2 :]])],
    ]
    pieces, spots = core_pieces(groups, owners)
    output_near = over_chips(after(gathered[:, :, columns:], *pieces[:6], *near[3]), owners)

    half_dim = HEAD_DIM // 2
    frequency = ROPE_BASE ** (-(jnp.arange(half_dim, dtype=F32) * 2.0) / HEAD_DIM)
    frequency = jnp.tile(frequency, LANES // half_dim)[None, :]

    token_low = jax.ShapeDtypeStruct((length, width), LOW)
    token_wide = jax.ShapeDtypeStruct((length, width), F32)
    table = jax.ShapeDtypeStruct((length, LANES), F32)
    query_rot, keyval_low, mixed_low, tail, cosine, sine = pl.pallas_call(
        functools.partial(attn_forward_kernel, spots),
        out_shape=(token_low, token_low, token_low, jax.ShapeDtypeStruct((width, LANES), LOW))
        + (table, table),
        in_specs=[smem_spec()] + [whole_spec()] * 3 + [hbm_spec()] * len(pieces),
        out_specs=[whole_spec()] * 6,
        scratch_shapes=[
            pltpu.VMEM((width, columns), LOW),
            pltpu.SemaphoreType.DMA((owners, planes)),
        ],
        compiler_params=params(),
        cost_estimate=cost(6),
        name="attn_forward",
    )(rows, after(tokens, *grad_planes[1:]), segments, frequency, *pieces)

    output_pieces, output_spots = core_pieces(
        [[(output_near[s], [(2 * s, w) for w in every])] for s in range(owners // 2)],
        owners,
        mixed_low,
    )

    grad_stack = jnp.concatenate(grad_planes, axis=0)

    payload, hidden, gates = pl.pallas_call(
        functools.partial(router_kernel, output_spots),
        out_shape=(
            jax.ShapeDtypeStruct((length + TAIL, width), LOW),
            token_wide,
            jax.ShapeDtypeStruct((length, LANES), F32),
        ),
        in_specs=[smem_spec()] + [whole_spec()] * 4 + [hbm_spec()] * len(output_pieces),
        out_specs=[whole_spec()] * 3,
        scratch_shapes=[
            pltpu.VMEM((width, width), LOW),
            pltpu.SemaphoreType.DMA((owners, planes)),
        ],
        compiler_params=params(),
        cost_estimate=cost(4),
        name="router",
    )(
        rows,
        tokens,
        mixed_low,
        tail,
        routes.T,
        *output_pieces,
    )

    row_chips = over_chips(payload, owners)
    row_home = over_cores(row_chips, owners)
    grad_other = partner(after(grad_stack, payload), owners)
    row_start = after(payload, row_home[1])
    row_planes = [across(row_start, w, planes) for w in range(2, planes)]
    row_near = across(jnp.stack(row_chips), 1, planes)
    grad_direct = after(grad_stack, *row_chips)
    grad_near = [aside(grad_direct, s, owners) for s in (1, 2)]

    def all_of(shape):
        return pl.BlockSpec(shape, lambda i: (0,) * len(shape))

    slab = width // planes
    slabs = (
        jax.ShapeDtypeStruct((local, slab, 2 * hidden_units), F32),
        jax.ShapeDtypeStruct((local, slab, hidden_units), F32),
    )
    home_blocks = [s * (p % 2) for s in range(owners // 2) for p in range(2)]
    grad_home = [part for s in range(owners // 2) for part in (grad_chips[s], grad_cores)]
    chip_rows = jax.ShapeDtypeStruct((owners // 2, length, width), LOW)
    chip_back = jax.ShapeDtypeStruct((owners // 2, length, width + LANES), LOW)
    back_even, back_odd, *kept = pl.pallas_call(
        functools.partial(expert_home_kernel, owners, local, block),
        grid=(1,),
        out_shape=(
            chip_back,
            chip_back,
            jax.ShapeDtypeStruct((owners // 2, local * block, 2 * length), LOW),
            jax.ShapeDtypeStruct((local, slots, hidden_units), LOW),
            jax.ShapeDtypeStruct((local, slots, 2 * hidden_units), LOW),
            jax.ShapeDtypeStruct((local, slots, slab), LOW),
            jax.ShapeDtypeStruct((local, slots, slab), LOW),
        ),
        in_specs=[smem_spec()]
        + [all_of((length + TAIL, width))] * owners
        + [pl.BlockSpec((length, width), lambda i, s=s: (s, 0)) for s in home_blocks]
        + [hbm_spec()] * 2,
        out_specs=[all_of(chip_back.shape)] * 2 + [hbm_spec()] * 5,
        scratch_shapes=[
            pltpu.VMEM(expert_up.shape, LOW),
            pltpu.VMEM(expert_down.shape, LOW),
            pltpu.VMEM((local, slots, width), LOW),
            pltpu.VMEM((local, slots, width), LOW),
            pltpu.VMEM((owners // 2, local * block, 2 * length), LOW),
            pltpu.VMEM((local, slots, LANES), F32),
            pltpu.VMEM((local, slots, hidden_units), LOW),
            pltpu.VMEM((local, slots, 2 * hidden_units), LOW),
            pltpu.VMEM((local, slots, width + LANES), LOW),
            pltpu.SemaphoreType.DMA((5, local)),
        ],
        compiler_params=params(),
        cost_estimate=cost(18),
        name="expert_home",
    )(place, *row_home, *grad_home, expert_up, expert_down)
    out_even, out_odd, up_grad, down_grad = pl.pallas_call(
        functools.partial(expert_finish_kernel, local, block),
        out_shape=(chip_rows, chip_rows) + slabs,
        in_specs=[whole_spec()] * 6,
        out_specs=[whole_spec()] * 4,
        scratch_shapes=[pltpu.VMEM((local, slots, width), LOW)],
        compiler_params=params(),
        cost_estimate=cost(8),
        name="expert_finish",
    )(*kept, expert_down)

    joined, back = to_owners(back_even, after(back_odd, *grad_near, *row_planes), owners)
    row_stack = jnp.concatenate(row_planes, axis=0)
    row_far = chips_split(after(row_stack, *back), owners)
    grad_away = [grad_stack, grad_other]
    grad_away += over_cores(grad_near, owners, *back)
    row_own = partner(after(row_stack, *joined), owners)

    def expert_away(start, count, place, up_grad, down_grad):
        chips = owners // 2
        pairs = chips * (planes - 1)
        return pl.pallas_call(
            functools.partial(
                expert_away_kernel, start, count, block, chips, planes - 2
            ),
            out_shape=slabs,
            in_specs=[smem_spec()] + [hbm_spec()] * (6 + 4 * chips),
            out_specs=[hbm_spec()] * 2,
            scratch_shapes=[
                pltpu.VMEM((count,) + expert_up.shape[1:], LOW),
                pltpu.VMEM((count,) + expert_down.shape[1:], LOW),
                pltpu.VMEM((count,) + slabs[0].shape[1:], F32),
                pltpu.VMEM((count,) + slabs[1].shape[1:], F32),
                pltpu.VMEM((pairs, 2 * (length + TAIL), width), LOW),
                pltpu.VMEM((pairs, 2 * length, width), LOW),
                pltpu.VMEM((count, pairs * block, width), LOW),
                pltpu.VMEM((count, pairs * block, width), LOW),
                pltpu.VMEM((count, pairs * block, LANES), F32),
                pltpu.SemaphoreType.DMA((6, count)),
                pltpu.SemaphoreType.DMA((2, 2, pairs)),
            ],
            input_output_aliases={5 + 4 * chips: 0, 6 + 4 * chips: 1},
            compiler_params=params(),
            cost_estimate=cost(7 * count),
            name="expert_away",
        )(place, *row_away, *grad_away, expert_up, expert_down, up_grad, down_grad)

    def share_pieces(wide):
        return jax.ShapeDtypeStruct((owners // 2, planes, share, wide), LOW)

    wide = columns + width
    tokens_grad, grads_even, grads_odd = pl.pallas_call(
        functools.partial(backward_kernel, spots, output_spots, owners // 2),
        out_shape=(token_wide, share_pieces(wide), share_pieces(wide)),
        in_specs=[smem_spec()]
        + [whole_spec()] * (12 + owners // 2)
        + [hbm_spec()] * (len(pieces) + len(output_pieces)),
        out_specs=[whole_spec()] + [hbm_spec()] * 2,
        scratch_shapes=[
            pltpu.VMEM((width, columns), LOW),
            pltpu.VMEM((width, width), LOW),
            pltpu.VMEM((width, wide), LOW),
            pltpu.VMEM((length, width), LOW),
            pltpu.VMEM((length, width), LOW),
            pltpu.SemaphoreType.DMA((owners, planes)),
            pltpu.SemaphoreType.DMA((owners, planes)),
            pltpu.SemaphoreType.DMA((owners, planes)),
        ],
        compiler_params=params(),
        cost_estimate=cost(17),
        name="backward",
    )(
        rows,
        tokens,
        segments,
        cosine,
        sine,
        payload,
        after(hidden, row_own, grad_other, out_even),
        query_rot,
        keyval_low,
        mixed_low,
        gates,
        out_grad,
        tail,
        *back,
        *pieces,
        *output_pieces,
    )

    grads_other = partner(
        after(grads_odd, row_near, row_far[1][0], row_far[2][0], *grad_away[3::2]), owners
    )
    half = grad_stack.shape[0] // 2
    grad_turn = [
        aside(after(grad_near[0][:half], tokens_grad), 2, owners),
        aside(after(grad_near[1][half:], tokens_grad), 1, owners),
    ]
    shares = [added(grads_even[s], grads_other[s]) for s in range(owners // 2)]
    grad_away += over_cores([jnp.concatenate(grad_turn, axis=0)], owners, shares[0])
    row_away = over_cores([row_near], owners, shares[0]) + [row_stack, row_own]
    row_away += over_cores(
        [jnp.concatenate(parts, axis=0) for parts in row_far[1:]], owners, shares[0]
    )
    first, second = to_neighbours(shares, owners)
    out_other = partner(after(out_odd, shares[0], *row_far[3], *grad_turn), owners)
    made = [added(out_even[s], out_other[s]) for s in range(owners // 2)]
    held = (first, second) + tuple(row_away[1::2]) + tuple(grad_away[7:]) + tuple(made)
    first, second = lax.optimization_barrier(held)[:2]
    far_made = aside(after(made[3], first), 3, owners)
    up_grad, down_grad = expert_away(0, 2, after(place, first, second), up_grad, down_grad)
    plane_sums = after(from_neighbours(shares, first, second, owners), up_grad, far_made)
    up_grad, down_grad = expert_away(2, 2, after(place, plane_sums), up_grad, down_grad)
    made = lax.optimization_barrier(tuple(made) + (plane_sums,))[: owners // 2]
    near_made = [aside(made[s], s, owners) for s in (1, 2)]
    summed = over_planes_sum(plane_sums, planes)
    made = [made[0]] + near_made + [far_made]
    layer_out = (hidden + sum(part.astype(F32) for part in made)).astype(LOW)

    return (
        layer_out,
        tokens_grad,
        summed[:, :width],
        summed[:, width : 2 * width],
        summed[:, columns:],
        summed[:, 2 * width : 2 * width + EXPERTS],
        summed[:, 2 * width + EXPERTS],
        summed[:, 2 * width + EXPERTS + 1],
        up_grad,
        down_grad,
    )


def solution(mesh):
    return jax.shard_map(
        functools.partial(on_device, mesh.shape["dp"], mesh.shape["expert"]),
        mesh=mesh,
        in_specs=(
            P(("dp", "expert"), None),
            P(("dp", "expert"), None),
            P(("dp", "expert"), None),
            P(("dp", "expert"), None),
            P(("dp", "expert"), None),
            P(("dp", "expert"), None),
            P(("dp", "expert"), None),
            P(("dp", "expert")),
            P(("dp", "expert")),
            P("expert", None, None),
            P("expert", None, None),
            P(("dp", "expert"), None),
        ),
        out_specs=(
            P(("dp", "expert"), None),
            P(("dp", "expert"), None),
            P(("dp", "expert"), None),
            P(("dp", "expert"), None),
            P(("dp", "expert"), None),
            P(("dp", "expert"), None),
            P(("dp", "expert")),
            P(("dp", "expert")),
            P("expert", "dp", None),
            P("expert", "dp", None),
        ),
        check_vma=False,
    )
```

```python
import functools

import jax
import jax.numpy as jnp
from jax import lax
from jax.sharding import PartitionSpec as P
from jax.experimental import pallas as pl
from jax.experimental.pallas import tpu as pltpu

HEAD_DIM = 64
FF = 512
EXPERTS = 32
TOP = 8
CAP = 40


EPS = 1e-05
ROPE_BASE = 10000.0
MASKED = -1e30
HIGH = lax.Precision.HIGHEST


def norm_forward(values, gain_vec):
    inverse = lax.rsqrt(jnp.mean(values * values, axis=-1, keepdims=True) + EPS)
    normed = values * inverse
    return (normed, inverse, (normed * gain_vec).astype(jnp.bfloat16))


def norm_backward(grad_out, normed, inverse, gain_vec):
    gain_grad = jnp.sum(grad_out * normed, axis=0)
    scaled = grad_out * gain_vec
    grad_in = inverse * (scaled - normed * jnp.mean(scaled * normed, axis=-1, keepdims=True))
    return (grad_in, gain_grad)


def rope_tables(segment_row):
    length = segment_row.shape[0]
    earlier = jnp.sum((segment_row[None, :] < segment_row[:, None]).astype(jnp.int32), axis=1)
    position = jnp.arange(length, dtype=jnp.int32) - earlier
    half_dim = HEAD_DIM // 2
    frequency = ROPE_BASE ** (-(jnp.arange(half_dim, dtype=jnp.float32) * 2.0) / HEAD_DIM)
    angles = position.astype(jnp.float32)[:, None] * frequency[None, :]
    cosine = jnp.concatenate([jnp.cos(angles), jnp.cos(angles)], axis=-1)[:, None, :]
    sine_table = jnp.concatenate([jnp.sin(angles), jnp.sin(angles)], axis=-1)[:, None, :]
    return (cosine, sine_table)


def rotate(values, cosine, sine_table):
    half_dim = values.shape[-1] // 2
    turned = jnp.concatenate([-values[..., half_dim:], values[..., :half_dim]], axis=-1)
    return values * cosine + turned * sine_table


def unrotate(grad_rows, cosine, sine_table):
    half_dim = grad_rows.shape[-1] // 2
    weighted = grad_rows * sine_table
    turned = jnp.concatenate([weighted[..., half_dim:], -weighted[..., :half_dim]], axis=-1)
    return grad_rows * cosine + turned


def on_device_wide(
    tokens,
    segments,
    routes,
    query_weight,
    keyval_weight,
    output_weight,
    router_weight,
    attn_gain,
    moe_gain,
    expert_up,
    expert_down,
    out_grad,
):
    owners = lax.axis_size("expert")
    local_experts = expert_up.shape[0]
    length = tokens.shape[0]
    model_width = tokens.shape[1]
    kv_heads = keyval_weight.shape[1] // (2 * HEAD_DIM)
    query_heads = query_weight.shape[1] // HEAD_DIM
    repeat = query_heads // kv_heads
    score_scale = HEAD_DIM ** (-0.5)
    query_full, keyval_full, output_full, router_full, attn_gains, moe_gains = (
        lax.all_gather(query_weight, ("dp", "expert"), axis=0, tiled=True),
        lax.all_gather(keyval_weight, ("dp", "expert"), axis=0, tiled=True),
        lax.all_gather(output_weight, ("dp", "expert"), axis=0, tiled=True),
        lax.all_gather(router_weight, ("dp", "expert"), axis=0, tiled=True),
        lax.all_gather(attn_gain, ("dp", "expert"), axis=0, tiled=True),
        lax.all_gather(moe_gain, ("dp", "expert"), axis=0, tiled=True),
    )
    resident = tokens.astype(jnp.float32)
    normed_one, inverse_one, attn_in = norm_forward(resident, attn_gains.astype(jnp.float32))
    query_proj = jnp.dot(attn_in, query_full, preferred_element_type=jnp.float32).reshape(
        length, query_heads, HEAD_DIM
    )
    keyval_proj = jnp.dot(attn_in, keyval_full, preferred_element_type=jnp.float32)
    key_rows = keyval_proj[:, : kv_heads * HEAD_DIM].reshape(length, kv_heads, HEAD_DIM)
    value_rows = keyval_proj[:, kv_heads * HEAD_DIM :].reshape(length, kv_heads, HEAD_DIM)
    cosine, sine_table = rope_tables(segments[0])
    query_rot = (
        rotate(query_proj, cosine, sine_table)
        .astype(jnp.bfloat16)
        .reshape(length, kv_heads, repeat, HEAD_DIM)
    )
    keys_rot = rotate(key_rows, cosine, sine_table).astype(jnp.bfloat16)
    values_low = value_rows.astype(jnp.bfloat16)
    places = jnp.arange(length)
    visible = (segments[0][:, None] == segments[0][None, :]) & (places[None, :] <= places[:, None])
    scores = jnp.einsum("ikrd,jkd->krij", query_rot, keys_rot, preferred_element_type=jnp.float32)
    attn_logits = jnp.where(visible, scores * score_scale, MASKED)
    attn_exps = jnp.exp(attn_logits - jnp.max(attn_logits, axis=-1, keepdims=True))
    attn_probs = attn_exps / jnp.sum(attn_exps, axis=-1, keepdims=True)
    probs_low = attn_probs.astype(jnp.bfloat16)
    mixed_heads = jnp.einsum(
        "krij,jkd->ikrd", probs_low, values_low, preferred_element_type=jnp.float32
    )
    mixed_low = mixed_heads.reshape(length, query_heads * HEAD_DIM).astype(jnp.bfloat16)
    hidden = resident + jnp.dot(mixed_low, output_full, preferred_element_type=jnp.float32)
    normed_two, inverse_two, moe_in = norm_forward(hidden, moe_gains.astype(jnp.float32))
    router_logits = jnp.dot(moe_in, router_full, preferred_element_type=jnp.float32)
    choose = (routes[:, :, None] == jnp.arange(EXPERTS, dtype=jnp.int32)[None, None, :]).astype(
        jnp.float32
    )
    chosen = jnp.sum(choose * router_logits[:, None, :], axis=-1)
    gate_exps = jnp.exp(chosen - jnp.max(chosen, axis=-1, keepdims=True))
    gate_probs = gate_exps / jnp.sum(gate_exps, axis=-1, keepdims=True)
    entries = routes.reshape(-1)
    entry_count = entries.shape[0]
    onehot = (entries[:, None] == jnp.arange(EXPERTS, dtype=jnp.int32)[None, :]).astype(jnp.int32)
    position = jnp.sum((jnp.cumsum(onehot, axis=0) - 1) * onehot, axis=1)
    slot_index = entries * CAP + position
    owner_entry = (
        jnp.full((EXPERTS * CAP,), entry_count, jnp.int32)
        .at[slot_index]
        .set(jnp.arange(entry_count, dtype=jnp.int32))
    )
    padded_in = jnp.concatenate([moe_in, jnp.zeros((1, model_width), jnp.bfloat16)], axis=0)
    send_rows = jnp.take(padded_in, owner_entry // TOP, axis=0).reshape(EXPERTS, CAP, model_width)
    received = lax.all_to_all(send_rows, "expert", split_axis=0, concat_axis=0, tiled=True)
    slots_now = received.shape[1]
    grouped = received.reshape(owners, local_experts, slots_now, model_width)
    pair_proj = jnp.einsum("secd,edf->secf", grouped, expert_up, preferred_element_type=jnp.float32)
    activated = (jax.nn.silu(pair_proj[..., :FF]) * pair_proj[..., FF:]).astype(jnp.bfloat16)
    produced = jnp.einsum(
        "secf,edf->secd", activated, expert_down, preferred_element_type=jnp.float32
    ).astype(jnp.bfloat16)
    returned = lax.all_to_all(
        produced.reshape(EXPERTS, slots_now, model_width),
        "expert",
        split_axis=0,
        concat_axis=0,
        tiled=True,
    )
    returned, kept_rows, kept_pair = (
        returned,
        received,
        pair_proj.reshape(EXPERTS, slots_now, 2 * FF),
    )
    gathered = (
        jnp.take(returned.reshape(EXPERTS * CAP, model_width), slot_index, axis=0)
        .astype(jnp.float32)
        .reshape(length, TOP, model_width)
    )
    layer_out = (hidden + jnp.sum(gate_probs[:, :, None] * gathered, axis=1)).astype(jnp.bfloat16)
    grad_top = out_grad.astype(jnp.float32)
    gate_grad = jnp.sum(gathered * grad_top[:, None, :], axis=-1)
    chosen_grad = gate_probs * (gate_grad - jnp.sum(gate_probs * gate_grad, axis=-1, keepdims=True))
    logits_grad = jnp.sum(chosen_grad[:, :, None] * choose, axis=1)
    row_grads = (
        (gate_probs[:, :, None] * grad_top[:, None, :])
        .astype(jnp.bfloat16)
        .reshape(entry_count, model_width)
    )
    padded_grads = jnp.concatenate([row_grads, jnp.zeros((1, model_width), jnp.bfloat16)], axis=0)
    send_grads = jnp.take(padded_grads, owner_entry, axis=0).reshape(EXPERTS, CAP, model_width)
    grads_in = lax.all_to_all(send_grads, "expert", split_axis=0, concat_axis=0, tiled=True)
    grouped_rows = kept_rows.reshape(owners, local_experts, CAP, model_width)
    grouped_grads = grads_in.reshape(owners, local_experts, CAP, model_width)
    pair_kept = kept_pair.reshape(owners, local_experts, CAP, 2 * FF)
    gate_half = pair_kept[..., :FF]
    up_half = pair_kept[..., FF:]
    sigmoid_gate = jax.nn.sigmoid(gate_half)
    silu_gate = jax.nn.silu(gate_half)
    activated = (silu_gate * up_half).astype(jnp.bfloat16)
    act_grad = jnp.einsum(
        "secd,edf->secf", grouped_grads, expert_down, preferred_element_type=jnp.float32
    )
    pair_grad = jnp.concatenate(
        [
            act_grad * up_half * sigmoid_gate * (1.0 + gate_half * (1.0 - sigmoid_gate)),
            act_grad * silu_gate,
        ],
        axis=-1,
    ).astype(jnp.bfloat16)
    rows_back = jnp.einsum(
        "secf,edf->secd", pair_grad, expert_up, preferred_element_type=jnp.float32
    ).astype(jnp.bfloat16)
    up_grad = jnp.einsum(
        "secd,secf->edf", grouped_rows, pair_grad, preferred_element_type=jnp.float32
    )
    down_grad = jnp.einsum(
        "secd,secf->edf", grouped_grads, activated, preferred_element_type=jnp.float32
    )
    returned_grads = lax.all_to_all(
        rows_back.reshape(EXPERTS, CAP, model_width),
        "expert",
        split_axis=0,
        concat_axis=0,
        tiled=True,
    )
    expert_up_grad, expert_down_grad = (
        lax.psum_scatter(
            up_grad.astype(jnp.bfloat16), "dp", scatter_dimension=1, tiled=True
        ).astype(jnp.float32),
        lax.psum_scatter(
            down_grad.astype(jnp.bfloat16), "dp", scatter_dimension=1, tiled=True
        ).astype(jnp.float32),
    )
    token_grads = (
        jnp.take(returned_grads.reshape(EXPERTS * CAP, model_width), slot_index, axis=0)
        .astype(jnp.float32)
        .reshape(length, TOP, model_width)
    )
    router_wide = router_full.astype(jnp.float32)
    moe_grad = jnp.sum(token_grads, axis=1) + jnp.dot(logits_grad, router_wide.T, precision=HIGH)
    hidden_norm_grad, moe_gain_grad = norm_backward(
        moe_grad, normed_two, inverse_two, moe_gains.astype(jnp.float32)
    )
    hidden_grad = grad_top + hidden_norm_grad
    attn_out_grad = hidden_grad.astype(jnp.bfloat16)
    mixed_grad = (
        jnp.einsum("td,cd->tc", attn_out_grad, output_full, preferred_element_type=jnp.float32)
        .astype(jnp.bfloat16)
        .reshape(length, kv_heads, repeat, HEAD_DIM)
    )
    probs_grad = jnp.einsum(
        "ikrd,jkd->krij", mixed_grad, values_low, preferred_element_type=jnp.float32
    )
    values_grad = jnp.einsum(
        "krij,ikrd->jkd", probs_low, mixed_grad, preferred_element_type=jnp.float32
    )
    scores_grad = (
        attn_probs
        * (probs_grad - jnp.sum(attn_probs * probs_grad, axis=-1, keepdims=True))
        * score_scale
    ).astype(jnp.bfloat16)
    query_rot_grad = jnp.einsum(
        "krij,jkd->ikrd", scores_grad, keys_rot, preferred_element_type=jnp.float32
    ).reshape(length, query_heads, HEAD_DIM)
    keys_rot_grad = jnp.einsum(
        "krij,ikrd->jkd", scores_grad, query_rot, preferred_element_type=jnp.float32
    )
    query_low = (
        unrotate(query_rot_grad, cosine, sine_table)
        .reshape(length, query_heads * HEAD_DIM)
        .astype(jnp.bfloat16)
    )
    keyval_low = jnp.concatenate(
        [
            unrotate(keys_rot_grad, cosine, sine_table).reshape(length, kv_heads * HEAD_DIM),
            values_grad.reshape(length, kv_heads * HEAD_DIM),
        ],
        axis=1,
    ).astype(jnp.bfloat16)
    attn_in_grad = jnp.einsum(
        "tc,dc->td", query_low, query_full, preferred_element_type=jnp.float32
    ) + jnp.einsum("tc,dc->td", keyval_low, keyval_full, preferred_element_type=jnp.float32)
    token_norm_grad, attn_gain_grad = norm_backward(
        attn_in_grad, normed_one, inverse_one, attn_gains.astype(jnp.float32)
    )
    tokens_grad = hidden_grad + token_norm_grad
    slab_count = lax.axis_size("dp")
    slab_index = lax.axis_index("dp")
    width_rows = model_width // slab_count
    head_rows = query_heads * HEAD_DIM // slab_count
    all_attn, all_query, all_keyval, all_mixed, all_outgrad = (
        lax.all_gather(attn_in, "dp", axis=0, tiled=True),
        lax.all_gather(query_low, "dp", axis=0, tiled=True),
        lax.all_gather(keyval_low, "dp", axis=0, tiled=True),
        lax.all_gather(mixed_low, "dp", axis=0, tiled=True),
        lax.all_gather(attn_out_grad, "dp", axis=0, tiled=True),
    )
    all_moe, all_logits, attn_gain_rows, moe_gain_rows = (
        lax.all_gather(
            moe_in.astype(jnp.float32).astype(jnp.bfloat16), "dp", axis=0, tiled=True
        ).astype(jnp.float32),
        lax.all_gather(logits_grad.astype(jnp.bfloat16), "dp", axis=0, tiled=True).astype(
            logits_grad.dtype
        ),
        lax.all_gather(
            attn_gain_grad[None, :].astype(jnp.bfloat16), "dp", axis=0, tiled=True
        ).astype(jnp.float32),
        lax.all_gather(
            moe_gain_grad[None, :].astype(jnp.bfloat16), "dp", axis=0, tiled=True
        ).astype(jnp.float32),
    )
    attn_cols = lax.dynamic_slice_in_dim(all_attn, slab_index * width_rows, width_rows, 1)
    mixed_cols = lax.dynamic_slice_in_dim(all_mixed, slab_index * head_rows, head_rows, 1)
    moe_cols = lax.dynamic_slice_in_dim(all_moe, slab_index * width_rows, width_rows, 1)
    query_part = jnp.einsum("td,tc->dc", attn_cols, all_query, preferred_element_type=jnp.float32)
    keyval_part = jnp.einsum("td,tc->dc", attn_cols, all_keyval, preferred_element_type=jnp.float32)
    output_part = jnp.einsum(
        "tc,td->cd", mixed_cols, all_outgrad, preferred_element_type=jnp.float32
    )
    router_part = jnp.dot(moe_cols.T, all_logits, precision=HIGH)
    attn_gain_part = lax.dynamic_slice_in_dim(
        jnp.sum(attn_gain_rows, axis=0), slab_index * width_rows, width_rows, 0
    )
    moe_gain_part = lax.dynamic_slice_in_dim(
        jnp.sum(moe_gain_rows, axis=0), slab_index * width_rows, width_rows, 0
    )
    query_share, keyval_share, output_share, router_share, attn_share, moe_share = (
        lax.psum_scatter(
            query_part.astype(jnp.bfloat16), "expert", scatter_dimension=0, tiled=True
        ).astype(jnp.float32),
        lax.psum_scatter(
            keyval_part.astype(jnp.bfloat16), "expert", scatter_dimension=0, tiled=True
        ).astype(jnp.float32),
        lax.psum_scatter(
            output_part.astype(jnp.bfloat16), "expert", scatter_dimension=0, tiled=True
        ).astype(jnp.float32),
        lax.psum_scatter(
            router_part.astype(jnp.bfloat16), "expert", scatter_dimension=0, tiled=True
        ).astype(jnp.float32),
        lax.psum_scatter(
            attn_gain_part.astype(jnp.bfloat16), "expert", scatter_dimension=0, tiled=True
        ).astype(jnp.float32),
        lax.psum_scatter(
            moe_gain_part.astype(jnp.bfloat16), "expert", scatter_dimension=0, tiled=True
        ).astype(jnp.float32),
    )
    return (
        layer_out,
        tokens_grad,
        query_share,
        keyval_share,
        output_share,
        router_share,
        attn_share,
        moe_share,
        expert_up_grad,
        expert_down_grad,
    )


LANES = 128
TAIL = 16
PIECE_LIMIT = 4096
VMEM_BYTES = 60 * 1024 * 1024
F32 = jnp.float32
LOW = jnp.bfloat16


def contract(left, right, left_dim, right_dim):
    return lax.dot_general(
        left, right, (((left_dim,), (right_dim,)), ((), ())), preferred_element_type=F32
    )


def lane_index(shape):
    return lax.broadcasted_iota(jnp.int32, shape, len(shape) - 1)


def row_index(shape):
    return lax.broadcasted_iota(jnp.int32, shape, len(shape) - 2)


def half_turn(chunk):
    first = lane_index(chunk.shape) % HEAD_DIM < HEAD_DIM // 2
    ahead = pltpu.roll(chunk, LANES - HEAD_DIM // 2, 1)
    behind = pltpu.roll(chunk, HEAD_DIM // 2, 1)
    return jnp.where(first, ahead, behind)


def both_heads(chunk, pick):
    swapped = pltpu.roll(chunk, HEAD_DIM, 1)
    first = lane_index(chunk.shape) < HEAD_DIM
    if pick == 0:
        return jnp.where(first, chunk, swapped)
    return jnp.where(first, swapped, chunk)


def split_heads(chunk):
    first = lane_index(chunk.shape) < HEAD_DIM
    zero = jnp.zeros_like(chunk)
    return jnp.concatenate([jnp.where(first, chunk, zero), jnp.where(first, zero, chunk)], axis=0)


def join_heads(stacked):
    length = stacked.shape[0] // 2
    top, bottom = stacked[:length], stacked[length:]
    return jnp.where(lane_index(top.shape) < HEAD_DIM, top, bottom)


def three_parts(values):
    high = values.astype(LOW).astype(F32)
    rest = values - high
    middle = rest.astype(LOW).astype(F32)
    return (high, middle, rest - middle)


def gain_select():
    shape = (8, LANES)
    return (lane_index(shape) == EXPERTS + row_index(shape)) & (row_index(shape) < 2)


def load_weights(rows_ref, spots, piece_refs, weights, sems):
    copies = []
    for spot, piece in zip(spots, piece_refs):
        for i, (p, w) in enumerate(spot):
            size = piece.shape[1]
            start = pl.multiple_of(rows_ref[p, w] * size, size)
            copies.append(
                pltpu.make_async_copy(piece.at[i], weights.at[pl.ds(start, size)], sems.at[p, w])
            )
    for copy in copies:
        copy.start()
    return copies


def store_sums(rows_ref, sums, grads_even, grads_odd, sems):
    copies = []
    for p in range(2 * grads_even.shape[0]):
        target = grads_even if p % 2 == 0 else grads_odd
        for w in range(target.shape[1]):
            size = target.shape[2]
            start = pl.multiple_of(rows_ref[p, w] * size, size)
            copies.append(
                pltpu.make_async_copy(
                    sums.at[pl.ds(start, size)], target.at[p // 2, w], sems.at[p, w]
                )
            )
    for copy in copies:
        copy.start()
    return copies


def softmax_rows(q_pair, k_both, visible):
    scores = contract(q_pair, k_both, 1, 1) * (HEAD_DIM ** (-0.5))
    logits = jnp.where(visible, scores, MASKED)
    exps = jnp.exp(logits - jnp.max(logits, axis=-1, keepdims=True))
    return exps / jnp.sum(exps, axis=-1, keepdims=True)


def segment_tables(seg_row, frequency):
    length = seg_row.shape[1]
    shape = (length, length)
    across_row = jnp.broadcast_to(seg_row.astype(F32), shape)
    down_col = across_row.T
    seen = (down_col == across_row) & (lane_index(shape) <= row_index(shape))
    visible = jnp.concatenate([seen, seen], axis=0)
    if frequency is None:
        return visible
    earlier = jnp.sum(jnp.where(across_row < down_col, 1.0, 0.0), axis=1, keepdims=True)
    angles = (row_index(shape).astype(F32) - earlier) * frequency
    sine = jnp.sin(angles)
    first = lane_index(shape) % HEAD_DIM < HEAD_DIM // 2
    return (visible, jnp.cos(angles), jnp.where(first, -sine, sine))


def attn_forward_kernel(spots, *refs):
    count = len(spots)
    rows_ref, tokens_ref, seg_row, frequency = refs[:4]
    pieces = refs[4 : 4 + count]
    query_ref, keyval_ref, mixed_ref, tail_ref, cos_ref, sin_ref, weights, sems = refs[4 + count :]
    copies = load_weights(rows_ref, spots, pieces, weights, sems)
    tokens = tokens_ref[...].astype(F32)
    inverse = lax.rsqrt(jnp.mean(tokens * tokens, axis=-1, keepdims=True) + EPS)
    normed = tokens * inverse
    width = tokens.shape[1]
    visible, cosine, sine = segment_tables(seg_row[...], frequency[...])
    cos_ref[...] = cosine
    sin_ref[...] = sine
    for copy in copies:
        copy.wait()
    tail = weights[:, 2 * width :]
    tail_ref[...] = tail
    gains = contract(gain_select().astype(F32).astype(LOW), tail, 1, 1)
    attn_in = (normed * gains[0:1]).astype(LOW)
    keyval = contract(attn_in, weights[:, width : 2 * width], 1, 0)
    query = contract(attn_in, weights[:, :width], 1, 0)
    half = width // 2
    for m in range(half // LANES):
        keys = keyval[:, m * LANES : (m + 1) * LANES]
        keys = (keys * cosine + half_turn(keys) * sine).astype(LOW)
        values = keyval[:, half + m * LANES : half + (m + 1) * LANES].astype(LOW)
        keyval_ref[:, m * LANES : (m + 1) * LANES] = keys
        keyval_ref[:, half + m * LANES : half + (m + 1) * LANES] = values
        for pick in range(2):
            k_both = both_heads(keys.astype(F32), pick).astype(LOW)
            v_both = both_heads(values.astype(F32), pick).astype(LOW)
            chunk = slice((2 * m + pick) * LANES, (2 * m + pick + 1) * LANES)
            queries = query[:, chunk]
            queries = (queries * cosine + half_turn(queries) * sine).astype(LOW)
            query_ref[:, chunk] = queries
            q_pair = split_heads(queries.astype(F32)).astype(LOW)
            probs = softmax_rows(q_pair, k_both, visible).astype(LOW)
            mixed_ref[:, chunk] = join_heads(contract(probs, v_both, 1, 0)).astype(LOW)


def router_kernel(spots, *refs):
    count = len(spots)
    rows_ref, tokens_ref, mixed_ref, tail_ref, routes_t = refs[:5]
    pieces = refs[5 : 5 + count]
    payload, hidden_ref, gates_ref, weights, sems = refs[5 + count :]
    copies = load_weights(rows_ref, spots, pieces, weights, sems)
    tokens = tokens_ref[...].astype(F32)
    length = tokens.shape[0]
    tail = tail_ref[...]
    gains = contract(gain_select().astype(F32).astype(LOW), tail, 1, 1)
    for copy in copies:
        copy.wait()
    hidden = tokens + contract(mixed_ref[...], weights[...], 1, 0)
    hidden_ref[...] = hidden
    inverse_two = lax.rsqrt(jnp.mean(hidden * hidden, axis=-1, keepdims=True) + EPS)
    moe_in = (hidden * inverse_two * gains[1:2]).astype(LOW)
    payload[:length] = moe_in
    logits = contract(moe_in, tail, 1, 0)
    turned = routes_t[...]
    experts = row_index((LANES, length))
    chosen = experts == turned[0:1]
    for k in range(1, TOP):
        chosen = chosen | (experts == turned[k : k + 1])
    chosen = jnp.where(chosen, 1.0, 0.0).T > 0.5
    logits = jnp.where(chosen, logits, MASKED)
    exps = jnp.where(chosen, jnp.exp(logits - jnp.max(logits, axis=-1, keepdims=True)), 0.0)
    gates = exps / jnp.sum(exps, axis=-1, keepdims=True)
    gates_ref[...] = gates
    gates_t = gates.T
    for k in range(TOP):
        row = turned[k : k + 1]
        gate = jnp.sum(jnp.where(experts == row, gates_t, 0.0), axis=0, keepdims=True)
        high, middle, rest = three_parts(gate)
        place = row_index((TAIL, length))
        block = jnp.where(place == 0, high, jnp.where(place == 1, middle, jnp.where(place == 2, rest, 0.0)))
        block = jnp.where(place == 3, row.astype(F32), block)
        payload[length:, k * length : (k + 1) * length] = block.astype(LOW)


def slot_places(first_expert, local, tails, before):
    length = tails[0].shape[1] // TOP
    ids = row_index((8, length))
    ids = jnp.where(ids < local, ids + first_expert, -1).astype(F32)
    masks, gates = [], []
    for tail in tails:
        mask = jnp.zeros((8, length), F32)
        gate = jnp.zeros((8, length), F32)
        for k in range(TOP):
            part = tail[:, k * length : (k + 1) * length].astype(F32)
            hit = part[3:4] == ids
            mask = jnp.where(hit, 1.0, mask)
            gate = jnp.where(hit, part[0:1] + part[1:2] + part[2:3], gate)
        masks.append(mask)
        gates.append(gate)
    pairs = range(0, len(tails), 2)
    mask = jnp.concatenate([jnp.concatenate(masks[i : i + 2], axis=1) for i in pairs], axis=0)
    gate = jnp.concatenate([jnp.concatenate(gates[i : i + 2], axis=1) for i in pairs], axis=0)
    place = contract(mask.astype(LOW), before, 1, 0)
    return (jnp.where(mask > 0, place, -1.0), gate)


def gather_pair(local, block, pair, place, gate, row_pair, grad_pair, out):
    rows_out, grads_out, select_out, gate_out = out
    slots = row_index((block, place.shape[1])).astype(F32)
    parts = []
    for j in range(local):
        hit = slots == place[j : j + 1]
        parts.append(jnp.where(hit, 1.0, 0.0))
        held = jnp.where(hit, gate[j : j + 1], 0.0)
        held = jnp.sum(held, axis=1, keepdims=True)
        gate_out[j, pair * block : (pair + 1) * block] = jnp.broadcast_to(held, (block, LANES))
    select = jnp.concatenate(parts, axis=0).astype(LOW)
    if select_out is not None:
        select_out[pair] = select
    rows = contract(select, jnp.concatenate(row_pair, axis=0), 1, 0).astype(LOW)
    grads = contract(select, jnp.concatenate(grad_pair, axis=0), 1, 0).astype(LOW)
    for j in range(local):
        rows_out[j, pair * block : (pair + 1) * block] = rows[j * block : (j + 1) * block]
        grads_out[j, pair * block : (pair + 1) * block] = grads[j * block : (j + 1) * block]


def earlier_matrix(length):
    shape = (2 * length, 2 * length)
    return jnp.where(row_index(shape) < lane_index(shape), 1.0, 0.0).astype(LOW)


def expert_step(j, rows, grads, gate_ref, up, down):
    hidden_units = down.shape[1]
    pair = contract(rows[j], up, 1, 0)
    raw = contract(grads[j], down, 1, 0)
    gate_half, up_half = pair[:, :hidden_units], pair[:, hidden_units:]
    gate = gate_ref[j][:, 0:1]
    sigmoid = 1.0 / (1.0 + jnp.exp(-gate_half))
    silu = gate_half * sigmoid
    activated = silu * up_half
    scaled = (gate * activated).astype(LOW)
    act_grad = gate * raw
    pair_grad = jnp.concatenate(
        [act_grad * up_half * sigmoid * (1.0 + gate_half * (1.0 - sigmoid)), act_grad * silu],
        axis=1,
    ).astype(LOW)
    gate_grad = jnp.sum(activated * raw, axis=1, keepdims=True)
    return (scaled, pair_grad, gate_grad)


def fetch_experts(local, up_hbm, down_hbm, up, down, sems):
    copies = []
    for j in range(local):
        copies.append(
            (
                pltpu.make_async_copy(up_hbm.at[j], up.at[j], sems.at[0, j]),
                pltpu.make_async_copy(down_hbm.at[j], down.at[j], sems.at[1, j]),
            )
        )
        for copy in copies[j]:
            copy.start()
    return copies


def expert_home_kernel(owners, local, block, *refs):
    place_ref = refs[0]
    rows_in = refs[1 : 1 + owners]
    grads_in = refs[1 + owners : 1 + 2 * owners]
    up_hbm, down_hbm = refs[1 + 2 * owners : 3 + 2 * owners]
    back_even, back_odd = refs[3 + 2 * owners : 5 + 2 * owners]
    kept = refs[5 + 2 * owners : 10 + 2 * owners]
    scratch = refs[10 + 2 * owners :]
    up, down, rows, grads, select, gate_ref, scaled, pair_grads, returned, sems = scratch
    copies = fetch_experts(local, up_hbm, down_hbm, up, down, sems)
    length = rows_in[0].shape[0] - TAIL
    width = rows_in[0].shape[1]
    first_expert = place_ref[0] * local
    slab = kept[3].shape[2]
    columns = pl.ds(pl.multiple_of(place_ref[1] * slab, slab), slab)
    before = earlier_matrix(length)
    place, gate = slot_places(first_expert, local, [ref[length:] for ref in rows_in], before)
    for s in range(owners // 2):
        gather_pair(
            local,
            block,
            s,
            place[8 * s : 8 * s + 8],
            gate[8 * s : 8 * s + 8],
            [rows_in[2 * s][:length], rows_in[2 * s + 1][:length]],
            [grads_in[2 * s][...], grads_in[2 * s + 1][...]],
            (rows, grads, select, gate_ref),
        )
    sent = [
        pltpu.make_async_copy(select, kept[0], sems.at[2, 0]),
        pltpu.make_async_copy(rows.at[:, :, columns], kept[3], sems.at[2, 1]),
        pltpu.make_async_copy(grads.at[:, :, columns], kept[4], sems.at[2, 2]),
    ]
    for copy in sent:
        copy.start()
    for j in range(local):
        for copy in copies[j]:
            copy.wait()
    for j in range(local):
        made, pair_grad, gate_grad = expert_step(j, rows, grads, gate_ref, up[j], down[j])
        scaled[j] = made
        pair_grads[j] = pair_grad
        sent.append(pltpu.make_async_copy(scaled.at[j], kept[1].at[j], sems.at[3, j]))
        sent.append(pltpu.make_async_copy(pair_grads.at[j], kept[2].at[j], sems.at[4, j]))
        sent[-2].start()
        sent[-1].start()
        returned[j, :, :width] = contract(pair_grad, up[j], 1, 1).astype(LOW)
        lanes = lane_index((made.shape[0], LANES)) - first_expert - j
        high, middle, rest = three_parts(gate_grad)
        tail = jnp.where(lanes == 0, high, 0.0)
        tail = jnp.where(lanes == EXPERTS, middle, tail)
        tail = jnp.where(lanes == 2 * EXPERTS, rest, tail)
        returned[j, :, width:] = tail.astype(LOW)
    for s in range(owners // 2):
        span = slice(s * block, (s + 1) * block)
        back = jnp.concatenate([returned[j, span] for j in range(local)], axis=0)
        back = contract(select[s], back, 0, 0).astype(LOW)
        back_even[s] = back[:length]
        back_odd[s] = back[length:]
    for copy in sent:
        copy.wait()


def expert_finish_kernel(local, block, *refs):
    select, scaled, pair_grads, rows, grads, down = refs[:6]
    out_even, out_odd, up_grad, down_grad, produced = refs[6:]
    length = out_even.shape[1]
    for j in range(local):
        produced[j] = contract(scaled[j], down[j], 1, 1).astype(LOW)
        up_grad[j] = contract(rows[j], pair_grads[j], 0, 0)
        down_grad[j] = contract(grads[j], scaled[j], 0, 0)
    for s in range(out_even.shape[0]):
        span = slice(s * block, (s + 1) * block)
        made = jnp.concatenate([produced[j, span] for j in range(local)], axis=0)
        made = contract(select[s], made, 0, 0).astype(LOW)
        out_even[s] = made[:length]
        out_odd[s] = made[length:]


def expert_away_kernel(start, count, block, chips, far, *refs):
    place_ref = refs[0]
    rows_in = refs[1 : 3 + 2 * chips]
    grads_in = refs[3 + 2 * chips : 3 + 4 * chips]
    up_hbm, down_hbm, up_first, down_first = refs[3 + 4 * chips : 7 + 4 * chips]
    up_grad, down_grad = refs[7 + 4 * chips : 9 + 4 * chips]
    scratch = refs[9 + 4 * chips :]
    up, down, up_sum, down_sum, rows_buf, grads_buf, rows, grads, gate_ref, sems, pair_sems = scratch
    length = grads_buf.shape[1] // 2
    tall = length + TAIL
    pairs = []
    for i in range(far + 1):
        for s in range(chips):
            spot = len(pairs)
            copies = []
            for side in range(2):
                grad_from = grads_in[2 * s + side].at[pl.ds(i * length, length)]
                if i == 0:
                    row_from = rows_in[side].at[s]
                else:
                    row_from = rows_in[2 + 2 * s + side].at[pl.ds((i - 1) * tall, tall)]
                row_to = rows_buf.at[spot, pl.ds(side * tall, tall)]
                grad_to = grads_buf.at[spot, pl.ds(side * length, length)]
                copies.append(pltpu.make_async_copy(row_from, row_to, pair_sems.at[0, side, spot]))
                copies.append(pltpu.make_async_copy(grad_from, grad_to, pair_sems.at[1, side, spot]))
            pairs.append(copies)
    for copies in pairs:
        for copy in copies:
            copy.start()
    held = []
    for j in range(count):
        held.append(
            [
                pltpu.make_async_copy(up_hbm.at[start + j], up.at[j], sems.at[0, j]),
                pltpu.make_async_copy(down_hbm.at[start + j], down.at[j], sems.at[1, j]),
                pltpu.make_async_copy(up_first.at[start + j], up_sum.at[j], sems.at[2, j]),
                pltpu.make_async_copy(down_first.at[start + j], down_sum.at[j], sems.at[3, j]),
            ]
        )
    for copies in held:
        for copy in copies:
            copy.start()
    first_expert = place_ref[0] * (up_hbm.shape[0]) + start
    slab = up_sum.shape[1]
    columns = pl.ds(pl.multiple_of(place_ref[1] * slab, slab), slab)
    before = earlier_matrix(length)
    for i, copies in enumerate(pairs):
        for copy in copies:
            copy.wait()
        tails = [rows_buf[i, length:tall], rows_buf[i, tall + length :]]
        place, gate = slot_places(first_expert, count, tails, before)
        gather_pair(
            count,
            block,
            i,
            place,
            gate,
            [rows_buf[i, :length], rows_buf[i, tall : tall + length]],
            [grads_buf[i]],
            (rows, grads, None, gate_ref),
        )
    for copies in held:
        for copy in copies:
            copy.wait()
    sent = []
    for j in range(count):
        scaled, pair_grad, _ = expert_step(j, rows, grads, gate_ref, up[j], down[j])
        up_sum[j] += contract(rows[j, :, columns], pair_grad, 0, 0)
        down_sum[j] += contract(grads[j, :, columns], scaled, 0, 0)
        sent.append(pltpu.make_async_copy(up_sum.at[j], up_grad.at[start + j], sems.at[4, j]))
        sent.append(pltpu.make_async_copy(down_sum.at[j], down_grad.at[start + j], sems.at[5, j]))
        sent[-2].start()
        sent[-1].start()
    for copy in sent:
        copy.wait()


def backward_kernel(spots, output_spots, shares, *refs):
    rows_ref, tokens_ref, seg_row, cos_ref, sin_ref, payload, hidden_ref = refs[:7]
    query_ref, keyval_ref, mixed_ref, gates_ref, out_grad_ref, tail_ref = refs[7:13]
    refs = refs[13:]
    back, refs = refs[:shares], refs[shares:]
    pieces, refs = refs[: len(spots)], refs[len(spots) :]
    output_pieces, refs = refs[: len(output_spots)], refs[len(output_spots) :]
    tokens_grad, grads_even, grads_odd = refs[:3]
    weights, output, sums, query_low, keyval_low, sems, output_sems, out_sems = refs[3:]
    output_copies = load_weights(rows_ref, output_spots, output_pieces, output, output_sems)
    copies = load_weights(rows_ref, spots, pieces, weights, sems)
    length, width = tokens_ref.shape
    half = width // 2
    columns = weights.shape[1]
    total = back[0][...].astype(F32)
    for share in back[1:]:
        total = total + share[...].astype(F32)
    parts = total[:, width:]
    lanes = lane_index(parts.shape)
    gate_grad = parts + pltpu.roll(parts, LANES - EXPERTS, 1) + pltpu.roll(parts, LANES - 2 * EXPERTS, 1)
    gate_grad = jnp.where(lanes < EXPERTS, gate_grad, 0.0)
    gates = gates_ref[...]
    logits_grad = gates * (gate_grad - jnp.sum(gates * gate_grad, axis=-1, keepdims=True))
    hidden = hidden_ref[...]
    inverse_two = lax.rsqrt(jnp.mean(hidden * hidden, axis=-1, keepdims=True) + EPS)
    normed_two = hidden * inverse_two
    tail = tail_ref[...]
    gains = contract(gain_select().astype(F32).astype(LOW), tail, 1, 1)
    high = logits_grad.astype(LOW)
    rest = (logits_grad - high.astype(F32)).astype(LOW)
    moe_grad = total[:, :width] + contract(high, tail, 1, 1) + contract(rest, tail, 1, 1)
    moe_gain_grad = jnp.sum(moe_grad * normed_two, axis=0, keepdims=True)
    scaled = moe_grad * gains[1:2]
    hidden_grad = out_grad_ref[...].astype(F32) + inverse_two * (
        scaled - normed_two * jnp.mean(scaled * normed_two, axis=-1, keepdims=True)
    )
    attn_out_grad = hidden_grad.astype(LOW)
    for copy in output_copies:
        copy.wait()
    mixed_grad = contract(attn_out_grad, output[...], 1, 1)
    sums[:, columns:] = contract(mixed_ref[...], attn_out_grad, 0, 0).astype(LOW)
    tokens = tokens_ref[...].astype(F32)
    inverse_one = lax.rsqrt(jnp.mean(tokens * tokens, axis=-1, keepdims=True) + EPS)
    normed_one = tokens * inverse_one
    cosine, sine = cos_ref[...], sin_ref[...]
    visible = segment_tables(seg_row[...], None)
    groups = range(width // LANES)
    chunks = [slice(g * LANES, (g + 1) * LANES) for g in groups]
    keys = [keyval_ref[:, chunks[m]].astype(F32) for m in range(half // LANES)]
    values = [keyval_ref[:, half + m * LANES : half + (m + 1) * LANES].astype(F32) for m in range(half // LANES)]
    k_both = [both_heads(keys[g // 2], g % 2).astype(LOW) for g in groups]
    v_both = [both_heads(values[g // 2], g % 2).astype(LOW) for g in groups]
    q_pair = [split_heads(query_ref[:, chunk].astype(F32)).astype(LOW) for chunk in chunks]
    probs = [softmax_rows(q_pair[g], k_both[g], visible) for g in groups]
    m_pair = [split_heads(mixed_grad[:, chunk]).astype(LOW) for chunk in chunks]
    probs_grad = [contract(m_pair[g], v_both[g], 1, 1) for g in groups]
    value_sides = [contract(probs[g].astype(LOW), m_pair[g], 0, 0) for g in groups]
    scores_grad = [
        (
            probs[g]
            * (probs_grad[g] - jnp.sum(probs[g] * probs_grad[g], axis=-1, keepdims=True))
            * (HEAD_DIM ** (-0.5))
        ).astype(LOW)
        for g in groups
    ]
    query_grad = [join_heads(contract(scores_grad[g], k_both[g], 1, 0)) for g in groups]
    key_sides = [contract(scores_grad[g], q_pair[g], 0, 0) for g in groups]
    for g in groups:
        turned = query_grad[g] * cosine - half_turn(query_grad[g]) * sine
        query_low[:, chunks[g]] = turned.astype(LOW)
    key_sides = [side + pltpu.roll(side, HEAD_DIM, 1) for side in key_sides]
    value_sides = [side + pltpu.roll(side, HEAD_DIM, 1) for side in value_sides]
    first = lane_index((length, LANES)) < HEAD_DIM
    for m in range(half // LANES):
        keys_grad = jnp.where(first, key_sides[2 * m], key_sides[2 * m + 1])
        values_grad = jnp.where(first, value_sides[2 * m], value_sides[2 * m + 1])
        turned = keys_grad * cosine - half_turn(keys_grad) * sine
        keyval_low[:, chunks[m]] = turned.astype(LOW)
        keyval_low[:, half + m * LANES : half + (m + 1) * LANES] = values_grad.astype(LOW)
    for copy in copies:
        copy.wait()
    attn_in_grad = contract(query_low[...], weights[:, :width], 1, 1) + contract(
        keyval_low[...], weights[:, width : 2 * width], 1, 1
    )
    attn_in = (normed_one * gains[0:1]).astype(LOW)
    sums[:, :width] = contract(attn_in, query_low[...], 0, 0).astype(LOW)
    sums[:, width : 2 * width] = contract(attn_in, keyval_low[...], 0, 0).astype(LOW)
    attn_gain_grad = jnp.sum(attn_in_grad * normed_one, axis=0, keepdims=True)
    place = row_index((8, width))
    gain_grads = jnp.where(place == 0, attn_gain_grad, jnp.where(place == 1, moe_gain_grad, 0.0))
    sums[:, 2 * width : columns] = (
        contract(payload[:length], high, 0, 0)
        + contract(gain_grads.astype(LOW), gain_select().astype(F32).astype(LOW), 0, 0)
    ).astype(LOW)
    out_copies = store_sums(rows_ref, sums, grads_even, grads_odd, out_sems)
    scaled = attn_in_grad * gains[0:1]
    tokens_grad[...] = hidden_grad + inverse_one * (
        scaled - normed_one * jnp.mean(scaled * normed_one, axis=-1, keepdims=True)
    )
    for copy in out_copies:
        copy.wait()


def swap(values, axis, size, distance):
    return lax.ppermute(values, axis, [(i, i ^ distance) for i in range(size)])


def across(values, distance, planes):
    return swap(values, "dp", planes, distance)


def aside(values, s, owners):
    return swap(values, "expert", owners, 2 * s)


def partner(values, owners):
    return swap(values, "expert", owners, 1)


def after(values, *earlier):
    return lax.optimization_barrier((values,) + earlier)[0]


def over_chips(values, owners):
    return [values] + [aside(values, s, owners) for s in range(1, owners // 2)]


def over_cores(near, owners, *earlier):
    pieces = []
    for piece in near:
        pieces += [piece, partner(after(piece, *earlier) if earlier else piece, owners)]
    return pieces


def chips_split(values, owners, *earlier):
    half = values.shape[0] // 2
    first, second = aside(values, 1, owners), aside(values, 2, owners)
    far = [first[:half], second[half:]]
    if earlier:
        far = [after(part, *earlier) for part in far]
    far = [aside(far[0], 2, owners), aside(far[1], 1, owners)]
    return [[values], [first], [second], far]


def core_pieces(groups, owners, *earlier):
    pieces, spots = [], []
    for group in groups:
        parts = [part for part, _ in group]
        merged = parts[0] if len(parts) == 1 else jnp.concatenate(parts, axis=0)
        merged = after(merged, *earlier) if earlier else merged
        for part, spot in group:
            pieces.append(part)
            spots.append(spot)
        pieces.append(partner(merged, owners))
        spots.append([(p + 1, w) for _, spot in group for p, w in spot])
    return (pieces, spots)


def core_pieces_whole(near, owners):
    pieces = []
    for parts in near:
        piece = parts[0] if len(parts) == 1 else jnp.concatenate(parts, axis=0)
        pieces.append((piece, partner(piece, owners)))
    return pieces


def added(left, right):
    return (left.astype(F32) + right.astype(F32)).astype(LOW)


def to_owners(even, odd, owners, *earlier):
    other = partner(odd, owners)
    joined = [added(even[s], other[s]) for s in range(owners // 2)]
    if earlier:
        joined = lax.optimization_barrier(tuple(joined) + earlier)[: owners // 2]
    sent = [joined[0]] + [aside(joined[s], s, owners) for s in range(1, owners // 2)]
    return (joined, sent)


def to_neighbours(joined, owners):
    half = joined[3].shape[0] // 2
    low_turn = aside(joined[3][:half], 1, owners)
    top_turn = aside(joined[3][half:], 2, owners)
    low_turn, top_turn = lax.optimization_barrier((low_turn, top_turn))
    first = jnp.concatenate([joined[1][:half], added(joined[1][half:], top_turn)], axis=0)
    second = jnp.concatenate([added(joined[2][:half], low_turn), joined[2][half:]], axis=0)
    return (first, second)


def from_neighbours(joined, first, second, owners):
    parts = [joined[0], aside(first, 1, owners), aside(second, 2, owners)]
    return sum(part.astype(F32) for part in parts).astype(LOW)


def over_planes_sum(parts, planes):
    total = parts[0].astype(F32)
    for w in range(1, planes):
        total = total + across(parts[w], w, planes).astype(F32)
    return total


def cost(us):
    return pl.CostEstimate(flops=int(us * 1153e6), bytes_accessed=0, transcendentals=0)


def params():
    return pltpu.CompilerParams(vmem_limit_bytes=VMEM_BYTES)


def whole_spec():
    return pl.BlockSpec(memory_space=pltpu.VMEM)


def hbm_spec():
    return pl.BlockSpec(memory_space=pl.ANY)


def smem_spec():
    return pl.BlockSpec(memory_space=pltpu.SMEM)


def on_device(
    planes,
    owners,
    tokens,
    segments,
    routes,
    query_weight,
    keyval_weight,
    output_weight,
    router_weight,
    attn_gain,
    moe_gain,
    expert_up,
    expert_down,
    out_grad,
):
    length, width = tokens.shape
    if planes != 4 or owners != 8 or planes * owners * length > PIECE_LIMIT:
        return on_device_wide(
            tokens,
            segments,
            routes,
            query_weight,
            keyval_weight,
            output_weight,
            router_weight,
            attn_gain,
            moe_gain,
            expert_up,
            expert_down,
            out_grad,
        )
    local = expert_up.shape[0]
    hidden_units = expert_down.shape[2]
    block = 2 * CAP
    slots = owners // 2 * block
    plane = lax.axis_index("dp")
    owner = lax.axis_index("expert")
    share = query_weight.shape[0]
    rows = (plane ^ jnp.arange(planes))[None, :] * owners + (owner ^ jnp.arange(owners))[:, None]
    rows = rows.astype(jnp.int32)
    place = jnp.stack([owner, plane]).astype(jnp.int32)
    extra = jnp.concatenate(
        [
            router_weight,
            attn_gain[:, None],
            moe_gain[:, None],
            jnp.zeros((share, LANES - EXPERTS - 2), LOW),
        ],
        axis=1,
    )
    packed = jnp.concatenate([query_weight, keyval_weight, extra, output_weight], axis=1)
    columns = packed.shape[1] - width

    early = [across(packed, w, planes) for w in range(1, planes)]
    grad_chips = over_chips(out_grad, owners)
    grad_cores = partner(jnp.concatenate(grad_chips, axis=0), owners)
    gathered = jnp.stack([packed] + early)
    grad_start = after(out_grad, *early)
    grad_planes = [across(grad_start, w, planes) for w in range(1, planes)]
    near = chips_split(
        after(gathered[:, :, :columns], *grad_chips), owners, grad_planes[0]
    )
    every = list(range(planes))
    groups = [[(near[s][0], [(2 * s, w) for w in every])] for s in range(3)]
    groups += [
        [(near[3][0], [(6, w) for w in every[: planes // 2]])],
        [(near[3][1], [(6, w) for w in every[planes // 2 :]])],
    ]
    pieces, spots = core_pieces(groups, owners)
    output_near = over_chips(after(gathered[:, :, columns:], *pieces[:6], *near[3]), owners)

    half_dim = HEAD_DIM // 2
    frequency = ROPE_BASE ** (-(jnp.arange(half_dim, dtype=F32) * 2.0) / HEAD_DIM)
    frequency = jnp.tile(frequency, LANES // half_dim)[None, :]

    token_low = jax.ShapeDtypeStruct((length, width), LOW)
    token_wide = jax.ShapeDtypeStruct((length, width), F32)
    table = jax.ShapeDtypeStruct((length, LANES), F32)
    query_rot, keyval_low, mixed_low, tail, cosine, sine = pl.pallas_call(
        functools.partial(attn_forward_kernel, spots),
        out_shape=(token_low, token_low, token_low, jax.ShapeDtypeStruct((width, LANES), LOW))
        + (table, table),
        in_specs=[smem_spec()] + [whole_spec()] * 3 + [hbm_spec()] * len(pieces),
        out_specs=[whole_spec()] * 6,
        scratch_shapes=[
            pltpu.VMEM((width, columns), LOW),
            pltpu.SemaphoreType.DMA((owners, planes)),
        ],
        compiler_params=params(),
        cost_estimate=cost(6),
        name="attn_forward",
    )(rows, after(tokens, grad_planes[1]), segments, frequency, *pieces)

    output_pieces, output_spots = core_pieces(
        [[(output_near[s], [(2 * s, w) for w in every])] for s in range(owners // 2)],
        owners,
        mixed_low,
    )

    grad_stack = jnp.concatenate(grad_planes, axis=0)

    payload, hidden, gates = pl.pallas_call(
        functools.partial(router_kernel, output_spots),
        out_shape=(
            jax.ShapeDtypeStruct((length + TAIL, width), LOW),
            token_wide,
            jax.ShapeDtypeStruct((length, LANES), F32),
        ),
        in_specs=[smem_spec()] + [whole_spec()] * 4 + [hbm_spec()] * len(output_pieces),
        out_specs=[whole_spec()] * 3,
        scratch_shapes=[
            pltpu.VMEM((width, width), LOW),
            pltpu.SemaphoreType.DMA((owners, planes)),
        ],
        compiler_params=params(),
        cost_estimate=cost(4),
        name="router",
    )(
        rows,
        tokens,
        mixed_low,
        tail,
        routes.T,
        *output_pieces,
    )

    row_chips = over_chips(payload, owners)
    row_home = over_cores(row_chips[:3], owners) + over_cores(row_chips[3:], owners, grad_stack)
    grad_other = partner(after(grad_stack, payload), owners)
    row_start = after(payload, row_home[1])
    row_planes = [across(row_start, w, planes) for w in range(2, planes)]
    row_near = across(jnp.stack(row_chips), 1, planes)
    grad_direct = after(grad_stack, *row_chips)
    grad_near = [aside(grad_direct, s, owners) for s in (1, 2)]

    def all_of(shape):
        return pl.BlockSpec(shape, lambda i: (0,) * len(shape))

    slab = width // planes
    slabs = (
        jax.ShapeDtypeStruct((local, slab, 2 * hidden_units), F32),
        jax.ShapeDtypeStruct((local, slab, hidden_units), F32),
    )
    home_blocks = [s * (p % 2) for s in range(owners // 2) for p in range(2)]
    grad_home = [part for s in range(owners // 2) for part in (grad_chips[s], grad_cores)]
    chip_rows = jax.ShapeDtypeStruct((owners // 2, length, width), LOW)
    chip_back = jax.ShapeDtypeStruct((owners // 2, length, width + LANES), LOW)
    back_even, back_odd, *kept = pl.pallas_call(
        functools.partial(expert_home_kernel, owners, local, block),
        grid=(1,),
        out_shape=(
            chip_back,
            chip_back,
            jax.ShapeDtypeStruct((owners // 2, local * block, 2 * length), LOW),
            jax.ShapeDtypeStruct((local, slots, hidden_units), LOW),
            jax.ShapeDtypeStruct((local, slots, 2 * hidden_units), LOW),
            jax.ShapeDtypeStruct((local, slots, slab), LOW),
            jax.ShapeDtypeStruct((local, slots, slab), LOW),
        ),
        in_specs=[smem_spec()]
        + [all_of((length + TAIL, width))] * owners
        + [pl.BlockSpec((length, width), lambda i, s=s: (s, 0)) for s in home_blocks]
        + [hbm_spec()] * 2,
        out_specs=[all_of(chip_back.shape)] * 2 + [hbm_spec()] * 5,
        scratch_shapes=[
            pltpu.VMEM(expert_up.shape, LOW),
            pltpu.VMEM(expert_down.shape, LOW),
            pltpu.VMEM((local, slots, width), LOW),
            pltpu.VMEM((local, slots, width), LOW),
            pltpu.VMEM((owners // 2, local * block, 2 * length), LOW),
            pltpu.VMEM((local, slots, LANES), F32),
            pltpu.VMEM((local, slots, hidden_units), LOW),
            pltpu.VMEM((local, slots, 2 * hidden_units), LOW),
            pltpu.VMEM((local, slots, width + LANES), LOW),
            pltpu.SemaphoreType.DMA((5, local)),
        ],
        compiler_params=params(),
        cost_estimate=cost(18),
        name="expert_home",
    )(place, *row_home, *grad_home, expert_up, expert_down)
    out_even, out_odd, up_grad, down_grad = pl.pallas_call(
        functools.partial(expert_finish_kernel, local, block),
        out_shape=(chip_rows, chip_rows) + slabs,
        in_specs=[whole_spec()] * 6,
        out_specs=[whole_spec()] * 4,
        scratch_shapes=[pltpu.VMEM((local, slots, width), LOW)],
        compiler_params=params(),
        cost_estimate=cost(8),
        name="expert_finish",
    )(*kept, expert_down)

    joined, back = to_owners(back_even, after(back_odd, grad_other, *grad_near, *row_planes), owners)
    row_stack = jnp.concatenate(row_planes, axis=0)
    row_far = chips_split(after(row_stack, *back), owners)
    grad_away = [grad_stack, grad_other]
    grad_away += over_cores(grad_near, owners, *back)
    row_own = partner(after(row_stack, *joined), owners)

    def expert_away(start, count, place, up_grad, down_grad):
        chips = owners // 2
        pairs = chips * (planes - 1)
        return pl.pallas_call(
            functools.partial(
                expert_away_kernel, start, count, block, chips, planes - 2
            ),
            out_shape=slabs,
            in_specs=[smem_spec()] + [hbm_spec()] * (6 + 4 * chips),
            out_specs=[hbm_spec()] * 2,
            scratch_shapes=[
                pltpu.VMEM((count,) + expert_up.shape[1:], LOW),
                pltpu.VMEM((count,) + expert_down.shape[1:], LOW),
                pltpu.VMEM((count,) + slabs[0].shape[1:], F32),
                pltpu.VMEM((count,) + slabs[1].shape[1:], F32),
                pltpu.VMEM((pairs, 2 * (length + TAIL), width), LOW),
                pltpu.VMEM((pairs, 2 * length, width), LOW),
                pltpu.VMEM((count, pairs * block, width), LOW),
                pltpu.VMEM((count, pairs * block, width), LOW),
                pltpu.VMEM((count, pairs * block, LANES), F32),
                pltpu.SemaphoreType.DMA((6, count)),
                pltpu.SemaphoreType.DMA((2, 2, pairs)),
            ],
            input_output_aliases={5 + 4 * chips: 0, 6 + 4 * chips: 1},
            compiler_params=params(),
            cost_estimate=cost(7 * count),
            name="expert_away",
        )(place, *row_away, *grad_away, expert_up, expert_down, up_grad, down_grad)

    def share_pieces(wide):
        return jax.ShapeDtypeStruct((owners // 2, planes, share, wide), LOW)

    wide = columns + width
    tokens_grad, grads_even, grads_odd = pl.pallas_call(
        functools.partial(backward_kernel, spots, output_spots, owners // 2),
        out_shape=(token_wide, share_pieces(wide), share_pieces(wide)),
        in_specs=[smem_spec()]
        + [whole_spec()] * (12 + owners // 2)
        + [hbm_spec()] * (len(pieces) + len(output_pieces)),
        out_specs=[whole_spec()] + [hbm_spec()] * 2,
        scratch_shapes=[
            pltpu.VMEM((width, columns), LOW),
            pltpu.VMEM((width, width), LOW),
            pltpu.VMEM((width, wide), LOW),
            pltpu.VMEM((length, width), LOW),
            pltpu.VMEM((length, width), LOW),
            pltpu.SemaphoreType.DMA((owners, planes)),
            pltpu.SemaphoreType.DMA((owners, planes)),
            pltpu.SemaphoreType.DMA((owners, planes)),
        ],
        compiler_params=params(),
        cost_estimate=cost(17),
        name="backward",
    )(
        rows,
        tokens,
        segments,
        cosine,
        sine,
        payload,
        after(hidden, row_own, out_even),
        query_rot,
        keyval_low,
        mixed_low,
        gates,
        out_grad,
        tail,
        *back,
        *pieces,
        *output_pieces,
    )

    grads_other = partner(
        after(grads_odd, row_near, row_far[1][0], row_far[2][0], *grad_away[3::2]), owners
    )
    half = grad_stack.shape[0] // 2
    grad_turn = [
        aside(after(grad_near[0][:half], tokens_grad), 2, owners),
        aside(after(grad_near[1][half:], tokens_grad), 1, owners),
    ]
    shares = [added(grads_even[s], grads_other[s]) for s in range(owners // 2)]
    grad_away += over_cores([jnp.concatenate(grad_turn, axis=0)], owners, shares[0])
    row_away = over_cores([row_near], owners, shares[0]) + [row_stack, row_own]
    row_away += over_cores(
        [jnp.concatenate(parts, axis=0) for parts in row_far[1:]], owners, shares[0]
    )
    first, second = to_neighbours(shares, owners)
    out_other = partner(after(out_odd, shares[0], *row_far[3], *grad_turn), owners)
    made = [added(out_even[s], out_other[s]) for s in range(owners // 2)]
    held = (first, second) + tuple(row_away[1::2]) + tuple(grad_away[7:]) + tuple(made)
    first, second = lax.optimization_barrier(held)[:2]
    far_made = aside(after(made[3], first), 3, owners)
    up_grad, down_grad = expert_away(0, 2, after(place, first, second), up_grad, down_grad)
    plane_sums = after(from_neighbours(shares, first, second, owners), up_grad, far_made)
    up_grad, down_grad = expert_away(2, 2, after(place, plane_sums), up_grad, down_grad)
    made = lax.optimization_barrier(tuple(made) + (plane_sums,))[: owners // 2]
    near_made = [aside(made[s], s, owners) for s in (1, 2)]
    summed = over_planes_sum(plane_sums, planes)
    made = [made[0]] + near_made + [far_made]
    layer_out = (hidden + sum(part.astype(F32) for part in made)).astype(LOW)

    return (
        layer_out,
        tokens_grad,
        summed[:, :width],
        summed[:, width : 2 * width],
        summed[:, columns:],
        summed[:, 2 * width : 2 * width + EXPERTS],
        summed[:, 2 * width + EXPERTS],
        summed[:, 2 * width + EXPERTS + 1],
        up_grad,
        down_grad,
    )


def solution(mesh):
    return jax.shard_map(
        functools.partial(on_device, mesh.shape["dp"], mesh.shape["expert"]),
        mesh=mesh,
        in_specs=(
            P(("dp", "expert"), None),
            P(("dp", "expert"), None),
            P(("dp", "expert"), None),
            P(("dp", "expert"), None),
            P(("dp", "expert"), None),
            P(("dp", "expert"), None),
            P(("dp", "expert"), None),
            P(("dp", "expert")),
            P(("dp", "expert")),
            P("expert", None, None),
            P("expert", None, None),
            P(("dp", "expert"), None),
        ),
        out_specs=(
            P(("dp", "expert"), None),
            P(("dp", "expert"), None),
            P(("dp", "expert"), None),
            P(("dp", "expert"), None),
            P(("dp", "expert"), None),
            P(("dp", "expert"), None),
            P(("dp", "expert")),
            P(("dp", "expert")),
            P("expert", "dp", None),
            P("expert", "dp", None),
        ),
        check_vma=False,
    )
```

```python
import functools

import jax
import jax.numpy as jnp
from jax import lax
from jax.sharding import PartitionSpec as P
from jax.experimental import pallas as pl
from jax.experimental.pallas import tpu as pltpu

HEAD_DIM = 64
FF = 512
EXPERTS = 32
TOP = 8
CAP = 40


EPS = 1e-05
ROPE_BASE = 10000.0
MASKED = -1e30
HIGH = lax.Precision.HIGHEST


def norm_forward(values, gain_vec):
    inverse = lax.rsqrt(jnp.mean(values * values, axis=-1, keepdims=True) + EPS)
    normed = values * inverse
    return (normed, inverse, (normed * gain_vec).astype(jnp.bfloat16))


def norm_backward(grad_out, normed, inverse, gain_vec):
    gain_grad = jnp.sum(grad_out * normed, axis=0)
    scaled = grad_out * gain_vec
    grad_in = inverse * (scaled - normed * jnp.mean(scaled * normed, axis=-1, keepdims=True))
    return (grad_in, gain_grad)


def rope_tables(segment_row):
    length = segment_row.shape[0]
    earlier = jnp.sum((segment_row[None, :] < segment_row[:, None]).astype(jnp.int32), axis=1)
    position = jnp.arange(length, dtype=jnp.int32) - earlier
    half_dim = HEAD_DIM // 2
    frequency = ROPE_BASE ** (-(jnp.arange(half_dim, dtype=jnp.float32) * 2.0) / HEAD_DIM)
    angles = position.astype(jnp.float32)[:, None] * frequency[None, :]
    cosine = jnp.concatenate([jnp.cos(angles), jnp.cos(angles)], axis=-1)[:, None, :]
    sine_table = jnp.concatenate([jnp.sin(angles), jnp.sin(angles)], axis=-1)[:, None, :]
    return (cosine, sine_table)


def rotate(values, cosine, sine_table):
    half_dim = values.shape[-1] // 2
    turned = jnp.concatenate([-values[..., half_dim:], values[..., :half_dim]], axis=-1)
    return values * cosine + turned * sine_table


def unrotate(grad_rows, cosine, sine_table):
    half_dim = grad_rows.shape[-1] // 2
    weighted = grad_rows * sine_table
    turned = jnp.concatenate([weighted[..., half_dim:], -weighted[..., :half_dim]], axis=-1)
    return grad_rows * cosine + turned


def on_device_wide(
    tokens,
    segments,
    routes,
    query_weight,
    keyval_weight,
    output_weight,
    router_weight,
    attn_gain,
    moe_gain,
    expert_up,
    expert_down,
    out_grad,
):
    owners = lax.axis_size("expert")
    local_experts = expert_up.shape[0]
    length = tokens.shape[0]
    model_width = tokens.shape[1]
    kv_heads = keyval_weight.shape[1] // (2 * HEAD_DIM)
    query_heads = query_weight.shape[1] // HEAD_DIM
    repeat = query_heads // kv_heads
    score_scale = HEAD_DIM ** (-0.5)
    query_full, keyval_full, output_full, router_full, attn_gains, moe_gains = (
        lax.all_gather(query_weight, ("dp", "expert"), axis=0, tiled=True),
        lax.all_gather(keyval_weight, ("dp", "expert"), axis=0, tiled=True),
        lax.all_gather(output_weight, ("dp", "expert"), axis=0, tiled=True),
        lax.all_gather(router_weight, ("dp", "expert"), axis=0, tiled=True),
        lax.all_gather(attn_gain, ("dp", "expert"), axis=0, tiled=True),
        lax.all_gather(moe_gain, ("dp", "expert"), axis=0, tiled=True),
    )
    resident = tokens.astype(jnp.float32)
    normed_one, inverse_one, attn_in = norm_forward(resident, attn_gains.astype(jnp.float32))
    query_proj = jnp.dot(attn_in, query_full, preferred_element_type=jnp.float32).reshape(
        length, query_heads, HEAD_DIM
    )
    keyval_proj = jnp.dot(attn_in, keyval_full, preferred_element_type=jnp.float32)
    key_rows = keyval_proj[:, : kv_heads * HEAD_DIM].reshape(length, kv_heads, HEAD_DIM)
    value_rows = keyval_proj[:, kv_heads * HEAD_DIM :].reshape(length, kv_heads, HEAD_DIM)
    cosine, sine_table = rope_tables(segments[0])
    query_rot = (
        rotate(query_proj, cosine, sine_table)
        .astype(jnp.bfloat16)
        .reshape(length, kv_heads, repeat, HEAD_DIM)
    )
    keys_rot = rotate(key_rows, cosine, sine_table).astype(jnp.bfloat16)
    values_low = value_rows.astype(jnp.bfloat16)
    places = jnp.arange(length)
    visible = (segments[0][:, None] == segments[0][None, :]) & (places[None, :] <= places[:, None])
    scores = jnp.einsum("ikrd,jkd->krij", query_rot, keys_rot, preferred_element_type=jnp.float32)
    attn_logits = jnp.where(visible, scores * score_scale, MASKED)
    attn_exps = jnp.exp(attn_logits - jnp.max(attn_logits, axis=-1, keepdims=True))
    attn_probs = attn_exps / jnp.sum(attn_exps, axis=-1, keepdims=True)
    probs_low = attn_probs.astype(jnp.bfloat16)
    mixed_heads = jnp.einsum(
        "krij,jkd->ikrd", probs_low, values_low, preferred_element_type=jnp.float32
    )
    mixed_low = mixed_heads.reshape(length, query_heads * HEAD_DIM).astype(jnp.bfloat16)
    hidden = resident + jnp.dot(mixed_low, output_full, preferred_element_type=jnp.float32)
    normed_two, inverse_two, moe_in = norm_forward(hidden, moe_gains.astype(jnp.float32))
    router_logits = jnp.dot(moe_in, router_full, preferred_element_type=jnp.float32)
    choose = (routes[:, :, None] == jnp.arange(EXPERTS, dtype=jnp.int32)[None, None, :]).astype(
        jnp.float32
    )
    chosen = jnp.sum(choose * router_logits[:, None, :], axis=-1)
    gate_exps = jnp.exp(chosen - jnp.max(chosen, axis=-1, keepdims=True))
    gate_probs = gate_exps / jnp.sum(gate_exps, axis=-1, keepdims=True)
    entries = routes.reshape(-1)
    entry_count = entries.shape[0]
    onehot = (entries[:, None] == jnp.arange(EXPERTS, dtype=jnp.int32)[None, :]).astype(jnp.int32)
    position = jnp.sum((jnp.cumsum(onehot, axis=0) - 1) * onehot, axis=1)
    slot_index = entries * CAP + position
    owner_entry = (
        jnp.full((EXPERTS * CAP,), entry_count, jnp.int32)
        .at[slot_index]
        .set(jnp.arange(entry_count, dtype=jnp.int32))
    )
    padded_in = jnp.concatenate([moe_in, jnp.zeros((1, model_width), jnp.bfloat16)], axis=0)
    send_rows = jnp.take(padded_in, owner_entry // TOP, axis=0).reshape(EXPERTS, CAP, model_width)
    received = lax.all_to_all(send_rows, "expert", split_axis=0, concat_axis=0, tiled=True)
    slots_now = received.shape[1]
    grouped = received.reshape(owners, local_experts, slots_now, model_width)
    pair_proj = jnp.einsum("secd,edf->secf", grouped, expert_up, preferred_element_type=jnp.float32)
    activated = (jax.nn.silu(pair_proj[..., :FF]) * pair_proj[..., FF:]).astype(jnp.bfloat16)
    produced = jnp.einsum(
        "secf,edf->secd", activated, expert_down, preferred_element_type=jnp.float32
    ).astype(jnp.bfloat16)
    returned = lax.all_to_all(
        produced.reshape(EXPERTS, slots_now, model_width),
        "expert",
        split_axis=0,
        concat_axis=0,
        tiled=True,
    )
    returned, kept_rows, kept_pair = (
        returned,
        received,
        pair_proj.reshape(EXPERTS, slots_now, 2 * FF),
    )
    gathered = (
        jnp.take(returned.reshape(EXPERTS * CAP, model_width), slot_index, axis=0)
        .astype(jnp.float32)
        .reshape(length, TOP, model_width)
    )
    layer_out = (hidden + jnp.sum(gate_probs[:, :, None] * gathered, axis=1)).astype(jnp.bfloat16)
    grad_top = out_grad.astype(jnp.float32)
    gate_grad = jnp.sum(gathered * grad_top[:, None, :], axis=-1)
    chosen_grad = gate_probs * (gate_grad - jnp.sum(gate_probs * gate_grad, axis=-1, keepdims=True))
    logits_grad = jnp.sum(chosen_grad[:, :, None] * choose, axis=1)
    row_grads = (
        (gate_probs[:, :, None] * grad_top[:, None, :])
        .astype(jnp.bfloat16)
        .reshape(entry_count, model_width)
    )
    padded_grads = jnp.concatenate([row_grads, jnp.zeros((1, model_width), jnp.bfloat16)], axis=0)
    send_grads = jnp.take(padded_grads, owner_entry, axis=0).reshape(EXPERTS, CAP, model_width)
    grads_in = lax.all_to_all(send_grads, "expert", split_axis=0, concat_axis=0, tiled=True)
    grouped_rows = kept_rows.reshape(owners, local_experts, CAP, model_width)
    grouped_grads = grads_in.reshape(owners, local_experts, CAP, model_width)
    pair_kept = kept_pair.reshape(owners, local_experts, CAP, 2 * FF)
    gate_half = pair_kept[..., :FF]
    up_half = pair_kept[..., FF:]
    sigmoid_gate = jax.nn.sigmoid(gate_half)
    silu_gate = jax.nn.silu(gate_half)
    activated = (silu_gate * up_half).astype(jnp.bfloat16)
    act_grad = jnp.einsum(
        "secd,edf->secf", grouped_grads, expert_down, preferred_element_type=jnp.float32
    )
    pair_grad = jnp.concatenate(
        [
            act_grad * up_half * sigmoid_gate * (1.0 + gate_half * (1.0 - sigmoid_gate)),
            act_grad * silu_gate,
        ],
        axis=-1,
    ).astype(jnp.bfloat16)
    rows_back = jnp.einsum(
        "secf,edf->secd", pair_grad, expert_up, preferred_element_type=jnp.float32
    ).astype(jnp.bfloat16)
    up_grad = jnp.einsum(
        "secd,secf->edf", grouped_rows, pair_grad, preferred_element_type=jnp.float32
    )
    down_grad = jnp.einsum(
        "secd,secf->edf", grouped_grads, activated, preferred_element_type=jnp.float32
    )
    returned_grads = lax.all_to_all(
        rows_back.reshape(EXPERTS, CAP, model_width),
        "expert",
        split_axis=0,
        concat_axis=0,
        tiled=True,
    )
    expert_up_grad, expert_down_grad = (
        lax.psum_scatter(
            up_grad.astype(jnp.bfloat16), "dp", scatter_dimension=1, tiled=True
        ).astype(jnp.float32),
        lax.psum_scatter(
            down_grad.astype(jnp.bfloat16), "dp", scatter_dimension=1, tiled=True
        ).astype(jnp.float32),
    )
    token_grads = (
        jnp.take(returned_grads.reshape(EXPERTS * CAP, model_width), slot_index, axis=0)
        .astype(jnp.float32)
        .reshape(length, TOP, model_width)
    )
    router_wide = router_full.astype(jnp.float32)
    moe_grad = jnp.sum(token_grads, axis=1) + jnp.dot(logits_grad, router_wide.T, precision=HIGH)
    hidden_norm_grad, moe_gain_grad = norm_backward(
        moe_grad, normed_two, inverse_two, moe_gains.astype(jnp.float32)
    )
    hidden_grad = grad_top + hidden_norm_grad
    attn_out_grad = hidden_grad.astype(jnp.bfloat16)
    mixed_grad = (
        jnp.einsum("td,cd->tc", attn_out_grad, output_full, preferred_element_type=jnp.float32)
        .astype(jnp.bfloat16)
        .reshape(length, kv_heads, repeat, HEAD_DIM)
    )
    probs_grad = jnp.einsum(
        "ikrd,jkd->krij", mixed_grad, values_low, preferred_element_type=jnp.float32
    )
    values_grad = jnp.einsum(
        "krij,ikrd->jkd", probs_low, mixed_grad, preferred_element_type=jnp.float32
    )
    scores_grad = (
        attn_probs
        * (probs_grad - jnp.sum(attn_probs * probs_grad, axis=-1, keepdims=True))
        * score_scale
    ).astype(jnp.bfloat16)
    query_rot_grad = jnp.einsum(
        "krij,jkd->ikrd", scores_grad, keys_rot, preferred_element_type=jnp.float32
    ).reshape(length, query_heads, HEAD_DIM)
    keys_rot_grad = jnp.einsum(
        "krij,ikrd->jkd", scores_grad, query_rot, preferred_element_type=jnp.float32
    )
    query_low = (
        unrotate(query_rot_grad, cosine, sine_table)
        .reshape(length, query_heads * HEAD_DIM)
        .astype(jnp.bfloat16)
    )
    keyval_low = jnp.concatenate(
        [
            unrotate(keys_rot_grad, cosine, sine_table).reshape(length, kv_heads * HEAD_DIM),
            values_grad.reshape(length, kv_heads * HEAD_DIM),
        ],
        axis=1,
    ).astype(jnp.bfloat16)
    attn_in_grad = jnp.einsum(
        "tc,dc->td", query_low, query_full, preferred_element_type=jnp.float32
    ) + jnp.einsum("tc,dc->td", keyval_low, keyval_full, preferred_element_type=jnp.float32)
    token_norm_grad, attn_gain_grad = norm_backward(
        attn_in_grad, normed_one, inverse_one, attn_gains.astype(jnp.float32)
    )
    tokens_grad = hidden_grad + token_norm_grad
    slab_count = lax.axis_size("dp")
    slab_index = lax.axis_index("dp")
    width_rows = model_width // slab_count
    head_rows = query_heads * HEAD_DIM // slab_count
    all_attn, all_query, all_keyval, all_mixed, all_outgrad = (
        lax.all_gather(attn_in, "dp", axis=0, tiled=True),
        lax.all_gather(query_low, "dp", axis=0, tiled=True),
        lax.all_gather(keyval_low, "dp", axis=0, tiled=True),
        lax.all_gather(mixed_low, "dp", axis=0, tiled=True),
        lax.all_gather(attn_out_grad, "dp", axis=0, tiled=True),
    )
    all_moe, all_logits, attn_gain_rows, moe_gain_rows = (
        lax.all_gather(
            moe_in.astype(jnp.float32).astype(jnp.bfloat16), "dp", axis=0, tiled=True
        ).astype(jnp.float32),
        lax.all_gather(logits_grad.astype(jnp.bfloat16), "dp", axis=0, tiled=True).astype(
            logits_grad.dtype
        ),
        lax.all_gather(
            attn_gain_grad[None, :].astype(jnp.bfloat16), "dp", axis=0, tiled=True
        ).astype(jnp.float32),
        lax.all_gather(
            moe_gain_grad[None, :].astype(jnp.bfloat16), "dp", axis=0, tiled=True
        ).astype(jnp.float32),
    )
    attn_cols = lax.dynamic_slice_in_dim(all_attn, slab_index * width_rows, width_rows, 1)
    mixed_cols = lax.dynamic_slice_in_dim(all_mixed, slab_index * head_rows, head_rows, 1)
    moe_cols = lax.dynamic_slice_in_dim(all_moe, slab_index * width_rows, width_rows, 1)
    query_part = jnp.einsum("td,tc->dc", attn_cols, all_query, preferred_element_type=jnp.float32)
    keyval_part = jnp.einsum("td,tc->dc", attn_cols, all_keyval, preferred_element_type=jnp.float32)
    output_part = jnp.einsum(
        "tc,td->cd", mixed_cols, all_outgrad, preferred_element_type=jnp.float32
    )
    router_part = jnp.dot(moe_cols.T, all_logits, precision=HIGH)
    attn_gain_part = lax.dynamic_slice_in_dim(
        jnp.sum(attn_gain_rows, axis=0), slab_index * width_rows, width_rows, 0
    )
    moe_gain_part = lax.dynamic_slice_in_dim(
        jnp.sum(moe_gain_rows, axis=0), slab_index * width_rows, width_rows, 0
    )
    query_share, keyval_share, output_share, router_share, attn_share, moe_share = (
        lax.psum_scatter(
            query_part.astype(jnp.bfloat16), "expert", scatter_dimension=0, tiled=True
        ).astype(jnp.float32),
        lax.psum_scatter(
            keyval_part.astype(jnp.bfloat16), "expert", scatter_dimension=0, tiled=True
        ).astype(jnp.float32),
        lax.psum_scatter(
            output_part.astype(jnp.bfloat16), "expert", scatter_dimension=0, tiled=True
        ).astype(jnp.float32),
        lax.psum_scatter(
            router_part.astype(jnp.bfloat16), "expert", scatter_dimension=0, tiled=True
        ).astype(jnp.float32),
        lax.psum_scatter(
            attn_gain_part.astype(jnp.bfloat16), "expert", scatter_dimension=0, tiled=True
        ).astype(jnp.float32),
        lax.psum_scatter(
            moe_gain_part.astype(jnp.bfloat16), "expert", scatter_dimension=0, tiled=True
        ).astype(jnp.float32),
    )
    return (
        layer_out,
        tokens_grad,
        query_share,
        keyval_share,
        output_share,
        router_share,
        attn_share,
        moe_share,
        expert_up_grad,
        expert_down_grad,
    )


LANES = 128
TAIL = 16
PIECE_LIMIT = 4096
VMEM_BYTES = 60 * 1024 * 1024
F32 = jnp.float32
LOW = jnp.bfloat16


def contract(left, right, left_dim, right_dim):
    return lax.dot_general(
        left, right, (((left_dim,), (right_dim,)), ((), ())), preferred_element_type=F32
    )


def lane_index(shape):
    return lax.broadcasted_iota(jnp.int32, shape, len(shape) - 1)


def row_index(shape):
    return lax.broadcasted_iota(jnp.int32, shape, len(shape) - 2)


def half_turn(chunk):
    first = lane_index(chunk.shape) % HEAD_DIM < HEAD_DIM // 2
    ahead = pltpu.roll(chunk, LANES - HEAD_DIM // 2, 1)
    behind = pltpu.roll(chunk, HEAD_DIM // 2, 1)
    return jnp.where(first, ahead, behind)


def both_heads(chunk, pick):
    swapped = pltpu.roll(chunk, HEAD_DIM, 1)
    first = lane_index(chunk.shape) < HEAD_DIM
    if pick == 0:
        return jnp.where(first, chunk, swapped)
    return jnp.where(first, swapped, chunk)


def split_heads(chunk):
    first = lane_index(chunk.shape) < HEAD_DIM
    zero = jnp.zeros_like(chunk)
    return jnp.concatenate([jnp.where(first, chunk, zero), jnp.where(first, zero, chunk)], axis=0)


def join_heads(stacked):
    length = stacked.shape[0] // 2
    top, bottom = stacked[:length], stacked[length:]
    return jnp.where(lane_index(top.shape) < HEAD_DIM, top, bottom)


def three_parts(values):
    high = values.astype(LOW).astype(F32)
    rest = values - high
    middle = rest.astype(LOW).astype(F32)
    return (high, middle, rest - middle)


def gain_select():
    shape = (8, LANES)
    return (lane_index(shape) == EXPERTS + row_index(shape)) & (row_index(shape) < 2)


def load_weights(rows_ref, spots, piece_refs, weights, sems):
    copies = []
    for spot, piece in zip(spots, piece_refs):
        for i, (p, w) in enumerate(spot):
            size = piece.shape[1]
            start = pl.multiple_of(rows_ref[p, w] * size, size)
            copies.append(
                pltpu.make_async_copy(piece.at[i], weights.at[pl.ds(start, size)], sems.at[p, w])
            )
    for copy in copies:
        copy.start()
    return copies


def store_sums(rows_ref, sums, grads_even, grads_odd, sems):
    copies = []
    for p in range(2 * grads_even.shape[0]):
        target = grads_even if p % 2 == 0 else grads_odd
        for w in range(target.shape[1]):
            size = target.shape[2]
            start = pl.multiple_of(rows_ref[p, w] * size, size)
            copies.append(
                pltpu.make_async_copy(
                    sums.at[pl.ds(start, size)], target.at[p // 2, w], sems.at[p, w]
                )
            )
    for copy in copies:
        copy.start()
    return copies


def softmax_rows(q_pair, k_both, visible):
    scores = contract(q_pair, k_both, 1, 1) * (HEAD_DIM ** (-0.5))
    logits = jnp.where(visible, scores, MASKED)
    exps = jnp.exp(logits - jnp.max(logits, axis=-1, keepdims=True))
    return exps / jnp.sum(exps, axis=-1, keepdims=True)


def segment_tables(seg_row, frequency):
    length = seg_row.shape[1]
    shape = (length, length)
    across_row = jnp.broadcast_to(seg_row.astype(F32), shape)
    down_col = across_row.T
    seen = (down_col == across_row) & (lane_index(shape) <= row_index(shape))
    visible = jnp.concatenate([seen, seen], axis=0)
    if frequency is None:
        return visible
    earlier = jnp.sum(jnp.where(across_row < down_col, 1.0, 0.0), axis=1, keepdims=True)
    angles = (row_index(shape).astype(F32) - earlier) * frequency
    sine = jnp.sin(angles)
    first = lane_index(shape) % HEAD_DIM < HEAD_DIM // 2
    return (visible, jnp.cos(angles), jnp.where(first, -sine, sine))


def attn_forward_kernel(spots, *refs):
    count = len(spots)
    rows_ref, tokens_ref, seg_row, frequency = refs[:4]
    pieces = refs[4 : 4 + count]
    query_ref, keyval_ref, mixed_ref, tail_ref, cos_ref, sin_ref, weights, sems = refs[4 + count :]
    copies = load_weights(rows_ref, spots, pieces, weights, sems)
    tokens = tokens_ref[...].astype(F32)
    inverse = lax.rsqrt(jnp.mean(tokens * tokens, axis=-1, keepdims=True) + EPS)
    normed = tokens * inverse
    width = tokens.shape[1]
    visible, cosine, sine = segment_tables(seg_row[...], frequency[...])
    cos_ref[...] = cosine
    sin_ref[...] = sine
    for copy in copies:
        copy.wait()
    tail = weights[:, 2 * width :]
    tail_ref[...] = tail
    gains = contract(gain_select().astype(F32).astype(LOW), tail, 1, 1)
    attn_in = (normed * gains[0:1]).astype(LOW)
    keyval = contract(attn_in, weights[:, width : 2 * width], 1, 0)
    query = contract(attn_in, weights[:, :width], 1, 0)
    half = width // 2
    for m in range(half // LANES):
        keys = keyval[:, m * LANES : (m + 1) * LANES]
        keys = (keys * cosine + half_turn(keys) * sine).astype(LOW)
        values = keyval[:, half + m * LANES : half + (m + 1) * LANES].astype(LOW)
        keyval_ref[:, m * LANES : (m + 1) * LANES] = keys
        keyval_ref[:, half + m * LANES : half + (m + 1) * LANES] = values
        for pick in range(2):
            k_both = both_heads(keys.astype(F32), pick).astype(LOW)
            v_both = both_heads(values.astype(F32), pick).astype(LOW)
            chunk = slice((2 * m + pick) * LANES, (2 * m + pick + 1) * LANES)
            queries = query[:, chunk]
            queries = (queries * cosine + half_turn(queries) * sine).astype(LOW)
            query_ref[:, chunk] = queries
            q_pair = split_heads(queries.astype(F32)).astype(LOW)
            probs = softmax_rows(q_pair, k_both, visible).astype(LOW)
            mixed_ref[:, chunk] = join_heads(contract(probs, v_both, 1, 0)).astype(LOW)


def router_kernel(spots, *refs):
    count = len(spots)
    rows_ref, tokens_ref, mixed_ref, tail_ref, routes_t = refs[:5]
    pieces = refs[5 : 5 + count]
    payload, hidden_ref, gates_ref, weights, sems = refs[5 + count :]
    copies = load_weights(rows_ref, spots, pieces, weights, sems)
    tokens = tokens_ref[...].astype(F32)
    length = tokens.shape[0]
    tail = tail_ref[...]
    gains = contract(gain_select().astype(F32).astype(LOW), tail, 1, 1)
    for copy in copies:
        copy.wait()
    hidden = tokens + contract(mixed_ref[...], weights[...], 1, 0)
    hidden_ref[...] = hidden
    inverse_two = lax.rsqrt(jnp.mean(hidden * hidden, axis=-1, keepdims=True) + EPS)
    moe_in = (hidden * inverse_two * gains[1:2]).astype(LOW)
    payload[:length] = moe_in
    logits = contract(moe_in, tail, 1, 0)
    turned = routes_t[...]
    experts = row_index((LANES, length))
    chosen = experts == turned[0:1]
    for k in range(1, TOP):
        chosen = chosen | (experts == turned[k : k + 1])
    chosen = jnp.where(chosen, 1.0, 0.0).T > 0.5
    logits = jnp.where(chosen, logits, MASKED)
    exps = jnp.where(chosen, jnp.exp(logits - jnp.max(logits, axis=-1, keepdims=True)), 0.0)
    gates = exps / jnp.sum(exps, axis=-1, keepdims=True)
    gates_ref[...] = gates
    gates_t = gates.T
    for k in range(TOP):
        row = turned[k : k + 1]
        gate = jnp.sum(jnp.where(experts == row, gates_t, 0.0), axis=0, keepdims=True)
        high, middle, rest = three_parts(gate)
        place = row_index((TAIL, length))
        block = jnp.where(place == 0, high, jnp.where(place == 1, middle, jnp.where(place == 2, rest, 0.0)))
        block = jnp.where(place == 3, row.astype(F32), block)
        payload[length:, k * length : (k + 1) * length] = block.astype(LOW)


def slot_places(first_expert, local, tails, before):
    length = tails[0].shape[1] // TOP
    ids = row_index((8, length))
    ids = jnp.where(ids < local, ids + first_expert, -1).astype(F32)
    masks, gates = [], []
    for tail in tails:
        mask = jnp.zeros((8, length), F32)
        gate = jnp.zeros((8, length), F32)
        for k in range(TOP):
            part = tail[:, k * length : (k + 1) * length].astype(F32)
            hit = part[3:4] == ids
            mask = jnp.where(hit, 1.0, mask)
            gate = jnp.where(hit, part[0:1] + part[1:2] + part[2:3], gate)
        masks.append(mask)
        gates.append(gate)
    pairs = range(0, len(tails), 2)
    mask = jnp.concatenate([jnp.concatenate(masks[i : i + 2], axis=1) for i in pairs], axis=0)
    gate = jnp.concatenate([jnp.concatenate(gates[i : i + 2], axis=1) for i in pairs], axis=0)
    place = contract(mask.astype(LOW), before, 1, 0)
    return (jnp.where(mask > 0, place, -1.0), gate)


def gather_pair(local, block, pair, place, gate, row_pair, grad_pair, out):
    rows_out, grads_out, select_out, gate_out = out
    slots = row_index((block, place.shape[1])).astype(F32)
    parts = []
    for j in range(local):
        hit = slots == place[j : j + 1]
        parts.append(jnp.where(hit, 1.0, 0.0))
        held = jnp.where(hit, gate[j : j + 1], 0.0)
        held = jnp.sum(held, axis=1, keepdims=True)
        gate_out[j, pair * block : (pair + 1) * block] = jnp.broadcast_to(held, (block, LANES))
    select = jnp.concatenate(parts, axis=0).astype(LOW)
    if select_out is not None:
        select_out[pair] = select
    rows = contract(select, jnp.concatenate(row_pair, axis=0), 1, 0).astype(LOW)
    grads = contract(select, jnp.concatenate(grad_pair, axis=0), 1, 0).astype(LOW)
    for j in range(local):
        rows_out[j, pair * block : (pair + 1) * block] = rows[j * block : (j + 1) * block]
        grads_out[j, pair * block : (pair + 1) * block] = grads[j * block : (j + 1) * block]


def earlier_matrix(length):
    shape = (2 * length, 2 * length)
    return jnp.where(row_index(shape) < lane_index(shape), 1.0, 0.0).astype(LOW)


def expert_step(j, rows, grads, gate_ref, up, down):
    hidden_units = down.shape[1]
    pair = contract(rows[j], up, 1, 0)
    raw = contract(grads[j], down, 1, 0)
    gate_half, up_half = pair[:, :hidden_units], pair[:, hidden_units:]
    gate = gate_ref[j][:, 0:1]
    sigmoid = 1.0 / (1.0 + jnp.exp(-gate_half))
    silu = gate_half * sigmoid
    activated = silu * up_half
    scaled = (gate * activated).astype(LOW)
    act_grad = gate * raw
    pair_grad = jnp.concatenate(
        [act_grad * up_half * sigmoid * (1.0 + gate_half * (1.0 - sigmoid)), act_grad * silu],
        axis=1,
    ).astype(LOW)
    gate_grad = jnp.sum(activated * raw, axis=1, keepdims=True)
    return (scaled, pair_grad, gate_grad)


def fetch_experts(local, up_hbm, down_hbm, up, down, sems):
    copies = []
    for j in range(local):
        copies.append(
            (
                pltpu.make_async_copy(up_hbm.at[j], up.at[j], sems.at[0, j]),
                pltpu.make_async_copy(down_hbm.at[j], down.at[j], sems.at[1, j]),
            )
        )
        for copy in copies[j]:
            copy.start()
    return copies


def expert_home_kernel(owners, local, block, *refs):
    place_ref = refs[0]
    rows_in = refs[1 : 1 + owners]
    grads_in = refs[1 + owners : 1 + 2 * owners]
    up_hbm, down_hbm = refs[1 + 2 * owners : 3 + 2 * owners]
    back_even, back_odd = refs[3 + 2 * owners : 5 + 2 * owners]
    kept = refs[5 + 2 * owners : 10 + 2 * owners]
    scratch = refs[10 + 2 * owners :]
    up, down, rows, grads, select, gate_ref, scaled, pair_grads, returned, sems = scratch
    copies = fetch_experts(local, up_hbm, down_hbm, up, down, sems)
    length = rows_in[0].shape[0] - TAIL
    width = rows_in[0].shape[1]
    first_expert = place_ref[0] * local
    slab = kept[3].shape[2]
    columns = pl.ds(pl.multiple_of(place_ref[1] * slab, slab), slab)
    before = earlier_matrix(length)
    place, gate = slot_places(first_expert, local, [ref[length:] for ref in rows_in], before)
    for s in range(owners // 2):
        gather_pair(
            local,
            block,
            s,
            place[8 * s : 8 * s + 8],
            gate[8 * s : 8 * s + 8],
            [rows_in[2 * s][:length], rows_in[2 * s + 1][:length]],
            [grads_in[2 * s][...], grads_in[2 * s + 1][...]],
            (rows, grads, select, gate_ref),
        )
    sent = [
        pltpu.make_async_copy(select, kept[0], sems.at[2, 0]),
        pltpu.make_async_copy(rows.at[:, :, columns], kept[3], sems.at[2, 1]),
        pltpu.make_async_copy(grads.at[:, :, columns], kept[4], sems.at[2, 2]),
    ]
    for copy in sent:
        copy.start()
    for j in range(local):
        for copy in copies[j]:
            copy.wait()
    for j in range(local):
        made, pair_grad, gate_grad = expert_step(j, rows, grads, gate_ref, up[j], down[j])
        scaled[j] = made
        pair_grads[j] = pair_grad
        sent.append(pltpu.make_async_copy(scaled.at[j], kept[1].at[j], sems.at[3, j]))
        sent.append(pltpu.make_async_copy(pair_grads.at[j], kept[2].at[j], sems.at[4, j]))
        sent[-2].start()
        sent[-1].start()
        returned[j, :, :width] = contract(pair_grad, up[j], 1, 1).astype(LOW)
        lanes = lane_index((made.shape[0], LANES)) - first_expert - j
        high, middle, rest = three_parts(gate_grad)
        tail = jnp.where(lanes == 0, high, 0.0)
        tail = jnp.where(lanes == EXPERTS, middle, tail)
        tail = jnp.where(lanes == 2 * EXPERTS, rest, tail)
        returned[j, :, width:] = tail.astype(LOW)
    for s in range(owners // 2):
        span = slice(s * block, (s + 1) * block)
        back = jnp.concatenate([returned[j, span] for j in range(local)], axis=0)
        back = contract(select[s], back, 0, 0).astype(LOW)
        back_even[s] = back[:length]
        back_odd[s] = back[length:]
    for copy in sent:
        copy.wait()


def expert_finish_kernel(local, block, *refs):
    select, scaled, pair_grads, rows, grads, down = refs[:6]
    out_even, out_odd, up_grad, down_grad, produced = refs[6:]
    length = out_even.shape[1]
    for j in range(local):
        produced[j] = contract(scaled[j], down[j], 1, 1).astype(LOW)
        up_grad[j] = contract(rows[j], pair_grads[j], 0, 0)
        down_grad[j] = contract(grads[j], scaled[j], 0, 0)
    for s in range(out_even.shape[0]):
        span = slice(s * block, (s + 1) * block)
        made = jnp.concatenate([produced[j, span] for j in range(local)], axis=0)
        made = contract(select[s], made, 0, 0).astype(LOW)
        out_even[s] = made[:length]
        out_odd[s] = made[length:]


def expert_away_kernel(start, count, block, chips, far, *refs):
    place_ref = refs[0]
    rows_in = refs[1 : 3 + 2 * chips]
    grads_in = refs[3 + 2 * chips : 3 + 4 * chips]
    up_hbm, down_hbm, up_first, down_first = refs[3 + 4 * chips : 7 + 4 * chips]
    up_grad, down_grad = refs[7 + 4 * chips : 9 + 4 * chips]
    scratch = refs[9 + 4 * chips :]
    up, down, up_sum, down_sum, rows_buf, grads_buf, rows, grads, gate_ref, sems, pair_sems = scratch
    length = grads_buf.shape[1] // 2
    tall = length + TAIL
    pairs = []
    for i in range(far + 1):
        for s in range(chips):
            spot = len(pairs)
            copies = []
            for side in range(2):
                grad_from = grads_in[2 * s + side].at[pl.ds(i * length, length)]
                if i == 0:
                    row_from = rows_in[side].at[s]
                else:
                    row_from = rows_in[2 + 2 * s + side].at[pl.ds((i - 1) * tall, tall)]
                row_to = rows_buf.at[spot, pl.ds(side * tall, tall)]
                grad_to = grads_buf.at[spot, pl.ds(side * length, length)]
                copies.append(pltpu.make_async_copy(row_from, row_to, pair_sems.at[0, side, spot]))
                copies.append(pltpu.make_async_copy(grad_from, grad_to, pair_sems.at[1, side, spot]))
            pairs.append(copies)
    for copies in pairs:
        for copy in copies:
            copy.start()
    held = []
    for j in range(count):
        held.append(
            [
                pltpu.make_async_copy(up_hbm.at[start + j], up.at[j], sems.at[0, j]),
                pltpu.make_async_copy(down_hbm.at[start + j], down.at[j], sems.at[1, j]),
                pltpu.make_async_copy(up_first.at[start + j], up_sum.at[j], sems.at[2, j]),
                pltpu.make_async_copy(down_first.at[start + j], down_sum.at[j], sems.at[3, j]),
            ]
        )
    for copies in held:
        for copy in copies:
            copy.start()
    first_expert = place_ref[0] * (up_hbm.shape[0]) + start
    slab = up_sum.shape[1]
    columns = pl.ds(pl.multiple_of(place_ref[1] * slab, slab), slab)
    before = earlier_matrix(length)
    for i, copies in enumerate(pairs):
        for copy in copies:
            copy.wait()
        tails = [rows_buf[i, length:tall], rows_buf[i, tall + length :]]
        place, gate = slot_places(first_expert, count, tails, before)
        gather_pair(
            count,
            block,
            i,
            place,
            gate,
            [rows_buf[i, :length], rows_buf[i, tall : tall + length]],
            [grads_buf[i]],
            (rows, grads, None, gate_ref),
        )
    for copies in held:
        for copy in copies:
            copy.wait()
    sent = []
    for j in range(count):
        scaled, pair_grad, _ = expert_step(j, rows, grads, gate_ref, up[j], down[j])
        up_sum[j] += contract(rows[j, :, columns], pair_grad, 0, 0)
        down_sum[j] += contract(grads[j, :, columns], scaled, 0, 0)
        sent.append(pltpu.make_async_copy(up_sum.at[j], up_grad.at[start + j], sems.at[4, j]))
        sent.append(pltpu.make_async_copy(down_sum.at[j], down_grad.at[start + j], sems.at[5, j]))
        sent[-2].start()
        sent[-1].start()
    for copy in sent:
        copy.wait()


def backward_kernel(spots, output_spots, shares, *refs):
    rows_ref, tokens_ref, seg_row, cos_ref, sin_ref, payload, hidden_ref = refs[:7]
    query_ref, keyval_ref, mixed_ref, gates_ref, out_grad_ref, tail_ref = refs[7:13]
    refs = refs[13:]
    back, refs = refs[:shares], refs[shares:]
    pieces, refs = refs[: len(spots)], refs[len(spots) :]
    output_pieces, refs = refs[: len(output_spots)], refs[len(output_spots) :]
    tokens_grad, grads_even, grads_odd = refs[:3]
    weights, output, sums, query_low, keyval_low, sems, output_sems, out_sems = refs[3:]
    output_copies = load_weights(rows_ref, output_spots, output_pieces, output, output_sems)
    copies = load_weights(rows_ref, spots, pieces, weights, sems)
    length, width = tokens_ref.shape
    half = width // 2
    columns = weights.shape[1]
    total = back[0][...].astype(F32)
    for share in back[1:]:
        total = total + share[...].astype(F32)
    parts = total[:, width:]
    lanes = lane_index(parts.shape)
    gate_grad = parts + pltpu.roll(parts, LANES - EXPERTS, 1) + pltpu.roll(parts, LANES - 2 * EXPERTS, 1)
    gate_grad = jnp.where(lanes < EXPERTS, gate_grad, 0.0)
    gates = gates_ref[...]
    logits_grad = gates * (gate_grad - jnp.sum(gates * gate_grad, axis=-1, keepdims=True))
    hidden = hidden_ref[...]
    inverse_two = lax.rsqrt(jnp.mean(hidden * hidden, axis=-1, keepdims=True) + EPS)
    normed_two = hidden * inverse_two
    tail = tail_ref[...]
    gains = contract(gain_select().astype(F32).astype(LOW), tail, 1, 1)
    high = logits_grad.astype(LOW)
    rest = (logits_grad - high.astype(F32)).astype(LOW)
    moe_grad = total[:, :width] + contract(high, tail, 1, 1) + contract(rest, tail, 1, 1)
    moe_gain_grad = jnp.sum(moe_grad * normed_two, axis=0, keepdims=True)
    scaled = moe_grad * gains[1:2]
    hidden_grad = out_grad_ref[...].astype(F32) + inverse_two * (
        scaled - normed_two * jnp.mean(scaled * normed_two, axis=-1, keepdims=True)
    )
    attn_out_grad = hidden_grad.astype(LOW)
    for copy in output_copies:
        copy.wait()
    mixed_grad = contract(attn_out_grad, output[...], 1, 1)
    sums[:, columns:] = contract(mixed_ref[...], attn_out_grad, 0, 0).astype(LOW)
    tokens = tokens_ref[...].astype(F32)
    inverse_one = lax.rsqrt(jnp.mean(tokens * tokens, axis=-1, keepdims=True) + EPS)
    normed_one = tokens * inverse_one
    cosine, sine = cos_ref[...], sin_ref[...]
    visible = segment_tables(seg_row[...], None)
    groups = range(width // LANES)
    chunks = [slice(g * LANES, (g + 1) * LANES) for g in groups]
    keys = [keyval_ref[:, chunks[m]].astype(F32) for m in range(half // LANES)]
    values = [keyval_ref[:, half + m * LANES : half + (m + 1) * LANES].astype(F32) for m in range(half // LANES)]
    k_both = [both_heads(keys[g // 2], g % 2).astype(LOW) for g in groups]
    v_both = [both_heads(values[g // 2], g % 2).astype(LOW) for g in groups]
    q_pair = [split_heads(query_ref[:, chunk].astype(F32)).astype(LOW) for chunk in chunks]
    probs = [softmax_rows(q_pair[g], k_both[g], visible) for g in groups]
    m_pair = [split_heads(mixed_grad[:, chunk]).astype(LOW) for chunk in chunks]
    probs_grad = [contract(m_pair[g], v_both[g], 1, 1) for g in groups]
    value_sides = [contract(probs[g].astype(LOW), m_pair[g], 0, 0) for g in groups]
    scores_grad = [
        (
            probs[g]
            * (probs_grad[g] - jnp.sum(probs[g] * probs_grad[g], axis=-1, keepdims=True))
            * (HEAD_DIM ** (-0.5))
        ).astype(LOW)
        for g in groups
    ]
    query_grad = [join_heads(contract(scores_grad[g], k_both[g], 1, 0)) for g in groups]
    key_sides = [contract(scores_grad[g], q_pair[g], 0, 0) for g in groups]
    for g in groups:
        turned = query_grad[g] * cosine - half_turn(query_grad[g]) * sine
        query_low[:, chunks[g]] = turned.astype(LOW)
    key_sides = [side + pltpu.roll(side, HEAD_DIM, 1) for side in key_sides]
    value_sides = [side + pltpu.roll(side, HEAD_DIM, 1) for side in value_sides]
    first = lane_index((length, LANES)) < HEAD_DIM
    for m in range(half // LANES):
        keys_grad = jnp.where(first, key_sides[2 * m], key_sides[2 * m + 1])
        values_grad = jnp.where(first, value_sides[2 * m], value_sides[2 * m + 1])
        turned = keys_grad * cosine - half_turn(keys_grad) * sine
        keyval_low[:, chunks[m]] = turned.astype(LOW)
        keyval_low[:, half + m * LANES : half + (m + 1) * LANES] = values_grad.astype(LOW)
    for copy in copies:
        copy.wait()
    attn_in_grad = contract(query_low[...], weights[:, :width], 1, 1) + contract(
        keyval_low[...], weights[:, width : 2 * width], 1, 1
    )
    attn_in = (normed_one * gains[0:1]).astype(LOW)
    sums[:, :width] = contract(attn_in, query_low[...], 0, 0).astype(LOW)
    sums[:, width : 2 * width] = contract(attn_in, keyval_low[...], 0, 0).astype(LOW)
    attn_gain_grad = jnp.sum(attn_in_grad * normed_one, axis=0, keepdims=True)
    place = row_index((8, width))
    gain_grads = jnp.where(place == 0, attn_gain_grad, jnp.where(place == 1, moe_gain_grad, 0.0))
    sums[:, 2 * width : columns] = (
        contract(payload[:length], high, 0, 0)
        + contract(gain_grads.astype(LOW), gain_select().astype(F32).astype(LOW), 0, 0)
    ).astype(LOW)
    out_copies = store_sums(rows_ref, sums, grads_even, grads_odd, out_sems)
    scaled = attn_in_grad * gains[0:1]
    tokens_grad[...] = hidden_grad + inverse_one * (
        scaled - normed_one * jnp.mean(scaled * normed_one, axis=-1, keepdims=True)
    )
    for copy in out_copies:
        copy.wait()


def swap(values, axis, size, distance):
    return lax.ppermute(values, axis, [(i, i ^ distance) for i in range(size)])


def across(values, distance, planes):
    return swap(values, "dp", planes, distance)


def aside(values, s, owners):
    return swap(values, "expert", owners, 2 * s)


def partner(values, owners):
    return swap(values, "expert", owners, 1)


def after(values, *earlier):
    return lax.optimization_barrier((values,) + earlier)[0]


def over_chips(values, owners):
    return [values] + [aside(values, s, owners) for s in range(1, owners // 2)]


def over_cores(near, owners, *earlier):
    pieces = []
    for piece in near:
        pieces += [piece, partner(after(piece, *earlier) if earlier else piece, owners)]
    return pieces


def chips_split(values, owners, *earlier):
    half = values.shape[0] // 2
    first, second = aside(values, 1, owners), aside(values, 2, owners)
    far = [first[:half], second[half:]]
    if earlier:
        far = [after(part, *earlier) for part in far]
    far = [aside(far[0], 2, owners), aside(far[1], 1, owners)]
    return [[values], [first], [second], far]


def core_pieces(groups, owners, *earlier):
    pieces, spots = [], []
    for group in groups:
        parts = [part for part, _ in group]
        merged = parts[0] if len(parts) == 1 else jnp.concatenate(parts, axis=0)
        merged = after(merged, *earlier) if earlier else merged
        for part, spot in group:
            pieces.append(part)
            spots.append(spot)
        pieces.append(partner(merged, owners))
        spots.append([(p + 1, w) for _, spot in group for p, w in spot])
    return (pieces, spots)


def core_pieces_whole(near, owners):
    pieces = []
    for parts in near:
        piece = parts[0] if len(parts) == 1 else jnp.concatenate(parts, axis=0)
        pieces.append((piece, partner(piece, owners)))
    return pieces


def added(left, right):
    return (left.astype(F32) + right.astype(F32)).astype(LOW)


def to_owners(even, odd, owners, *earlier):
    other = partner(odd, owners)
    joined = [added(even[s], other[s]) for s in range(owners // 2)]
    if earlier:
        joined = lax.optimization_barrier(tuple(joined) + earlier)[: owners // 2]
    sent = [joined[0]] + [aside(joined[s], s, owners) for s in range(1, owners // 2)]
    return (joined, sent)


def to_neighbours(joined, owners):
    half = joined[3].shape[0] // 2
    low_turn = aside(joined[3][:half], 1, owners)
    top_turn = aside(joined[3][half:], 2, owners)
    low_turn, top_turn = lax.optimization_barrier((low_turn, top_turn))
    first = jnp.concatenate([joined[1][:half], added(joined[1][half:], top_turn)], axis=0)
    second = jnp.concatenate([added(joined[2][:half], low_turn), joined[2][half:]], axis=0)
    return (first, second)


def from_neighbours(joined, first, second, owners):
    parts = [joined[0], aside(first, 1, owners), aside(second, 2, owners)]
    return sum(part.astype(F32) for part in parts).astype(LOW)


def over_planes_sum(parts, planes):
    total = parts[0].astype(F32)
    for w in range(1, planes):
        total = total + across(parts[w], w, planes).astype(F32)
    return total


def cost(us):
    return pl.CostEstimate(flops=int(us * 1153e6), bytes_accessed=0, transcendentals=0)


def params():
    return pltpu.CompilerParams(vmem_limit_bytes=VMEM_BYTES)


def whole_spec():
    return pl.BlockSpec(memory_space=pltpu.VMEM)


def hbm_spec():
    return pl.BlockSpec(memory_space=pl.ANY)


def smem_spec():
    return pl.BlockSpec(memory_space=pltpu.SMEM)


def on_device(
    planes,
    owners,
    tokens,
    segments,
    routes,
    query_weight,
    keyval_weight,
    output_weight,
    router_weight,
    attn_gain,
    moe_gain,
    expert_up,
    expert_down,
    out_grad,
):
    length, width = tokens.shape
    if planes != 4 or owners != 8 or planes * owners * length > PIECE_LIMIT:
        return on_device_wide(
            tokens,
            segments,
            routes,
            query_weight,
            keyval_weight,
            output_weight,
            router_weight,
            attn_gain,
            moe_gain,
            expert_up,
            expert_down,
            out_grad,
        )
    local = expert_up.shape[0]
    hidden_units = expert_down.shape[2]
    block = 2 * CAP
    slots = owners // 2 * block
    plane = lax.axis_index("dp")
    owner = lax.axis_index("expert")
    share = query_weight.shape[0]
    rows = (plane ^ jnp.arange(planes))[None, :] * owners + (owner ^ jnp.arange(owners))[:, None]
    rows = rows.astype(jnp.int32)
    place = jnp.stack([owner, plane]).astype(jnp.int32)
    lanes = jnp.arange(LANES)[None, :]
    extra = jnp.pad(router_weight, ((0, 0), (0, LANES - EXPERTS)))
    extra = jnp.where(lanes == EXPERTS, attn_gain[:, None], extra)
    extra = jnp.where(lanes == EXPERTS + 1, moe_gain[:, None], extra)
    packed = jnp.concatenate([query_weight, keyval_weight, extra, output_weight], axis=1)
    columns = packed.shape[1] - width

    early = [across(packed, w, planes) for w in range(1, planes)]
    grad_chips = over_chips(out_grad, owners)
    grad_cores = partner(jnp.concatenate(grad_chips, axis=0), owners)
    gathered = jnp.stack([packed] + early)
    grad_start = after(out_grad, *early)
    grad_planes = [across(grad_start, w, planes) for w in range(1, planes)]
    near = chips_split(
        after(gathered[:, :, :columns], *grad_chips), owners, grad_planes[0]
    )
    every = list(range(planes))
    groups = [[(near[s][0], [(2 * s, w) for w in every])] for s in range(3)]
    groups += [
        [(near[3][0], [(6, w) for w in every[: planes // 2]])],
        [(near[3][1], [(6, w) for w in every[planes // 2 :]])],
    ]
    pieces, spots = core_pieces(groups, owners)
    output_near = over_chips(after(gathered[:, :, columns:], *pieces[:6], *near[3]), owners)

    half_dim = HEAD_DIM // 2
    frequency = ROPE_BASE ** (-(jnp.arange(half_dim, dtype=F32) * 2.0) / HEAD_DIM)
    frequency = jnp.tile(frequency, LANES // half_dim)[None, :]

    token_low = jax.ShapeDtypeStruct((length, width), LOW)
    token_wide = jax.ShapeDtypeStruct((length, width), F32)
    table = jax.ShapeDtypeStruct((length, LANES), F32)
    query_rot, keyval_low, mixed_low, tail, cosine, sine = pl.pallas_call(
        functools.partial(attn_forward_kernel, spots),
        out_shape=(token_low, token_low, token_low, jax.ShapeDtypeStruct((width, LANES), LOW))
        + (table, table),
        in_specs=[smem_spec()] + [whole_spec()] * 3 + [hbm_spec()] * len(pieces),
        out_specs=[whole_spec()] * 6,
        scratch_shapes=[
            pltpu.VMEM((width, columns), LOW),
            pltpu.SemaphoreType.DMA((owners, planes)),
        ],
        compiler_params=params(),
        cost_estimate=cost(6),
        name="attn_forward",
    )(rows, after(tokens, grad_planes[1]), segments, frequency, *pieces)

    output_pieces, output_spots = core_pieces(
        [[(output_near[s], [(2 * s, w) for w in every])] for s in range(owners // 2)],
        owners,
        mixed_low,
    )

    grad_stack = jnp.concatenate(grad_planes, axis=0)

    payload, hidden, gates = pl.pallas_call(
        functools.partial(router_kernel, output_spots),
        out_shape=(
            jax.ShapeDtypeStruct((length + TAIL, width), LOW),
            token_wide,
            jax.ShapeDtypeStruct((length, LANES), F32),
        ),
        in_specs=[smem_spec()] + [whole_spec()] * 4 + [hbm_spec()] * len(output_pieces),
        out_specs=[whole_spec()] * 3,
        scratch_shapes=[
            pltpu.VMEM((width, width), LOW),
            pltpu.SemaphoreType.DMA((owners, planes)),
        ],
        compiler_params=params(),
        cost_estimate=cost(4),
        name="router",
    )(
        rows,
        tokens,
        after(mixed_low, grad_cores),
        tail,
        routes.T,
        *output_pieces,
    )

    row_chips = over_chips(payload, owners)
    row_home = over_cores(row_chips[:3], owners) + over_cores(row_chips[3:], owners, grad_stack)
    grad_other = partner(after(grad_stack, payload), owners)
    row_start = after(payload, row_home[1])
    row_planes = [across(row_start, w, planes) for w in range(2, planes)]
    row_near = across(jnp.stack(row_chips), 1, planes)
    grad_direct = after(grad_stack, *row_chips)
    grad_near = [aside(grad_direct, s, owners) for s in (1, 2)]

    def all_of(shape):
        return pl.BlockSpec(shape, lambda i: (0,) * len(shape))

    slab = width // planes
    slabs = (
        jax.ShapeDtypeStruct((local, slab, 2 * hidden_units), F32),
        jax.ShapeDtypeStruct((local, slab, hidden_units), F32),
    )
    home_blocks = [s * (p % 2) for s in range(owners // 2) for p in range(2)]
    grad_home = [part for s in range(owners // 2) for part in (grad_chips[s], grad_cores)]
    chip_rows = jax.ShapeDtypeStruct((owners // 2, length, width), LOW)
    chip_back = jax.ShapeDtypeStruct((owners // 2, length, width + LANES), LOW)
    back_even, back_odd, *kept = pl.pallas_call(
        functools.partial(expert_home_kernel, owners, local, block),
        grid=(1,),
        out_shape=(
            chip_back,
            chip_back,
            jax.ShapeDtypeStruct((owners // 2, local * block, 2 * length), LOW),
            jax.ShapeDtypeStruct((local, slots, hidden_units), LOW),
            jax.ShapeDtypeStruct((local, slots, 2 * hidden_units), LOW),
            jax.ShapeDtypeStruct((local, slots, slab), LOW),
            jax.ShapeDtypeStruct((local, slots, slab), LOW),
        ),
        in_specs=[smem_spec()]
        + [all_of((length + TAIL, width))] * owners
        + [pl.BlockSpec((length, width), lambda i, s=s: (s, 0)) for s in home_blocks]
        + [hbm_spec()] * 2,
        out_specs=[all_of(chip_back.shape)] * 2 + [hbm_spec()] * 5,
        scratch_shapes=[
            pltpu.VMEM(expert_up.shape, LOW),
            pltpu.VMEM(expert_down.shape, LOW),
            pltpu.VMEM((local, slots, width), LOW),
            pltpu.VMEM((local, slots, width), LOW),
            pltpu.VMEM((owners // 2, local * block, 2 * length), LOW),
            pltpu.VMEM((local, slots, LANES), F32),
            pltpu.VMEM((local, slots, hidden_units), LOW),
            pltpu.VMEM((local, slots, 2 * hidden_units), LOW),
            pltpu.VMEM((local, slots, width + LANES), LOW),
            pltpu.SemaphoreType.DMA((5, local)),
        ],
        compiler_params=params(),
        cost_estimate=cost(18),
        name="expert_home",
    )(place, *row_home, *grad_home, expert_up, expert_down)
    out_even, out_odd, up_grad, down_grad = pl.pallas_call(
        functools.partial(expert_finish_kernel, local, block),
        out_shape=(chip_rows, chip_rows) + slabs,
        in_specs=[whole_spec()] * 6,
        out_specs=[whole_spec()] * 4,
        scratch_shapes=[pltpu.VMEM((local, slots, width), LOW)],
        compiler_params=params(),
        cost_estimate=cost(8),
        name="expert_finish",
    )(*kept, expert_down)

    joined, back = to_owners(back_even, after(back_odd, grad_other, *grad_near, *row_planes), owners)
    late_rows = lax.optimization_barrier(tuple(row_planes) + tuple(joined))
    row_stack = jnp.concatenate(late_rows[: planes - 2], axis=0)
    row_far = chips_split(after(row_stack, *back), owners)
    grad_away = [grad_stack, grad_other]
    grad_away += over_cores(grad_near, owners, *back)
    row_own = partner(after(row_stack, *joined), owners)

    def expert_away(start, count, place, up_grad, down_grad):
        chips = owners // 2
        pairs = chips * (planes - 1)
        return pl.pallas_call(
            functools.partial(
                expert_away_kernel, start, count, block, chips, planes - 2
            ),
            out_shape=slabs,
            in_specs=[smem_spec()] + [hbm_spec()] * (6 + 4 * chips),
            out_specs=[hbm_spec()] * 2,
            scratch_shapes=[
                pltpu.VMEM((count,) + expert_up.shape[1:], LOW),
                pltpu.VMEM((count,) + expert_down.shape[1:], LOW),
                pltpu.VMEM((count,) + slabs[0].shape[1:], F32),
                pltpu.VMEM((count,) + slabs[1].shape[1:], F32),
                pltpu.VMEM((pairs, 2 * (length + TAIL), width), LOW),
                pltpu.VMEM((pairs, 2 * length, width), LOW),
                pltpu.VMEM((count, pairs * block, width), LOW),
                pltpu.VMEM((count, pairs * block, width), LOW),
                pltpu.VMEM((count, pairs * block, LANES), F32),
                pltpu.SemaphoreType.DMA((6, count)),
                pltpu.SemaphoreType.DMA((2, 2, pairs)),
            ],
            input_output_aliases={5 + 4 * chips: 0, 6 + 4 * chips: 1},
            compiler_params=params(),
            cost_estimate=cost(7 * count),
            name="expert_away",
        )(place, *row_away, *grad_away, expert_up, expert_down, up_grad, down_grad)

    def share_pieces(wide):
        return jax.ShapeDtypeStruct((owners // 2, planes, share, wide), LOW)

    wide = columns + width
    tokens_grad, grads_even, grads_odd = pl.pallas_call(
        functools.partial(backward_kernel, spots, output_spots, owners // 2),
        out_shape=(token_wide, share_pieces(wide), share_pieces(wide)),
        in_specs=[smem_spec()]
        + [whole_spec()] * (12 + owners // 2)
        + [hbm_spec()] * (len(pieces) + len(output_pieces)),
        out_specs=[whole_spec()] + [hbm_spec()] * 2,
        scratch_shapes=[
            pltpu.VMEM((width, columns), LOW),
            pltpu.VMEM((width, width), LOW),
            pltpu.VMEM((width, wide), LOW),
            pltpu.VMEM((length, width), LOW),
            pltpu.VMEM((length, width), LOW),
            pltpu.SemaphoreType.DMA((owners, planes)),
            pltpu.SemaphoreType.DMA((owners, planes)),
            pltpu.SemaphoreType.DMA((owners, planes)),
        ],
        compiler_params=params(),
        cost_estimate=cost(17),
        name="backward",
    )(
        rows,
        tokens,
        segments,
        cosine,
        sine,
        payload,
        after(hidden, row_own, out_even),
        query_rot,
        keyval_low,
        mixed_low,
        gates,
        out_grad,
        tail,
        *back,
        *pieces,
        *output_pieces,
    )

    grads_other = partner(
        after(grads_odd, row_near, row_far[1][0], row_far[2][0], *grad_away[3::2]), owners
    )
    half = grad_stack.shape[0] // 2
    grad_turn = [
        aside(after(grad_near[0][:half], tokens_grad), 2, owners),
        aside(after(grad_near[1][half:], tokens_grad), 1, owners),
    ]
    shares = [added(grads_even[s], grads_other[s]) for s in range(owners // 2)]
    grad_away += over_cores([jnp.concatenate(grad_turn, axis=0)], owners, shares[0])
    row_away = over_cores([row_near], owners, shares[0]) + [row_stack, row_own]
    row_away += over_cores(
        [jnp.concatenate(parts, axis=0) for parts in row_far[1:]], owners, shares[0]
    )
    first, second = to_neighbours(shares, owners)
    out_other = partner(after(out_odd, shares[0], *row_far[3], *grad_turn), owners)
    made = [added(out_even[s], out_other[s]) for s in range(owners // 2)]
    held = (first, second) + tuple(row_away[1::2]) + tuple(grad_away[7:]) + tuple(made)
    first, second = lax.optimization_barrier(held)[:2]
    far_made = aside(after(made[3], first), 3, owners)
    up_grad, down_grad = expert_away(0, 2, after(place, first, second), up_grad, down_grad)
    plane_sums = after(from_neighbours(shares, first, second, owners), up_grad, far_made)
    up_grad, down_grad = expert_away(2, 2, after(place, plane_sums), up_grad, down_grad)
    made = lax.optimization_barrier(tuple(made) + (plane_sums,))[: owners // 2]
    near_made = [aside(made[s], s, owners) for s in (1, 2)]
    summed = over_planes_sum(plane_sums, planes)
    made = [made[0]] + near_made + [far_made]
    layer_out = (hidden + sum(part.astype(F32) for part in made)).astype(LOW)

    return (
        layer_out,
        tokens_grad,
        summed[:, :width],
        summed[:, width : 2 * width],
        summed[:, columns:],
        summed[:, 2 * width : 2 * width + EXPERTS],
        summed[:, 2 * width + EXPERTS],
        summed[:, 2 * width + EXPERTS + 1],
        up_grad,
        down_grad,
    )


def solution(mesh):
    return jax.shard_map(
        functools.partial(on_device, mesh.shape["dp"], mesh.shape["expert"]),
        mesh=mesh,
        in_specs=(
            P(("dp", "expert"), None),
            P(("dp", "expert"), None),
            P(("dp", "expert"), None),
            P(("dp", "expert"), None),
            P(("dp", "expert"), None),
            P(("dp", "expert"), None),
            P(("dp", "expert"), None),
            P(("dp", "expert")),
            P(("dp", "expert")),
            P("expert", None, None),
            P("expert", None, None),
            P(("dp", "expert"), None),
        ),
        out_specs=(
            P(("dp", "expert"), None),
            P(("dp", "expert"), None),
            P(("dp", "expert"), None),
            P(("dp", "expert"), None),
            P(("dp", "expert"), None),
            P(("dp", "expert"), None),
            P(("dp", "expert")),
            P(("dp", "expert")),
            P("expert", "dp", None),
            P("expert", "dp", None),
        ),
        check_vma=False,
    )
```

```python
import functools

import jax
import jax.numpy as jnp
from jax import lax
from jax.sharding import PartitionSpec as P
from jax.experimental import pallas as pl
from jax.experimental.pallas import tpu as pltpu

HEAD_DIM = 64
FF = 512
EXPERTS = 32
TOP = 8
CAP = 40


EPS = 1e-05
ROPE_BASE = 10000.0
MASKED = -1e30
HIGH = lax.Precision.HIGHEST


def norm_forward(values, gain_vec):
    inverse = lax.rsqrt(jnp.mean(values * values, axis=-1, keepdims=True) + EPS)
    normed = values * inverse
    return (normed, inverse, (normed * gain_vec).astype(jnp.bfloat16))


def norm_backward(grad_out, normed, inverse, gain_vec):
    gain_grad = jnp.sum(grad_out * normed, axis=0)
    scaled = grad_out * gain_vec
    grad_in = inverse * (scaled - normed * jnp.mean(scaled * normed, axis=-1, keepdims=True))
    return (grad_in, gain_grad)


def rope_tables(segment_row):
    length = segment_row.shape[0]
    earlier = jnp.sum((segment_row[None, :] < segment_row[:, None]).astype(jnp.int32), axis=1)
    position = jnp.arange(length, dtype=jnp.int32) - earlier
    half_dim = HEAD_DIM // 2
    frequency = ROPE_BASE ** (-(jnp.arange(half_dim, dtype=jnp.float32) * 2.0) / HEAD_DIM)
    angles = position.astype(jnp.float32)[:, None] * frequency[None, :]
    cosine = jnp.concatenate([jnp.cos(angles), jnp.cos(angles)], axis=-1)[:, None, :]
    sine_table = jnp.concatenate([jnp.sin(angles), jnp.sin(angles)], axis=-1)[:, None, :]
    return (cosine, sine_table)


def rotate(values, cosine, sine_table):
    half_dim = values.shape[-1] // 2
    turned = jnp.concatenate([-values[..., half_dim:], values[..., :half_dim]], axis=-1)
    return values * cosine + turned * sine_table


def unrotate(grad_rows, cosine, sine_table):
    half_dim = grad_rows.shape[-1] // 2
    weighted = grad_rows * sine_table
    turned = jnp.concatenate([weighted[..., half_dim:], -weighted[..., :half_dim]], axis=-1)
    return grad_rows * cosine + turned


def on_device_wide(
    tokens,
    segments,
    routes,
    query_weight,
    keyval_weight,
    output_weight,
    router_weight,
    attn_gain,
    moe_gain,
    expert_up,
    expert_down,
    out_grad,
):
    owners = lax.axis_size("expert")
    local_experts = expert_up.shape[0]
    length = tokens.shape[0]
    model_width = tokens.shape[1]
    kv_heads = keyval_weight.shape[1] // (2 * HEAD_DIM)
    query_heads = query_weight.shape[1] // HEAD_DIM
    repeat = query_heads // kv_heads
    score_scale = HEAD_DIM ** (-0.5)
    query_full, keyval_full, output_full, router_full, attn_gains, moe_gains = (
        lax.all_gather(query_weight, ("dp", "expert"), axis=0, tiled=True),
        lax.all_gather(keyval_weight, ("dp", "expert"), axis=0, tiled=True),
        lax.all_gather(output_weight, ("dp", "expert"), axis=0, tiled=True),
        lax.all_gather(router_weight, ("dp", "expert"), axis=0, tiled=True),
        lax.all_gather(attn_gain, ("dp", "expert"), axis=0, tiled=True),
        lax.all_gather(moe_gain, ("dp", "expert"), axis=0, tiled=True),
    )
    resident = tokens.astype(jnp.float32)
    normed_one, inverse_one, attn_in = norm_forward(resident, attn_gains.astype(jnp.float32))
    query_proj = jnp.dot(attn_in, query_full, preferred_element_type=jnp.float32).reshape(
        length, query_heads, HEAD_DIM
    )
    keyval_proj = jnp.dot(attn_in, keyval_full, preferred_element_type=jnp.float32)
    key_rows = keyval_proj[:, : kv_heads * HEAD_DIM].reshape(length, kv_heads, HEAD_DIM)
    value_rows = keyval_proj[:, kv_heads * HEAD_DIM :].reshape(length, kv_heads, HEAD_DIM)
    cosine, sine_table = rope_tables(segments[0])
    query_rot = (
        rotate(query_proj, cosine, sine_table)
        .astype(jnp.bfloat16)
        .reshape(length, kv_heads, repeat, HEAD_DIM)
    )
    keys_rot = rotate(key_rows, cosine, sine_table).astype(jnp.bfloat16)
    values_low = value_rows.astype(jnp.bfloat16)
    places = jnp.arange(length)
    visible = (segments[0][:, None] == segments[0][None, :]) & (places[None, :] <= places[:, None])
    scores = jnp.einsum("ikrd,jkd->krij", query_rot, keys_rot, preferred_element_type=jnp.float32)
    attn_logits = jnp.where(visible, scores * score_scale, MASKED)
    attn_exps = jnp.exp(attn_logits - jnp.max(attn_logits, axis=-1, keepdims=True))
    attn_probs = attn_exps / jnp.sum(attn_exps, axis=-1, keepdims=True)
    probs_low = attn_probs.astype(jnp.bfloat16)
    mixed_heads = jnp.einsum(
        "krij,jkd->ikrd", probs_low, values_low, preferred_element_type=jnp.float32
    )
    mixed_low = mixed_heads.reshape(length, query_heads * HEAD_DIM).astype(jnp.bfloat16)
    hidden = resident + jnp.dot(mixed_low, output_full, preferred_element_type=jnp.float32)
    normed_two, inverse_two, moe_in = norm_forward(hidden, moe_gains.astype(jnp.float32))
    router_logits = jnp.dot(moe_in, router_full, preferred_element_type=jnp.float32)
    choose = (routes[:, :, None] == jnp.arange(EXPERTS, dtype=jnp.int32)[None, None, :]).astype(
        jnp.float32
    )
    chosen = jnp.sum(choose * router_logits[:, None, :], axis=-1)
    gate_exps = jnp.exp(chosen - jnp.max(chosen, axis=-1, keepdims=True))
    gate_probs = gate_exps / jnp.sum(gate_exps, axis=-1, keepdims=True)
    entries = routes.reshape(-1)
    entry_count = entries.shape[0]
    onehot = (entries[:, None] == jnp.arange(EXPERTS, dtype=jnp.int32)[None, :]).astype(jnp.int32)
    position = jnp.sum((jnp.cumsum(onehot, axis=0) - 1) * onehot, axis=1)
    slot_index = entries * CAP + position
    owner_entry = (
        jnp.full((EXPERTS * CAP,), entry_count, jnp.int32)
        .at[slot_index]
        .set(jnp.arange(entry_count, dtype=jnp.int32))
    )
    padded_in = jnp.concatenate([moe_in, jnp.zeros((1, model_width), jnp.bfloat16)], axis=0)
    send_rows = jnp.take(padded_in, owner_entry // TOP, axis=0).reshape(EXPERTS, CAP, model_width)
    received = lax.all_to_all(send_rows, "expert", split_axis=0, concat_axis=0, tiled=True)
    slots_now = received.shape[1]
    grouped = received.reshape(owners, local_experts, slots_now, model_width)
    pair_proj = jnp.einsum("secd,edf->secf", grouped, expert_up, preferred_element_type=jnp.float32)
    activated = (jax.nn.silu(pair_proj[..., :FF]) * pair_proj[..., FF:]).astype(jnp.bfloat16)
    produced = jnp.einsum(
        "secf,edf->secd", activated, expert_down, preferred_element_type=jnp.float32
    ).astype(jnp.bfloat16)
    returned = lax.all_to_all(
        produced.reshape(EXPERTS, slots_now, model_width),
        "expert",
        split_axis=0,
        concat_axis=0,
        tiled=True,
    )
    returned, kept_rows, kept_pair = (
        returned,
        received,
        pair_proj.reshape(EXPERTS, slots_now, 2 * FF),
    )
    gathered = (
        jnp.take(returned.reshape(EXPERTS * CAP, model_width), slot_index, axis=0)
        .astype(jnp.float32)
        .reshape(length, TOP, model_width)
    )
    layer_out = (hidden + jnp.sum(gate_probs[:, :, None] * gathered, axis=1)).astype(jnp.bfloat16)
    grad_top = out_grad.astype(jnp.float32)
    gate_grad = jnp.sum(gathered * grad_top[:, None, :], axis=-1)
    chosen_grad = gate_probs * (gate_grad - jnp.sum(gate_probs * gate_grad, axis=-1, keepdims=True))
    logits_grad = jnp.sum(chosen_grad[:, :, None] * choose, axis=1)
    row_grads = (
        (gate_probs[:, :, None] * grad_top[:, None, :])
        .astype(jnp.bfloat16)
        .reshape(entry_count, model_width)
    )
    padded_grads = jnp.concatenate([row_grads, jnp.zeros((1, model_width), jnp.bfloat16)], axis=0)
    send_grads = jnp.take(padded_grads, owner_entry, axis=0).reshape(EXPERTS, CAP, model_width)
    grads_in = lax.all_to_all(send_grads, "expert", split_axis=0, concat_axis=0, tiled=True)
    grouped_rows = kept_rows.reshape(owners, local_experts, CAP, model_width)
    grouped_grads = grads_in.reshape(owners, local_experts, CAP, model_width)
    pair_kept = kept_pair.reshape(owners, local_experts, CAP, 2 * FF)
    gate_half = pair_kept[..., :FF]
    up_half = pair_kept[..., FF:]
    sigmoid_gate = jax.nn.sigmoid(gate_half)
    silu_gate = jax.nn.silu(gate_half)
    activated = (silu_gate * up_half).astype(jnp.bfloat16)
    act_grad = jnp.einsum(
        "secd,edf->secf", grouped_grads, expert_down, preferred_element_type=jnp.float32
    )
    pair_grad = jnp.concatenate(
        [
            act_grad * up_half * sigmoid_gate * (1.0 + gate_half * (1.0 - sigmoid_gate)),
            act_grad * silu_gate,
        ],
        axis=-1,
    ).astype(jnp.bfloat16)
    rows_back = jnp.einsum(
        "secf,edf->secd", pair_grad, expert_up, preferred_element_type=jnp.float32
    ).astype(jnp.bfloat16)
    up_grad = jnp.einsum(
        "secd,secf->edf", grouped_rows, pair_grad, preferred_element_type=jnp.float32
    )
    down_grad = jnp.einsum(
        "secd,secf->edf", grouped_grads, activated, preferred_element_type=jnp.float32
    )
    returned_grads = lax.all_to_all(
        rows_back.reshape(EXPERTS, CAP, model_width),
        "expert",
        split_axis=0,
        concat_axis=0,
        tiled=True,
    )
    expert_up_grad, expert_down_grad = (
        lax.psum_scatter(
            up_grad.astype(jnp.bfloat16), "dp", scatter_dimension=1, tiled=True
        ).astype(jnp.float32),
        lax.psum_scatter(
            down_grad.astype(jnp.bfloat16), "dp", scatter_dimension=1, tiled=True
        ).astype(jnp.float32),
    )
    token_grads = (
        jnp.take(returned_grads.reshape(EXPERTS * CAP, model_width), slot_index, axis=0)
        .astype(jnp.float32)
        .reshape(length, TOP, model_width)
    )
    router_wide = router_full.astype(jnp.float32)
    moe_grad = jnp.sum(token_grads, axis=1) + jnp.dot(logits_grad, router_wide.T, precision=HIGH)
    hidden_norm_grad, moe_gain_grad = norm_backward(
        moe_grad, normed_two, inverse_two, moe_gains.astype(jnp.float32)
    )
    hidden_grad = grad_top + hidden_norm_grad
    attn_out_grad = hidden_grad.astype(jnp.bfloat16)
    mixed_grad = (
        jnp.einsum("td,cd->tc", attn_out_grad, output_full, preferred_element_type=jnp.float32)
        .astype(jnp.bfloat16)
        .reshape(length, kv_heads, repeat, HEAD_DIM)
    )
    probs_grad = jnp.einsum(
        "ikrd,jkd->krij", mixed_grad, values_low, preferred_element_type=jnp.float32
    )
    values_grad = jnp.einsum(
        "krij,ikrd->jkd", probs_low, mixed_grad, preferred_element_type=jnp.float32
    )
    scores_grad = (
        attn_probs
        * (probs_grad - jnp.sum(attn_probs * probs_grad, axis=-1, keepdims=True))
        * score_scale
    ).astype(jnp.bfloat16)
    query_rot_grad = jnp.einsum(
        "krij,jkd->ikrd", scores_grad, keys_rot, preferred_element_type=jnp.float32
    ).reshape(length, query_heads, HEAD_DIM)
    keys_rot_grad = jnp.einsum(
        "krij,ikrd->jkd", scores_grad, query_rot, preferred_element_type=jnp.float32
    )
    query_low = (
        unrotate(query_rot_grad, cosine, sine_table)
        .reshape(length, query_heads * HEAD_DIM)
        .astype(jnp.bfloat16)
    )
    keyval_low = jnp.concatenate(
        [
            unrotate(keys_rot_grad, cosine, sine_table).reshape(length, kv_heads * HEAD_DIM),
            values_grad.reshape(length, kv_heads * HEAD_DIM),
        ],
        axis=1,
    ).astype(jnp.bfloat16)
    attn_in_grad = jnp.einsum(
        "tc,dc->td", query_low, query_full, preferred_element_type=jnp.float32
    ) + jnp.einsum("tc,dc->td", keyval_low, keyval_full, preferred_element_type=jnp.float32)
    token_norm_grad, attn_gain_grad = norm_backward(
        attn_in_grad, normed_one, inverse_one, attn_gains.astype(jnp.float32)
    )
    tokens_grad = hidden_grad + token_norm_grad
    slab_count = lax.axis_size("dp")
    slab_index = lax.axis_index("dp")
    width_rows = model_width // slab_count
    head_rows = query_heads * HEAD_DIM // slab_count
    all_attn, all_query, all_keyval, all_mixed, all_outgrad = (
        lax.all_gather(attn_in, "dp", axis=0, tiled=True),
        lax.all_gather(query_low, "dp", axis=0, tiled=True),
        lax.all_gather(keyval_low, "dp", axis=0, tiled=True),
        lax.all_gather(mixed_low, "dp", axis=0, tiled=True),
        lax.all_gather(attn_out_grad, "dp", axis=0, tiled=True),
    )
    all_moe, all_logits, attn_gain_rows, moe_gain_rows = (
        lax.all_gather(
            moe_in.astype(jnp.float32).astype(jnp.bfloat16), "dp", axis=0, tiled=True
        ).astype(jnp.float32),
        lax.all_gather(logits_grad.astype(jnp.bfloat16), "dp", axis=0, tiled=True).astype(
            logits_grad.dtype
        ),
        lax.all_gather(
            attn_gain_grad[None, :].astype(jnp.bfloat16), "dp", axis=0, tiled=True
        ).astype(jnp.float32),
        lax.all_gather(
            moe_gain_grad[None, :].astype(jnp.bfloat16), "dp", axis=0, tiled=True
        ).astype(jnp.float32),
    )
    attn_cols = lax.dynamic_slice_in_dim(all_attn, slab_index * width_rows, width_rows, 1)
    mixed_cols = lax.dynamic_slice_in_dim(all_mixed, slab_index * head_rows, head_rows, 1)
    moe_cols = lax.dynamic_slice_in_dim(all_moe, slab_index * width_rows, width_rows, 1)
    query_part = jnp.einsum("td,tc->dc", attn_cols, all_query, preferred_element_type=jnp.float32)
    keyval_part = jnp.einsum("td,tc->dc", attn_cols, all_keyval, preferred_element_type=jnp.float32)
    output_part = jnp.einsum(
        "tc,td->cd", mixed_cols, all_outgrad, preferred_element_type=jnp.float32
    )
    router_part = jnp.dot(moe_cols.T, all_logits, precision=HIGH)
    attn_gain_part = lax.dynamic_slice_in_dim(
        jnp.sum(attn_gain_rows, axis=0), slab_index * width_rows, width_rows, 0
    )
    moe_gain_part = lax.dynamic_slice_in_dim(
        jnp.sum(moe_gain_rows, axis=0), slab_index * width_rows, width_rows, 0
    )
    query_share, keyval_share, output_share, router_share, attn_share, moe_share = (
        lax.psum_scatter(
            query_part.astype(jnp.bfloat16), "expert", scatter_dimension=0, tiled=True
        ).astype(jnp.float32),
        lax.psum_scatter(
            keyval_part.astype(jnp.bfloat16), "expert", scatter_dimension=0, tiled=True
        ).astype(jnp.float32),
        lax.psum_scatter(
            output_part.astype(jnp.bfloat16), "expert", scatter_dimension=0, tiled=True
        ).astype(jnp.float32),
        lax.psum_scatter(
            router_part.astype(jnp.bfloat16), "expert", scatter_dimension=0, tiled=True
        ).astype(jnp.float32),
        lax.psum_scatter(
            attn_gain_part.astype(jnp.bfloat16), "expert", scatter_dimension=0, tiled=True
        ).astype(jnp.float32),
        lax.psum_scatter(
            moe_gain_part.astype(jnp.bfloat16), "expert", scatter_dimension=0, tiled=True
        ).astype(jnp.float32),
    )
    return (
        layer_out,
        tokens_grad,
        query_share,
        keyval_share,
        output_share,
        router_share,
        attn_share,
        moe_share,
        expert_up_grad,
        expert_down_grad,
    )


LANES = 128
TAIL = 16
PIECE_LIMIT = 4096
VMEM_BYTES = 60 * 1024 * 1024
F32 = jnp.float32
LOW = jnp.bfloat16


def contract(left, right, left_dim, right_dim):
    return lax.dot_general(
        left, right, (((left_dim,), (right_dim,)), ((), ())), preferred_element_type=F32
    )


def lane_index(shape):
    return lax.broadcasted_iota(jnp.int32, shape, len(shape) - 1)


def row_index(shape):
    return lax.broadcasted_iota(jnp.int32, shape, len(shape) - 2)


def half_turn(chunk):
    first = lane_index(chunk.shape) % HEAD_DIM < HEAD_DIM // 2
    ahead = pltpu.roll(chunk, LANES - HEAD_DIM // 2, 1)
    behind = pltpu.roll(chunk, HEAD_DIM // 2, 1)
    return jnp.where(first, ahead, behind)


def both_heads(chunk, pick):
    swapped = pltpu.roll(chunk, HEAD_DIM, 1)
    first = lane_index(chunk.shape) < HEAD_DIM
    if pick == 0:
        return jnp.where(first, chunk, swapped)
    return jnp.where(first, swapped, chunk)


def split_heads(chunk):
    first = lane_index(chunk.shape) < HEAD_DIM
    zero = jnp.zeros_like(chunk)
    return jnp.concatenate([jnp.where(first, chunk, zero), jnp.where(first, zero, chunk)], axis=0)


def join_heads(stacked):
    length = stacked.shape[0] // 2
    top, bottom = stacked[:length], stacked[length:]
    return jnp.where(lane_index(top.shape) < HEAD_DIM, top, bottom)


def three_parts(values):
    high = values.astype(LOW).astype(F32)
    rest = values - high
    middle = rest.astype(LOW).astype(F32)
    return (high, middle, rest - middle)


def gain_select():
    shape = (8, LANES)
    return (lane_index(shape) == EXPERTS + row_index(shape)) & (row_index(shape) < 2)


def load_weights(rows_ref, spots, piece_refs, weights, sems):
    copies = []
    for spot, piece in zip(spots, piece_refs):
        for i, (p, w) in enumerate(spot):
            size = piece.shape[1]
            start = pl.multiple_of(rows_ref[p, w] * size, size)
            copies.append(
                pltpu.make_async_copy(piece.at[i], weights.at[pl.ds(start, size)], sems.at[p, w])
            )
    for copy in copies:
        copy.start()
    return copies


def store_sums(rows_ref, sums, grads_even, grads_odd, sems):
    copies = []
    for p in range(2 * grads_even.shape[0]):
        target = grads_even if p % 2 == 0 else grads_odd
        for w in range(target.shape[1]):
            size = target.shape[2]
            start = pl.multiple_of(rows_ref[p, w] * size, size)
            copies.append(
                pltpu.make_async_copy(
                    sums.at[pl.ds(start, size)], target.at[p // 2, w], sems.at[p, w]
                )
            )
    for copy in copies:
        copy.start()
    return copies


def softmax_rows(q_pair, k_both, visible):
    scores = contract(q_pair, k_both, 1, 1) * (HEAD_DIM ** (-0.5))
    logits = jnp.where(visible, scores, MASKED)
    exps = jnp.exp(logits - jnp.max(logits, axis=-1, keepdims=True))
    return exps / jnp.sum(exps, axis=-1, keepdims=True)


def segment_tables(seg_row, frequency):
    length = seg_row.shape[1]
    shape = (length, length)
    across_row = jnp.broadcast_to(seg_row.astype(F32), shape)
    down_col = across_row.T
    seen = (down_col == across_row) & (lane_index(shape) <= row_index(shape))
    visible = jnp.concatenate([seen, seen], axis=0)
    if frequency is None:
        return visible
    earlier = jnp.sum(jnp.where(across_row < down_col, 1.0, 0.0), axis=1, keepdims=True)
    angles = (row_index(shape).astype(F32) - earlier) * frequency
    sine = jnp.sin(angles)
    first = lane_index(shape) % HEAD_DIM < HEAD_DIM // 2
    return (visible, jnp.cos(angles), jnp.where(first, -sine, sine))


def attn_forward_kernel(spots, *refs):
    count = len(spots)
    rows_ref, tokens_ref, seg_row, frequency = refs[:4]
    pieces = refs[4 : 4 + count]
    query_ref, keyval_ref, mixed_ref, tail_ref, cos_ref, sin_ref, weights, sems = refs[4 + count :]
    copies = load_weights(rows_ref, spots, pieces, weights, sems)
    tokens = tokens_ref[...].astype(F32)
    inverse = lax.rsqrt(jnp.mean(tokens * tokens, axis=-1, keepdims=True) + EPS)
    normed = tokens * inverse
    width = tokens.shape[1]
    visible, cosine, sine = segment_tables(seg_row[...], frequency[...])
    cos_ref[...] = cosine
    sin_ref[...] = sine
    for copy in copies:
        copy.wait()
    tail = weights[:, 2 * width :]
    tail_ref[...] = tail
    gains = contract(gain_select().astype(F32).astype(LOW), tail, 1, 1)
    attn_in = (normed * gains[0:1]).astype(LOW)
    keyval = contract(attn_in, weights[:, width : 2 * width], 1, 0)
    query = contract(attn_in, weights[:, :width], 1, 0)
    half = width // 2
    for m in range(half // LANES):
        keys = keyval[:, m * LANES : (m + 1) * LANES]
        keys = (keys * cosine + half_turn(keys) * sine).astype(LOW)
        values = keyval[:, half + m * LANES : half + (m + 1) * LANES].astype(LOW)
        keyval_ref[:, m * LANES : (m + 1) * LANES] = keys
        keyval_ref[:, half + m * LANES : half + (m + 1) * LANES] = values
        for pick in range(2):
            k_both = both_heads(keys.astype(F32), pick).astype(LOW)
            v_both = both_heads(values.astype(F32), pick).astype(LOW)
            chunk = slice((2 * m + pick) * LANES, (2 * m + pick + 1) * LANES)
            queries = query[:, chunk]
            queries = (queries * cosine + half_turn(queries) * sine).astype(LOW)
            query_ref[:, chunk] = queries
            q_pair = split_heads(queries.astype(F32)).astype(LOW)
            probs = softmax_rows(q_pair, k_both, visible).astype(LOW)
            mixed_ref[:, chunk] = join_heads(contract(probs, v_both, 1, 0)).astype(LOW)


def router_kernel(spots, *refs):
    count = len(spots)
    rows_ref, tokens_ref, mixed_ref, tail_ref, routes_t = refs[:5]
    pieces = refs[5 : 5 + count]
    payload, hidden_ref, gates_ref, weights, sems = refs[5 + count :]
    copies = load_weights(rows_ref, spots, pieces, weights, sems)
    tokens = tokens_ref[...].astype(F32)
    length = tokens.shape[0]
    tail = tail_ref[...]
    gains = contract(gain_select().astype(F32).astype(LOW), tail, 1, 1)
    for copy in copies:
        copy.wait()
    hidden = tokens + contract(mixed_ref[...], weights[...], 1, 0)
    hidden_ref[...] = hidden
    inverse_two = lax.rsqrt(jnp.mean(hidden * hidden, axis=-1, keepdims=True) + EPS)
    moe_in = (hidden * inverse_two * gains[1:2]).astype(LOW)
    payload[:length] = moe_in
    logits = contract(moe_in, tail, 1, 0)
    turned = routes_t[...]
    experts = row_index((LANES, length))
    chosen = experts == turned[0:1]
    for k in range(1, TOP):
        chosen = chosen | (experts == turned[k : k + 1])
    chosen = jnp.where(chosen, 1.0, 0.0).T > 0.5
    logits = jnp.where(chosen, logits, MASKED)
    exps = jnp.where(chosen, jnp.exp(logits - jnp.max(logits, axis=-1, keepdims=True)), 0.0)
    gates = exps / jnp.sum(exps, axis=-1, keepdims=True)
    gates_ref[...] = gates
    gates_t = gates.T
    for k in range(TOP):
        row = turned[k : k + 1]
        gate = jnp.sum(jnp.where(experts == row, gates_t, 0.0), axis=0, keepdims=True)
        high, middle, rest = three_parts(gate)
        place = row_index((TAIL, length))
        block = jnp.where(place == 0, high, jnp.where(place == 1, middle, jnp.where(place == 2, rest, 0.0)))
        block = jnp.where(place == 3, row.astype(F32), block)
        payload[length:, k * length : (k + 1) * length] = block.astype(LOW)


def slot_places(first_expert, local, tails, before):
    length = tails[0].shape[1] // TOP
    ids = row_index((8, length))
    ids = jnp.where(ids < local, ids + first_expert, -1).astype(F32)
    masks, gates = [], []
    for tail in tails:
        mask = jnp.zeros((8, length), F32)
        gate = jnp.zeros((8, length), F32)
        for k in range(TOP):
            part = tail[:, k * length : (k + 1) * length].astype(F32)
            hit = part[3:4] == ids
            mask = jnp.where(hit, 1.0, mask)
            gate = jnp.where(hit, part[0:1] + part[1:2] + part[2:3], gate)
        masks.append(mask)
        gates.append(gate)
    pairs = range(0, len(tails), 2)
    mask = jnp.concatenate([jnp.concatenate(masks[i : i + 2], axis=1) for i in pairs], axis=0)
    gate = jnp.concatenate([jnp.concatenate(gates[i : i + 2], axis=1) for i in pairs], axis=0)
    place = contract(mask.astype(LOW), before, 1, 0)
    return (jnp.where(mask > 0, place, -1.0), gate)


def gather_pair(local, block, pair, place, gate, row_pair, grad_pair, out):
    rows_out, grads_out, select_out, gate_out = out
    slots = row_index((block, place.shape[1])).astype(F32)
    parts = []
    for j in range(local):
        hit = slots == place[j : j + 1]
        parts.append(jnp.where(hit, 1.0, 0.0))
        held = jnp.where(hit, gate[j : j + 1], 0.0)
        held = jnp.sum(held, axis=1, keepdims=True)
        gate_out[j, pair * block : (pair + 1) * block] = jnp.broadcast_to(held, (block, LANES))
    select = jnp.concatenate(parts, axis=0).astype(LOW)
    if select_out is not None:
        select_out[pair] = select
    rows = contract(select, jnp.concatenate(row_pair, axis=0), 1, 0).astype(LOW)
    grads = contract(select, jnp.concatenate(grad_pair, axis=0), 1, 0).astype(LOW)
    for j in range(local):
        rows_out[j, pair * block : (pair + 1) * block] = rows[j * block : (j + 1) * block]
        grads_out[j, pair * block : (pair + 1) * block] = grads[j * block : (j + 1) * block]


def earlier_matrix(length):
    shape = (2 * length, 2 * length)
    return jnp.where(row_index(shape) < lane_index(shape), 1.0, 0.0).astype(LOW)


def expert_step(j, rows, grads, gate_ref, up, down):
    hidden_units = down.shape[1]
    pair = contract(rows[j], up, 1, 0)
    raw = contract(grads[j], down, 1, 0)
    gate_half, up_half = pair[:, :hidden_units], pair[:, hidden_units:]
    gate = gate_ref[j][:, 0:1]
    sigmoid = 1.0 / (1.0 + jnp.exp(-gate_half))
    silu = gate_half * sigmoid
    activated = silu * up_half
    scaled = (gate * activated).astype(LOW)
    act_grad = gate * raw
    pair_grad = jnp.concatenate(
        [act_grad * up_half * sigmoid * (1.0 + gate_half * (1.0 - sigmoid)), act_grad * silu],
        axis=1,
    ).astype(LOW)
    gate_grad = jnp.sum(activated * raw, axis=1, keepdims=True)
    return (scaled, pair_grad, gate_grad)


def fetch_experts(local, up_hbm, down_hbm, up, down, sems):
    copies = []
    for j in range(local):
        copies.append(
            (
                pltpu.make_async_copy(up_hbm.at[j], up.at[j], sems.at[0, j]),
                pltpu.make_async_copy(down_hbm.at[j], down.at[j], sems.at[1, j]),
            )
        )
        for copy in copies[j]:
            copy.start()
    return copies


def expert_home_kernel(owners, local, block, *refs):
    place_ref = refs[0]
    rows_in = refs[1 : 1 + owners]
    grads_in = refs[1 + owners : 1 + 2 * owners]
    up_hbm, down_hbm = refs[1 + 2 * owners : 3 + 2 * owners]
    back_even, back_odd = refs[3 + 2 * owners : 5 + 2 * owners]
    kept = refs[5 + 2 * owners : 10 + 2 * owners]
    scratch = refs[10 + 2 * owners :]
    up, down, rows, grads, select, gate_ref, scaled, pair_grads, returned, sems = scratch
    copies = fetch_experts(local, up_hbm, down_hbm, up, down, sems)
    length = rows_in[0].shape[0] - TAIL
    width = rows_in[0].shape[1]
    first_expert = place_ref[0] * local
    slab = kept[3].shape[2]
    columns = pl.ds(pl.multiple_of(place_ref[1] * slab, slab), slab)
    before = earlier_matrix(length)
    place, gate = slot_places(first_expert, local, [ref[length:] for ref in rows_in], before)
    for s in range(owners // 2):
        gather_pair(
            local,
            block,
            s,
            place[8 * s : 8 * s + 8],
            gate[8 * s : 8 * s + 8],
            [rows_in[2 * s][:length], rows_in[2 * s + 1][:length]],
            [grads_in[2 * s][...], grads_in[2 * s + 1][...]],
            (rows, grads, select, gate_ref),
        )
    sent = [
        pltpu.make_async_copy(select, kept[0], sems.at[2, 0]),
        pltpu.make_async_copy(rows.at[:, :, columns], kept[3], sems.at[2, 1]),
        pltpu.make_async_copy(grads.at[:, :, columns], kept[4], sems.at[2, 2]),
    ]
    for copy in sent:
        copy.start()
    for j in range(local):
        for copy in copies[j]:
            copy.wait()
    for j in range(local):
        made, pair_grad, gate_grad = expert_step(j, rows, grads, gate_ref, up[j], down[j])
        scaled[j] = made
        pair_grads[j] = pair_grad
        sent.append(pltpu.make_async_copy(scaled.at[j], kept[1].at[j], sems.at[3, j]))
        sent.append(pltpu.make_async_copy(pair_grads.at[j], kept[2].at[j], sems.at[4, j]))
        sent[-2].start()
        sent[-1].start()
        returned[j, :, :width] = contract(pair_grad, up[j], 1, 1).astype(LOW)
        lanes = lane_index((made.shape[0], LANES)) - first_expert - j
        high, middle, rest = three_parts(gate_grad)
        tail = jnp.where(lanes == 0, high, 0.0)
        tail = jnp.where(lanes == EXPERTS, middle, tail)
        tail = jnp.where(lanes == 2 * EXPERTS, rest, tail)
        returned[j, :, width:] = tail.astype(LOW)
    for s in range(owners // 2):
        span = slice(s * block, (s + 1) * block)
        back = jnp.concatenate([returned[j, span] for j in range(local)], axis=0)
        back = contract(select[s], back, 0, 0).astype(LOW)
        back_even[s] = back[:length]
        back_odd[s] = back[length:]
    for copy in sent:
        copy.wait()


def expert_finish_kernel(local, block, *refs):
    select, scaled, pair_grads, rows, grads, down = refs[:6]
    out_even, out_odd, up_grad, down_grad, produced = refs[6:]
    length = out_even.shape[1]
    for j in range(local):
        produced[j] = contract(scaled[j], down[j], 1, 1).astype(LOW)
        up_grad[j] = contract(rows[j], pair_grads[j], 0, 0)
        down_grad[j] = contract(grads[j], scaled[j], 0, 0)
    for s in range(out_even.shape[0]):
        span = slice(s * block, (s + 1) * block)
        made = jnp.concatenate([produced[j, span] for j in range(local)], axis=0)
        made = contract(select[s], made, 0, 0).astype(LOW)
        out_even[s] = made[:length]
        out_odd[s] = made[length:]


def expert_away_kernel(start, count, block, chips, far, *refs):
    place_ref = refs[0]
    rows_in = refs[1 : 3 + 2 * chips]
    grads_in = refs[3 + 2 * chips : 3 + 4 * chips]
    up_hbm, down_hbm, up_first, down_first = refs[3 + 4 * chips : 7 + 4 * chips]
    up_grad, down_grad = refs[7 + 4 * chips : 9 + 4 * chips]
    scratch = refs[9 + 4 * chips :]
    up, down, up_sum, down_sum, rows_buf, grads_buf, rows, grads, gate_ref, sems, pair_sems = scratch
    length = grads_buf.shape[1] // 2
    tall = length + TAIL
    pairs = []
    for i in range(far + 1):
        for s in range(chips):
            spot = len(pairs)
            copies = []
            for side in range(2):
                grad_from = grads_in[2 * s + side].at[pl.ds(i * length, length)]
                if i == 0:
                    row_from = rows_in[side].at[s]
                else:
                    row_from = rows_in[2 + 2 * s + side].at[pl.ds((i - 1) * tall, tall)]
                row_to = rows_buf.at[spot, pl.ds(side * tall, tall)]
                grad_to = grads_buf.at[spot, pl.ds(side * length, length)]
                copies.append(pltpu.make_async_copy(row_from, row_to, pair_sems.at[0, side, spot]))
                copies.append(pltpu.make_async_copy(grad_from, grad_to, pair_sems.at[1, side, spot]))
            pairs.append(copies)
    for copies in pairs:
        for copy in copies:
            copy.start()
    held = []
    for j in range(count):
        held.append(
            [
                pltpu.make_async_copy(up_hbm.at[start + j], up.at[j], sems.at[0, j]),
                pltpu.make_async_copy(down_hbm.at[start + j], down.at[j], sems.at[1, j]),
                pltpu.make_async_copy(up_first.at[start + j], up_sum.at[j], sems.at[2, j]),
                pltpu.make_async_copy(down_first.at[start + j], down_sum.at[j], sems.at[3, j]),
            ]
        )
    for copies in held:
        for copy in copies:
            copy.start()
    first_expert = place_ref[0] * (up_hbm.shape[0]) + start
    slab = up_sum.shape[1]
    columns = pl.ds(pl.multiple_of(place_ref[1] * slab, slab), slab)
    before = earlier_matrix(length)
    for i, copies in enumerate(pairs):
        for copy in copies:
            copy.wait()
        tails = [rows_buf[i, length:tall], rows_buf[i, tall + length :]]
        place, gate = slot_places(first_expert, count, tails, before)
        gather_pair(
            count,
            block,
            i,
            place,
            gate,
            [rows_buf[i, :length], rows_buf[i, tall : tall + length]],
            [grads_buf[i]],
            (rows, grads, None, gate_ref),
        )
    for copies in held:
        for copy in copies:
            copy.wait()
    sent = []
    for j in range(count):
        scaled, pair_grad, _ = expert_step(j, rows, grads, gate_ref, up[j], down[j])
        up_sum[j] += contract(rows[j, :, columns], pair_grad, 0, 0)
        down_sum[j] += contract(grads[j, :, columns], scaled, 0, 0)
        sent.append(pltpu.make_async_copy(up_sum.at[j], up_grad.at[start + j], sems.at[4, j]))
        sent.append(pltpu.make_async_copy(down_sum.at[j], down_grad.at[start + j], sems.at[5, j]))
        sent[-2].start()
        sent[-1].start()
    for copy in sent:
        copy.wait()


def backward_kernel(spots, output_spots, shares, *refs):
    rows_ref, tokens_ref, seg_row, cos_ref, sin_ref, payload, hidden_ref = refs[:7]
    query_ref, keyval_ref, mixed_ref, gates_ref, out_grad_ref, tail_ref = refs[7:13]
    refs = refs[13:]
    back, refs = refs[:shares], refs[shares:]
    pieces, refs = refs[: len(spots)], refs[len(spots) :]
    output_pieces, refs = refs[: len(output_spots)], refs[len(output_spots) :]
    tokens_grad, grads_even, grads_odd = refs[:3]
    weights, output, sums, query_low, keyval_low, sems, output_sems, out_sems = refs[3:]
    output_copies = load_weights(rows_ref, output_spots, output_pieces, output, output_sems)
    copies = load_weights(rows_ref, spots, pieces, weights, sems)
    length, width = tokens_ref.shape
    half = width // 2
    columns = weights.shape[1]
    total = back[0][...].astype(F32)
    for share in back[1:]:
        total = total + share[...].astype(F32)
    parts = total[:, width:]
    lanes = lane_index(parts.shape)
    gate_grad = parts + pltpu.roll(parts, LANES - EXPERTS, 1) + pltpu.roll(parts, LANES - 2 * EXPERTS, 1)
    gate_grad = jnp.where(lanes < EXPERTS, gate_grad, 0.0)
    gates = gates_ref[...]
    logits_grad = gates * (gate_grad - jnp.sum(gates * gate_grad, axis=-1, keepdims=True))
    hidden = hidden_ref[...]
    inverse_two = lax.rsqrt(jnp.mean(hidden * hidden, axis=-1, keepdims=True) + EPS)
    normed_two = hidden * inverse_two
    tail = tail_ref[...]
    gains = contract(gain_select().astype(F32).astype(LOW), tail, 1, 1)
    high = logits_grad.astype(LOW)
    rest = (logits_grad - high.astype(F32)).astype(LOW)
    moe_grad = total[:, :width] + contract(high, tail, 1, 1) + contract(rest, tail, 1, 1)
    moe_gain_grad = jnp.sum(moe_grad * normed_two, axis=0, keepdims=True)
    scaled = moe_grad * gains[1:2]
    hidden_grad = out_grad_ref[...].astype(F32) + inverse_two * (
        scaled - normed_two * jnp.mean(scaled * normed_two, axis=-1, keepdims=True)
    )
    attn_out_grad = hidden_grad.astype(LOW)
    for copy in output_copies:
        copy.wait()
    mixed_grad = contract(attn_out_grad, output[...], 1, 1)
    sums[:, columns:] = contract(mixed_ref[...], attn_out_grad, 0, 0).astype(LOW)
    tokens = tokens_ref[...].astype(F32)
    inverse_one = lax.rsqrt(jnp.mean(tokens * tokens, axis=-1, keepdims=True) + EPS)
    normed_one = tokens * inverse_one
    cosine, sine = cos_ref[...], sin_ref[...]
    visible = segment_tables(seg_row[...], None)
    groups = range(width // LANES)
    chunks = [slice(g * LANES, (g + 1) * LANES) for g in groups]
    keys = [keyval_ref[:, chunks[m]].astype(F32) for m in range(half // LANES)]
    values = [keyval_ref[:, half + m * LANES : half + (m + 1) * LANES].astype(F32) for m in range(half // LANES)]
    k_both = [both_heads(keys[g // 2], g % 2).astype(LOW) for g in groups]
    v_both = [both_heads(values[g // 2], g % 2).astype(LOW) for g in groups]
    q_pair = [split_heads(query_ref[:, chunk].astype(F32)).astype(LOW) for chunk in chunks]
    probs = [softmax_rows(q_pair[g], k_both[g], visible) for g in groups]
    m_pair = [split_heads(mixed_grad[:, chunk]).astype(LOW) for chunk in chunks]
    probs_grad = [contract(m_pair[g], v_both[g], 1, 1) for g in groups]
    value_sides = [contract(probs[g].astype(LOW), m_pair[g], 0, 0) for g in groups]
    scores_grad = [
        (
            probs[g]
            * (probs_grad[g] - jnp.sum(probs[g] * probs_grad[g], axis=-1, keepdims=True))
            * (HEAD_DIM ** (-0.5))
        ).astype(LOW)
        for g in groups
    ]
    query_grad = [join_heads(contract(scores_grad[g], k_both[g], 1, 0)) for g in groups]
    key_sides = [contract(scores_grad[g], q_pair[g], 0, 0) for g in groups]
    for g in groups:
        turned = query_grad[g] * cosine - half_turn(query_grad[g]) * sine
        query_low[:, chunks[g]] = turned.astype(LOW)
    key_sides = [side + pltpu.roll(side, HEAD_DIM, 1) for side in key_sides]
    value_sides = [side + pltpu.roll(side, HEAD_DIM, 1) for side in value_sides]
    first = lane_index((length, LANES)) < HEAD_DIM
    for m in range(half // LANES):
        keys_grad = jnp.where(first, key_sides[2 * m], key_sides[2 * m + 1])
        values_grad = jnp.where(first, value_sides[2 * m], value_sides[2 * m + 1])
        turned = keys_grad * cosine - half_turn(keys_grad) * sine
        keyval_low[:, chunks[m]] = turned.astype(LOW)
        keyval_low[:, half + m * LANES : half + (m + 1) * LANES] = values_grad.astype(LOW)
    for copy in copies:
        copy.wait()
    attn_in_grad = contract(query_low[...], weights[:, :width], 1, 1) + contract(
        keyval_low[...], weights[:, width : 2 * width], 1, 1
    )
    attn_in = (normed_one * gains[0:1]).astype(LOW)
    sums[:, :width] = contract(attn_in, query_low[...], 0, 0).astype(LOW)
    sums[:, width : 2 * width] = contract(attn_in, keyval_low[...], 0, 0).astype(LOW)
    attn_gain_grad = jnp.sum(attn_in_grad * normed_one, axis=0, keepdims=True)
    place = row_index((8, width))
    gain_grads = jnp.where(place == 0, attn_gain_grad, jnp.where(place == 1, moe_gain_grad, 0.0))
    sums[:, 2 * width : columns] = (
        contract(payload[:length], high, 0, 0)
        + contract(gain_grads.astype(LOW), gain_select().astype(F32).astype(LOW), 0, 0)
    ).astype(LOW)
    out_copies = store_sums(rows_ref, sums, grads_even, grads_odd, out_sems)
    scaled = attn_in_grad * gains[0:1]
    tokens_grad[...] = hidden_grad + inverse_one * (
        scaled - normed_one * jnp.mean(scaled * normed_one, axis=-1, keepdims=True)
    )
    for copy in out_copies:
        copy.wait()


def swap(values, axis, size, distance):
    return lax.ppermute(values, axis, [(i, i ^ distance) for i in range(size)])


def across(values, distance, planes):
    return swap(values, "dp", planes, distance)


def aside(values, s, owners):
    return swap(values, "expert", owners, 2 * s)


def partner(values, owners):
    return swap(values, "expert", owners, 1)


def after(values, *earlier):
    return lax.optimization_barrier((values,) + earlier)[0]


def over_chips(values, owners):
    return [values] + [aside(values, s, owners) for s in range(1, owners // 2)]


def over_cores(near, owners, *earlier):
    pieces = []
    for piece in near:
        pieces += [piece, partner(after(piece, *earlier) if earlier else piece, owners)]
    return pieces


def chips_split(values, owners, *earlier):
    half = values.shape[0] // 2
    first, second = aside(values, 1, owners), aside(values, 2, owners)
    far = [first[:half], second[half:]]
    if earlier:
        far = [after(part, *earlier) for part in far]
    far = [aside(far[0], 2, owners), aside(far[1], 1, owners)]
    return [[values], [first], [second], far]


def core_pieces(groups, owners, *earlier):
    pieces, spots = [], []
    for group in groups:
        parts = [part for part, _ in group]
        merged = parts[0] if len(parts) == 1 else jnp.concatenate(parts, axis=0)
        merged = after(merged, *earlier) if earlier else merged
        for part, spot in group:
            pieces.append(part)
            spots.append(spot)
        pieces.append(partner(merged, owners))
        spots.append([(p + 1, w) for _, spot in group for p, w in spot])
    return (pieces, spots)


def core_pieces_whole(near, owners):
    pieces = []
    for parts in near:
        piece = parts[0] if len(parts) == 1 else jnp.concatenate(parts, axis=0)
        pieces.append((piece, partner(piece, owners)))
    return pieces


def added(left, right):
    return (left.astype(F32) + right.astype(F32)).astype(LOW)


def to_owners(even, odd, owners, *earlier):
    other = partner(odd, owners)
    joined = [added(even[s], other[s]) for s in range(owners // 2)]
    if earlier:
        joined = lax.optimization_barrier(tuple(joined) + earlier)[: owners // 2]
    sent = [joined[0]] + [aside(joined[s], s, owners) for s in range(1, owners // 2)]
    return (joined, sent)


def to_neighbours(joined, owners):
    half = joined[3].shape[0] // 2
    low_turn = aside(joined[3][:half], 1, owners)
    top_turn = aside(joined[3][half:], 2, owners)
    low_turn, top_turn = lax.optimization_barrier((low_turn, top_turn))
    first = jnp.concatenate([joined[1][:half], added(joined[1][half:], top_turn)], axis=0)
    second = jnp.concatenate([added(joined[2][:half], low_turn), joined[2][half:]], axis=0)
    return (first, second)


def from_neighbours(joined, first, second, owners):
    parts = [joined[0], aside(first, 1, owners), aside(second, 2, owners)]
    return sum(part.astype(F32) for part in parts).astype(LOW)


def over_planes_sum(parts, planes):
    total = parts[0].astype(F32)
    for w in range(1, planes):
        total = total + across(parts[w], w, planes).astype(F32)
    return total


def cost(us):
    return pl.CostEstimate(flops=int(us * 1153e6), bytes_accessed=0, transcendentals=0)


def params():
    return pltpu.CompilerParams(vmem_limit_bytes=VMEM_BYTES)


def whole_spec():
    return pl.BlockSpec(memory_space=pltpu.VMEM)


def hbm_spec():
    return pl.BlockSpec(memory_space=pl.ANY)


def smem_spec():
    return pl.BlockSpec(memory_space=pltpu.SMEM)


def on_device(
    planes,
    owners,
    tokens,
    segments,
    routes,
    query_weight,
    keyval_weight,
    output_weight,
    router_weight,
    attn_gain,
    moe_gain,
    expert_up,
    expert_down,
    out_grad,
):
    length, width = tokens.shape
    if planes != 4 or owners != 8 or planes * owners * length > PIECE_LIMIT:
        return on_device_wide(
            tokens,
            segments,
            routes,
            query_weight,
            keyval_weight,
            output_weight,
            router_weight,
            attn_gain,
            moe_gain,
            expert_up,
            expert_down,
            out_grad,
        )
    local = expert_up.shape[0]
    hidden_units = expert_down.shape[2]
    block = 2 * CAP
    slots = owners // 2 * block
    plane = lax.axis_index("dp")
    owner = lax.axis_index("expert")
    share = query_weight.shape[0]
    rows = (plane ^ jnp.arange(planes))[None, :] * owners + (owner ^ jnp.arange(owners))[:, None]
    rows = rows.astype(jnp.int32)
    place = jnp.stack([owner, plane]).astype(jnp.int32)
    lanes = jnp.arange(LANES)[None, :]
    extra = jnp.pad(router_weight, ((0, 0), (0, LANES - EXPERTS)))
    extra = jnp.where(lanes == EXPERTS, attn_gain[:, None], extra)
    extra = jnp.where(lanes == EXPERTS + 1, moe_gain[:, None], extra)
    packed = jnp.concatenate([query_weight, keyval_weight, extra, output_weight], axis=1)
    columns = packed.shape[1] - width

    early = [across(packed, w, planes) for w in range(1, planes)]
    grad_chips = over_chips(out_grad, owners)
    grad_cores = partner(jnp.concatenate(grad_chips, axis=0), owners)
    gathered = jnp.stack([packed] + early)
    grad_start = after(out_grad, *early)
    grad_planes = [across(grad_start, w, planes) for w in range(1, planes)]
    near = chips_split(
        after(gathered[:, :, :columns], *grad_chips), owners, grad_planes[0]
    )
    every = list(range(planes))
    groups = [[(near[s][0], [(2 * s, w) for w in every])] for s in range(3)]
    groups += [
        [(near[3][0], [(6, w) for w in every[: planes // 2]])],
        [(near[3][1], [(6, w) for w in every[planes // 2 :]])],
    ]
    pieces, spots = core_pieces(groups, owners)
    output_near = over_chips(after(gathered[:, :, columns:], *pieces[:6], *near[3]), owners)

    half_dim = HEAD_DIM // 2
    frequency = ROPE_BASE ** (-(jnp.arange(half_dim, dtype=F32) * 2.0) / HEAD_DIM)
    frequency = jnp.tile(frequency, LANES // half_dim)[None, :]

    token_low = jax.ShapeDtypeStruct((length, width), LOW)
    token_wide = jax.ShapeDtypeStruct((length, width), F32)
    table = jax.ShapeDtypeStruct((length, LANES), F32)
    query_rot, keyval_low, mixed_low, tail, cosine, sine = pl.pallas_call(
        functools.partial(attn_forward_kernel, spots),
        out_shape=(token_low, token_low, token_low, jax.ShapeDtypeStruct((width, LANES), LOW))
        + (table, table),
        in_specs=[smem_spec()] + [whole_spec()] * 3 + [hbm_spec()] * len(pieces),
        out_specs=[whole_spec()] * 6,
        scratch_shapes=[
            pltpu.VMEM((width, columns), LOW),
            pltpu.SemaphoreType.DMA((owners, planes)),
        ],
        compiler_params=params(),
        cost_estimate=cost(6),
        name="attn_forward",
    )(rows, after(tokens, grad_planes[1]), segments, frequency, *pieces)

    output_pieces, output_spots = core_pieces(
        [[(output_near[s], [(2 * s, w) for w in every])] for s in range(owners // 2)],
        owners,
        mixed_low,
    )

    grad_stack = jnp.concatenate(grad_planes, axis=0)

    payload, hidden, gates = pl.pallas_call(
        functools.partial(router_kernel, output_spots),
        out_shape=(
            jax.ShapeDtypeStruct((length + TAIL, width), LOW),
            token_wide,
            jax.ShapeDtypeStruct((length, LANES), F32),
        ),
        in_specs=[smem_spec()] + [whole_spec()] * 4 + [hbm_spec()] * len(output_pieces),
        out_specs=[whole_spec()] * 3,
        scratch_shapes=[
            pltpu.VMEM((width, width), LOW),
            pltpu.SemaphoreType.DMA((owners, planes)),
        ],
        compiler_params=params(),
        cost_estimate=cost(4),
        name="router",
    )(
        rows,
        tokens,
        after(mixed_low, grad_cores),
        tail,
        routes.T,
        *output_pieces,
    )

    row_chips = over_chips(payload, owners)
    row_home = over_cores(row_chips[:3], owners) + over_cores(row_chips[3:], owners, grad_stack)
    grad_other = partner(after(grad_stack, payload), owners)
    row_start = after(payload, row_home[1])
    row_planes = [across(row_start, w, planes) for w in range(2, planes)]
    grad_direct = after(grad_stack, *row_chips)
    grad_near = [aside(grad_direct, s, owners) for s in (1, 2)]

    def all_of(shape):
        return pl.BlockSpec(shape, lambda i: (0,) * len(shape))

    slab = width // planes
    slabs = (
        jax.ShapeDtypeStruct((local, slab, 2 * hidden_units), F32),
        jax.ShapeDtypeStruct((local, slab, hidden_units), F32),
    )
    home_blocks = [s * (p % 2) for s in range(owners // 2) for p in range(2)]
    grad_home = [part for s in range(owners // 2) for part in (grad_chips[s], grad_cores)]
    chip_rows = jax.ShapeDtypeStruct((owners // 2, length, width), LOW)
    chip_back = jax.ShapeDtypeStruct((owners // 2, length, width + LANES), LOW)
    back_even, back_odd, *kept = pl.pallas_call(
        functools.partial(expert_home_kernel, owners, local, block),
        grid=(1,),
        out_shape=(
            chip_back,
            chip_back,
            jax.ShapeDtypeStruct((owners // 2, local * block, 2 * length), LOW),
            jax.ShapeDtypeStruct((local, slots, hidden_units), LOW),
            jax.ShapeDtypeStruct((local, slots, 2 * hidden_units), LOW),
            jax.ShapeDtypeStruct((local, slots, slab), LOW),
            jax.ShapeDtypeStruct((local, slots, slab), LOW),
        ),
        in_specs=[smem_spec()]
        + [all_of((length + TAIL, width))] * owners
        + [pl.BlockSpec((length, width), lambda i, s=s: (s, 0)) for s in home_blocks]
        + [hbm_spec()] * 2,
        out_specs=[all_of(chip_back.shape)] * 2 + [hbm_spec()] * 5,
        scratch_shapes=[
            pltpu.VMEM(expert_up.shape, LOW),
            pltpu.VMEM(expert_down.shape, LOW),
            pltpu.VMEM((local, slots, width), LOW),
            pltpu.VMEM((local, slots, width), LOW),
            pltpu.VMEM((owners // 2, local * block, 2 * length), LOW),
            pltpu.VMEM((local, slots, LANES), F32),
            pltpu.VMEM((local, slots, hidden_units), LOW),
            pltpu.VMEM((local, slots, 2 * hidden_units), LOW),
            pltpu.VMEM((local, slots, width + LANES), LOW),
            pltpu.SemaphoreType.DMA((5, local)),
        ],
        compiler_params=params(),
        cost_estimate=cost(18),
        name="expert_home",
    )(place, *row_home, *grad_home, expert_up, expert_down)
    out_even, out_odd, up_grad, down_grad = pl.pallas_call(
        functools.partial(expert_finish_kernel, local, block),
        out_shape=(chip_rows, chip_rows) + slabs,
        in_specs=[whole_spec()] * 6,
        out_specs=[whole_spec()] * 4,
        scratch_shapes=[pltpu.VMEM((local, slots, width), LOW)],
        compiler_params=params(),
        cost_estimate=cost(8),
        name="expert_finish",
    )(*kept, expert_down)

    joined, back = to_owners(back_even, after(back_odd, grad_other, *grad_near, *row_planes), owners)
    late_rows = lax.optimization_barrier(tuple(row_planes) + tuple(row_chips) + tuple(joined))
    row_stack = jnp.concatenate(late_rows[: planes - 2], axis=0)
    row_near = across(jnp.stack(late_rows[planes - 2 : planes + 2]), 1, planes)
    row_far = chips_split(after(row_stack, *back), owners)
    grad_away = [grad_stack, grad_other]
    grad_away += over_cores(grad_near, owners, *back)
    row_own = partner(after(row_stack, *joined), owners)

    def expert_away(start, count, place, up_grad, down_grad):
        chips = owners // 2
        pairs = chips * (planes - 1)
        return pl.pallas_call(
            functools.partial(
                expert_away_kernel, start, count, block, chips, planes - 2
            ),
            out_shape=slabs,
            in_specs=[smem_spec()] + [hbm_spec()] * (6 + 4 * chips),
            out_specs=[hbm_spec()] * 2,
            scratch_shapes=[
                pltpu.VMEM((count,) + expert_up.shape[1:], LOW),
                pltpu.VMEM((count,) + expert_down.shape[1:], LOW),
                pltpu.VMEM((count,) + slabs[0].shape[1:], F32),
                pltpu.VMEM((count,) + slabs[1].shape[1:], F32),
                pltpu.VMEM((pairs, 2 * (length + TAIL), width), LOW),
                pltpu.VMEM((pairs, 2 * length, width), LOW),
                pltpu.VMEM((count, pairs * block, width), LOW),
                pltpu.VMEM((count, pairs * block, width), LOW),
                pltpu.VMEM((count, pairs * block, LANES), F32),
                pltpu.SemaphoreType.DMA((6, count)),
                pltpu.SemaphoreType.DMA((2, 2, pairs)),
            ],
            input_output_aliases={5 + 4 * chips: 0, 6 + 4 * chips: 1},
            compiler_params=params(),
            cost_estimate=cost(7 * count),
            name="expert_away",
        )(place, *row_away, *grad_away, expert_up, expert_down, up_grad, down_grad)

    def share_pieces(wide):
        return jax.ShapeDtypeStruct((owners // 2, planes, share, wide), LOW)

    wide = columns + width
    tokens_grad, grads_even, grads_odd = pl.pallas_call(
        functools.partial(backward_kernel, spots, output_spots, owners // 2),
        out_shape=(token_wide, share_pieces(wide), share_pieces(wide)),
        in_specs=[smem_spec()]
        + [whole_spec()] * (12 + owners // 2)
        + [hbm_spec()] * (len(pieces) + len(output_pieces)),
        out_specs=[whole_spec()] + [hbm_spec()] * 2,
        scratch_shapes=[
            pltpu.VMEM((width, columns), LOW),
            pltpu.VMEM((width, width), LOW),
            pltpu.VMEM((width, wide), LOW),
            pltpu.VMEM((length, width), LOW),
            pltpu.VMEM((length, width), LOW),
            pltpu.SemaphoreType.DMA((owners, planes)),
            pltpu.SemaphoreType.DMA((owners, planes)),
            pltpu.SemaphoreType.DMA((owners, planes)),
        ],
        compiler_params=params(),
        cost_estimate=cost(17),
        name="backward",
    )(
        rows,
        tokens,
        segments,
        cosine,
        sine,
        payload,
        after(hidden, row_own, out_even),
        query_rot,
        keyval_low,
        mixed_low,
        gates,
        out_grad,
        tail,
        *back,
        *pieces,
        *output_pieces,
    )

    grads_other = partner(
        after(grads_odd, row_far[1][0], row_far[2][0], *grad_away[3::2]), owners
    )
    half = grad_stack.shape[0] // 2
    grad_turn = [
        aside(after(grad_near[0][:half], tokens_grad), 2, owners),
        aside(after(grad_near[1][half:], tokens_grad), 1, owners),
    ]
    shares = [added(grads_even[s], grads_other[s]) for s in range(owners // 2)]
    grad_away += over_cores([jnp.concatenate(grad_turn, axis=0)], owners, shares[0])
    row_away = over_cores([row_near], owners, shares[0]) + [row_stack, row_own]
    row_away += over_cores(
        [jnp.concatenate(parts, axis=0) for parts in row_far[1:]], owners, shares[0]
    )
    first, second = to_neighbours(shares, owners)
    out_other = partner(after(out_odd, shares[0], *row_far[3], *grad_turn), owners)
    made = [added(out_even[s], out_other[s]) for s in range(owners // 2)]
    held = (first, second) + tuple(row_away[1::2]) + tuple(grad_away[7:]) + tuple(made)
    first, second = lax.optimization_barrier(held)[:2]
    far_made = aside(after(made[3], first), 3, owners)
    up_grad, down_grad = expert_away(0, 2, after(place, first, second), up_grad, down_grad)
    plane_sums = after(from_neighbours(shares, first, second, owners), up_grad, far_made)
    up_grad, down_grad = expert_away(2, 2, after(place, plane_sums), up_grad, down_grad)
    made = lax.optimization_barrier(tuple(made) + (plane_sums,))[: owners // 2]
    near_made = [aside(made[s], s, owners) for s in (1, 2)]
    summed = over_planes_sum(plane_sums, planes)
    made = [made[0]] + near_made + [far_made]
    layer_out = (hidden + sum(part.astype(F32) for part in made)).astype(LOW)

    return (
        layer_out,
        tokens_grad,
        summed[:, :width],
        summed[:, width : 2 * width],
        summed[:, columns:],
        summed[:, 2 * width : 2 * width + EXPERTS],
        summed[:, 2 * width + EXPERTS],
        summed[:, 2 * width + EXPERTS + 1],
        up_grad,
        down_grad,
    )


def solution(mesh):
    return jax.shard_map(
        functools.partial(on_device, mesh.shape["dp"], mesh.shape["expert"]),
        mesh=mesh,
        in_specs=(
            P(("dp", "expert"), None),
            P(("dp", "expert"), None),
            P(("dp", "expert"), None),
            P(("dp", "expert"), None),
            P(("dp", "expert"), None),
            P(("dp", "expert"), None),
            P(("dp", "expert"), None),
            P(("dp", "expert")),
            P(("dp", "expert")),
            P("expert", None, None),
            P("expert", None, None),
            P(("dp", "expert"), None),
        ),
        out_specs=(
            P(("dp", "expert"), None),
            P(("dp", "expert"), None),
            P(("dp", "expert"), None),
            P(("dp", "expert"), None),
            P(("dp", "expert"), None),
            P(("dp", "expert"), None),
            P(("dp", "expert")),
            P(("dp", "expert")),
            P("expert", "dp", None),
            P("expert", "dp", None),
        ),
        check_vma=False,
    )
```
